32 devices in a mesh: dp: 16 (over z, x, core), ctx: 2 (over y).
Axes of the slice: x: 2, y: 2, z: 4, core: 2. Of those that a mesh axis runs over, the one named last changes fastest.
Arguments:
- projections: bfloat16 [8192, 6144], P(('dp', 'ctx')), may hold values from -6 to 6
- block_source: int32 [16, 2, 2], P('dp', 'ctx'), may hold values from 0 to 63, as said below
- clip_ids: int32 [16, 4], P('dp'), may hold values from 0 to 2, as said below
- out_weight: bfloat16 [2048, 1536], P('dp'), may hold values from -1 to 1
Outputs:
- mixed: bfloat16 [8192, 1536], P(('dp', 'ctx'))
The draws below stay inside these ranges and needn't reach their ends.
Inputs may be any that keep to these rules, and one draw needn't show every extreme that they name: `block_source`: arrival block a lies on the device numbered a // 2 in dp-major order (dp index a // (2 * 2), ctx index (a // 2) % 2). The block that fills pack block (o, j, l) lies on the device with the same ctx index j and dp index o or o XOR 1. Every arrival block fills exactly one pack block. `clip_ids`: in each pack the clip numbers start at 0, never fall and rise by at most one from block to block; every clip spans 1 to 2 blocks, and in every pack some clip spans exactly 2 blocks.
All inputs are finite; a program needn't handle non-finite values.
Results may differ from the reference program's by a relative error of at most 0.0057.
Values may be sent and summed in bfloat16 or wider, within the bound.
No kernel may reach another device: no remote copies, remote signals or barrier semaphores. Data moves between devices by JAX's collectives and lax.ppermute only.
A program may use at most 64 MiB of HBM per device.

```python
import math
import jax
import jax.numpy as jnp
from jax import lax

HEADS = 16
HEAD = 128
DOUT = 1536
BLK = 128
BLK_DEV = 2
HW = 2048
ROWS = 8192
N_DP = 16
N_CTX = 2


def draw_projections(key, part):
    key_base = jax.random.fold_in(key, 0)
    drawn = jnp.clip(jax.random.normal(key_base, (ROWS, HEADS, 3, HEAD), jnp.float32), -6.0, 6.0)
    return drawn.reshape(ROWS, HEADS * 3 * HEAD).astype(jnp.bfloat16)


def draw_block_source(key, part):
    window_size = 2 * BLK_DEV
    pair_count = N_DP // 2
    key_scores, key_force = jax.random.split(jax.random.fold_in(key, 11))
    scores = jax.random.randint(key_scores, (N_CTX, pair_count, window_size), 0, 1 << 20)
    scores = scores * window_size + jnp.arange(window_size, dtype=jnp.int32)
    shuffled = jnp.argsort(scores, axis=-1).astype(jnp.int32)
    forced = jax.random.randint(key_force, (N_CTX,), 0, pair_count)
    swapped = (jnp.arange(window_size, dtype=jnp.int32) + BLK_DEV) % window_size
    is_forced = jnp.arange(pair_count, dtype=jnp.int32)[None, :] == forced[:, None]
    shuffled = jnp.where(is_forced[:, :, None], swapped[None, None, :], shuffled)
    source_dp = 2 * jnp.arange(pair_count, dtype=jnp.int32)[None, :, None] + shuffled // BLK_DEV
    source_slot = shuffled % BLK_DEV
    column = jnp.arange(N_CTX, dtype=jnp.int32)[:, None, None]
    arrival = (source_dp * N_CTX + column) * BLK_DEV + source_slot
    arranged = arrival.reshape(N_CTX, N_DP, BLK_DEV)
    return jnp.transpose(arranged, (1, 0, 2)).astype(jnp.int32)


def draw_clip_ids(key, part):
    pack_blocks = BLK_DEV * N_CTX
    longest = max(pack_blocks // 2, 1)
    key_length, key_which, key_pack = jax.random.split(jax.random.fold_in(key, 23), 3)
    lengths = jax.random.randint(key_length, (N_DP, pack_blocks), 1, longest + 1)
    chosen_pack = jax.random.randint(key_pack, (), 0, N_DP)
    pack_order = jnp.arange(N_DP, dtype=jnp.int32)
    lengths = jnp.where((pack_order == chosen_pack)[:, None], 1, lengths)
    which = jax.random.randint(key_which, (N_DP,), 0, 2)
    positions = jnp.arange(pack_blocks, dtype=jnp.int32)
    lengths = jnp.where(positions[None, :] == which[:, None], longest, lengths)
    ends = jnp.cumsum(lengths, axis=1)
    clip_number = jnp.sum((ends[:, None, :] <= positions[None, :, None]).astype(jnp.int32), axis=2)
    return clip_number.astype(jnp.int32)


def steps_of(stream_key, dims, cuts, smallest, top_value):
    loudness = 1.0
    for position, blocks in cuts:
        draws = jax.random.uniform(jax.random.fold_in(jax.random.fold_in(stream_key, 6), position), (blocks,), jnp.float32, smallest / len(cuts), top_value / len(cuts))
        loudness = loudness * jnp.repeat(jnp.exp(draws), dims[position] // blocks).reshape((-1,) + (1,) * (len(dims) - 1 - position))
    return loudness


def noise(key, extent, scale, reach, cuts=(), held_as=jnp.bfloat16):
    array = scale * jax.random.normal(key, extent, jnp.float32)
    if cuts:
        array = array * steps_of(key, extent, cuts, -0.22, 0.18)
    return jnp.clip(array, -reach, reach).astype(held_as)


def setup_inputs(seed: int = 0) -> dict:
    key_of = jax.random.split(jax.random.key(seed), 5)
    return {
        "projections": draw_projections(jax.random.fold_in(key_of[4], 71), 0),
        "block_source": draw_block_source(jax.random.fold_in(key_of[4], 71), 0),
        "clip_ids": draw_clip_ids(jax.random.fold_in(key_of[4], 71), 0),
        "out_weight": noise(key_of[3], (HW, DOUT), (HW // 64) ** -0.5, 1.0, ((0, 16),)),
    }


big_negative = -1e+30

def soft_weights(scores, allowed):
    masked = jnp.where(allowed, scores, big_negative)
    row_max = lax.optimization_barrier(jnp.max(masked, axis=-1, keepdims=True))
    exponent = jnp.exp(masked - row_max)
    return (exponent / lax.optimization_barrier(jnp.sum(exponent, axis=-1, keepdims=True))).astype(jnp.bfloat16)

def reference(projections, block_source, clip_ids, out_weight):
    pack_rows = BLK_DEV * N_CTX * BLK
    blocks = projections.reshape(-1, BLK, HEADS * 3 * HEAD)
    packed = jnp.take(blocks, block_source.reshape(-1).astype(jnp.int32), axis=0)
    packed = packed.reshape(N_DP, pack_rows, HEADS, 3, HEAD)
    scaling = 1.0 / math.sqrt(HEAD)

    def one_pack(arguments):
        pack, clips = arguments
        token_clip = jnp.repeat(clips, BLK)
        allowed = token_clip[:, None] == token_clip[None, :]
        by_head = jnp.transpose(pack, (1, 0, 2, 3))

        def one_head(head_data):
            queries = head_data[:, 0].astype(jnp.float32)
            key_rows = head_data[:, 1].astype(jnp.float32)
            value_rows = head_data[:, 2].astype(jnp.float32)
            scores = jnp.einsum('qe,ke->qk', queries, key_rows) * scaling
            weights = soft_weights(scores, allowed)
            return jnp.einsum('qk,ke->qe', weights.astype(jnp.float32), value_rows).astype(jnp.bfloat16)
        attended = lax.map(one_head, by_head)
        attended = jnp.transpose(attended, (1, 0, 2)).reshape(pack_rows, HEADS * HEAD)
        return jnp.dot(attended, out_weight, preferred_element_type=jnp.float32).astype(jnp.bfloat16)
    outputs = lax.map(one_pack, (packed, clip_ids))
    return outputs.reshape(N_DP * pack_rows, DOUT)
```

```python
import functools
import math

import jax
import jax.numpy as jnp
from jax import lax
from jax.experimental import pallas as pl
from jax.experimental.pallas import tpu as pltpu
from jax.sharding import PartitionSpec as P

HEAD = 128


big_negative = -1e30
MIB = 1 << 20


def partner(value, axis, bit):
    mask = 2**bit
    pairs = [(source, source ^ mask) for source in range(lax.axis_size(axis))]
    return lax.ppermute(value, axis, pairs)


def soft_weights(scores, allowed):
    masked = jnp.where(allowed, scores, big_negative)
    row_max = jnp.max(masked, axis=-1, keepdims=True)
    exponent = jnp.exp(masked - row_max)
    return (exponent / jnp.sum(exponent, axis=-1, keepdims=True)).astype(jnp.bfloat16)


def attend_dense(queries, key_rows, value_rows, token_clip, scaling):
    token_count, head_count, head_size = queries.shape
    step_size = min(token_count, 512)
    step_count = token_count // step_size
    query_steps = queries.reshape(step_count, step_size, head_count, head_size)
    clip_steps = token_clip.reshape(step_count, step_size)

    def one_step(arguments):
        query_block, clip_block = arguments
        scores = (
            jnp.einsum("qhe,khe->hqk", query_block, key_rows, preferred_element_type=jnp.float32)
            * scaling
        )
        allowed = (clip_block[:, None] == token_clip[None, :])[None]
        weights = soft_weights(scores, allowed)
        return jnp.einsum(
            "hqk,khe->qhe", weights, value_rows, preferred_element_type=jnp.float32
        ).astype(jnp.bfloat16)

    outputs = lax.map(one_step, (query_steps, clip_steps))
    return outputs.reshape(token_count, head_count, head_size)


def body_general(projections, block_source, clip_ids, out_weight):
    ctx_count = lax.axis_size("ctx")
    local_rows, row_width = projections.shape
    local_blocks = block_source.shape[2]
    block_rows = local_rows // local_blocks
    own_blocks = projections.reshape(local_blocks, block_rows, row_width)
    partner_blocks = partner(own_blocks, "dp", 0)
    source_ids = block_source.reshape(local_blocks)
    from_partner = source_ids // (local_blocks * ctx_count) != lax.axis_index("dp")
    chosen_slot = source_ids % local_blocks + local_blocks * from_partner.astype(jnp.int32)
    candidates = jnp.concatenate([own_blocks, partner_blocks], axis=0)
    packed = jnp.take(candidates, chosen_slot, axis=0)
    local_heads = row_width // (3 * HEAD) // ctx_count
    grouped = packed.reshape(local_rows, ctx_count, local_heads, 3 * HEAD)
    block_clip = clip_ids.reshape(-1)
    token_clip = jnp.repeat(block_clip, block_rows)
    scaling = 1.0 / math.sqrt(HEAD)
    regrouped = lax.all_to_all(grouped, "ctx", split_axis=1, concat_axis=0, tiled=True)
    token_count = regrouped.shape[0]
    item_count = regrouped.shape[2]
    features = regrouped.reshape(token_count, item_count, 3 * HEAD)
    queries = features[:, :, :HEAD]
    key_rows = features[:, :, HEAD : 2 * HEAD]
    value_rows = features[:, :, 2 * HEAD :]
    attended = attend_dense(queries, key_rows, value_rows, token_clip, scaling)
    merged = attended.reshape(local_rows * ctx_count, local_heads * HEAD)
    attention_rows = lax.all_to_all(merged, "ctx", split_axis=0, concat_axis=1, tiled=True)
    result = jnp.dot(
        attention_rows,
        lax.all_gather(out_weight, "dp", axis=0, tiled=True),
        preferred_element_type=jnp.float32,
    )
    return result.astype(jnp.bfloat16)


def place(source_ref, slot):
    source = source_ref[0, 0, slot]
    own = source // (2 * source_ref.shape[2]) == lax.axis_index("dp")
    return jnp.logical_not(own), lax.rem(source, source_ref.shape[2])


def start_from(located, own_ref, partner_ref, columns, target, sem):
    away, slot = located

    @pl.when(jnp.logical_not(away))
    def _():
        pltpu.make_async_copy(own_ref.at[slot, :, columns], target, sem).start()

    @pl.when(away)
    def _():
        pltpu.make_async_copy(partner_ref.at[slot, :, columns], target, sem).start()


def wait_from(own_ref, columns, target, sem):
    pltpu.make_async_copy(own_ref.at[0, :, columns], target, sem).wait()


def head_kv(head):
    return pl.ds(head * 3 * HEAD + HEAD, 2 * HEAD)


def pack_edge_kernel(source_ref, own_ref, partner_ref, *rest):
    outs, sems = rest[:-1], rest[-1]
    edge = 1 - lax.axis_index("ctx")
    located = place(source_ref, edge)
    heads = outs[0].shape[1] // (2 * HEAD)
    copies = []
    for part, out in enumerate(outs):
        for index in range(heads):
            head = part * heads + index
            target = out.at[:, pl.ds(index * 2 * HEAD, 2 * HEAD)]
            copies.append((head_kv(head), target, sems.at[head]))
    for columns, target, sem in copies:
        start_from(located, own_ref, partner_ref, columns, target, sem)
    for columns, target, sem in copies:
        wait_from(own_ref, columns, target, sem)


def one_head(queries, keys, values, more_keys, more_values, allowed):
    scaling = math.log2(math.e) / math.sqrt(HEAD)
    contract_last = (((1,), (1,)), ((), ()))
    own = lax.dot_general(queries, keys, contract_last, preferred_element_type=jnp.float32)
    more = lax.dot_general(queries, more_keys, contract_last, preferred_element_type=jnp.float32)
    own = own * scaling
    more = jnp.where(allowed, more * scaling, big_negative)
    row_max = jnp.max(jnp.maximum(own, more), axis=-1, keepdims=True)
    own = jnp.exp2(own - row_max)
    more = jnp.exp2(more - row_max)
    total = jnp.sum(own + more, axis=-1, keepdims=True)
    weights = jnp.concatenate([own, more], axis=1).astype(jnp.bfloat16)
    both = jnp.concatenate([values, more_values], axis=0)
    mixed = jnp.dot(weights, both, preferred_element_type=jnp.float32)
    return (mixed / total).astype(jnp.bfloat16)


def inner_kernel(source_ref, clip_ref, own_ref, partner_ref, out_ref, held, sems):
    ctx = lax.axis_index("ctx")
    inner, edge = ctx, 1 - ctx
    first = ctx * 2
    allowed = clip_ref[0, first] == clip_ref[0, first + 1]
    groups = sems.shape[1]
    width = held.shape[2] // groups
    places = [place(source_ref, inner), place(source_ref, edge)]
    for group in range(groups):
        columns = pl.ds(group * width, width)
        for which in range(2):
            start_from(
                places[which],
                own_ref,
                partner_ref,
                columns,
                held.at[which, :, columns],
                sems.at[which, group],
            )
    heads = width // (3 * HEAD)
    for group in range(groups):
        columns = pl.ds(group * width, width)
        for which in range(2):
            wait_from(own_ref, columns, held.at[which, :, columns], sems.at[which, group])
        for head in range(group * heads, (group + 1) * heads):
            at = head * 3 * HEAD
            out_ref[:, head * HEAD : (head + 1) * HEAD] = one_head(
                held[0, :, at : at + HEAD],
                held[0, :, at + HEAD : at + 2 * HEAD],
                held[0, :, at + 2 * HEAD : at + 3 * HEAD],
                held[1, :, at + HEAD : at + 2 * HEAD],
                held[1, :, at + 2 * HEAD : at + 3 * HEAD],
                allowed,
            )


def edge_kernel(
    first_head, source_ref, clip_ref, own_ref, partner_ref, halo_ref, out_ref, held, other, sems, more_sems
):
    ctx = lax.axis_index("ctx")
    inner, edge = ctx, 1 - ctx
    edge_clip = clip_ref[0, 1 + ctx]
    crosses = edge_clip == clip_ref[0, 2 - ctx]
    allowed = jnp.logical_or(crosses, edge_clip == clip_ref[0, 3 * ctx])
    heads = out_ref.shape[1] // HEAD
    edge_place, inner_place = place(source_ref, edge), place(source_ref, inner)
    held_columns = [pl.ds((first_head + head) * 3 * HEAD, 3 * HEAD) for head in range(heads)]
    other_columns = [pl.ds(head * 2 * HEAD, 2 * HEAD) for head in range(heads)]
    for head in range(heads):
        start_from(
            edge_place, own_ref, partner_ref, held_columns[head], held.at[head], sems.at[head]
        )

        @pl.when(crosses)
        def _():
            pltpu.make_async_copy(
                halo_ref.at[:, other_columns[head]], other.at[head], more_sems.at[head]
            ).start()

        @pl.when(jnp.logical_not(crosses))
        def _():
            start_from(
                inner_place,
                own_ref,
                partner_ref,
                head_kv(first_head + head),
                other.at[head],
                more_sems.at[head],
            )

    for head in range(heads):
        wait_from(own_ref, held_columns[head], held.at[head], sems.at[head])
        pltpu.make_async_copy(
            halo_ref.at[:, other_columns[head]], other.at[head], more_sems.at[head]
        ).wait()
        out_ref[:, head * HEAD : (head + 1) * HEAD] = one_head(
            held[head, :, :HEAD],
            held[head, :, HEAD : 2 * HEAD],
            held[head, :, 2 * HEAD :],
            other[head, :, :HEAD],
            other[head, :, HEAD:],
            allowed,
        )


def project_kernel(shifts, inner_ref, *rest):
    pair_count = 2 * len(shifts)
    edge_refs = rest[: len(rest) - 2 * pair_count - 5]
    rest = rest[len(edge_refs) :]
    shard_refs = rest[: 2 * pair_count]
    out_ref, rows, weight, row_sems, weight_sems = rest[2 * pair_count :]
    ctx, index = lax.axis_index("ctx"), lax.axis_index("dp")
    core, side, line = lax.rem(index, 2), lax.rem(index // 2, 2), index // 4
    depth, width = weight.shape[2:]
    block = inner_ref.shape[0]
    copies = []
    inner_rows = pl.ds(pl.multiple_of(ctx * block, block), block)
    edge_rows = pl.ds(pl.multiple_of((1 - ctx) * block, block), block)
    copies.append(pltpu.make_async_copy(inner_ref, rows.at[inner_rows, :], row_sems.at[0]))
    part = edge_refs[0].shape[1]
    for number, ref in enumerate(edge_refs):
        target = rows.at[edge_rows, pl.ds(number * part, part)]
        copies.append(pltpu.make_async_copy(ref, target, row_sems.at[1 + number]))
    pair_copies = []
    for pair in range(pair_count):
        pair_copies.append(
            [
                pltpu.make_async_copy(
                    shard_refs[2 * pair], weight.at[pair, core], weight_sems.at[pair, 0]
                ),
                pltpu.make_async_copy(
                    shard_refs[2 * pair + 1], weight.at[pair, 1 - core], weight_sems.at[pair, 1]
                ),
            ]
        )
    for copy in copies:
        copy.start()
    for both in pair_copies:
        for copy in both:
            copy.start()
    for copy in copies:
        copy.wait()
    total = jnp.zeros((rows.shape[0], width), jnp.float32)
    for pair in range(pair_count):
        for copy in pair_copies[pair]:
            copy.wait()
        shift = shifts[pair // 2]
        lines = len(shifts)
        from_line = lax.rem(line + lines - shift, lines)
        from_side = side if pair % 2 == 0 else 1 - side
        first = (from_line * 2 + from_side) * 2 * depth
        features = rows[:, pl.ds(pl.multiple_of(first, 2 * depth), 2 * depth)]
        total = total + jnp.dot(
            features,
            weight[pair].reshape(2 * depth, width),
            preferred_element_type=jnp.float32,
        )
    out_ref[...] = total.astype(jnp.bfloat16)


SMEM = functools.partial(pl.BlockSpec, memory_space=pltpu.SMEM)
ANY = functools.partial(pl.BlockSpec, memory_space=pl.ANY)
VMEM = functools.partial(pl.BlockSpec, memory_space=pltpu.VMEM)


def gather_shards(shard):
    count = lax.axis_size("dp")
    lines = count // 4

    def along(value, step):
        pairs = [(source, (source + 4 * step) % count) for source in range(count)]
        return lax.ppermute(value, "dp", pairs)

    held = {0: shard}
    ahead, back = shard, shard
    for step in range(1, lines // 2 + 1):
        ahead = along(ahead, 1)
        held[step] = ahead
        if lines - step not in held:
            back = along(back, -1)
            held[lines - step] = back
    shards = []
    for value in held.values():
        across = partner(value, "dp", 1)
        shards += [value, partner(value, "dp", 0), across, partner(across, "dp", 0)]
    return list(held), shards


def body_edge(projections, block_source, clip_ids, out_weight):
    local_rows, row_width = projections.shape
    block_rows = local_rows // 2
    heads = row_width // (3 * HEAD)
    features = heads * HEAD
    parts = 2
    own = projections.reshape(2, block_rows, row_width)
    from_partner = partner(own, "dp", 0)
    shifts, shards = gather_shards(out_weight)
    bf16 = jnp.bfloat16

    packed = pl.pallas_call(
        pack_edge_kernel,
        out_shape=[jax.ShapeDtypeStruct((block_rows, 2 * features // parts), bf16)] * parts,
        in_specs=[SMEM(), ANY(), ANY()],
        out_specs=[ANY()] * parts,
        scratch_shapes=[pltpu.SemaphoreType.DMA((heads,))],
        cost_estimate=pl.CostEstimate(
            flops=0, bytes_accessed=8 * block_rows * features, transcendentals=0
        ),
        name="pack_edge",
    )(block_source, own, from_partner)
    halos = [lax.ppermute(part, "ctx", [(0, 1), (1, 0)]) for part in packed]

    def cost(head_count):
        return pl.CostEstimate(
            flops=8 * block_rows * block_rows * HEAD * head_count,
            bytes_accessed=14 * block_rows * HEAD * head_count,
            transcendentals=2 * block_rows * block_rows * head_count,
        )

    groups = 4
    inner = pl.pallas_call(
        inner_kernel,
        out_shape=jax.ShapeDtypeStruct((block_rows, features), bf16),
        in_specs=[SMEM(), SMEM(), ANY(), ANY()],
        out_specs=VMEM(),
        scratch_shapes=[
            pltpu.VMEM((2, block_rows, row_width), bf16),
            pltpu.SemaphoreType.DMA((2, groups)),
        ],
        cost_estimate=cost(heads),
        compiler_params=pltpu.CompilerParams(vmem_limit_bytes=16 * MIB),
        name="inner_rows",
    )(block_source, clip_ids, own, from_partner)

    part_heads = heads // parts
    edges = []
    for part in range(parts):
        edges.append(
            pl.pallas_call(
                functools.partial(edge_kernel, part * part_heads),
                out_shape=jax.ShapeDtypeStruct((block_rows, part_heads * HEAD), bf16),
                in_specs=[SMEM(), SMEM(), ANY(), ANY(), ANY()],
                out_specs=VMEM(),
                scratch_shapes=[
                    pltpu.VMEM((part_heads, block_rows, 3 * HEAD), bf16),
                    pltpu.VMEM((part_heads, block_rows, 2 * HEAD), bf16),
                    pltpu.SemaphoreType.DMA((part_heads,)),
                    pltpu.SemaphoreType.DMA((part_heads,)),
                ],
                cost_estimate=cost(part_heads),
                compiler_params=pltpu.CompilerParams(vmem_limit_bytes=16 * MIB),
                name="edge_rows",
            )(block_source, clip_ids, own, from_partner, halos[part])
        )

    depth, width = out_weight.shape
    pair_count = len(shards) // 2
    return pl.pallas_call(
        functools.partial(project_kernel, shifts),
        out_shape=jax.ShapeDtypeStruct((local_rows, width), bf16),
        in_specs=[ANY()] * (1 + parts + len(shards)),
        out_specs=VMEM(),
        scratch_shapes=[
            pltpu.VMEM((local_rows, features), bf16),
            pltpu.VMEM((pair_count, 2, depth, width), bf16),
            pltpu.SemaphoreType.DMA((1 + parts,)),
            pltpu.SemaphoreType.DMA((pair_count, 2)),
        ],
        cost_estimate=pl.CostEstimate(
            flops=2 * local_rows * features * width,
            bytes_accessed=2 * features * width,
            transcendentals=0,
        ),
        compiler_params=pltpu.CompilerParams(vmem_limit_bytes=24 * MIB),
        name="project",
    )(inner, *edges, *shards)


def body(projections, block_source, clip_ids, out_weight):
    heads = projections.shape[1] // (3 * HEAD)
    two_and_two = lax.axis_size("ctx") == 2 and block_source.shape[2] == 2
    whole_tiles = out_weight.shape[0] % HEAD == 0 and heads % 4 == 0
    if two_and_two and whole_tiles and lax.axis_size("dp") % 4 == 0:
        return body_edge(projections, block_source, clip_ids, out_weight)
    return body_general(projections, block_source, clip_ids, out_weight)


def solution(mesh):
    return jax.shard_map(
        body,
        mesh=mesh,
        in_specs=(P(("dp", "ctx"), None), P("dp", "ctx", None), P("dp", None), P("dp", None)),
        out_specs=P(("dp", "ctx"), None),
        check_vma=False,
    )
```

```python
import functools
import math

import jax
import jax.numpy as jnp
from jax import lax
from jax.experimental import pallas as pl
from jax.experimental.pallas import tpu as pltpu
from jax.sharding import PartitionSpec as P

HEAD = 128


big_negative = -1e30
MIB = 1 << 20


def partner(value, axis, bit):
    mask = 2**bit
    pairs = [(source, source ^ mask) for source in range(lax.axis_size(axis))]
    return lax.ppermute(value, axis, pairs)


def soft_weights(scores, allowed):
    masked = jnp.where(allowed, scores, big_negative)
    row_max = jnp.max(masked, axis=-1, keepdims=True)
    exponent = jnp.exp(masked - row_max)
    return (exponent / jnp.sum(exponent, axis=-1, keepdims=True)).astype(jnp.bfloat16)


def attend_dense(queries, key_rows, value_rows, token_clip, scaling):
    token_count, head_count, head_size = queries.shape
    step_size = min(token_count, 512)
    step_count = token_count // step_size
    query_steps = queries.reshape(step_count, step_size, head_count, head_size)
    clip_steps = token_clip.reshape(step_count, step_size)

    def one_step(arguments):
        query_block, clip_block = arguments
        scores = (
            jnp.einsum("qhe,khe->hqk", query_block, key_rows, preferred_element_type=jnp.float32)
            * scaling
        )
        allowed = (clip_block[:, None] == token_clip[None, :])[None]
        weights = soft_weights(scores, allowed)
        return jnp.einsum(
            "hqk,khe->qhe", weights, value_rows, preferred_element_type=jnp.float32
        ).astype(jnp.bfloat16)

    outputs = lax.map(one_step, (query_steps, clip_steps))
    return outputs.reshape(token_count, head_count, head_size)


def body_general(projections, block_source, clip_ids, out_weight):
    ctx_count = lax.axis_size("ctx")
    local_rows, row_width = projections.shape
    local_blocks = block_source.shape[2]
    block_rows = local_rows // local_blocks
    own_blocks = projections.reshape(local_blocks, block_rows, row_width)
    partner_blocks = partner(own_blocks, "dp", 0)
    source_ids = block_source.reshape(local_blocks)
    from_partner = source_ids // (local_blocks * ctx_count) != lax.axis_index("dp")
    chosen_slot = source_ids % local_blocks + local_blocks * from_partner.astype(jnp.int32)
    candidates = jnp.concatenate([own_blocks, partner_blocks], axis=0)
    packed = jnp.take(candidates, chosen_slot, axis=0)
    local_heads = row_width // (3 * HEAD) // ctx_count
    grouped = packed.reshape(local_rows, ctx_count, local_heads, 3 * HEAD)
    block_clip = clip_ids.reshape(-1)
    token_clip = jnp.repeat(block_clip, block_rows)
    scaling = 1.0 / math.sqrt(HEAD)
    regrouped = lax.all_to_all(grouped, "ctx", split_axis=1, concat_axis=0, tiled=True)
    token_count = regrouped.shape[0]
    item_count = regrouped.shape[2]
    features = regrouped.reshape(token_count, item_count, 3 * HEAD)
    queries = features[:, :, :HEAD]
    key_rows = features[:, :, HEAD : 2 * HEAD]
    value_rows = features[:, :, 2 * HEAD :]
    attended = attend_dense(queries, key_rows, value_rows, token_clip, scaling)
    merged = attended.reshape(local_rows * ctx_count, local_heads * HEAD)
    attention_rows = lax.all_to_all(merged, "ctx", split_axis=0, concat_axis=1, tiled=True)
    result = jnp.dot(
        attention_rows,
        lax.all_gather(out_weight, "dp", axis=0, tiled=True),
        preferred_element_type=jnp.float32,
    )
    return result.astype(jnp.bfloat16)


def place(source_ref, slot):
    source = source_ref[0, 0, slot]
    own = source // (2 * source_ref.shape[2]) == lax.axis_index("dp")
    return jnp.logical_not(own), lax.rem(source, source_ref.shape[2])


def load(located, own_ref, partner_ref, first, width):
    away, slot = located
    columns = slice(first, first + width)
    return jnp.where(away, partner_ref[slot, :, columns], own_ref[slot, :, columns])


def pack_edge_kernel(source_ref, own_ref, partner_ref, out_ref):
    edge = place(source_ref, 1 - lax.axis_index("ctx"))
    for head in range(out_ref.shape[1] // (2 * HEAD)):
        first = head * 3 * HEAD + HEAD
        out_ref[:, head * 2 * HEAD : (head + 1) * 2 * HEAD] = load(
            edge, own_ref, partner_ref, first, 2 * HEAD
        )


def attend(heads, load_queries, load_own, load_more, allowed, out_ref):
    scaling = math.log2(math.e) / math.sqrt(HEAD)
    contract_last = (((1,), (1,)), ((), ()))
    ones = jnp.ones((2 * out_ref.shape[0], HEAD), jnp.bfloat16)
    group = 4
    for start in range(0, heads, group):
        scores = []
        for head in range(start, start + group):
            queries = load_queries(head)
            pair = []
            for loader in (load_own, load_more):
                pair.append(
                    lax.dot_general(
                        queries, loader(head, 0), contract_last, preferred_element_type=jnp.float32
                    )
                    * scaling
                )
            scores.append(pair)
        weights = []
        for own, more in scores:
            more = jnp.where(allowed, more, big_negative)
            row_max = jnp.max(jnp.maximum(own, more), axis=-1, keepdims=True)
            weights.append(
                jnp.concatenate(
                    [
                        jnp.exp2(own - row_max).astype(jnp.bfloat16),
                        jnp.exp2(more - row_max).astype(jnp.bfloat16),
                    ],
                    axis=1,
                )
            )
        for head in range(start, start + group):
            values = jnp.concatenate([load_own(head, 1), load_more(head, 1)], axis=0)
            sums = jnp.dot(
                weights[head - start],
                jnp.concatenate([values, ones], axis=1),
                preferred_element_type=jnp.float32,
            )
            out_ref[:, head * HEAD : (head + 1) * HEAD] = (
                sums[:, :HEAD] / sums[:, HEAD:]
            ).astype(jnp.bfloat16)


def inner_kernel(source_ref, clip_ref, own_ref, partner_ref, out_ref):
    ctx = lax.axis_index("ctx")
    allowed = clip_ref[0, 2 * ctx] == clip_ref[0, 2 * ctx + 1]
    inner, edge = place(source_ref, ctx), place(source_ref, 1 - ctx)

    def loader(located):
        def get(head, which):
            first = head * 3 * HEAD + (1 + which) * HEAD
            return load(located, own_ref, partner_ref, first, HEAD)

        return get

    attend(
        out_ref.shape[1] // HEAD,
        lambda head: loader(inner)(head, -1),
        loader(inner),
        loader(edge),
        allowed,
        out_ref,
    )


def edge_kernel(source_ref, clip_ref, own_ref, partner_ref, halo_ref, out_ref):
    ctx = lax.axis_index("ctx")
    edge_clip = clip_ref[0, 1 + ctx]
    crosses = edge_clip == clip_ref[0, 2 - ctx]
    allowed = jnp.logical_or(crosses, edge_clip == clip_ref[0, 3 * ctx])
    inner, edge = place(source_ref, ctx), place(source_ref, 1 - ctx)

    def load_own(head, which):
        first = head * 3 * HEAD + (1 + which) * HEAD
        return load(edge, own_ref, partner_ref, first, HEAD)

    def load_more(head, which):
        first = head * 3 * HEAD + (1 + which) * HEAD
        at = (2 * head + which) * HEAD
        here = load(inner, own_ref, partner_ref, first, HEAD)
        return jnp.where(crosses, halo_ref[:, at : at + HEAD], here)

    attend(
        out_ref.shape[1] // HEAD,
        lambda head: load_own(head, -1),
        load_own,
        load_more,
        allowed,
        out_ref,
    )


def project_kernel(origins, inner_ref, edge_ref, *rest):
    shard_refs, (out_ref, features) = rest[: len(origins)], rest[len(origins) :]
    ctx, index = lax.axis_index("ctx"), lax.axis_index("dp")
    core, side, line = lax.rem(index, 2), lax.rem(index // 2, 2), index // 4
    lines = lax.axis_size("dp") // 4
    block = inner_ref.shape[0]
    depth, width = shard_refs[0].shape
    for number, (steps, other_side, other_core) in enumerate(origins):
        from_line = lax.rem(line + lines - steps, lines)
        from_side = 1 - side if other_side else side
        from_core = 1 - core if other_core else core
        shard = (from_line * 2 + from_side) * 2 + from_core
        there = pl.ds(pl.multiple_of(shard * depth, depth), depth)
        at = slice(number * depth, (number + 1) * depth)
        features[:block, at] = inner_ref[:, there]
        features[block:, at] = edge_ref[:, there]
    inner_at = pl.ds(pl.multiple_of(ctx * block, block), block)
    edge_at = pl.ds(pl.multiple_of((1 - ctx) * block, block), block)
    tile = 2 * HEAD
    for first in range(0, width, tile):
        columns = slice(first, first + tile)
        weight = jnp.concatenate([ref[:, columns] for ref in shard_refs], axis=0)
        total = jnp.dot(features[...], weight, preferred_element_type=jnp.float32)
        total = total.astype(jnp.bfloat16)
        out_ref[inner_at, columns] = total[:block]
        out_ref[edge_at, columns] = total[block:]


SMEM = functools.partial(pl.BlockSpec, memory_space=pltpu.SMEM)
VMEM = functools.partial(pl.BlockSpec, memory_space=pltpu.VMEM)


def after(value, *others):
    return lax.optimization_barrier((value, *others))[0]


def body_edge(projections, block_source, clip_ids, out_weight):
    local_rows, row_width = projections.shape
    block_rows = local_rows // 2
    heads = row_width // (3 * HEAD)
    features = heads * HEAD
    count = lax.axis_size("dp")
    lines = count // 4
    onward = [(source, (source + 4) % count) for source in range(count)]
    bf16 = jnp.bfloat16
    params = pltpu.CompilerParams(vmem_limit_bytes=16 * MIB)

    def cost(microseconds):
        return pl.CostEstimate(
            flops=0, bytes_accessed=int(3.69e6 * microseconds), transcendentals=0
        )

    own = projections.reshape(2, block_rows, row_width)

    def pack(source):
        return pl.pallas_call(
            pack_edge_kernel,
            out_shape=jax.ShapeDtypeStruct((block_rows, 2 * features), bf16),
            in_specs=[SMEM(), VMEM(), VMEM()],
            out_specs=VMEM(),
            cost_estimate=cost(1),
            compiler_params=params,
            name="pack_edge",
        )(source, own, from_partner)

    def inner_rows(source):
        return pl.pallas_call(
            inner_kernel,
            out_shape=jax.ShapeDtypeStruct((block_rows, features), bf16),
            in_specs=[SMEM(), SMEM(), VMEM(), VMEM()],
            out_specs=VMEM(),
            cost_estimate=cost(3),
            compiler_params=params,
            name="inner_rows",
        )(source, clip_ids, own, from_partner)

    def edge_rows(source):
        return pl.pallas_call(
            edge_kernel,
            out_shape=jax.ShapeDtypeStruct((block_rows, features), bf16),
            in_specs=[SMEM(), SMEM(), VMEM(), VMEM(), VMEM()],
            out_specs=VMEM(),
            cost_estimate=cost(4),
            compiler_params=params,
            name="edge_rows",
        )(source, clip_ids, own, from_partner, halo)

    shards = {}
    from_partner = partner(own, "dp", 0)
    shard, across = out_weight, None
    for step in range(lines):
        last = step == lines - 1
        onward_shard = None if last else lax.ppermute(shard, "dp", onward)
        source = after(block_source, shard)
        shards[step, False, False] = shard
        shards[step, False, True] = partner(shard, "dp", 0)
        if step:
            shards[step - 1, True, False] = across
            shards[step - 1, True, True] = partner(across, "dp", 0)
            across = partner(after(shard, across), "dp", 1)
        else:
            across = partner(shard, "dp", 1)
        done = []
        if step == 0:
            done = [pack(block_source)]
            halo = lax.ppermute(done[0], "ctx", [(0, 1), (1, 0)])
        elif step == 1:
            inner = inner_rows(source)
            done = [inner]
        if last:
            edge = edge_rows(source)
            across = after(across, edge)
        else:
            shard = after(onward_shard, *done)
    shards[lines - 1, True, False] = across
    shards[lines - 1, True, True] = partner(across, "dp", 0)
    width = out_weight.shape[1]
    return pl.pallas_call(
        functools.partial(project_kernel, list(shards)),
        out_shape=jax.ShapeDtypeStruct((local_rows, width), bf16),
        in_specs=[VMEM()] * (2 + len(shards)),
        out_specs=VMEM(),
        scratch_shapes=[
            pltpu.VMEM((local_rows, features), bf16),
        ],
        cost_estimate=cost(3),
        compiler_params=params,
        name="project",
    )(inner, edge, *shards.values())


def body(projections, block_source, clip_ids, out_weight):
    heads = projections.shape[1] // (3 * HEAD)
    two_and_two = lax.axis_size("ctx") == 2 and block_source.shape[2] == 2
    whole_tiles = out_weight.shape[0] % HEAD == 0 and heads % 8 == 0
    if two_and_two and whole_tiles and lax.axis_size("dp") % 4 == 0:
        return body_edge(projections, block_source, clip_ids, out_weight)
    return body_general(projections, block_source, clip_ids, out_weight)


def solution(mesh):
    return jax.shard_map(
        body,
        mesh=mesh,
        in_specs=(P(("dp", "ctx"), None), P("dp", "ctx", None), P("dp", None), P("dp", None)),
        out_specs=P(("dp", "ctx"), None),
        check_vma=False,
    )
```

```python
import functools
import math

import jax
import jax.numpy as jnp
from jax import lax
from jax.experimental import pallas as pl
from jax.experimental.pallas import tpu as pltpu
from jax.sharding import PartitionSpec as P

HEAD = 128


big_negative = -1e30
MIB = 1 << 20


def partner(value, axis, bit):
    mask = 2**bit
    pairs = [(source, source ^ mask) for source in range(lax.axis_size(axis))]
    return lax.ppermute(value, axis, pairs)


def soft_weights(scores, allowed):
    masked = jnp.where(allowed, scores, big_negative)
    row_max = jnp.max(masked, axis=-1, keepdims=True)
    exponent = jnp.exp(masked - row_max)
    return (exponent / jnp.sum(exponent, axis=-1, keepdims=True)).astype(jnp.bfloat16)


def attend_dense(queries, key_rows, value_rows, token_clip, scaling):
    token_count, head_count, head_size = queries.shape
    step_size = min(token_count, 512)
    step_count = token_count // step_size
    query_steps = queries.reshape(step_count, step_size, head_count, head_size)
    clip_steps = token_clip.reshape(step_count, step_size)

    def one_step(arguments):
        query_block, clip_block = arguments
        scores = (
            jnp.einsum("qhe,khe->hqk", query_block, key_rows, preferred_element_type=jnp.float32)
            * scaling
        )
        allowed = (clip_block[:, None] == token_clip[None, :])[None]
        weights = soft_weights(scores, allowed)
        return jnp.einsum(
            "hqk,khe->qhe", weights, value_rows, preferred_element_type=jnp.float32
        ).astype(jnp.bfloat16)

    outputs = lax.map(one_step, (query_steps, clip_steps))
    return outputs.reshape(token_count, head_count, head_size)


def body_general(projections, block_source, clip_ids, out_weight):
    ctx_count = lax.axis_size("ctx")
    local_rows, row_width = projections.shape
    local_blocks = block_source.shape[2]
    block_rows = local_rows // local_blocks
    own_blocks = projections.reshape(local_blocks, block_rows, row_width)
    partner_blocks = partner(own_blocks, "dp", 0)
    source_ids = block_source.reshape(local_blocks)
    from_partner = source_ids // (local_blocks * ctx_count) != lax.axis_index("dp")
    chosen_slot = source_ids % local_blocks + local_blocks * from_partner.astype(jnp.int32)
    candidates = jnp.concatenate([own_blocks, partner_blocks], axis=0)
    packed = jnp.take(candidates, chosen_slot, axis=0)
    local_heads = row_width // (3 * HEAD) // ctx_count
    grouped = packed.reshape(local_rows, ctx_count, local_heads, 3 * HEAD)
    block_clip = clip_ids.reshape(-1)
    token_clip = jnp.repeat(block_clip, block_rows)
    scaling = 1.0 / math.sqrt(HEAD)
    regrouped = lax.all_to_all(grouped, "ctx", split_axis=1, concat_axis=0, tiled=True)
    token_count = regrouped.shape[0]
    item_count = regrouped.shape[2]
    features = regrouped.reshape(token_count, item_count, 3 * HEAD)
    queries = features[:, :, :HEAD]
    key_rows = features[:, :, HEAD : 2 * HEAD]
    value_rows = features[:, :, 2 * HEAD :]
    attended = attend_dense(queries, key_rows, value_rows, token_clip, scaling)
    merged = attended.reshape(local_rows * ctx_count, local_heads * HEAD)
    attention_rows = lax.all_to_all(merged, "ctx", split_axis=0, concat_axis=1, tiled=True)
    result = jnp.dot(
        attention_rows,
        lax.all_gather(out_weight, "dp", axis=0, tiled=True),
        preferred_element_type=jnp.float32,
    )
    return result.astype(jnp.bfloat16)


def place(source_ref, slot):
    source = source_ref[0, 0, slot]
    own = source // (2 * source_ref.shape[2]) == lax.axis_index("dp")
    return jnp.logical_not(own), lax.rem(source, source_ref.shape[2])


def load(located, own_ref, partner_ref, first, width):
    away, slot = located
    columns = slice(first, first + width)
    return jnp.where(away, partner_ref[slot, :, columns], own_ref[slot, :, columns])


def pack_edge_kernel(source_ref, own_ref, partner_ref, *outs):
    edge = place(source_ref, 1 - lax.axis_index("ctx"))
    first = 0
    for out in outs:
        for at in range(0, out.shape[1], 2 * HEAD):
            out[:, at : at + 2 * HEAD] = load(edge, own_ref, partner_ref, first + HEAD, 2 * HEAD)
            first += 3 * HEAD


def attend(heads, load_queries, load_own, load_more, allowed, out_ref):
    scaling = math.log2(math.e) / math.sqrt(HEAD)
    contract_last = (((1,), (1,)), ((), ()))
    ones = jnp.ones((2 * out_ref.shape[0], HEAD), jnp.bfloat16)
    group = 4
    for start in range(0, heads, group):
        scores = []
        for head in range(start, start + group):
            queries = load_queries(head)
            pair = []
            for loader in (load_own, load_more):
                pair.append(
                    lax.dot_general(
                        queries, loader(head, 0), contract_last, preferred_element_type=jnp.float32
                    )
                    * scaling
                )
            scores.append(pair)
        weights = []
        for own, more in scores:
            more = jnp.where(allowed, more, big_negative)
            row_max = jnp.max(jnp.maximum(own, more), axis=-1, keepdims=True)
            weights.append(
                jnp.concatenate(
                    [
                        jnp.exp2(own - row_max).astype(jnp.bfloat16),
                        jnp.exp2(more - row_max).astype(jnp.bfloat16),
                    ],
                    axis=1,
                )
            )
        for head in range(start, start + group):
            values = jnp.concatenate([load_own(head, 1), load_more(head, 1)], axis=0)
            sums = jnp.dot(
                weights[head - start],
                jnp.concatenate([values, ones], axis=1),
                preferred_element_type=jnp.float32,
            )
            out_ref[:, head * HEAD : (head + 1) * HEAD] = (
                sums[:, :HEAD] / sums[:, HEAD:]
            ).astype(jnp.bfloat16)


def inner_kernel(source_ref, clip_ref, own_ref, partner_ref, out_ref):
    ctx = lax.axis_index("ctx")
    allowed = clip_ref[0, 2 * ctx] == clip_ref[0, 2 * ctx + 1]
    inner, edge = place(source_ref, ctx), place(source_ref, 1 - ctx)

    def loader(located):
        def get(head, which):
            first = head * 3 * HEAD + (1 + which) * HEAD
            return load(located, own_ref, partner_ref, first, HEAD)

        return get

    attend(
        out_ref.shape[1] // HEAD,
        lambda head: loader(inner)(head, -1),
        loader(inner),
        loader(edge),
        allowed,
        out_ref,
    )


def edge_kernel(first_head, source_ref, clip_ref, own_ref, partner_ref, halo_ref, out_ref):
    ctx = lax.axis_index("ctx")
    edge_clip = clip_ref[0, 1 + ctx]
    crosses = edge_clip == clip_ref[0, 2 - ctx]
    allowed = jnp.logical_or(crosses, edge_clip == clip_ref[0, 3 * ctx])
    inner, edge = place(source_ref, ctx), place(source_ref, 1 - ctx)

    def load_own(head, which):
        first = (first_head + head) * 3 * HEAD + (1 + which) * HEAD
        return load(edge, own_ref, partner_ref, first, HEAD)

    def load_more(head, which):
        first = (first_head + head) * 3 * HEAD + (1 + which) * HEAD
        at = (2 * head + which) * HEAD
        here = load(inner, own_ref, partner_ref, first, HEAD)
        return jnp.where(crosses, halo_ref[:, at : at + HEAD], here)

    attend(
        out_ref.shape[1] // HEAD,
        lambda head: load_own(head, -1),
        load_own,
        load_more,
        allowed,
        out_ref,
    )


def project_kernel(masks, parts, total_ref, inner_ref, *rest):
    edge_refs, shard_refs = rest[:parts], rest[parts : parts + len(masks)]
    out_ref, edge_rows, features = rest[parts + len(masks) :]
    first = 0
    for ref in edge_refs:
        edge_rows[:, first : first + ref.shape[1]] = ref[...]
        first += ref.shape[1]
    index = lax.axis_index("dp")
    block = inner_ref.shape[0]
    depth, width = shard_refs[0].shape
    for number, mask in enumerate(masks):
        there = pl.ds(pl.multiple_of(jnp.bitwise_xor(index, mask) * depth, depth), depth)
        at = slice(number * depth, (number + 1) * depth)
        features[:block, at] = inner_ref[:, there]
        features[block:, at] = edge_rows[:, there]
    ctx = lax.axis_index("ctx")
    inner_at = pl.ds(pl.multiple_of(ctx * block, block), block)
    edge_at = pl.ds(pl.multiple_of((1 - ctx) * block, block), block)
    tile = 2 * HEAD
    for first in range(0, width, tile):
        columns = slice(first, first + tile)
        weight = jnp.concatenate([ref[:, columns] for ref in shard_refs], axis=0)
        total = jnp.dot(features[...], weight, preferred_element_type=jnp.float32)
        if total_ref is None:
            out_ref[:, columns] = total
        else:
            total = (total + total_ref[:, columns]).astype(jnp.bfloat16)
            out_ref[inner_at, columns] = total[:block]
            out_ref[edge_at, columns] = total[block:]


def stage_kernel(source_ref, own_ref, out_ref, sem):
    copy = pltpu.make_async_copy(own_ref, out_ref, sem)
    copy.start()
    copy.wait()


SMEM = functools.partial(pl.BlockSpec, memory_space=pltpu.SMEM)
VMEM = functools.partial(pl.BlockSpec, memory_space=pltpu.VMEM)
ANY = functools.partial(pl.BlockSpec, memory_space=pl.ANY)


def after(value, *others):
    return lax.optimization_barrier((value, *others))[0]


def body_edge(projections, block_source, clip_ids, out_weight):
    local_rows, row_width = projections.shape
    block_rows = local_rows // 2
    heads = row_width // (3 * HEAD)
    features = heads * HEAD
    bf16 = jnp.bfloat16
    params = pltpu.CompilerParams(vmem_limit_bytes=16 * MIB)

    def call(kernel, name, microseconds, shape, in_specs, dtype=bf16, scratch=()):
        return pl.pallas_call(
            kernel,
            out_shape=jax.tree.map(
                lambda one: jax.ShapeDtypeStruct(one, dtype),
                shape,
                is_leaf=lambda one: isinstance(one, tuple),
            ),
            in_specs=in_specs,
            out_specs=[VMEM()] * len(shape) if isinstance(shape, list) else VMEM(),
            scratch_shapes=scratch,
            cost_estimate=pl.CostEstimate(
                flops=0, bytes_accessed=int(1e3 * microseconds), transcendentals=0
            ),
            compiler_params=params,
            name=name,
        )

    def along(value, pairs):
        moves = [(4 * here + rest, 4 * there + rest) for here, there in pairs for rest in range(4)]
        return lax.ppermute(value, "dp", moves)

    def to_side(value):
        return partner(value, "dp", 1)

    def to_core(value):
        return partner(value, "dp", 0)

    neighbours = [(0, 1), (1, 0), (2, 3), (3, 2)]
    middle = [(1, 2), (2, 1)]
    outward = [(1, 0), (2, 3)]
    line = lax.axis_index("dp") // 4
    at_end = jnp.logical_or(line == 0, line == 3)

    own = projections.reshape(2, block_rows, row_width)
    from_partner = to_core(own)
    shards = {0: out_weight}
    shard1 = along(shards[0], neighbours)
    next_to_middle = along(shards[0], middle)
    shards[2] = to_side(shards[0])
    staged = call(
        stage_kernel, "stage", 1.5, own.shape, [SMEM(), ANY()], scratch=[pltpu.SemaphoreType.DMA]
    )(block_source, own)
    part_heads = [heads // 2, heads // 2]
    packed = call(
        pack_edge_kernel,
        "pack_edge",
        1,
        [(block_rows, 2 * HEAD * some) for some in part_heads],
        [SMEM(), VMEM(), VMEM()],
    )(block_source, staged, from_partner)
    halos = [lax.ppermute(part, "ctx", [(0, 1), (1, 0)]) for part in packed]

    def edge_rows(part, source):
        some = part_heads[part]
        return call(
            functools.partial(edge_kernel, sum(part_heads[:part])),
            "edge_rows",
            2,
            (block_rows, some * HEAD),
            [SMEM(), SMEM()] + [VMEM()] * 3,
        )(source, clip_ids, staged, from_partner, halos[part])

    shard1, next_to_middle = lax.optimization_barrier((shard1, next_to_middle, *packed))[:2]
    shards[4] = shard1
    to_end = along(next_to_middle, outward)
    far_middle = along(shard1, middle)
    shards[6] = to_side(after(shard1, shards[2]))
    shards[5] = to_core(shard1)
    shards[3] = to_core(after(shards[2], shard1))
    shards[1] = to_core(after(shards[0], shard1))
    source = after(block_source, shards[5], shards[3], shards[1])
    inner = call(
        inner_kernel, "inner_rows", 3, (block_rows, features), [SMEM(), SMEM(), VMEM(), VMEM()]
    )(source, clip_ids, staged, from_partner)

    to_end, far_middle = lax.optimization_barrier((to_end, far_middle, inner))[:2]
    shards[8] = jnp.where(at_end, to_end, far_middle)
    far_end = along(far_middle, outward)
    shards[10] = to_side(after(shards[8], shards[6]))
    shards[9] = to_core(shards[8])
    shards[7] = to_core(after(shards[6], shards[8]))
    edges = [edge_rows(0, after(block_source, shards[9], shards[7]))]

    far_end = after(far_end, *edges)
    shards[12] = jnp.where(at_end, far_end, next_to_middle)
    shards[14] = to_side(after(shards[12], shards[10]))
    shards[13] = to_core(shards[12])
    shards[11] = to_core(after(shards[10], shards[12]))
    edges.append(edge_rows(1, after(block_source, shards[13], shards[11])))

    def project(total, shards, name, microseconds, dtype):
        kernel = functools.partial(project_kernel, list(shards), len(edges))
        if total is None:
            kernel = functools.partial(kernel, None)
        operands = [inner, *edges, *shards.values()]
        operands = operands if total is None else [total, *operands]
        depth, width = out_weight.shape
        return call(
            kernel,
            name,
            microseconds,
            (local_rows, width),
            [VMEM()] * len(operands),
            dtype=dtype,
            scratch=[
                pltpu.VMEM((block_rows, features), bf16),
                pltpu.VMEM((local_rows, len(shards) * depth), bf16),
            ],
        )(*operands)

    last = shards.pop(14)
    total = project(None, shards, "project_early", 3, jnp.float32)
    last = after(last, total)
    return project(total, {14: last, 15: to_core(last)}, "project_late", 1, bf16)


def body(projections, block_source, clip_ids, out_weight):
    heads = projections.shape[1] // (3 * HEAD)
    two_and_two = lax.axis_size("ctx") == 2 and block_source.shape[2] == 2
    whole_tiles = out_weight.shape[0] % HEAD == 0 and heads % 4 == 0
    if two_and_two and whole_tiles and lax.axis_size("dp") == 16:
        return body_edge(projections, block_source, clip_ids, out_weight)
    return body_general(projections, block_source, clip_ids, out_weight)


def solution(mesh):
    return jax.shard_map(
        body,
        mesh=mesh,
        in_specs=(P(("dp", "ctx"), None), P("dp", "ctx", None), P("dp", None), P("dp", None)),
        out_specs=P(("dp", "ctx"), None),
        check_vma=False,
    )
```

```python
import functools
import math

import jax
import jax.numpy as jnp
from jax import lax
from jax.experimental import pallas as pl
from jax.experimental.pallas import tpu as pltpu
from jax.sharding import PartitionSpec as P

HEAD = 128


big_negative = -1e30
MIB = 1 << 20


def partner(value, axis, bit):
    mask = 2**bit
    pairs = [(source, source ^ mask) for source in range(lax.axis_size(axis))]
    return lax.ppermute(value, axis, pairs)


def soft_weights(scores, allowed):
    masked = jnp.where(allowed, scores, big_negative)
    row_max = jnp.max(masked, axis=-1, keepdims=True)
    exponent = jnp.exp(masked - row_max)
    return (exponent / jnp.sum(exponent, axis=-1, keepdims=True)).astype(jnp.bfloat16)


def attend_dense(queries, key_rows, value_rows, token_clip, scaling):
    token_count, head_count, head_size = queries.shape
    step_size = min(token_count, 512)
    step_count = token_count // step_size
    query_steps = queries.reshape(step_count, step_size, head_count, head_size)
    clip_steps = token_clip.reshape(step_count, step_size)

    def one_step(arguments):
        query_block, clip_block = arguments
        scores = (
            jnp.einsum("qhe,khe->hqk", query_block, key_rows, preferred_element_type=jnp.float32)
            * scaling
        )
        allowed = (clip_block[:, None] == token_clip[None, :])[None]
        weights = soft_weights(scores, allowed)
        return jnp.einsum(
            "hqk,khe->qhe", weights, value_rows, preferred_element_type=jnp.float32
        ).astype(jnp.bfloat16)

    outputs = lax.map(one_step, (query_steps, clip_steps))
    return outputs.reshape(token_count, head_count, head_size)


def body_general(projections, block_source, clip_ids, out_weight):
    ctx_count = lax.axis_size("ctx")
    local_rows, row_width = projections.shape
    local_blocks = block_source.shape[2]
    block_rows = local_rows // local_blocks
    own_blocks = projections.reshape(local_blocks, block_rows, row_width)
    partner_blocks = partner(own_blocks, "dp", 0)
    source_ids = block_source.reshape(local_blocks)
    from_partner = source_ids // (local_blocks * ctx_count) != lax.axis_index("dp")
    chosen_slot = source_ids % local_blocks + local_blocks * from_partner.astype(jnp.int32)
    candidates = jnp.concatenate([own_blocks, partner_blocks], axis=0)
    packed = jnp.take(candidates, chosen_slot, axis=0)
    local_heads = row_width // (3 * HEAD) // ctx_count
    grouped = packed.reshape(local_rows, ctx_count, local_heads, 3 * HEAD)
    block_clip = clip_ids.reshape(-1)
    token_clip = jnp.repeat(block_clip, block_rows)
    scaling = 1.0 / math.sqrt(HEAD)
    regrouped = lax.all_to_all(grouped, "ctx", split_axis=1, concat_axis=0, tiled=True)
    token_count = regrouped.shape[0]
    item_count = regrouped.shape[2]
    features = regrouped.reshape(token_count, item_count, 3 * HEAD)
    queries = features[:, :, :HEAD]
    key_rows = features[:, :, HEAD : 2 * HEAD]
    value_rows = features[:, :, 2 * HEAD :]
    attended = attend_dense(queries, key_rows, value_rows, token_clip, scaling)
    merged = attended.reshape(local_rows * ctx_count, local_heads * HEAD)
    attention_rows = lax.all_to_all(merged, "ctx", split_axis=0, concat_axis=1, tiled=True)
    result = jnp.dot(
        attention_rows,
        lax.all_gather(out_weight, "dp", axis=0, tiled=True),
        preferred_element_type=jnp.float32,
    )
    return result.astype(jnp.bfloat16)


def pack_kernel(source_ref, own_ref, partner_ref, rows_ref, halo_ref, sems):
    ctx, dp = lax.axis_index("ctx"), lax.axis_index("dp")
    slots = own_ref.shape[0]
    for which, block in ((1, 1 - ctx), (0, ctx)):
        source = source_ref[0, 0, block]
        slot = lax.rem(source, slots)
        away = source // (2 * slots) != dp

        @pl.when(jnp.logical_not(away))
        def _():
            pltpu.make_async_copy(own_ref.at[slot], rows_ref.at[which], sems.at[which]).start()

        @pl.when(away)
        def _():
            pltpu.make_async_copy(partner_ref.at[slot], rows_ref.at[which], sems.at[which]).start()

    pltpu.make_async_copy(own_ref.at[0], rows_ref.at[1], sems.at[1]).wait()
    for head in range(halo_ref.shape[1] // (2 * HEAD)):
        first = head * 3 * HEAD + HEAD
        halo_ref[:, head * 2 * HEAD : (head + 1) * 2 * HEAD] = rows_ref[
            1, :, first : first + 2 * HEAD
        ]
    pltpu.make_async_copy(own_ref.at[0], rows_ref.at[0], sems.at[0]).wait()


def attend(heads, load_queries, load_own, load_more, allowed, out_ref):
    scaling = math.log2(math.e) / math.sqrt(HEAD)
    contract_last = (((1,), (1,)), ((), ()))
    ones = jnp.ones((2 * out_ref.shape[0], HEAD), jnp.bfloat16)
    group = 4
    for start in range(0, heads, group):
        scores = []
        for head in range(start, start + group):
            queries = load_queries(head)
            pair = []
            for loader in (load_own, load_more):
                pair.append(
                    lax.dot_general(
                        queries, loader(head, 0), contract_last, preferred_element_type=jnp.float32
                    )
                    * scaling
                )
            scores.append(pair)
        weights = []
        for own, more in scores:
            more = jnp.where(allowed, more, big_negative)
            row_max = jnp.max(jnp.maximum(own, more), axis=-1, keepdims=True)
            weights.append(
                jnp.concatenate(
                    [
                        jnp.exp2(own - row_max).astype(jnp.bfloat16),
                        jnp.exp2(more - row_max).astype(jnp.bfloat16),
                    ],
                    axis=1,
                )
            )
        for head in range(start, start + group):
            values = jnp.concatenate([load_own(head, 1), load_more(head, 1)], axis=0)
            sums = jnp.dot(
                weights[head - start],
                jnp.concatenate([values, ones], axis=1),
                preferred_element_type=jnp.float32,
            )
            out_ref[:, head * HEAD : (head + 1) * HEAD] = (
                sums[:, :HEAD] / sums[:, HEAD:]
            ).astype(jnp.bfloat16)


def inner_kernel(clip_ref, rows_ref, out_ref):
    ctx = lax.axis_index("ctx")
    allowed = clip_ref[0, 2 * ctx] == clip_ref[0, 2 * ctx + 1]

    def loader(block):
        def get(head, which):
            first = (head * 3 + 1 + which) * HEAD
            return rows_ref[block, :, first : first + HEAD]

        return get

    attend(
        out_ref.shape[1] // HEAD,
        lambda head: loader(0)(head, -1),
        loader(0),
        loader(1),
        allowed,
        out_ref,
    )


def edge_kernel(clip_ref, rows_ref, halo_ref, out_ref):
    ctx = lax.axis_index("ctx")
    edge_clip = clip_ref[0, 1 + ctx]
    crosses = edge_clip == clip_ref[0, 2 - ctx]
    allowed = jnp.logical_or(crosses, edge_clip == clip_ref[0, 3 * ctx])

    def load_own(head, which):
        first = (head * 3 + 1 + which) * HEAD
        return rows_ref[1, :, first : first + HEAD]

    def load_more(head, which):
        first = (head * 3 + 1 + which) * HEAD
        at = (2 * head + which) * HEAD
        return jnp.where(crosses, halo_ref[:, at : at + HEAD], rows_ref[0, :, first : first + HEAD])

    attend(
        out_ref.shape[1] // HEAD,
        lambda head: load_own(head, -1),
        load_own,
        load_more,
        allowed,
        out_ref,
    )


def ring_order(lines):
    return list(range(0, lines, 2)) + list(range(1, lines, 2))[::-1]


def arrange_kernel(origins, inner_ref, edge_ref, own_ref, other_ref):
    index = lax.axis_index("dp")
    core, side, line = lax.rem(index, 2), lax.rem(index // 2, 2), index // 4
    places = ring_order(lax.axis_size("dp") // 4)
    block = inner_ref.shape[0]
    depth = own_ref.shape[1] // len(origins)
    for number, (steps, other_side) in enumerate(origins):
        from_line = line
        for at, place in enumerate(places):
            from_line = jnp.where(line == place, places[at - steps], from_line)
        from_side = 1 - side if other_side else side
        at = slice(number * depth, (number + 1) * depth)
        for ref, from_core in ((own_ref, core), (other_ref, 1 - core)):
            shard = (from_line * 2 + from_side) * 2 + from_core
            there = pl.ds(pl.multiple_of(shard * depth, depth), depth)
            ref[:block, at] = inner_ref[:, there]
            ref[block:, at] = edge_ref[:, there]


def project_early_kernel(own_ref, theirs_ref, *rest):
    shard_refs, (own_total_ref, their_total_ref) = rest[:-2], rest[-2:]
    depths = sum(ref.shape[0] for ref in shard_refs)
    features = jnp.concatenate([own_ref[:, :depths], theirs_ref[:, :depths]], axis=0)
    rows = own_ref.shape[0]
    tile = 2 * HEAD
    for first in range(0, own_total_ref.shape[1], tile):
        columns = slice(first, first + tile)
        weight = jnp.concatenate([ref[:, columns] for ref in shard_refs], axis=0)
        total = jnp.dot(features, weight, preferred_element_type=jnp.float32)
        own_total_ref[:, columns] = total[:rows]
        their_total_ref[:, columns] = total[rows:].astype(jnp.bfloat16)


def project_late_kernel(own_ref, other_ref, total_ref, more_ref, *rest):
    shard_refs, out_ref = rest[:-1], rest[-1]
    depth = sum(ref.shape[0] for ref in shard_refs) // 2
    first = own_ref.shape[1] - depth
    features = jnp.concatenate([own_ref[:, first:], other_ref[:, first:]], axis=1)
    rows = own_ref.shape[0]
    block = rows // 2
    ctx = lax.axis_index("ctx")
    inner_at = pl.ds(pl.multiple_of(ctx * block, block), block)
    edge_at = pl.ds(pl.multiple_of((1 - ctx) * block, block), block)
    tile = 2 * HEAD
    for first in range(0, out_ref.shape[1], tile):
        columns = slice(first, first + tile)
        weight = jnp.concatenate([ref[:, columns] for ref in shard_refs], axis=0)
        total = jnp.dot(features, weight, preferred_element_type=jnp.float32)
        total = (total + (total_ref[:, columns] + more_ref[:, columns])).astype(jnp.bfloat16)
        out_ref[inner_at, columns] = total[:block]
        out_ref[edge_at, columns] = total[block:]


SMEM = functools.partial(pl.BlockSpec, memory_space=pltpu.SMEM)
VMEM = functools.partial(pl.BlockSpec, memory_space=pltpu.VMEM)
HBM = functools.partial(pl.BlockSpec, memory_space=pltpu.HBM)


def after(value, *others):
    return lax.optimization_barrier((value, *others))[0]


def body_edge(projections, block_source, clip_ids, out_weight):
    local_rows, row_width = projections.shape
    block_rows = local_rows // 2
    heads = row_width // (3 * HEAD)
    features = heads * HEAD
    depth, width = out_weight.shape
    count = lax.axis_size("dp")
    bf16 = jnp.bfloat16

    def call(kernel, name, shape, in_specs, dtypes=(bf16, bf16), scratch=()):
        many = isinstance(shape, list)
        shapes = [jax.ShapeDtypeStruct(*one) for one in zip(shape if many else [shape], dtypes)]
        return pl.pallas_call(
            kernel,
            out_shape=shapes if many else shapes[0],
            in_specs=in_specs,
            out_specs=[VMEM()] * len(shapes) if many else VMEM(),
            scratch_shapes=scratch,
            cost_estimate=pl.CostEstimate(flops=0, bytes_accessed=0, transcendentals=0),
            compiler_params=pltpu.CompilerParams(vmem_limit_bytes=8 * MIB),
            name=name,
        )

    def onward(value):
        places = ring_order(count // 4)
        moves = zip(places, places[1:] + places[:1], strict=True)
        return lax.ppermute(
            value, "dp", [(4 * here + rest, 4 * there + rest) for here, there in moves for rest in range(4)]
        )

    def to_side(value):
        return partner(value, "dp", 1)

    def to_core(value):
        return partner(value, "dp", 0)

    def inner_rows(*before):
        return call(inner_kernel, "inner_rows", (block_rows, features), [SMEM(), VMEM()])(
            after(clip_ids, *before), rows
        )

    own = projections.reshape(2, block_rows, row_width)
    shards = {(0, False): out_weight}
    from_partner = to_core(own)
    ahead = onward(out_weight)
    across = to_side(out_weight)
    rows, packed = call(
        pack_kernel,
        "pack",
        [(2, block_rows, row_width), (block_rows, 2 * features)],
        [SMEM(), HBM(), HBM()],
        scratch=[pltpu.SemaphoreType.DMA((2,))],
    )(block_source, own, from_partner)
    halo = lax.ppermute(packed, "ctx", [(0, 1), (1, 0)])

    ahead = after(ahead, packed)
    shards[1, False], shards[0, True] = ahead, across
    ahead, across = onward(ahead), to_side(after(ahead, across))
    inner = inner_rows(shards[1, False])

    ahead = after(ahead, inner)
    shards[2, False], shards[1, True] = ahead, across
    ahead, across = onward(ahead), to_side(after(ahead, across))
    edge = call(edge_kernel, "edge_rows", (block_rows, features), [SMEM(), VMEM(), VMEM()])(
        after(clip_ids, shards[2, False]), rows, halo
    )

    ahead = after(ahead, edge)
    shards[3, False], shards[2, True] = ahead, across
    half = depth // 2
    last = [to_side(ahead[:half]), onward(across[half:])]

    last_needed = [ahead, across]
    origins = [*shards, (3, True)]
    mine, others = call(
        functools.partial(arrange_kernel, origins),
        "arrange",
        [(local_rows, len(origins) * depth)] * 2,
        [VMEM()] * 2,
    )(inner, after(edge, *last_needed))
    theirs = to_core(others)
    total, their_total = call(
        project_early_kernel,
        "project_early",
        [(local_rows, width)] * 2,
        [VMEM()] * (2 + len(shards)),
        dtypes=[jnp.float32, bf16],
    )(mine, theirs, *shards.values())
    more = to_core(after(their_total, *last))
    last += [to_core(part) for part in last]
    return call(
        project_late_kernel, "project_late", (local_rows, width), [VMEM()] * (4 + len(last))
    )(mine, others, total, more, *last)


def body(projections, block_source, clip_ids, out_weight):
    heads = projections.shape[1] // (3 * HEAD)
    two_and_two = lax.axis_size("ctx") == 2 and block_source.shape[2] == 2
    whole_tiles = out_weight.shape[0] % HEAD == 0 and heads % 4 == 0
    if two_and_two and whole_tiles and lax.axis_size("dp") == 16:
        return body_edge(projections, block_source, clip_ids, out_weight)
    return body_general(projections, block_source, clip_ids, out_weight)


def solution(mesh):
    return jax.shard_map(
        body,
        mesh=mesh,
        in_specs=(P(("dp", "ctx"), None), P("dp", "ctx", None), P("dp", None), P("dp", None)),
        out_specs=P(("dp", "ctx"), None),
        check_vma=False,
    )
```

```python
import functools
import math

import jax
import jax.numpy as jnp
from jax import lax
from jax.experimental import pallas as pl
from jax.experimental.pallas import tpu as pltpu
from jax.sharding import PartitionSpec as P

HEAD = 128


big_negative = -1e30
MIB = 1 << 20


def partner(value, axis, bit):
    mask = 2**bit
    pairs = [(source, source ^ mask) for source in range(lax.axis_size(axis))]
    return lax.ppermute(value, axis, pairs)


def soft_weights(scores, allowed):
    masked = jnp.where(allowed, scores, big_negative)
    row_max = jnp.max(masked, axis=-1, keepdims=True)
    exponent = jnp.exp(masked - row_max)
    return (exponent / jnp.sum(exponent, axis=-1, keepdims=True)).astype(jnp.bfloat16)


def attend_dense(queries, key_rows, value_rows, token_clip, scaling):
    token_count, head_count, head_size = queries.shape
    step_size = min(token_count, 512)
    step_count = token_count // step_size
    query_steps = queries.reshape(step_count, step_size, head_count, head_size)
    clip_steps = token_clip.reshape(step_count, step_size)

    def one_step(arguments):
        query_block, clip_block = arguments
        scores = (
            jnp.einsum("qhe,khe->hqk", query_block, key_rows, preferred_element_type=jnp.float32)
            * scaling
        )
        allowed = (clip_block[:, None] == token_clip[None, :])[None]
        weights = soft_weights(scores, allowed)
        return jnp.einsum(
            "hqk,khe->qhe", weights, value_rows, preferred_element_type=jnp.float32
        ).astype(jnp.bfloat16)

    outputs = lax.map(one_step, (query_steps, clip_steps))
    return outputs.reshape(token_count, head_count, head_size)


def body_general(projections, block_source, clip_ids, out_weight):
    ctx_count = lax.axis_size("ctx")
    local_rows, row_width = projections.shape
    local_blocks = block_source.shape[2]
    block_rows = local_rows // local_blocks
    own_blocks = projections.reshape(local_blocks, block_rows, row_width)
    partner_blocks = partner(own_blocks, "dp", 0)
    source_ids = block_source.reshape(local_blocks)
    from_partner = source_ids // (local_blocks * ctx_count) != lax.axis_index("dp")
    chosen_slot = source_ids % local_blocks + local_blocks * from_partner.astype(jnp.int32)
    candidates = jnp.concatenate([own_blocks, partner_blocks], axis=0)
    packed = jnp.take(candidates, chosen_slot, axis=0)
    local_heads = row_width // (3 * HEAD) // ctx_count
    grouped = packed.reshape(local_rows, ctx_count, local_heads, 3 * HEAD)
    block_clip = clip_ids.reshape(-1)
    token_clip = jnp.repeat(block_clip, block_rows)
    scaling = 1.0 / math.sqrt(HEAD)
    regrouped = lax.all_to_all(grouped, "ctx", split_axis=1, concat_axis=0, tiled=True)
    token_count = regrouped.shape[0]
    item_count = regrouped.shape[2]
    features = regrouped.reshape(token_count, item_count, 3 * HEAD)
    queries = features[:, :, :HEAD]
    key_rows = features[:, :, HEAD : 2 * HEAD]
    value_rows = features[:, :, 2 * HEAD :]
    attended = attend_dense(queries, key_rows, value_rows, token_clip, scaling)
    merged = attended.reshape(local_rows * ctx_count, local_heads * HEAD)
    attention_rows = lax.all_to_all(merged, "ctx", split_axis=0, concat_axis=1, tiled=True)
    result = jnp.dot(
        attention_rows,
        lax.all_gather(out_weight, "dp", axis=0, tiled=True),
        preferred_element_type=jnp.float32,
    )
    return result.astype(jnp.bfloat16)


def pack_kernel(source_ref, own_ref, partner_ref, rows_ref, halo_ref, sems):
    ctx, dp = lax.axis_index("ctx"), lax.axis_index("dp")
    slots = own_ref.shape[0]
    for which, block in ((1, 1 - ctx), (0, ctx)):
        source = source_ref[0, 0, block]
        slot = lax.rem(source, slots)
        away = source // (2 * slots) != dp

        @pl.when(jnp.logical_not(away))
        def _():
            pltpu.make_async_copy(own_ref.at[slot], rows_ref.at[which], sems.at[which]).start()

        @pl.when(away)
        def _():
            pltpu.make_async_copy(partner_ref.at[slot], rows_ref.at[which], sems.at[which]).start()

    pltpu.make_async_copy(own_ref.at[0], rows_ref.at[1], sems.at[1]).wait()
    for head in range(halo_ref.shape[1] // (2 * HEAD)):
        first = head * 3 * HEAD + HEAD
        halo_ref[:, head * 2 * HEAD : (head + 1) * 2 * HEAD] = rows_ref[
            1, :, first : first + 2 * HEAD
        ]
    pltpu.make_async_copy(own_ref.at[0], rows_ref.at[0], sems.at[0]).wait()


def attend(heads, load_queries, load_own, load_more, allowed, out_ref):
    scaling = math.log2(math.e) / math.sqrt(HEAD)
    contract_last = (((1,), (1,)), ((), ()))
    ones = jnp.ones((2 * out_ref.shape[0], HEAD), jnp.bfloat16)
    group = 4
    for start in range(0, heads, group):
        scores = []
        for head in range(start, start + group):
            queries = load_queries(head)
            pair = []
            for loader in (load_own, load_more):
                pair.append(
                    lax.dot_general(
                        queries, loader(head, 0), contract_last, preferred_element_type=jnp.float32
                    )
                    * scaling
                )
            scores.append(pair)
        weights = []
        for own, more in scores:
            more = jnp.where(allowed, more, big_negative)
            row_max = jnp.max(jnp.maximum(own, more), axis=-1, keepdims=True)
            weights.append(
                jnp.concatenate(
                    [
                        jnp.exp2(own - row_max).astype(jnp.bfloat16),
                        jnp.exp2(more - row_max).astype(jnp.bfloat16),
                    ],
                    axis=1,
                )
            )
        for head in range(start, start + group):
            values = jnp.concatenate([load_own(head, 1), load_more(head, 1)], axis=0)
            sums = jnp.dot(
                weights[head - start],
                jnp.concatenate([values, ones], axis=1),
                preferred_element_type=jnp.float32,
            )
            out_ref[:, head * HEAD : (head + 1) * HEAD] = (
                sums[:, :HEAD] / sums[:, HEAD:]
            ).astype(jnp.bfloat16)


def inner_kernel(clip_ref, rows_ref, out_ref):
    ctx = lax.axis_index("ctx")
    allowed = clip_ref[0, 2 * ctx] == clip_ref[0, 2 * ctx + 1]

    def loader(block):
        def get(head, which):
            first = (head * 3 + 1 + which) * HEAD
            return rows_ref[block, :, first : first + HEAD]

        return get

    attend(
        out_ref.shape[1] // HEAD,
        lambda head: loader(0)(head, -1),
        loader(0),
        loader(1),
        allowed,
        out_ref,
    )


def edge_kernel(clip_ref, rows_ref, halo_ref, out_ref):
    ctx = lax.axis_index("ctx")
    edge_clip = clip_ref[0, 1 + ctx]
    crosses = edge_clip == clip_ref[0, 2 - ctx]
    allowed = jnp.logical_or(crosses, edge_clip == clip_ref[0, 3 * ctx])

    def load_own(head, which):
        first = (head * 3 + 1 + which) * HEAD
        return rows_ref[1, :, first : first + HEAD]

    def load_more(head, which):
        first = (head * 3 + 1 + which) * HEAD
        at = (2 * head + which) * HEAD
        return jnp.where(crosses, halo_ref[:, at : at + HEAD], rows_ref[0, :, first : first + HEAD])

    attend(
        out_ref.shape[1] // HEAD,
        lambda head: load_own(head, -1),
        load_own,
        load_more,
        allowed,
        out_ref,
    )


def ring_order(lines):
    return list(range(0, lines, 2)) + list(range(1, lines, 2))[::-1]


def arrange_kernel(origins, inner_ref, edge_ref, own_ref, other_ref):
    index = lax.axis_index("dp")
    core, side, line = lax.rem(index, 2), lax.rem(index // 2, 2), index // 4
    places = ring_order(lax.axis_size("dp") // 4)
    block = inner_ref.shape[0]
    depth = own_ref.shape[1] // len(origins)
    for number, (steps, other_side) in enumerate(origins):
        from_line = line
        for at, place in enumerate(places):
            from_line = jnp.where(line == place, places[at - steps], from_line)
        from_side = 1 - side if other_side else side
        at = slice(number * depth, (number + 1) * depth)
        for ref, from_core in ((own_ref, core), (other_ref, 1 - core)):
            shard = (from_line * 2 + from_side) * 2 + from_core
            there = pl.ds(pl.multiple_of(shard * depth, depth), depth)
            ref[:block, at] = inner_ref[:, there]
            ref[block:, at] = edge_ref[:, there]


def project_early_kernel(own_ref, theirs_ref, *rest):
    shard_refs, (own_total_ref, their_total_ref) = rest[:-2], rest[-2:]
    depths = sum(ref.shape[0] for ref in shard_refs)
    features = jnp.concatenate([own_ref[:, :depths], theirs_ref[:, :depths]], axis=0)
    rows = own_ref.shape[0]
    tile = 2 * HEAD
    for first in range(0, own_total_ref.shape[1], tile):
        columns = slice(first, first + tile)
        weight = jnp.concatenate([ref[:, columns] for ref in shard_refs], axis=0)
        total = jnp.dot(features, weight, preferred_element_type=jnp.float32)
        own_total_ref[:, columns] = total[:rows]
        their_total_ref[:, columns] = total[rows:].astype(jnp.bfloat16)


def project_late_kernel(own_ref, other_ref, total_ref, more_ref, *rest):
    shard_refs, out_ref = rest[:-1], rest[-1]
    first = own_ref.shape[1] - shard_refs[0].shape[0]
    features = jnp.concatenate([own_ref[:, first:], other_ref[:, first:]], axis=1)
    rows = own_ref.shape[0]
    block = rows // 2
    ctx = lax.axis_index("ctx")
    inner_at = pl.ds(pl.multiple_of(ctx * block, block), block)
    edge_at = pl.ds(pl.multiple_of((1 - ctx) * block, block), block)
    tile = 2 * HEAD
    for first in range(0, out_ref.shape[1], tile):
        columns = slice(first, first + tile)
        weight = jnp.concatenate([ref[:, columns] for ref in shard_refs], axis=0)
        total = jnp.dot(features, weight, preferred_element_type=jnp.float32)
        total = (total + (total_ref[:, columns] + more_ref[:, columns])).astype(jnp.bfloat16)
        out_ref[inner_at, columns] = total[:block]
        out_ref[edge_at, columns] = total[block:]


SMEM = functools.partial(pl.BlockSpec, memory_space=pltpu.SMEM)
VMEM = functools.partial(pl.BlockSpec, memory_space=pltpu.VMEM)
HBM = functools.partial(pl.BlockSpec, memory_space=pltpu.HBM)


def after(value, *others):
    return lax.optimization_barrier((value, *others))[0]


def body_edge(projections, block_source, clip_ids, out_weight):
    local_rows, row_width = projections.shape
    block_rows = local_rows // 2
    heads = row_width // (3 * HEAD)
    features = heads * HEAD
    depth, width = out_weight.shape
    count = lax.axis_size("dp")
    bf16 = jnp.bfloat16

    def call(kernel, name, shape, in_specs, dtypes=(bf16, bf16), scratch=()):
        many = isinstance(shape, list)
        shapes = [jax.ShapeDtypeStruct(*one) for one in zip(shape if many else [shape], dtypes)]
        return pl.pallas_call(
            kernel,
            out_shape=shapes if many else shapes[0],
            in_specs=in_specs,
            out_specs=[VMEM()] * len(shapes) if many else VMEM(),
            scratch_shapes=scratch,
            cost_estimate=pl.CostEstimate(flops=0, bytes_accessed=0, transcendentals=0),
            compiler_params=pltpu.CompilerParams(vmem_limit_bytes=8 * MIB),
            name=name,
        )

    def onward(value):
        places = ring_order(count // 4)
        moves = zip(places, places[1:] + places[:1], strict=True)
        return lax.ppermute(
            value, "dp", [(4 * here + rest, 4 * there + rest) for here, there in moves for rest in range(4)]
        )

    def to_side(value):
        return partner(value, "dp", 1)

    def to_core(value):
        return partner(value, "dp", 0)

    def inner_rows(*before):
        return call(inner_kernel, "inner_rows", (block_rows, features), [SMEM(), VMEM()])(
            after(clip_ids, *before), rows
        )

    own = pltpu.with_memory_space_constraint(
        projections.reshape(2, block_rows, row_width), pltpu.HBM
    )
    shards = {(0, False): out_weight}
    from_partner = pltpu.with_memory_space_constraint(to_core(own), pltpu.VMEM)
    ahead = onward(out_weight)
    across = to_side(out_weight)
    rows, packed = call(
        pack_kernel,
        "pack",
        [(2, block_rows, row_width), (block_rows, 2 * features)],
        [SMEM(), HBM(), VMEM()],
        scratch=[pltpu.SemaphoreType.DMA((2,))],
    )(block_source, own, from_partner)
    halo = lax.ppermute(packed, "ctx", [(0, 1), (1, 0)])

    ahead = after(ahead, packed)
    shards[1, False], shards[0, True] = ahead, across
    ahead, across = onward(ahead), to_side(after(ahead, across))
    inner = inner_rows(shards[1, False])

    ahead = after(ahead, inner)
    shards[2, False], shards[1, True] = ahead, across
    ahead, across = onward(ahead), to_side(after(ahead, across))
    edge = call(edge_kernel, "edge_rows", (block_rows, features), [SMEM(), VMEM(), VMEM()])(
        after(clip_ids, shards[2, False]), rows, halo
    )

    ahead = after(ahead, edge)
    shards[3, False], shards[2, True] = ahead, across
    last = to_side(after(ahead, across))

    origins = [*shards, (3, True)]
    mine, others = call(
        functools.partial(arrange_kernel, origins),
        "arrange",
        [(local_rows, len(origins) * depth)] * 2,
        [VMEM()] * 2,
    )(inner, edge)
    theirs = to_core(after(others, ahead, across))
    total, their_total = call(
        project_early_kernel,
        "project_early",
        [(local_rows, width)] * 2,
        [VMEM()] * (2 + len(shards)),
        dtypes=[jnp.float32, bf16],
    )(mine, theirs, *shards.values())
    more = to_core(after(their_total, last))
    return call(project_late_kernel, "project_late", (local_rows, width), [VMEM()] * 6)(
        mine, others, total, more, last, to_core(last)
    )


def body(projections, block_source, clip_ids, out_weight):
    heads = projections.shape[1] // (3 * HEAD)
    two_and_two = lax.axis_size("ctx") == 2 and block_source.shape[2] == 2
    whole_tiles = out_weight.shape[0] % HEAD == 0 and heads % 4 == 0
    if two_and_two and whole_tiles and lax.axis_size("dp") == 16:
        return body_edge(projections, block_source, clip_ids, out_weight)
    return body_general(projections, block_source, clip_ids, out_weight)


def solution(mesh):
    return jax.shard_map(
        body,
        mesh=mesh,
        in_specs=(P(("dp", "ctx"), None), P("dp", "ctx", None), P("dp", None), P("dp", None)),
        out_specs=P(("dp", "ctx"), None),
        check_vma=False,
    )
```

```python
import functools
import math

import jax
import jax.numpy as jnp
from jax import lax
from jax.experimental import pallas as pl
from jax.experimental.pallas import tpu as pltpu
from jax.sharding import PartitionSpec as P

HEAD = 128


big_negative = -1e30
MIB = 1 << 20


def partner(value, axis, bit):
    mask = 2**bit
    pairs = [(source, source ^ mask) for source in range(lax.axis_size(axis))]
    return lax.ppermute(value, axis, pairs)


def soft_weights(scores, allowed):
    masked = jnp.where(allowed, scores, big_negative)
    row_max = jnp.max(masked, axis=-1, keepdims=True)
    exponent = jnp.exp(masked - row_max)
    return (exponent / jnp.sum(exponent, axis=-1, keepdims=True)).astype(jnp.bfloat16)


def attend_dense(queries, key_rows, value_rows, token_clip, scaling):
    token_count, head_count, head_size = queries.shape
    step_size = min(token_count, 512)
    step_count = token_count // step_size
    query_steps = queries.reshape(step_count, step_size, head_count, head_size)
    clip_steps = token_clip.reshape(step_count, step_size)

    def one_step(arguments):
        query_block, clip_block = arguments
        scores = (
            jnp.einsum("qhe,khe->hqk", query_block, key_rows, preferred_element_type=jnp.float32)
            * scaling
        )
        allowed = (clip_block[:, None] == token_clip[None, :])[None]
        weights = soft_weights(scores, allowed)
        return jnp.einsum(
            "hqk,khe->qhe", weights, value_rows, preferred_element_type=jnp.float32
        ).astype(jnp.bfloat16)

    outputs = lax.map(one_step, (query_steps, clip_steps))
    return outputs.reshape(token_count, head_count, head_size)


def body_general(projections, block_source, clip_ids, out_weight):
    ctx_count = lax.axis_size("ctx")
    local_rows, row_width = projections.shape
    local_blocks = block_source.shape[2]
    block_rows = local_rows // local_blocks
    own_blocks = projections.reshape(local_blocks, block_rows, row_width)
    partner_blocks = partner(own_blocks, "dp", 0)
    source_ids = block_source.reshape(local_blocks)
    from_partner = source_ids // (local_blocks * ctx_count) != lax.axis_index("dp")
    chosen_slot = source_ids % local_blocks + local_blocks * from_partner.astype(jnp.int32)
    candidates = jnp.concatenate([own_blocks, partner_blocks], axis=0)
    packed = jnp.take(candidates, chosen_slot, axis=0)
    local_heads = row_width // (3 * HEAD) // ctx_count
    grouped = packed.reshape(local_rows, ctx_count, local_heads, 3 * HEAD)
    block_clip = clip_ids.reshape(-1)
    token_clip = jnp.repeat(block_clip, block_rows)
    scaling = 1.0 / math.sqrt(HEAD)
    regrouped = lax.all_to_all(grouped, "ctx", split_axis=1, concat_axis=0, tiled=True)
    token_count = regrouped.shape[0]
    item_count = regrouped.shape[2]
    features = regrouped.reshape(token_count, item_count, 3 * HEAD)
    queries = features[:, :, :HEAD]
    key_rows = features[:, :, HEAD : 2 * HEAD]
    value_rows = features[:, :, 2 * HEAD :]
    attended = attend_dense(queries, key_rows, value_rows, token_clip, scaling)
    merged = attended.reshape(local_rows * ctx_count, local_heads * HEAD)
    attention_rows = lax.all_to_all(merged, "ctx", split_axis=0, concat_axis=1, tiled=True)
    result = jnp.dot(
        attention_rows,
        lax.all_gather(out_weight, "dp", axis=0, tiled=True),
        preferred_element_type=jnp.float32,
    )
    return result.astype(jnp.bfloat16)


def stage_kernel(source_ref, own_ref, out_ref, sem):
    copy = pltpu.make_async_copy(own_ref, out_ref, sem)
    copy.start()
    copy.wait()


def pack_kernel(source_ref, own_ref, partner_ref, rows_ref, *rest):
    halo_refs, sems = rest[:-1], rest[-1]
    ctx, dp = lax.axis_index("ctx"), lax.axis_index("dp")
    slots = own_ref.shape[0]
    for which, block in ((1, 1 - ctx), (0, ctx)):
        source = source_ref[0, 0, block]
        slot = lax.rem(source, slots)
        away = source // (2 * slots) != dp

        @pl.when(jnp.logical_not(away))
        def _():
            pltpu.make_async_copy(own_ref.at[slot], rows_ref.at[which], sems.at[which]).start()

        @pl.when(away)
        def _():
            pltpu.make_async_copy(partner_ref.at[slot], rows_ref.at[which], sems.at[which]).start()

    pltpu.make_async_copy(own_ref.at[0], rows_ref.at[1], sems.at[1]).wait()
    first = HEAD
    for halo_ref in halo_refs:
        for at in range(0, halo_ref.shape[1], 2 * HEAD):
            halo_ref[:, at : at + 2 * HEAD] = rows_ref[1, :, first : first + 2 * HEAD]
            first += 3 * HEAD
    pltpu.make_async_copy(own_ref.at[0], rows_ref.at[0], sems.at[0]).wait()


def attend(heads, load_queries, load_own, load_more, allowed, out_ref):
    scaling = math.log2(math.e) / math.sqrt(HEAD)
    contract_last = (((1,), (1,)), ((), ()))
    ones = jnp.ones((2 * out_ref.shape[0], HEAD), jnp.bfloat16)
    group = 4
    for start in range(0, heads, group):
        scores = []
        for head in range(start, start + group):
            queries = load_queries(head)
            pair = []
            for loader in (load_own, load_more):
                pair.append(
                    lax.dot_general(
                        queries, loader(head, 0), contract_last, preferred_element_type=jnp.float32
                    )
                    * scaling
                )
            scores.append(pair)
        weights = []
        for own, more in scores:
            more = jnp.where(allowed, more, big_negative)
            row_max = jnp.max(jnp.maximum(own, more), axis=-1, keepdims=True)
            weights.append(
                jnp.concatenate(
                    [
                        jnp.exp2(own - row_max).astype(jnp.bfloat16),
                        jnp.exp2(more - row_max).astype(jnp.bfloat16),
                    ],
                    axis=1,
                )
            )
        for head in range(start, start + group):
            values = jnp.concatenate([load_own(head, 1), load_more(head, 1)], axis=0)
            sums = jnp.dot(
                weights[head - start],
                jnp.concatenate([values, ones], axis=1),
                preferred_element_type=jnp.float32,
            )
            out_ref[:, head * HEAD : (head + 1) * HEAD] = (
                sums[:, :HEAD] / sums[:, HEAD:]
            ).astype(jnp.bfloat16)


def inner_kernel(clip_ref, rows_ref, out_ref):
    ctx = lax.axis_index("ctx")
    allowed = clip_ref[0, 2 * ctx] == clip_ref[0, 2 * ctx + 1]

    def loader(block):
        def get(head, which):
            first = (head * 3 + 1 + which) * HEAD
            return rows_ref[block, :, first : first + HEAD]

        return get

    attend(
        out_ref.shape[1] // HEAD,
        lambda head: loader(0)(head, -1),
        loader(0),
        loader(1),
        allowed,
        out_ref,
    )


def edge_kernel(first_head, clip_ref, rows_ref, halo_ref, out_ref):
    ctx = lax.axis_index("ctx")
    edge_clip = clip_ref[0, 1 + ctx]
    crosses = edge_clip == clip_ref[0, 2 - ctx]
    allowed = jnp.logical_or(crosses, edge_clip == clip_ref[0, 3 * ctx])

    def load_own(head, which):
        first = ((first_head + head) * 3 + 1 + which) * HEAD
        return rows_ref[1, :, first : first + HEAD]

    def load_more(head, which):
        first = ((first_head + head) * 3 + 1 + which) * HEAD
        at = (2 * head + which) * HEAD
        return jnp.where(crosses, halo_ref[:, at : at + HEAD], rows_ref[0, :, first : first + HEAD])

    attend(
        out_ref.shape[1] // HEAD,
        lambda head: load_own(head, -1),
        load_own,
        load_more,
        allowed,
        out_ref,
    )


def ring_order(lines):
    return list(range(0, lines, 2)) + list(range(1, lines, 2))[::-1]


def arrange_kernel(origins, parts, inner_ref, *rest):
    edge_refs, (own_ref, *other_refs, edge_rows) = rest[:parts], rest[parts:]
    first = 0
    for ref in edge_refs:
        edge_rows[:, first : first + ref.shape[1]] = ref[...]
        first += ref.shape[1]
    index = lax.axis_index("dp")
    core, side, line = lax.rem(index, 2), lax.rem(index // 2, 2), index // 4
    places = ring_order(lax.axis_size("dp") // 4)
    block = inner_ref.shape[0]
    depth = own_ref.shape[1] // len(origins)
    for number, (steps, other_side) in enumerate(origins):
        from_line = line
        for at, place in enumerate(places):
            from_line = jnp.where(line == place, places[at - steps], from_line)
        from_side = 1 - side if other_side else side
        part, place = divmod(number, len(origins) // len(other_refs))
        for ref, at, from_core in ((own_ref, number, core), (other_refs[part], place, 1 - core)):
            shard = (from_line * 2 + from_side) * 2 + from_core
            there = pl.ds(pl.multiple_of(shard * depth, depth), depth)
            at = slice(at * depth, (at + 1) * depth)
            ref[:block, at] = inner_ref[:, there]
            ref[block:, at] = edge_rows[:, there]


def project_early_kernel(parts, own_ref, *rest):
    their_refs, shard_refs, (own_total_ref, their_total_ref) = rest[:parts], rest[parts:-2], rest[-2:]
    depths = sum(ref.shape[0] for ref in shard_refs)
    theirs = jnp.concatenate([ref[...] for ref in their_refs], axis=1)
    features = jnp.concatenate([own_ref[:, :depths], theirs[:, :depths]], axis=0)
    rows = own_ref.shape[0]
    tile = 2 * HEAD
    for first in range(0, own_total_ref.shape[1], tile):
        columns = slice(first, first + tile)
        weight = jnp.concatenate([ref[:, columns] for ref in shard_refs], axis=0)
        total = jnp.dot(features, weight, preferred_element_type=jnp.float32)
        own_total_ref[:, columns] = total[:rows]
        their_total_ref[:, columns] = total[rows:].astype(jnp.bfloat16)


def project_late_kernel(own_ref, other_ref, total_ref, more_ref, *rest):
    shard_refs, out_ref = rest[:-1], rest[-1]
    depth = sum(ref.shape[0] for ref in shard_refs) // 2
    features = jnp.concatenate([own_ref[:, -depth:], other_ref[:, -depth:]], axis=1)
    rows = own_ref.shape[0]
    block = rows // 2
    ctx = lax.axis_index("ctx")
    inner_at = pl.ds(pl.multiple_of(ctx * block, block), block)
    edge_at = pl.ds(pl.multiple_of((1 - ctx) * block, block), block)
    tile = 2 * HEAD
    for first in range(0, out_ref.shape[1], tile):
        columns = slice(first, first + tile)
        weight = jnp.concatenate([ref[:, columns] for ref in shard_refs], axis=0)
        total = jnp.dot(features, weight, preferred_element_type=jnp.float32)
        total = (total + (total_ref[:, columns] + more_ref[:, columns])).astype(jnp.bfloat16)
        out_ref[inner_at, columns] = total[:block]
        out_ref[edge_at, columns] = total[block:]


SMEM = functools.partial(pl.BlockSpec, memory_space=pltpu.SMEM)
VMEM = functools.partial(pl.BlockSpec, memory_space=pltpu.VMEM)
HBM = functools.partial(pl.BlockSpec, memory_space=pltpu.HBM)


def after(value, *others):
    return lax.optimization_barrier((value, *others))[0]


def body_edge(projections, block_source, clip_ids, out_weight):
    local_rows, row_width = projections.shape
    block_rows = local_rows // 2
    heads = row_width // (3 * HEAD)
    features = heads * HEAD
    depth, width = out_weight.shape
    count = lax.axis_size("dp")
    bf16 = jnp.bfloat16

    def call(kernel, name, shape, in_specs, dtypes=None, scratch=()):
        many = isinstance(shape, list)
        shapes = shape if many else [shape]
        dtypes = dtypes or [bf16] * len(shapes)
        shapes = [jax.ShapeDtypeStruct(*one) for one in zip(shapes, dtypes, strict=True)]
        return pl.pallas_call(
            kernel,
            out_shape=shapes if many else shapes[0],
            in_specs=in_specs,
            out_specs=[VMEM()] * len(shapes) if many else VMEM(),
            scratch_shapes=scratch,
            cost_estimate=pl.CostEstimate(flops=0, bytes_accessed=0, transcendentals=0),
            compiler_params=pltpu.CompilerParams(vmem_limit_bytes=8 * MIB),
            name=name,
        )

    def onward(value):
        places = ring_order(count // 4)
        moves = zip(places, places[1:] + places[:1], strict=True)
        return lax.ppermute(
            value, "dp", [(4 * here + rest, 4 * there + rest) for here, there in moves for rest in range(4)]
        )

    def to_side(value):
        return partner(value, "dp", 1)

    def to_core(value):
        return partner(value, "dp", 0)

    def inner_rows(*before):
        return call(inner_kernel, "inner_rows", (block_rows, features), [SMEM(), VMEM()])(
            after(clip_ids, *before), rows
        )

    own = pltpu.with_memory_space_constraint(
        projections.reshape(2, block_rows, row_width), pltpu.HBM
    )
    shards = {(0, False): [out_weight]}
    from_partner = pltpu.with_memory_space_constraint(to_core(own), pltpu.VMEM)
    ahead = onward(out_weight)
    across = to_side(out_weight)
    staged = call(
        stage_kernel,
        "stage",
        own.shape,
        [SMEM(), HBM()],
        scratch=[pltpu.SemaphoreType.DMA],
    )(block_source, own)
    part_heads = [heads // 2, heads // 2]
    rows, *packed = call(
        pack_kernel,
        "pack",
        [(2, block_rows, row_width)] + [(block_rows, 2 * HEAD * some) for some in part_heads],
        [SMEM(), VMEM(), VMEM()],
        scratch=[pltpu.SemaphoreType.DMA((2,))],
    )(block_source, staged, from_partner)
    halos = [lax.ppermute(part, "ctx", [(0, 1), (1, 0)]) for part in packed]

    def edge_rows(part, *before):
        some = part_heads[part]
        return call(
            functools.partial(edge_kernel, sum(part_heads[:part])),
            "edge_rows",
            (block_rows, some * HEAD),
            [SMEM(), VMEM(), VMEM()],
        )(after(clip_ids, *before), rows, halos[part])

    ahead = after(ahead, *packed)
    shards[1, False], shards[0, True] = [ahead], [across]
    ahead, across = onward(ahead), to_side(after(ahead, across))
    inner = inner_rows(*shards[1, False])

    edges = [edge_rows(0, inner)]
    ahead = after(ahead, *edges)
    shards[2, False], shards[1, True] = [ahead], [across]
    half = depth // 2
    halves = [onward(ahead[:half]), onward(ahead[half:])]
    across = to_side(after(ahead, across))
    edges.append(edge_rows(1, ahead))

    shards[3, False], shards[2, True] = halves, [across]
    last = [
        to_side(after(halves[0], halos[1])),
        to_side(after(halves[1], across, edges[1])),
    ]
    ready = to_core(last[0][: half // 2])
    last[1] = after(last[1], ready)
    last_swapped = [ready, to_core(last[0][half // 2 :]), to_core(last[1])]

    origins = [*shards, (3, True)]
    parts = 1
    mine, *others = call(
        functools.partial(arrange_kernel, origins, len(edges)),
        "arrange",
        [(local_rows, len(origins) * depth)] * 2,
        [VMEM()] * (1 + len(edges)),
        scratch=[pltpu.VMEM((block_rows, features), bf16)],
    )(inner, *edges)
    theirs = [to_core(part) for part in others]
    early = [part for shard in shards.values() for part in shard]
    total, their_total = call(
        functools.partial(project_early_kernel, parts),
        "project_early",
        [(local_rows, width)] * 2,
        [VMEM()] * (1 + parts + len(early)),
        dtypes=[jnp.float32, bf16],
    )(mine, *theirs, *early)
    more = to_core(after(their_total, last[1]))
    late = [*last, *last_swapped]
    return call(
        project_late_kernel, "project_late", (local_rows, width), [VMEM()] * (4 + len(late))
    )(mine, others[-1], total, more, *late)


def body(projections, block_source, clip_ids, out_weight):
    heads = projections.shape[1] // (3 * HEAD)
    two_and_two = lax.axis_size("ctx") == 2 and block_source.shape[2] == 2
    whole_tiles = out_weight.shape[0] % HEAD == 0 and heads % 4 == 0
    if two_and_two and whole_tiles and lax.axis_size("dp") == 16:
        return body_edge(projections, block_source, clip_ids, out_weight)
    return body_general(projections, block_source, clip_ids, out_weight)


def solution(mesh):
    return jax.shard_map(
        body,
        mesh=mesh,
        in_specs=(P(("dp", "ctx"), None), P("dp", "ctx", None), P("dp", None), P("dp", None)),
        out_specs=P(("dp", "ctx"), None),
        check_vma=False,
    )
```

```python
import functools
import math

import jax
import jax.numpy as jnp
from jax import lax
from jax.experimental import pallas as pl
from jax.experimental.pallas import tpu as pltpu
from jax.sharding import PartitionSpec as P

HEAD = 128


big_negative = -1e30
MIB = 1 << 20


def partner(value, axis, bit):
    mask = 2**bit
    pairs = [(source, source ^ mask) for source in range(lax.axis_size(axis))]
    return lax.ppermute(value, axis, pairs)


def soft_weights(scores, allowed):
    masked = jnp.where(allowed, scores, big_negative)
    row_max = jnp.max(masked, axis=-1, keepdims=True)
    exponent = jnp.exp(masked - row_max)
    return (exponent / jnp.sum(exponent, axis=-1, keepdims=True)).astype(jnp.bfloat16)


def attend_dense(queries, key_rows, value_rows, token_clip, scaling):
    token_count, head_count, head_size = queries.shape
    step_size = min(token_count, 512)
    step_count = token_count // step_size
    query_steps = queries.reshape(step_count, step_size, head_count, head_size)
    clip_steps = token_clip.reshape(step_count, step_size)

    def one_step(arguments):
        query_block, clip_block = arguments
        scores = (
            jnp.einsum("qhe,khe->hqk", query_block, key_rows, preferred_element_type=jnp.float32)
            * scaling
        )
        allowed = (clip_block[:, None] == token_clip[None, :])[None]
        weights = soft_weights(scores, allowed)
        return jnp.einsum(
            "hqk,khe->qhe", weights, value_rows, preferred_element_type=jnp.float32
        ).astype(jnp.bfloat16)

    outputs = lax.map(one_step, (query_steps, clip_steps))
    return outputs.reshape(token_count, head_count, head_size)


def body_general(projections, block_source, clip_ids, out_weight):
    ctx_count = lax.axis_size("ctx")
    local_rows, row_width = projections.shape
    local_blocks = block_source.shape[2]
    block_rows = local_rows // local_blocks
    own_blocks = projections.reshape(local_blocks, block_rows, row_width)
    partner_blocks = partner(own_blocks, "dp", 0)
    source_ids = block_source.reshape(local_blocks)
    from_partner = source_ids // (local_blocks * ctx_count) != lax.axis_index("dp")
    chosen_slot = source_ids % local_blocks + local_blocks * from_partner.astype(jnp.int32)
    candidates = jnp.concatenate([own_blocks, partner_blocks], axis=0)
    packed = jnp.take(candidates, chosen_slot, axis=0)
    local_heads = row_width // (3 * HEAD) // ctx_count
    grouped = packed.reshape(local_rows, ctx_count, local_heads, 3 * HEAD)
    block_clip = clip_ids.reshape(-1)
    token_clip = jnp.repeat(block_clip, block_rows)
    scaling = 1.0 / math.sqrt(HEAD)
    regrouped = lax.all_to_all(grouped, "ctx", split_axis=1, concat_axis=0, tiled=True)
    token_count = regrouped.shape[0]
    item_count = regrouped.shape[2]
    features = regrouped.reshape(token_count, item_count, 3 * HEAD)
    queries = features[:, :, :HEAD]
    key_rows = features[:, :, HEAD : 2 * HEAD]
    value_rows = features[:, :, 2 * HEAD :]
    attended = attend_dense(queries, key_rows, value_rows, token_clip, scaling)
    merged = attended.reshape(local_rows * ctx_count, local_heads * HEAD)
    attention_rows = lax.all_to_all(merged, "ctx", split_axis=0, concat_axis=1, tiled=True)
    result = jnp.dot(
        attention_rows,
        lax.all_gather(out_weight, "dp", axis=0, tiled=True),
        preferred_element_type=jnp.float32,
    )
    return result.astype(jnp.bfloat16)


def stage_kernel(source_ref, own_ref, out_ref, sem):
    copy = pltpu.make_async_copy(own_ref, out_ref, sem)
    copy.start()
    copy.wait()


def pack_kernel(source_ref, own_ref, partner_ref, rows_ref, *rest):
    halo_refs, sems = rest[:-1], rest[-1]
    ctx, dp = lax.axis_index("ctx"), lax.axis_index("dp")
    slots = own_ref.shape[0]
    for which, block in ((1, 1 - ctx), (0, ctx)):
        source = source_ref[0, 0, block]
        slot = lax.rem(source, slots)
        away = source // (2 * slots) != dp

        @pl.when(jnp.logical_not(away))
        def _():
            pltpu.make_async_copy(own_ref.at[slot], rows_ref.at[which], sems.at[which]).start()

        @pl.when(away)
        def _():
            pltpu.make_async_copy(partner_ref.at[slot], rows_ref.at[which], sems.at[which]).start()

    pltpu.make_async_copy(own_ref.at[0], rows_ref.at[1], sems.at[1]).wait()
    first = HEAD
    for halo_ref in halo_refs:
        for at in range(0, halo_ref.shape[1], 2 * HEAD):
            halo_ref[:, at : at + 2 * HEAD] = rows_ref[1, :, first : first + 2 * HEAD]
            first += 3 * HEAD
    pltpu.make_async_copy(own_ref.at[0], rows_ref.at[0], sems.at[0]).wait()


def attend(heads, load_queries, load_own, load_more, allowed, out_ref):
    scaling = math.log2(math.e) / math.sqrt(HEAD)
    contract_last = (((1,), (1,)), ((), ()))
    ones = jnp.ones((2 * out_ref.shape[0], HEAD), jnp.bfloat16)
    group = 4
    for start in range(0, heads, group):
        scores = []
        for head in range(start, start + group):
            queries = load_queries(head)
            pair = []
            for loader in (load_own, load_more):
                pair.append(
                    lax.dot_general(
                        queries, loader(head, 0), contract_last, preferred_element_type=jnp.float32
                    )
                    * scaling
                )
            scores.append(pair)
        weights = []
        for own, more in scores:
            more = jnp.where(allowed, more, big_negative)
            row_max = jnp.max(jnp.maximum(own, more), axis=-1, keepdims=True)
            weights.append(
                jnp.concatenate(
                    [
                        jnp.exp2(own - row_max).astype(jnp.bfloat16),
                        jnp.exp2(more - row_max).astype(jnp.bfloat16),
                    ],
                    axis=1,
                )
            )
        for head in range(start, start + group):
            values = jnp.concatenate([load_own(head, 1), load_more(head, 1)], axis=0)
            sums = jnp.dot(
                weights[head - start],
                jnp.concatenate([values, ones], axis=1),
                preferred_element_type=jnp.float32,
            )
            out_ref[:, head * HEAD : (head + 1) * HEAD] = (
                sums[:, :HEAD] / sums[:, HEAD:]
            ).astype(jnp.bfloat16)


def inner_kernel(clip_ref, rows_ref, out_ref):
    ctx = lax.axis_index("ctx")
    allowed = clip_ref[0, 2 * ctx] == clip_ref[0, 2 * ctx + 1]

    def loader(block):
        def get(head, which):
            first = (head * 3 + 1 + which) * HEAD
            return rows_ref[block, :, first : first + HEAD]

        return get

    attend(
        out_ref.shape[1] // HEAD,
        lambda head: loader(0)(head, -1),
        loader(0),
        loader(1),
        allowed,
        out_ref,
    )


def edge_kernel(first_head, clip_ref, rows_ref, halo_ref, out_ref):
    ctx = lax.axis_index("ctx")
    edge_clip = clip_ref[0, 1 + ctx]
    crosses = edge_clip == clip_ref[0, 2 - ctx]
    allowed = jnp.logical_or(crosses, edge_clip == clip_ref[0, 3 * ctx])

    def load_own(head, which):
        first = ((first_head + head) * 3 + 1 + which) * HEAD
        return rows_ref[1, :, first : first + HEAD]

    def load_more(head, which):
        first = ((first_head + head) * 3 + 1 + which) * HEAD
        at = (2 * head + which) * HEAD
        return jnp.where(crosses, halo_ref[:, at : at + HEAD], rows_ref[0, :, first : first + HEAD])

    attend(
        out_ref.shape[1] // HEAD,
        lambda head: load_own(head, -1),
        load_own,
        load_more,
        allowed,
        out_ref,
    )


def ring_order(lines):
    return list(range(0, lines, 2)) + list(range(1, lines, 2))[::-1]


def arrange_kernel(origins, parts, inner_ref, *rest):
    edge_refs, (own_ref, *other_refs, edge_rows) = rest[:parts], rest[parts:]
    first = 0
    for ref in edge_refs:
        edge_rows[:, first : first + ref.shape[1]] = ref[...]
        first += ref.shape[1]
    index = lax.axis_index("dp")
    core, side, line = lax.rem(index, 2), lax.rem(index // 2, 2), index // 4
    places = ring_order(lax.axis_size("dp") // 4)
    block = inner_ref.shape[0]
    depth = own_ref.shape[1] // len(origins)
    for number, (steps, other_side) in enumerate(origins):
        from_line = line
        for at, place in enumerate(places):
            from_line = jnp.where(line == place, places[at - steps], from_line)
        from_side = 1 - side if other_side else side
        part, place = divmod(number, len(origins) // len(other_refs))
        for ref, at, from_core in ((own_ref, number, core), (other_refs[part], place, 1 - core)):
            shard = (from_line * 2 + from_side) * 2 + from_core
            there = pl.ds(pl.multiple_of(shard * depth, depth), depth)
            at = slice(at * depth, (at + 1) * depth)
            ref[:block, at] = inner_ref[:, there]
            ref[block:, at] = edge_rows[:, there]


def project_early_kernel(parts, own_ref, *rest):
    their_refs, shard_refs, (own_total_ref, their_total_ref) = rest[:parts], rest[parts:-2], rest[-2:]
    depths = sum(ref.shape[0] for ref in shard_refs)
    theirs = jnp.concatenate([ref[...] for ref in their_refs], axis=1)
    features = jnp.concatenate([own_ref[:, :depths], theirs[:, :depths]], axis=0)
    rows = own_ref.shape[0]
    tile = 2 * HEAD
    for first in range(0, own_total_ref.shape[1], tile):
        columns = slice(first, first + tile)
        weight = jnp.concatenate([ref[:, columns] for ref in shard_refs], axis=0)
        total = jnp.dot(features, weight, preferred_element_type=jnp.float32)
        own_total_ref[:, columns] = total[:rows]
        their_total_ref[:, columns] = total[rows:].astype(jnp.bfloat16)


def project_late_kernel(own_ref, other_ref, total_ref, more_ref, *rest):
    shard_refs, out_ref = rest[:-1], rest[-1]
    depth = sum(ref.shape[0] for ref in shard_refs) // 2
    features = jnp.concatenate([own_ref[:, -depth:], other_ref[:, -depth:]], axis=1)
    rows = own_ref.shape[0]
    block = rows // 2
    ctx = lax.axis_index("ctx")
    inner_at = pl.ds(pl.multiple_of(ctx * block, block), block)
    edge_at = pl.ds(pl.multiple_of((1 - ctx) * block, block), block)
    tile = 2 * HEAD
    for first in range(0, out_ref.shape[1], tile):
        columns = slice(first, first + tile)
        weight = jnp.concatenate([ref[:, columns] for ref in shard_refs], axis=0)
        total = jnp.dot(features, weight, preferred_element_type=jnp.float32)
        total = (total + (total_ref[:, columns] + more_ref[:, columns])).astype(jnp.bfloat16)
        out_ref[inner_at, columns] = total[:block]
        out_ref[edge_at, columns] = total[block:]


SMEM = functools.partial(pl.BlockSpec, memory_space=pltpu.SMEM)
VMEM = functools.partial(pl.BlockSpec, memory_space=pltpu.VMEM)
HBM = functools.partial(pl.BlockSpec, memory_space=pltpu.HBM)


def after(value, *others):
    return lax.optimization_barrier((value, *others))[0]


def body_edge(projections, block_source, clip_ids, out_weight):
    local_rows, row_width = projections.shape
    block_rows = local_rows // 2
    heads = row_width // (3 * HEAD)
    features = heads * HEAD
    depth, width = out_weight.shape
    count = lax.axis_size("dp")
    bf16 = jnp.bfloat16

    def call(kernel, name, shape, in_specs, dtypes=None, scratch=()):
        many = isinstance(shape, list)
        shapes = shape if many else [shape]
        dtypes = dtypes or [bf16] * len(shapes)
        shapes = [jax.ShapeDtypeStruct(*one) for one in zip(shapes, dtypes, strict=True)]
        return pl.pallas_call(
            kernel,
            out_shape=shapes if many else shapes[0],
            in_specs=in_specs,
            out_specs=[VMEM()] * len(shapes) if many else VMEM(),
            scratch_shapes=scratch,
            cost_estimate=pl.CostEstimate(flops=0, bytes_accessed=0, transcendentals=0),
            compiler_params=pltpu.CompilerParams(vmem_limit_bytes=8 * MIB),
            name=name,
        )

    def onward(value):
        places = ring_order(count // 4)
        moves = zip(places, places[1:] + places[:1], strict=True)
        return lax.ppermute(
            value, "dp", [(4 * here + rest, 4 * there + rest) for here, there in moves for rest in range(4)]
        )

    def to_side(value):
        return partner(value, "dp", 1)

    def to_core(value):
        return partner(value, "dp", 0)

    def inner_rows(*before):
        return call(inner_kernel, "inner_rows", (block_rows, features), [SMEM(), VMEM()])(
            after(clip_ids, *before), rows
        )

    own = pltpu.with_memory_space_constraint(
        projections.reshape(2, block_rows, row_width), pltpu.HBM
    )
    shards = {(0, False): [out_weight]}
    from_partner = pltpu.with_memory_space_constraint(to_core(own), pltpu.VMEM)
    ahead = onward(out_weight)
    across = to_side(out_weight)
    staged = call(
        stage_kernel,
        "stage",
        own.shape,
        [SMEM(), HBM()],
        scratch=[pltpu.SemaphoreType.DMA],
    )(block_source, own)
    part_heads = [heads // 2, heads // 2]
    rows, *packed = call(
        pack_kernel,
        "pack",
        [(2, block_rows, row_width)] + [(block_rows, 2 * HEAD * some) for some in part_heads],
        [SMEM(), VMEM(), VMEM()],
        scratch=[pltpu.SemaphoreType.DMA((2,))],
    )(block_source, staged, from_partner)
    halos = [lax.ppermute(part, "ctx", [(0, 1), (1, 0)]) for part in packed]

    def edge_rows(part, *before):
        some = part_heads[part]
        return call(
            functools.partial(edge_kernel, sum(part_heads[:part])),
            "edge_rows",
            (block_rows, some * HEAD),
            [SMEM(), VMEM(), VMEM()],
        )(after(clip_ids, *before), rows, halos[part])

    ahead = after(ahead, *packed)
    shards[1, False], shards[0, True] = [ahead], [across]
    half = depth // 2
    seconds = [onward(ahead[:half]), onward(ahead[half:])]
    across = to_side(after(ahead, across))
    inner = inner_rows(*shards[1, False])
    edges = [edge_rows(0, inner)]

    seconds = [after(seconds[0], inner), after(seconds[1], *edges)]
    shards[2, False], shards[1, True] = seconds, [across]
    thirds = [onward(part) for part in seconds]
    acrosses = [onward(across[:half]), to_side(seconds[1])]
    edges.append(edge_rows(1, *seconds))

    shards[3, False], shards[2, True] = thirds, acrosses
    last = [to_side(thirds[0]), to_side(after(thirds[1], acrosses[1], edges[1]))]
    ready = to_core(after(last[0], acrosses[0])[: half // 2])
    last[1] = after(last[1], ready)
    last_swapped = [ready, to_core(last[0][half // 2 :]), to_core(last[1])]

    origins = [*shards, (3, True)]
    parts = 2
    mine, *others = call(
        functools.partial(arrange_kernel, origins, len(edges)),
        "arrange",
        [(local_rows, len(origins) * depth)] + [(local_rows, len(origins) // parts * depth)] * parts,
        [VMEM()] * (1 + len(edges)),
        scratch=[pltpu.VMEM((block_rows, features), bf16)],
    )(inner, *edges)
    theirs = [to_core(part) for part in others]
    early = [part for shard in shards.values() for part in shard]
    total, their_total = call(
        functools.partial(project_early_kernel, parts),
        "project_early",
        [(local_rows, width)] * 2,
        [VMEM()] * (1 + parts + len(early)),
        dtypes=[jnp.float32, bf16],
    )(mine, *theirs, *early)
    more = to_core(after(their_total, last[1]))
    late = [*last, *last_swapped]
    return call(
        project_late_kernel, "project_late", (local_rows, width), [VMEM()] * (4 + len(late))
    )(mine, others[-1], total, more, *late)


def body(projections, block_source, clip_ids, out_weight):
    heads = projections.shape[1] // (3 * HEAD)
    two_and_two = lax.axis_size("ctx") == 2 and block_source.shape[2] == 2
    whole_tiles = out_weight.shape[0] % HEAD == 0 and heads % 4 == 0
    if two_and_two and whole_tiles and lax.axis_size("dp") == 16:
        return body_edge(projections, block_source, clip_ids, out_weight)
    return body_general(projections, block_source, clip_ids, out_weight)


def solution(mesh):
    return jax.shard_map(
        body,
        mesh=mesh,
        in_specs=(P(("dp", "ctx"), None), P("dp", "ctx", None), P("dp", None), P("dp", None)),
        out_specs=P(("dp", "ctx"), None),
        check_vma=False,
    )
```

```python
import functools
import math

import jax
import jax.numpy as jnp
from jax import lax
from jax.experimental import pallas as pl
from jax.experimental.pallas import tpu as pltpu
from jax.sharding import PartitionSpec as P

HEAD = 128


big_negative = -1e30
MIB = 1 << 20
PARTS = 4


def partner(value, axis, bit):
    mask = 2**bit
    pairs = [(source, source ^ mask) for source in range(lax.axis_size(axis))]
    return lax.ppermute(value, axis, pairs)


def soft_weights(scores, allowed):
    masked = jnp.where(allowed, scores, big_negative)
    row_max = jnp.max(masked, axis=-1, keepdims=True)
    exponent = jnp.exp(masked - row_max)
    return (exponent / jnp.sum(exponent, axis=-1, keepdims=True)).astype(jnp.bfloat16)


def attend_dense(queries, key_rows, value_rows, token_clip, scaling):
    token_count, head_count, head_size = queries.shape
    step_size = min(token_count, 512)
    step_count = token_count // step_size
    query_steps = queries.reshape(step_count, step_size, head_count, head_size)
    clip_steps = token_clip.reshape(step_count, step_size)

    def one_step(arguments):
        query_block, clip_block = arguments
        scores = (
            jnp.einsum("qhe,khe->hqk", query_block, key_rows, preferred_element_type=jnp.float32)
            * scaling
        )
        allowed = (clip_block[:, None] == token_clip[None, :])[None]
        weights = soft_weights(scores, allowed)
        return jnp.einsum(
            "hqk,khe->qhe", weights, value_rows, preferred_element_type=jnp.float32
        ).astype(jnp.bfloat16)

    outputs = lax.map(one_step, (query_steps, clip_steps))
    return outputs.reshape(token_count, head_count, head_size)


def body_general(projections, block_source, clip_ids, out_weight):
    ctx_count = lax.axis_size("ctx")
    local_rows, row_width = projections.shape
    local_blocks = block_source.shape[2]
    block_rows = local_rows // local_blocks
    own_blocks = projections.reshape(local_blocks, block_rows, row_width)
    partner_blocks = partner(own_blocks, "dp", 0)
    source_ids = block_source.reshape(local_blocks)
    from_partner = source_ids // (local_blocks * ctx_count) != lax.axis_index("dp")
    chosen_slot = source_ids % local_blocks + local_blocks * from_partner.astype(jnp.int32)
    candidates = jnp.concatenate([own_blocks, partner_blocks], axis=0)
    packed = jnp.take(candidates, chosen_slot, axis=0)
    local_heads = row_width // (3 * HEAD) // ctx_count
    grouped = packed.reshape(local_rows, ctx_count, local_heads, 3 * HEAD)
    block_clip = clip_ids.reshape(-1)
    token_clip = jnp.repeat(block_clip, block_rows)
    scaling = 1.0 / math.sqrt(HEAD)
    regrouped = lax.all_to_all(grouped, "ctx", split_axis=1, concat_axis=0, tiled=True)
    token_count = regrouped.shape[0]
    item_count = regrouped.shape[2]
    features = regrouped.reshape(token_count, item_count, 3 * HEAD)
    queries = features[:, :, :HEAD]
    key_rows = features[:, :, HEAD : 2 * HEAD]
    value_rows = features[:, :, 2 * HEAD :]
    attended = attend_dense(queries, key_rows, value_rows, token_clip, scaling)
    merged = attended.reshape(local_rows * ctx_count, local_heads * HEAD)
    attention_rows = lax.all_to_all(merged, "ctx", split_axis=0, concat_axis=1, tiled=True)
    result = jnp.dot(
        attention_rows,
        lax.all_gather(out_weight, "dp", axis=0, tiled=True),
        preferred_element_type=jnp.float32,
    )
    return result.astype(jnp.bfloat16)


def stage_kernel(source_ref, own_ref, out_ref, sem):
    copy = pltpu.make_async_copy(own_ref, out_ref, sem)
    copy.start()
    copy.wait()


def pack_kernel(source_ref, own_ref, partner_ref, rows_ref, *rest):
    halo_refs, sems = rest[:-1], rest[-1]
    ctx, dp = lax.axis_index("ctx"), lax.axis_index("dp")
    slots = own_ref.shape[0]
    for which, block in ((1, 1 - ctx), (0, ctx)):
        source = source_ref[0, 0, block]
        slot = lax.rem(source, slots)
        away = source // (2 * slots) != dp

        @pl.when(jnp.logical_not(away))
        def _():
            pltpu.make_async_copy(own_ref.at[slot], rows_ref.at[which], sems.at[which]).start()

        @pl.when(away)
        def _():
            pltpu.make_async_copy(partner_ref.at[slot], rows_ref.at[which], sems.at[which]).start()

    pltpu.make_async_copy(own_ref.at[0], rows_ref.at[1], sems.at[1]).wait()
    first = HEAD
    for halo_ref in halo_refs:
        for at in range(0, halo_ref.shape[1], 2 * HEAD):
            halo_ref[:, at : at + 2 * HEAD] = rows_ref[1, :, first : first + 2 * HEAD]
            first += 3 * HEAD
    pltpu.make_async_copy(own_ref.at[0], rows_ref.at[0], sems.at[0]).wait()


def attend(heads, load_queries, load_own, load_more, allowed, out_ref):
    scaling = math.log2(math.e) / math.sqrt(HEAD)
    contract_last = (((1,), (1,)), ((), ()))
    ones = jnp.ones((2 * out_ref.shape[0], HEAD), jnp.bfloat16)
    group = 4
    for start in range(0, heads, group):
        scores = []
        for head in range(start, start + group):
            queries = load_queries(head)
            pair = []
            for loader in (load_own, load_more):
                pair.append(
                    lax.dot_general(
                        queries, loader(head, 0), contract_last, preferred_element_type=jnp.float32
                    )
                    * scaling
                )
            scores.append(pair)
        weights = []
        for own, more in scores:
            more = jnp.where(allowed, more, big_negative)
            row_max = jnp.max(jnp.maximum(own, more), axis=-1, keepdims=True)
            weights.append(
                jnp.concatenate(
                    [
                        jnp.exp2(own - row_max).astype(jnp.bfloat16),
                        jnp.exp2(more - row_max).astype(jnp.bfloat16),
                    ],
                    axis=1,
                )
            )
        for head in range(start, start + group):
            values = jnp.concatenate([load_own(head, 1), load_more(head, 1)], axis=0)
            sums = jnp.dot(
                weights[head - start],
                jnp.concatenate([values, ones], axis=1),
                preferred_element_type=jnp.float32,
            )
            out_ref[:, head * HEAD : (head + 1) * HEAD] = (
                sums[:, :HEAD] / sums[:, HEAD:]
            ).astype(jnp.bfloat16)


def inner_kernel(clip_ref, rows_ref, out_ref):
    ctx = lax.axis_index("ctx")
    allowed = clip_ref[0, 2 * ctx] == clip_ref[0, 2 * ctx + 1]

    def loader(block):
        def get(head, which):
            first = (head * 3 + 1 + which) * HEAD
            return rows_ref[block, :, first : first + HEAD]

        return get

    attend(
        out_ref.shape[1] // HEAD,
        lambda head: loader(0)(head, -1),
        loader(0),
        loader(1),
        allowed,
        out_ref,
    )


def edge_kernel(first_head, clip_ref, rows_ref, halo_ref, out_ref):
    ctx = lax.axis_index("ctx")
    edge_clip = clip_ref[0, 1 + ctx]
    crosses = edge_clip == clip_ref[0, 2 - ctx]
    allowed = jnp.logical_or(crosses, edge_clip == clip_ref[0, 3 * ctx])

    def load_own(head, which):
        first = ((first_head + head) * 3 + 1 + which) * HEAD
        return rows_ref[1, :, first : first + HEAD]

    def load_more(head, which):
        first = ((first_head + head) * 3 + 1 + which) * HEAD
        at = (2 * head + which) * HEAD
        return jnp.where(crosses, halo_ref[:, at : at + HEAD], rows_ref[0, :, first : first + HEAD])

    attend(
        out_ref.shape[1] // HEAD,
        lambda head: load_own(head, -1),
        load_own,
        load_more,
        allowed,
        out_ref,
    )


def ring_order(lines):
    return list(range(0, lines, 2)) + list(range(1, lines, 2))[::-1]


def arrange_kernel(origins, parts, inner_ref, *rest):
    edge_refs, (own_ref, *other_refs, edge_rows) = rest[:parts], rest[parts:]
    first = 0
    for ref in edge_refs:
        edge_rows[:, first : first + ref.shape[1]] = ref[...]
        first += ref.shape[1]
    index = lax.axis_index("dp")
    core, side, line = lax.rem(index, 2), lax.rem(index // 2, 2), index // 4
    places = ring_order(lax.axis_size("dp") // 4)
    block = inner_ref.shape[0]
    depth = own_ref.shape[1] // len(origins)
    for number, (steps, other_side) in enumerate(origins):
        from_line = line
        for at, place in enumerate(places):
            from_line = jnp.where(line == place, places[at - steps], from_line)
        from_side = 1 - side if other_side else side
        part, place = divmod(number, len(origins) // len(other_refs))
        for ref, at, from_core in ((own_ref, number, core), (other_refs[part], place, 1 - core)):
            shard = (from_line * 2 + from_side) * 2 + from_core
            there = pl.ds(pl.multiple_of(shard * depth, depth), depth)
            at = slice(at * depth, (at + 1) * depth)
            ref[:block, at] = inner_ref[:, there]
            ref[block:, at] = edge_rows[:, there]


def project_early_kernel(parts, own_ref, *rest):
    their_refs, shard_refs = rest[:parts], rest[parts : -1 - PARTS]
    own_total_ref, *their_total_refs = rest[-1 - PARTS :]
    depths = sum(ref.shape[0] for ref in shard_refs)
    theirs = jnp.concatenate([ref[...] for ref in their_refs], axis=1)
    features = jnp.concatenate([own_ref[:, :depths], theirs[:, :depths]], axis=0)
    rows = own_ref.shape[0]
    tile = own_total_ref.shape[1] // PARTS
    for part, their_total_ref in enumerate(their_total_refs):
        columns = slice(part * tile, (part + 1) * tile)
        weight = jnp.concatenate([ref[:, columns] for ref in shard_refs], axis=0)
        total = jnp.dot(features, weight, preferred_element_type=jnp.float32)
        own_total_ref[:, columns] = total[:rows]
        their_total_ref[...] = total[rows:].astype(jnp.bfloat16)


def last_features(own_ref, other_ref, depth, first, count):
    parts = []
    for ref in (own_ref, other_ref):
        start = ref.shape[1] - depth + first
        parts.append(ref[:, start : start + count])
    return jnp.concatenate(parts, axis=1)


def project_middle_kernel(depth, own_ref, other_ref, total_ref, *rest):
    more_refs, (shard_ref, *swapped_refs, out_ref) = rest[:PARTS], rest[PARTS:]
    features = last_features(own_ref, other_ref, depth, 0, shard_ref.shape[0])
    tile = out_ref.shape[1] // PARTS
    for part, more_ref in enumerate(more_refs):
        columns = slice(part * tile, (part + 1) * tile)
        weight = jnp.concatenate([ref[:, columns] for ref in (shard_ref, *swapped_refs)], axis=0)
        total = jnp.dot(features, weight, preferred_element_type=jnp.float32)
        out_ref[:, columns] = total + (total_ref[:, columns] + more_ref[...])


def project_late_kernel(depth, own_ref, other_ref, total_ref, shard_ref, swapped_ref, out_ref, held, sems):
    count = shard_ref.shape[0]
    features = last_features(own_ref, other_ref, depth, depth - count, count)
    block = own_ref.shape[0] // 2
    ctx = lax.axis_index("ctx")
    inner_at = pl.ds(pl.multiple_of(ctx * block, block), block)
    edge_at = pl.ds(pl.multiple_of((1 - ctx) * block, block), block)
    tile = out_ref.shape[1] // PARTS
    copies = []
    for part in range(PARTS):
        columns = slice(part * tile, (part + 1) * tile)
        weight = jnp.concatenate([shard_ref[:, columns], swapped_ref[:, columns]], axis=0)
        total = jnp.dot(features, weight, preferred_element_type=jnp.float32)
        total = (total + total_ref[:, columns]).astype(jnp.bfloat16)
        held[inner_at, columns] = total[:block]
        held[edge_at, columns] = total[block:]
        copies.append(
            pltpu.make_async_copy(held.at[:, columns], out_ref.at[:, columns], sems.at[part])
        )
        copies[-1].start()
    for copy in copies:
        copy.wait()


SMEM = functools.partial(pl.BlockSpec, memory_space=pltpu.SMEM)
VMEM = functools.partial(pl.BlockSpec, memory_space=pltpu.VMEM)
HBM = functools.partial(pl.BlockSpec, memory_space=pltpu.HBM)


def after(value, *others):
    return lax.optimization_barrier((value, *others))[0]


def body_edge(projections, block_source, clip_ids, out_weight):
    local_rows, row_width = projections.shape
    block_rows = local_rows // 2
    heads = row_width // (3 * HEAD)
    features = heads * HEAD
    depth, width = out_weight.shape
    count = lax.axis_size("dp")
    bf16 = jnp.bfloat16

    def call(kernel, name, shape, in_specs, dtypes=None, scratch=(), out_spec=VMEM()):
        many = isinstance(shape, list)
        shapes = shape if many else [shape]
        dtypes = dtypes or [bf16] * len(shapes)
        shapes = [jax.ShapeDtypeStruct(*one) for one in zip(shapes, dtypes, strict=True)]
        return pl.pallas_call(
            kernel,
            out_shape=shapes if many else shapes[0],
            in_specs=in_specs,
            out_specs=[out_spec] * len(shapes) if many else out_spec,
            scratch_shapes=scratch,
            cost_estimate=pl.CostEstimate(flops=0, bytes_accessed=0, transcendentals=0),
            compiler_params=pltpu.CompilerParams(vmem_limit_bytes=8 * MIB),
            name=name,
        )

    def onward(value):
        places = ring_order(count // 4)
        moves = zip(places, places[1:] + places[:1], strict=True)
        return lax.ppermute(
            value, "dp", [(4 * here + rest, 4 * there + rest) for here, there in moves for rest in range(4)]
        )

    def to_side(value):
        return partner(value, "dp", 1)

    def to_core(value):
        return partner(value, "dp", 0)

    def inner_rows(*before):
        return call(inner_kernel, "inner_rows", (block_rows, features), [SMEM(), VMEM()])(
            after(clip_ids, *before), rows
        )

    own = pltpu.with_memory_space_constraint(
        projections.reshape(2, block_rows, row_width), pltpu.HBM
    )
    shards = {(0, False): [out_weight]}
    from_partner = pltpu.with_memory_space_constraint(to_core(own), pltpu.VMEM)
    ahead = onward(out_weight)
    across = to_side(out_weight)
    staged = call(
        stage_kernel,
        "stage",
        own.shape,
        [SMEM(), HBM()],
        scratch=[pltpu.SemaphoreType.DMA],
    )(block_source, own)
    part_heads = [heads // 2, heads // 2]
    rows, *packed = call(
        pack_kernel,
        "pack",
        [(2, block_rows, row_width)] + [(block_rows, 2 * HEAD * some) for some in part_heads],
        [SMEM(), VMEM(), VMEM()],
        scratch=[pltpu.SemaphoreType.DMA((2,))],
    )(block_source, staged, from_partner)
    halos = [lax.ppermute(part, "ctx", [(0, 1), (1, 0)]) for part in packed]

    def edge_rows(part, *before):
        some = part_heads[part]
        return call(
            functools.partial(edge_kernel, sum(part_heads[:part])),
            "edge_rows",
            (block_rows, some * HEAD),
            [SMEM(), VMEM(), VMEM()],
        )(after(clip_ids, *before), rows, halos[part])

    ahead = after(ahead, *packed)
    shards[1, False], shards[0, True] = [ahead], [across]
    half = depth // 2
    across = to_side(after(ahead, across))
    seconds = [onward(ahead[:half]), onward(ahead[half:])]
    inner = inner_rows(*shards[1, False])
    edges = [edge_rows(0, inner)]

    seconds = [after(seconds[0], inner), after(seconds[1], *edges)]
    shards[2, False], shards[1, True] = seconds, [across]
    side_half = to_side(after(seconds[1], across))
    thirds = [onward(part) for part in seconds]
    acrosses = [onward(across[:half]), side_half]
    edges.append(edge_rows(1, *seconds))

    shards[3, False], shards[2, True] = thirds, acrosses
    last = [to_side(thirds[0]), to_side(after(thirds[1], acrosses[1], edges[1]))]
    ready = to_core(after(last[0], acrosses[0])[: half // 2])
    last[1] = after(last[1], ready)
    last_swapped = [ready, to_core(last[0][half // 2 :]), to_core(last[1])]

    origins = [*shards, (3, True)]
    parts = 2
    mine, *others = call(
        functools.partial(arrange_kernel, origins, len(edges)),
        "arrange",
        [(local_rows, len(origins) * depth)] + [(local_rows, len(origins) // parts * depth)] * parts,
        [VMEM()] * (1 + len(edges)),
        scratch=[pltpu.VMEM((block_rows, features), bf16)],
    )(inner, *edges)
    theirs = [to_core(part) for part in others]
    early = [part for shard in shards.values() for part in shard]
    total, *their_totals = call(
        functools.partial(project_early_kernel, parts),
        "project_early",
        [(local_rows, width)] + [(local_rows, width // PARTS)] * PARTS,
        [VMEM()] * (1 + parts + len(early)),
        dtypes=[jnp.float32] + [bf16] * PARTS,
    )(mine, *theirs, *early)
    mores = [to_core(part) for part in their_totals]
    total = call(
        functools.partial(project_middle_kernel, depth),
        "project_middle",
        (local_rows, width),
        [VMEM()] * (4 + PARTS + len(last_swapped[:-1])),
        dtypes=[jnp.float32],
    )(mine, others[-1], total, *mores, last[0], *last_swapped[:-1])
    return call(
        functools.partial(project_late_kernel, depth),
        "project_late",
        (local_rows, width),
        [VMEM()] * 5,
        scratch=[pltpu.VMEM((local_rows, width), bf16), pltpu.SemaphoreType.DMA((PARTS,))],
        out_spec=HBM(),
    )(mine, others[-1], total, last[1], last_swapped[-1])


def body(projections, block_source, clip_ids, out_weight):
    heads = projections.shape[1] // (3 * HEAD)
    two_and_two = lax.axis_size("ctx") == 2 and block_source.shape[2] == 2
    whole_tiles = out_weight.shape[0] % HEAD == 0 and heads % 4 == 0
    if two_and_two and whole_tiles and lax.axis_size("dp") == 16:
        return body_edge(projections, block_source, clip_ids, out_weight)
    return body_general(projections, block_source, clip_ids, out_weight)


def solution(mesh):
    return jax.shard_map(
        body,
        mesh=mesh,
        in_specs=(P(("dp", "ctx"), None), P("dp", "ctx", None), P("dp", None), P("dp", None)),
        out_specs=P(("dp", "ctx"), None),
        check_vma=False,
    )
```

```python
import functools
import math

import jax
import jax.numpy as jnp
from jax import lax
from jax.experimental import pallas as pl
from jax.experimental.pallas import tpu as pltpu
from jax.sharding import PartitionSpec as P

HEAD = 128


big_negative = -1e30
MIB = 1 << 20


def partner(value, axis, bit):
    mask = 2**bit
    pairs = [(source, source ^ mask) for source in range(lax.axis_size(axis))]
    return lax.ppermute(value, axis, pairs)


def soft_weights(scores, allowed):
    masked = jnp.where(allowed, scores, big_negative)
    row_max = jnp.max(masked, axis=-1, keepdims=True)
    exponent = jnp.exp(masked - row_max)
    return (exponent / jnp.sum(exponent, axis=-1, keepdims=True)).astype(jnp.bfloat16)


def attend_dense(queries, key_rows, value_rows, token_clip, scaling):
    token_count, head_count, head_size = queries.shape
    step_size = min(token_count, 512)
    step_count = token_count // step_size
    query_steps = queries.reshape(step_count, step_size, head_count, head_size)
    clip_steps = token_clip.reshape(step_count, step_size)

    def one_step(arguments):
        query_block, clip_block = arguments
        scores = (
            jnp.einsum("qhe,khe->hqk", query_block, key_rows, preferred_element_type=jnp.float32)
            * scaling
        )
        allowed = (clip_block[:, None] == token_clip[None, :])[None]
        weights = soft_weights(scores, allowed)
        return jnp.einsum(
            "hqk,khe->qhe", weights, value_rows, preferred_element_type=jnp.float32
        ).astype(jnp.bfloat16)

    outputs = lax.map(one_step, (query_steps, clip_steps))
    return outputs.reshape(token_count, head_count, head_size)


def body_general(projections, block_source, clip_ids, out_weight):
    ctx_count = lax.axis_size("ctx")
    local_rows, row_width = projections.shape
    local_blocks = block_source.shape[2]
    block_rows = local_rows // local_blocks
    own_blocks = projections.reshape(local_blocks, block_rows, row_width)
    partner_blocks = partner(own_blocks, "dp", 0)
    source_ids = block_source.reshape(local_blocks)
    from_partner = source_ids // (local_blocks * ctx_count) != lax.axis_index("dp")
    chosen_slot = source_ids % local_blocks + local_blocks * from_partner.astype(jnp.int32)
    candidates = jnp.concatenate([own_blocks, partner_blocks], axis=0)
    packed = jnp.take(candidates, chosen_slot, axis=0)
    local_heads = row_width // (3 * HEAD) // ctx_count
    grouped = packed.reshape(local_rows, ctx_count, local_heads, 3 * HEAD)
    block_clip = clip_ids.reshape(-1)
    token_clip = jnp.repeat(block_clip, block_rows)
    scaling = 1.0 / math.sqrt(HEAD)
    regrouped = lax.all_to_all(grouped, "ctx", split_axis=1, concat_axis=0, tiled=True)
    token_count = regrouped.shape[0]
    item_count = regrouped.shape[2]
    features = regrouped.reshape(token_count, item_count, 3 * HEAD)
    queries = features[:, :, :HEAD]
    key_rows = features[:, :, HEAD : 2 * HEAD]
    value_rows = features[:, :, 2 * HEAD :]
    attended = attend_dense(queries, key_rows, value_rows, token_clip, scaling)
    merged = attended.reshape(local_rows * ctx_count, local_heads * HEAD)
    attention_rows = lax.all_to_all(merged, "ctx", split_axis=0, concat_axis=1, tiled=True)
    result = jnp.dot(
        attention_rows,
        lax.all_gather(out_weight, "dp", axis=0, tiled=True),
        preferred_element_type=jnp.float32,
    )
    return result.astype(jnp.bfloat16)


def stage_kernel(source_ref, own_ref, out_ref, sem):
    copy = pltpu.make_async_copy(own_ref, out_ref, sem)
    copy.start()
    copy.wait()


def pack_kernel(source_ref, own_ref, partner_ref, rows_ref, *rest):
    halo_refs, sems = rest[:-1], rest[-1]
    ctx, dp = lax.axis_index("ctx"), lax.axis_index("dp")
    slots = own_ref.shape[0]
    for which, block in ((1, 1 - ctx), (0, ctx)):
        source = source_ref[0, 0, block]
        slot = lax.rem(source, slots)
        away = source // (2 * slots) != dp

        @pl.when(jnp.logical_not(away))
        def _():
            pltpu.make_async_copy(own_ref.at[slot], rows_ref.at[which], sems.at[which]).start()

        @pl.when(away)
        def _():
            pltpu.make_async_copy(partner_ref.at[slot], rows_ref.at[which], sems.at[which]).start()

    pltpu.make_async_copy(own_ref.at[0], rows_ref.at[1], sems.at[1]).wait()
    first = HEAD
    for halo_ref in halo_refs:
        for at in range(0, halo_ref.shape[1], 2 * HEAD):
            halo_ref[:, at : at + 2 * HEAD] = rows_ref[1, :, first : first + 2 * HEAD]
            first += 3 * HEAD
    pltpu.make_async_copy(own_ref.at[0], rows_ref.at[0], sems.at[0]).wait()


def attend(heads, load_queries, load_own, load_more, allowed, out_ref):
    scaling = math.log2(math.e) / math.sqrt(HEAD)
    contract_last = (((1,), (1,)), ((), ()))
    ones = jnp.ones((2 * out_ref.shape[0], HEAD), jnp.bfloat16)
    group = 4
    for start in range(0, heads, group):
        scores = []
        for head in range(start, start + group):
            queries = load_queries(head)
            pair = []
            for loader in (load_own, load_more):
                pair.append(
                    lax.dot_general(
                        queries, loader(head, 0), contract_last, preferred_element_type=jnp.float32
                    )
                    * scaling
                )
            scores.append(pair)
        weights = []
        for own, more in scores:
            more = jnp.where(allowed, more, big_negative)
            row_max = jnp.max(jnp.maximum(own, more), axis=-1, keepdims=True)
            weights.append(
                jnp.concatenate(
                    [
                        jnp.exp2(own - row_max).astype(jnp.bfloat16),
                        jnp.exp2(more - row_max).astype(jnp.bfloat16),
                    ],
                    axis=1,
                )
            )
        for head in range(start, start + group):
            values = jnp.concatenate([load_own(head, 1), load_more(head, 1)], axis=0)
            sums = jnp.dot(
                weights[head - start],
                jnp.concatenate([values, ones], axis=1),
                preferred_element_type=jnp.float32,
            )
            out_ref[:, head * HEAD : (head + 1) * HEAD] = (
                sums[:, :HEAD] / sums[:, HEAD:]
            ).astype(jnp.bfloat16)


def inner_kernel(clip_ref, rows_ref, out_ref):
    ctx = lax.axis_index("ctx")
    allowed = clip_ref[0, 2 * ctx] == clip_ref[0, 2 * ctx + 1]

    def loader(block):
        def get(head, which):
            first = (head * 3 + 1 + which) * HEAD
            return rows_ref[block, :, first : first + HEAD]

        return get

    attend(
        out_ref.shape[1] // HEAD,
        lambda head: loader(0)(head, -1),
        loader(0),
        loader(1),
        allowed,
        out_ref,
    )


def edge_kernel(first_head, clip_ref, rows_ref, halo_ref, out_ref):
    ctx = lax.axis_index("ctx")
    edge_clip = clip_ref[0, 1 + ctx]
    crosses = edge_clip == clip_ref[0, 2 - ctx]
    allowed = jnp.logical_or(crosses, edge_clip == clip_ref[0, 3 * ctx])

    def load_own(head, which):
        first = ((first_head + head) * 3 + 1 + which) * HEAD
        return rows_ref[1, :, first : first + HEAD]

    def load_more(head, which):
        first = ((first_head + head) * 3 + 1 + which) * HEAD
        at = (2 * head + which) * HEAD
        return jnp.where(crosses, halo_ref[:, at : at + HEAD], rows_ref[0, :, first : first + HEAD])

    attend(
        out_ref.shape[1] // HEAD,
        lambda head: load_own(head, -1),
        load_own,
        load_more,
        allowed,
        out_ref,
    )


def ring_order(lines):
    return list(range(0, lines, 2)) + list(range(1, lines, 2))[::-1]


def arrange_kernel(origins, parts, inner_ref, *rest):
    edge_refs, (own_ref, *other_refs, edge_rows) = rest[:parts], rest[parts:]
    first = 0
    for ref in edge_refs:
        edge_rows[:, first : first + ref.shape[1]] = ref[...]
        first += ref.shape[1]
    index = lax.axis_index("dp")
    core, side, line = lax.rem(index, 2), lax.rem(index // 2, 2), index // 4
    places = ring_order(lax.axis_size("dp") // 4)
    block = inner_ref.shape[0]
    depth = own_ref.shape[1] // len(origins)
    for number, (steps, other_side) in enumerate(origins):
        from_line = line
        for at, place in enumerate(places):
            from_line = jnp.where(line == place, places[at - steps], from_line)
        from_side = 1 - side if other_side else side
        part, place = divmod(number, len(origins) // len(other_refs))
        for ref, at, from_core in ((own_ref, number, core), (other_refs[part], place, 1 - core)):
            shard = (from_line * 2 + from_side) * 2 + from_core
            there = pl.ds(pl.multiple_of(shard * depth, depth), depth)
            at = slice(at * depth, (at + 1) * depth)
            ref[:block, at] = inner_ref[:, there]
            ref[block:, at] = edge_rows[:, there]


def project_kernel(parts, first, own_ref, *rest):
    their_refs, shard_refs, (own_total_ref, their_total_ref) = rest[:parts], rest[parts:-2], rest[-2:]
    theirs = jnp.concatenate([ref[...] for ref in their_refs], axis=1)
    features = jnp.concatenate([own_ref[...], theirs], axis=0)
    rows = own_ref.shape[0]
    tile = 2 * HEAD
    for at in range(0, own_total_ref.shape[1], tile):
        here = slice(at, at + tile)
        columns = slice(first + at, first + at + tile)
        weight = jnp.concatenate([ref[:, columns] for ref in shard_refs], axis=0)
        total = jnp.dot(features, weight, preferred_element_type=jnp.float32)
        own_total_ref[:, here] = total[:rows]
        their_total_ref[:, here] = total[rows:].astype(jnp.bfloat16)


def finish_kernel(*refs):
    totals, out_ref, held, sems = refs[:-3], refs[-3], refs[-2], refs[-1]
    half = len(totals) // 2
    block = out_ref.shape[0] // 2
    ctx = lax.axis_index("ctx")
    copies = []
    for which, place in ((0, ctx), (1, 1 - ctx)):
        rows = slice(which * block, (which + 1) * block)
        first = 0
        for total_ref, more_ref in zip(totals[:half], totals[half:], strict=True):
            columns = slice(first, first + total_ref.shape[1])
            held[rows, columns] = (total_ref[rows] + more_ref[rows]).astype(jnp.bfloat16)
            first += total_ref.shape[1]
        target = out_ref.at[pl.ds(pl.multiple_of(place * block, block), block)]
        copies.append(pltpu.make_async_copy(held.at[rows], target, sems.at[which]))
        copies[-1].start()
    for copy in copies:
        copy.wait()


SMEM = functools.partial(pl.BlockSpec, memory_space=pltpu.SMEM)
VMEM = functools.partial(pl.BlockSpec, memory_space=pltpu.VMEM)
HBM = functools.partial(pl.BlockSpec, memory_space=pltpu.HBM)


def after(value, *others):
    return lax.optimization_barrier((value, *others))[0]


def body_edge(projections, block_source, clip_ids, out_weight):
    local_rows, row_width = projections.shape
    block_rows = local_rows // 2
    heads = row_width // (3 * HEAD)
    features = heads * HEAD
    depth, width = out_weight.shape
    count = lax.axis_size("dp")
    bf16 = jnp.bfloat16

    def call(kernel, name, shape, in_specs, dtypes=None, scratch=(), out_spec=VMEM()):
        many = isinstance(shape, list)
        shapes = shape if many else [shape]
        dtypes = dtypes or [bf16] * len(shapes)
        shapes = [jax.ShapeDtypeStruct(*one) for one in zip(shapes, dtypes, strict=True)]
        return pl.pallas_call(
            kernel,
            out_shape=shapes if many else shapes[0],
            in_specs=in_specs,
            out_specs=[out_spec] * len(shapes) if many else out_spec,
            scratch_shapes=scratch,
            cost_estimate=pl.CostEstimate(flops=0, bytes_accessed=0, transcendentals=0),
            compiler_params=pltpu.CompilerParams(vmem_limit_bytes=8 * MIB),
            name=name,
        )

    def around(value, step):
        places = ring_order(count // 4)
        moves = [(here, places[(at + step) % len(places)]) for at, here in enumerate(places)]
        return lax.ppermute(
            value, "dp", [(4 * here + rest, 4 * there + rest) for here, there in moves for rest in range(4)]
        )

    def to_side(value):
        return partner(value, "dp", 1)

    def to_core(value):
        return partner(value, "dp", 0)

    own = pltpu.with_memory_space_constraint(
        projections.reshape(2, block_rows, row_width), pltpu.HBM
    )
    shards = {(0, False): [out_weight]}
    from_partner = pltpu.with_memory_space_constraint(to_core(own), pltpu.VMEM)
    ahead = around(out_weight, 1)
    across = to_side(out_weight)
    back = around(out_weight, -1)
    staged = call(
        stage_kernel,
        "stage",
        own.shape,
        [SMEM(), HBM()],
        scratch=[pltpu.SemaphoreType.DMA],
    )(block_source, own)
    part_heads = [heads // 2, heads // 2]
    rows, *packed = call(
        pack_kernel,
        "pack",
        [(2, block_rows, row_width)] + [(block_rows, 2 * HEAD * some) for some in part_heads],
        [SMEM(), VMEM(), VMEM()],
        scratch=[pltpu.SemaphoreType.DMA((2,))],
    )(block_source, staged, from_partner)
    halos = [lax.ppermute(part, "ctx", [(0, 1), (1, 0)]) for part in packed]

    def edge_rows(part, *before):
        some = part_heads[part]
        return call(
            functools.partial(edge_kernel, sum(part_heads[:part])),
            "edge_rows",
            (block_rows, some * HEAD),
            [SMEM(), VMEM(), VMEM()],
        )(after(clip_ids, *before), rows, halos[part])

    ahead = after(ahead, *packed)
    shards[1, False], shards[0, True] = [ahead], [across]
    across = to_side(after(ahead, across))
    second = around(ahead, 1)
    inner = call(inner_kernel, "inner_rows", (block_rows, features), [SMEM(), VMEM()])(
        after(clip_ids, ahead), rows
    )
    edges = [edge_rows(0, inner)]

    back = after(back, inner)
    shards[3, False], shards[3, True] = [back], [to_side(back)]
    shards[1, True] = [across]
    second = after(second, *edges)
    shards[2, False] = [second]
    half = depth // 2
    shards[2, True] = [around(across[:half], 1), to_side(second[half:])]
    edges.append(edge_rows(1, second))

    origins = list(shards)
    parts = 4
    mine, *others = call(
        functools.partial(arrange_kernel, origins, len(edges)),
        "arrange",
        [(local_rows, len(origins) * depth)] + [(local_rows, len(origins) // parts * depth)] * parts,
        [VMEM()] * (1 + len(edges)),
        scratch=[pltpu.VMEM((block_rows, features), bf16)],
    )(inner, *edges)
    theirs = [to_core(part) for part in others]
    pieces = [piece for shard in shards.values() for piece in shard]
    totals, mores = [], []
    first = 0
    for columns in (width // 3 * 2, width // 3):
        total, their_total = call(
            functools.partial(project_kernel, parts, first),
            "project",
            [(local_rows, columns)] * 2,
            [VMEM()] * (1 + parts + len(pieces)),
            dtypes=[jnp.float32, bf16],
        )(mine, *theirs, *pieces)
        totals.append(total)
        mores.append(to_core(their_total))
        first += columns
    return call(
        finish_kernel,
        "finish",
        (local_rows, width),
        [VMEM()] * 4,
        scratch=[pltpu.VMEM((local_rows, width), bf16), pltpu.SemaphoreType.DMA((2,))],
        out_spec=HBM(),
    )(*totals, *mores)


def body(projections, block_source, clip_ids, out_weight):
    heads = projections.shape[1] // (3 * HEAD)
    two_and_two = lax.axis_size("ctx") == 2 and block_source.shape[2] == 2
    whole_tiles = out_weight.shape[0] % HEAD == 0 and heads % 4 == 0
    if two_and_two and whole_tiles and lax.axis_size("dp") == 16:
        return body_edge(projections, block_source, clip_ids, out_weight)
    return body_general(projections, block_source, clip_ids, out_weight)


def solution(mesh):
    return jax.shard_map(
        body,
        mesh=mesh,
        in_specs=(P(("dp", "ctx"), None), P("dp", "ctx", None), P("dp", None), P("dp", None)),
        out_specs=P(("dp", "ctx"), None),
        check_vma=False,
    )
```

```python
import functools
import math

import jax
import jax.numpy as jnp
from jax import lax
from jax.experimental import pallas as pl
from jax.experimental.pallas import tpu as pltpu
from jax.sharding import PartitionSpec as P

HEAD = 128


big_negative = -1e30
MIB = 1 << 20


def partner(value, axis, bit):
    mask = 2**bit
    pairs = [(source, source ^ mask) for source in range(lax.axis_size(axis))]
    return lax.ppermute(value, axis, pairs)


def soft_weights(scores, allowed):
    masked = jnp.where(allowed, scores, big_negative)
    row_max = jnp.max(masked, axis=-1, keepdims=True)
    exponent = jnp.exp(masked - row_max)
    return (exponent / jnp.sum(exponent, axis=-1, keepdims=True)).astype(jnp.bfloat16)


def attend_dense(queries, key_rows, value_rows, token_clip, scaling):
    token_count, head_count, head_size = queries.shape
    step_size = min(token_count, 512)
    step_count = token_count // step_size
    query_steps = queries.reshape(step_count, step_size, head_count, head_size)
    clip_steps = token_clip.reshape(step_count, step_size)

    def one_step(arguments):
        query_block, clip_block = arguments
        scores = (
            jnp.einsum("qhe,khe->hqk", query_block, key_rows, preferred_element_type=jnp.float32)
            * scaling
        )
        allowed = (clip_block[:, None] == token_clip[None, :])[None]
        weights = soft_weights(scores, allowed)
        return jnp.einsum(
            "hqk,khe->qhe", weights, value_rows, preferred_element_type=jnp.float32
        ).astype(jnp.bfloat16)

    outputs = lax.map(one_step, (query_steps, clip_steps))
    return outputs.reshape(token_count, head_count, head_size)


def body_general(projections, block_source, clip_ids, out_weight):
    ctx_count = lax.axis_size("ctx")
    local_rows, row_width = projections.shape
    local_blocks = block_source.shape[2]
    block_rows = local_rows // local_blocks
    own_blocks = projections.reshape(local_blocks, block_rows, row_width)
    partner_blocks = partner(own_blocks, "dp", 0)
    source_ids = block_source.reshape(local_blocks)
    from_partner = source_ids // (local_blocks * ctx_count) != lax.axis_index("dp")
    chosen_slot = source_ids % local_blocks + local_blocks * from_partner.astype(jnp.int32)
    candidates = jnp.concatenate([own_blocks, partner_blocks], axis=0)
    packed = jnp.take(candidates, chosen_slot, axis=0)
    local_heads = row_width // (3 * HEAD) // ctx_count
    grouped = packed.reshape(local_rows, ctx_count, local_heads, 3 * HEAD)
    block_clip = clip_ids.reshape(-1)
    token_clip = jnp.repeat(block_clip, block_rows)
    scaling = 1.0 / math.sqrt(HEAD)
    regrouped = lax.all_to_all(grouped, "ctx", split_axis=1, concat_axis=0, tiled=True)
    token_count = regrouped.shape[0]
    item_count = regrouped.shape[2]
    features = regrouped.reshape(token_count, item_count, 3 * HEAD)
    queries = features[:, :, :HEAD]
    key_rows = features[:, :, HEAD : 2 * HEAD]
    value_rows = features[:, :, 2 * HEAD :]
    attended = attend_dense(queries, key_rows, value_rows, token_clip, scaling)
    merged = attended.reshape(local_rows * ctx_count, local_heads * HEAD)
    attention_rows = lax.all_to_all(merged, "ctx", split_axis=0, concat_axis=1, tiled=True)
    result = jnp.dot(
        attention_rows,
        lax.all_gather(out_weight, "dp", axis=0, tiled=True),
        preferred_element_type=jnp.float32,
    )
    return result.astype(jnp.bfloat16)


def stage_kernel(source_ref, own_ref, out_ref, sem):
    copy = pltpu.make_async_copy(own_ref, out_ref, sem)
    copy.start()
    copy.wait()


def pack_kernel(source_ref, own_ref, partner_ref, rows_ref, *rest):
    halo_refs, sems = rest[:-1], rest[-1]
    ctx, dp = lax.axis_index("ctx"), lax.axis_index("dp")
    slots = own_ref.shape[0]
    for which, block in ((1, 1 - ctx), (0, ctx)):
        source = source_ref[0, 0, block]
        slot = lax.rem(source, slots)
        away = source // (2 * slots) != dp

        @pl.when(jnp.logical_not(away))
        def _():
            pltpu.make_async_copy(own_ref.at[slot], rows_ref.at[which], sems.at[which]).start()

        @pl.when(away)
        def _():
            pltpu.make_async_copy(partner_ref.at[slot], rows_ref.at[which], sems.at[which]).start()

    pltpu.make_async_copy(own_ref.at[0], rows_ref.at[1], sems.at[1]).wait()
    first = HEAD
    for halo_ref in halo_refs:
        for at in range(0, halo_ref.shape[1], 2 * HEAD):
            halo_ref[:, at : at + 2 * HEAD] = rows_ref[1, :, first : first + 2 * HEAD]
            first += 3 * HEAD
    pltpu.make_async_copy(own_ref.at[0], rows_ref.at[0], sems.at[0]).wait()


def attend(heads, load_queries, load_own, load_more, allowed, out_ref, other_ref):
    scaling = math.log2(math.e) / math.sqrt(HEAD)
    contract_last = (((1,), (1,)), ((), ()))
    ones = jnp.ones((2 * out_ref.shape[0], HEAD), jnp.bfloat16)
    odd_core = lax.rem(lax.axis_index("dp"), 2) == 1
    for start in range(0, heads, 4):
        group = min(4, heads - start)
        scores = []
        for head in range(start, start + group):
            queries = load_queries(head)
            pair = []
            for loader in (load_own, load_more):
                pair.append(
                    lax.dot_general(
                        queries, loader(head, 0), contract_last, preferred_element_type=jnp.float32
                    )
                    * scaling
                )
            scores.append(pair)
        weights = []
        for own, more in scores:
            more = jnp.where(allowed, more, big_negative)
            row_max = jnp.max(jnp.maximum(own, more), axis=-1, keepdims=True)
            weights.append(
                jnp.concatenate(
                    [
                        jnp.exp2(own - row_max).astype(jnp.bfloat16),
                        jnp.exp2(more - row_max).astype(jnp.bfloat16),
                    ],
                    axis=1,
                )
            )
        outs = []
        for head in range(start, start + group):
            values = jnp.concatenate([load_own(head, 1), load_more(head, 1)], axis=0)
            sums = jnp.dot(
                weights[head - start],
                jnp.concatenate([values, ones], axis=1),
                preferred_element_type=jnp.float32,
            )
            outs.append(sums[:, :HEAD] / sums[:, HEAD:])
            out_ref[:, head * HEAD : (head + 1) * HEAD] = outs[-1].astype(jnp.bfloat16)
        for pair in range(group // 2):
            at = (start // 2 + pair) * HEAD
            other = jnp.where(odd_core, outs[2 * pair], outs[2 * pair + 1])
            other_ref[:, at : at + HEAD] = other.astype(jnp.bfloat16)


def inner_kernel(clip_ref, rows_ref, out_ref, other_ref):
    ctx = lax.axis_index("ctx")
    allowed = clip_ref[0, 2 * ctx] == clip_ref[0, 2 * ctx + 1]

    def loader(block):
        def get(head, which):
            first = (head * 3 + 1 + which) * HEAD
            return rows_ref[block, :, first : first + HEAD]

        return get

    attend(
        out_ref.shape[1] // HEAD,
        lambda head: loader(0)(head, -1),
        loader(0),
        loader(1),
        allowed,
        out_ref,
        other_ref,
    )


def edge_kernel(first_head, clip_ref, rows_ref, halo_ref, out_ref, other_ref):
    ctx = lax.axis_index("ctx")
    edge_clip = clip_ref[0, 1 + ctx]
    crosses = edge_clip == clip_ref[0, 2 - ctx]
    allowed = jnp.logical_or(crosses, edge_clip == clip_ref[0, 3 * ctx])

    def load_own(head, which):
        first = ((first_head + head) * 3 + 1 + which) * HEAD
        return rows_ref[1, :, first : first + HEAD]

    def load_more(head, which):
        first = ((first_head + head) * 3 + 1 + which) * HEAD
        at = (2 * head + which) * HEAD
        return jnp.where(crosses, halo_ref[:, at : at + HEAD], rows_ref[0, :, first : first + HEAD])

    attend(
        out_ref.shape[1] // HEAD,
        lambda head: load_own(head, -1),
        load_own,
        load_more,
        allowed,
        out_ref,
        other_ref,
    )


def ring_order(lines):
    return list(range(0, lines, 2)) + list(range(1, lines, 2))[::-1]


def arrange_kernel(origins, parts, *refs):
    (inner_ref, *edge_refs), rest = refs[: 1 + parts], refs[1 + parts :]
    (their_inner_ref, *their_edge_refs), (out_ref, edge_rows, their_edge_rows) = rest[:-3], rest[-3:]
    for refs, held in ((edge_refs, edge_rows), (their_edge_refs, their_edge_rows)):
        first = 0
        for ref in refs:
            held[:, first : first + ref.shape[1]] = ref[...]
            first += ref.shape[1]
    index = lax.axis_index("dp")
    core, side, line = lax.rem(index, 2), lax.rem(index // 2, 2), index // 4
    places = ring_order(lax.axis_size("dp") // 4)
    block = inner_ref.shape[0]
    depth = out_ref.shape[1] // len(origins)
    for number, (steps, other_side) in enumerate(origins):
        from_line = line
        for at, place in enumerate(places):
            from_line = jnp.where(line == place, places[at - steps], from_line)
        pair = from_line * 2 + (1 - side if other_side else side)
        at = slice(number * depth, (number + 1) * depth)
        here = pl.ds(pl.multiple_of((pair * 2 + core) * depth, depth), depth)
        there = pl.ds(pl.multiple_of(pair * depth, depth), depth)
        out_ref[:block, at] = inner_ref[:, here]
        out_ref[block : 2 * block, at] = edge_rows[:, here]
        out_ref[2 * block : 3 * block, at] = their_inner_ref[:, there]
        out_ref[3 * block :, at] = their_edge_rows[:, there]


def project_kernel(first, features_ref, *rest):
    shard_refs, (own_total_ref, their_total_ref) = rest[:-2], rest[-2:]
    rows = own_total_ref.shape[0]
    tile = 2 * HEAD
    for at in range(0, own_total_ref.shape[1], tile):
        here = slice(at, at + tile)
        columns = slice(first + at, first + at + tile)
        weight = jnp.concatenate([ref[:, columns] for ref in shard_refs], axis=0)
        total = jnp.dot(features_ref[...], weight, preferred_element_type=jnp.float32)
        own_total_ref[:, here] = total[:rows]
        their_total_ref[:, here] = total[rows:].astype(jnp.bfloat16)


def finish_kernel(*refs):
    totals, out_ref, held, sems = refs[:-3], refs[-3], refs[-2], refs[-1]
    half = len(totals) // 2
    block = out_ref.shape[0] // 2
    ctx = lax.axis_index("ctx")
    copies = []
    for which, place in ((0, ctx), (1, 1 - ctx)):
        rows = slice(which * block, (which + 1) * block)
        first = 0
        for total_ref, more_ref in zip(totals[:half], totals[half:], strict=True):
            columns = slice(first, first + total_ref.shape[1])
            held[rows, columns] = (total_ref[rows] + more_ref[rows]).astype(jnp.bfloat16)
            first += total_ref.shape[1]
        target = out_ref.at[pl.ds(pl.multiple_of(place * block, block), block)]
        copies.append(pltpu.make_async_copy(held.at[rows], target, sems.at[which]))
        copies[-1].start()
    for copy in copies:
        copy.wait()


SMEM = functools.partial(pl.BlockSpec, memory_space=pltpu.SMEM)
VMEM = functools.partial(pl.BlockSpec, memory_space=pltpu.VMEM)
HBM = functools.partial(pl.BlockSpec, memory_space=pltpu.HBM)


def after(value, *others):
    return lax.optimization_barrier((value, *others))[0]


def body_edge(projections, block_source, clip_ids, out_weight):
    local_rows, row_width = projections.shape
    block_rows = local_rows // 2
    heads = row_width // (3 * HEAD)
    features = heads * HEAD
    depth, width = out_weight.shape
    count = lax.axis_size("dp")
    bf16 = jnp.bfloat16

    def call(kernel, name, shape, in_specs, dtypes=None, scratch=(), out_spec=VMEM()):
        many = isinstance(shape, list)
        shapes = shape if many else [shape]
        dtypes = dtypes or [bf16] * len(shapes)
        shapes = [jax.ShapeDtypeStruct(*one) for one in zip(shapes, dtypes, strict=True)]
        return pl.pallas_call(
            kernel,
            out_shape=shapes if many else shapes[0],
            in_specs=in_specs,
            out_specs=[out_spec] * len(shapes) if many else out_spec,
            scratch_shapes=scratch,
            cost_estimate=pl.CostEstimate(flops=0, bytes_accessed=0, transcendentals=0),
            compiler_params=pltpu.CompilerParams(vmem_limit_bytes=8 * MIB),
            name=name,
        )

    def around(value, step):
        places = ring_order(count // 4)
        moves = [(here, places[(at + step) % len(places)]) for at, here in enumerate(places)]
        return lax.ppermute(
            value, "dp", [(4 * here + rest, 4 * there + rest) for here, there in moves for rest in range(4)]
        )

    def to_side(value):
        return partner(value, "dp", 1)

    def to_core(value):
        return partner(value, "dp", 0)

    own = pltpu.with_memory_space_constraint(
        projections.reshape(2, block_rows, row_width), pltpu.HBM
    )
    shards = {(0, False): [out_weight]}
    from_partner = pltpu.with_memory_space_constraint(to_core(own), pltpu.VMEM)
    ahead = around(out_weight, 1)
    across = to_side(out_weight)
    staged = call(
        stage_kernel,
        "stage",
        own.shape,
        [SMEM(), HBM()],
        scratch=[pltpu.SemaphoreType.DMA],
    )(block_source, own)
    part_heads = [heads * 8 // 16, heads * 8 // 16]
    rows, *packed = call(
        pack_kernel,
        "pack",
        [(2, block_rows, row_width)] + [(block_rows, 2 * HEAD * some) for some in part_heads],
        [SMEM(), VMEM(), VMEM()],
        scratch=[pltpu.SemaphoreType.DMA((2,))],
    )(block_source, staged, from_partner)
    halos = [lax.ppermute(part, "ctx", [(0, 1), (1, 0)]) for part in packed]

    def edge_rows(part, *before):
        some = part_heads[part]
        return call(
            functools.partial(edge_kernel, sum(part_heads[:part])),
            "edge_rows",
            [(block_rows, some * HEAD), (block_rows, some // 2 * HEAD)],
            [SMEM(), VMEM(), VMEM()],
        )(after(clip_ids, *before), rows, halos[part])

    back = around(after(out_weight, staged), -1)
    ahead = after(ahead, *packed)
    shards[1, False], shards[0, True] = [ahead], [across]
    across = to_side(after(ahead, across))
    second = around(ahead, 1)
    inner, inner_other = call(
        inner_kernel,
        "inner_rows",
        [(block_rows, features), (block_rows, features // 2)],
        [SMEM(), VMEM()],
    )(after(clip_ids, ahead), rows)
    theirs = [to_core(inner_other)]

    back = after(back, inner)
    shards[3, False], shards[3, True] = [back], [to_side(back)]
    shards[1, True] = [across]
    second = after(second, *theirs)
    shards[2, False] = [second]
    half = depth // 2
    shards[2, True] = [around(across[:half], 1), to_side(second[half:])]
    edges, edge_others = zip(*[edge_rows(part) for part in range(len(part_heads))], strict=True)
    theirs.append(to_core(edge_others[0]))
    theirs.append(to_core(after(edge_others[1], theirs[-1])))

    origins = list(shards)
    arranged = call(
        functools.partial(arrange_kernel, origins, len(edges)),
        "arrange",
        (2 * local_rows, len(origins) * depth),
        [VMEM()] * (1 + len(edges) + len(theirs)),
        scratch=[
            pltpu.VMEM((block_rows, features), bf16),
            pltpu.VMEM((block_rows, features // 2), bf16),
        ],
    )(inner, *edges, *theirs)
    pieces = [piece for shard in shards.values() for piece in shard]
    totals, mores = [], []
    first = 0
    for columns in (width // 3 * 2, width // 3):
        total, their_total = call(
            functools.partial(project_kernel, first),
            "project",
            [(local_rows, columns)] * 2,
            [VMEM()] * (1 + len(pieces)),
            dtypes=[jnp.float32, bf16],
        )(arranged, *pieces)
        totals.append(total)
        mores.append(to_core(their_total))
        first += columns
    return call(
        finish_kernel,
        "finish",
        (local_rows, width),
        [VMEM()] * 4,
        scratch=[pltpu.VMEM((local_rows, width), bf16), pltpu.SemaphoreType.DMA((2,))],
        out_spec=HBM(),
    )(*totals, *mores)


def body(projections, block_source, clip_ids, out_weight):
    heads = projections.shape[1] // (3 * HEAD)
    two_and_two = lax.axis_size("ctx") == 2 and block_source.shape[2] == 2
    whole_tiles = out_weight.shape[0] % HEAD == 0 and heads % 16 == 0
    if two_and_two and whole_tiles and lax.axis_size("dp") == 16:
        return body_edge(projections, block_source, clip_ids, out_weight)
    return body_general(projections, block_source, clip_ids, out_weight)


def solution(mesh):
    return jax.shard_map(
        body,
        mesh=mesh,
        in_specs=(P(("dp", "ctx"), None), P("dp", "ctx", None), P("dp", None), P("dp", None)),
        out_specs=P(("dp", "ctx"), None),
        check_vma=False,
    )
```

```python
import functools
import math

import jax
import jax.numpy as jnp
from jax import lax
from jax.experimental import pallas as pl
from jax.experimental.pallas import tpu as pltpu
from jax.sharding import PartitionSpec as P

HEAD = 128


big_negative = -1e30
MIB = 1 << 20


def partner(value, axis, bit):
    mask = 2**bit
    pairs = [(source, source ^ mask) for source in range(lax.axis_size(axis))]
    return lax.ppermute(value, axis, pairs)


def soft_weights(scores, allowed):
    masked = jnp.where(allowed, scores, big_negative)
    row_max = jnp.max(masked, axis=-1, keepdims=True)
    exponent = jnp.exp(masked - row_max)
    return (exponent / jnp.sum(exponent, axis=-1, keepdims=True)).astype(jnp.bfloat16)


def attend_dense(queries, key_rows, value_rows, token_clip, scaling):
    token_count, head_count, head_size = queries.shape
    step_size = min(token_count, 512)
    step_count = token_count // step_size
    query_steps = queries.reshape(step_count, step_size, head_count, head_size)
    clip_steps = token_clip.reshape(step_count, step_size)

    def one_step(arguments):
        query_block, clip_block = arguments
        scores = (
            jnp.einsum("qhe,khe->hqk", query_block, key_rows, preferred_element_type=jnp.float32)
            * scaling
        )
        allowed = (clip_block[:, None] == token_clip[None, :])[None]
        weights = soft_weights(scores, allowed)
        return jnp.einsum(
            "hqk,khe->qhe", weights, value_rows, preferred_element_type=jnp.float32
        ).astype(jnp.bfloat16)

    outputs = lax.map(one_step, (query_steps, clip_steps))
    return outputs.reshape(token_count, head_count, head_size)


def body_general(projections, block_source, clip_ids, out_weight):
    ctx_count = lax.axis_size("ctx")
    local_rows, row_width = projections.shape
    local_blocks = block_source.shape[2]
    block_rows = local_rows // local_blocks
    own_blocks = projections.reshape(local_blocks, block_rows, row_width)
    partner_blocks = partner(own_blocks, "dp", 0)
    source_ids = block_source.reshape(local_blocks)
    from_partner = source_ids // (local_blocks * ctx_count) != lax.axis_index("dp")
    chosen_slot = source_ids % local_blocks + local_blocks * from_partner.astype(jnp.int32)
    candidates = jnp.concatenate([own_blocks, partner_blocks], axis=0)
    packed = jnp.take(candidates, chosen_slot, axis=0)
    local_heads = row_width // (3 * HEAD) // ctx_count
    grouped = packed.reshape(local_rows, ctx_count, local_heads, 3 * HEAD)
    block_clip = clip_ids.reshape(-1)
    token_clip = jnp.repeat(block_clip, block_rows)
    scaling = 1.0 / math.sqrt(HEAD)
    regrouped = lax.all_to_all(grouped, "ctx", split_axis=1, concat_axis=0, tiled=True)
    token_count = regrouped.shape[0]
    item_count = regrouped.shape[2]
    features = regrouped.reshape(token_count, item_count, 3 * HEAD)
    queries = features[:, :, :HEAD]
    key_rows = features[:, :, HEAD : 2 * HEAD]
    value_rows = features[:, :, 2 * HEAD :]
    attended = attend_dense(queries, key_rows, value_rows, token_clip, scaling)
    merged = attended.reshape(local_rows * ctx_count, local_heads * HEAD)
    attention_rows = lax.all_to_all(merged, "ctx", split_axis=0, concat_axis=1, tiled=True)
    result = jnp.dot(
        attention_rows,
        lax.all_gather(out_weight, "dp", axis=0, tiled=True),
        preferred_element_type=jnp.float32,
    )
    return result.astype(jnp.bfloat16)


def stage_kernel(source_ref, own_ref, out_ref, sem):
    copy = pltpu.make_async_copy(own_ref, out_ref, sem)
    copy.start()
    copy.wait()


def pack_kernel(source_ref, own_ref, partner_ref, rows_ref, *rest):
    halo_refs, sems = rest[:-1], rest[-1]
    ctx, dp = lax.axis_index("ctx"), lax.axis_index("dp")
    slots = own_ref.shape[0]
    for which, block in ((1, 1 - ctx), (0, ctx)):
        source = source_ref[0, 0, block]
        slot = lax.rem(source, slots)
        away = source // (2 * slots) != dp

        @pl.when(jnp.logical_not(away))
        def _():
            pltpu.make_async_copy(own_ref.at[slot], rows_ref.at[which], sems.at[which]).start()

        @pl.when(away)
        def _():
            pltpu.make_async_copy(partner_ref.at[slot], rows_ref.at[which], sems.at[which]).start()

    pltpu.make_async_copy(own_ref.at[0], rows_ref.at[1], sems.at[1]).wait()
    first = HEAD
    for halo_ref in halo_refs:
        for at in range(0, halo_ref.shape[1], 2 * HEAD):
            halo_ref[:, at : at + 2 * HEAD] = rows_ref[1, :, first : first + 2 * HEAD]
            first += 3 * HEAD
    pltpu.make_async_copy(own_ref.at[0], rows_ref.at[0], sems.at[0]).wait()


def attend(heads, load_queries, load_own, load_more, allowed, out_ref, other_ref):
    scaling = math.log2(math.e) / math.sqrt(HEAD)
    contract_last = (((1,), (1,)), ((), ()))
    ones = jnp.ones((2 * out_ref.shape[0], HEAD), jnp.bfloat16)
    odd_core = lax.rem(lax.axis_index("dp"), 2) == 1
    for start in range(0, heads, 4):
        group = min(4, heads - start)
        scores = []
        for head in range(start, start + group):
            queries = load_queries(head)
            pair = []
            for loader in (load_own, load_more):
                pair.append(
                    lax.dot_general(
                        queries, loader(head, 0), contract_last, preferred_element_type=jnp.float32
                    )
                    * scaling
                )
            scores.append(pair)
        weights = []
        for own, more in scores:
            more = jnp.where(allowed, more, big_negative)
            row_max = jnp.max(jnp.maximum(own, more), axis=-1, keepdims=True)
            weights.append(
                jnp.concatenate(
                    [
                        jnp.exp2(own - row_max).astype(jnp.bfloat16),
                        jnp.exp2(more - row_max).astype(jnp.bfloat16),
                    ],
                    axis=1,
                )
            )
        outs = []
        for head in range(start, start + group):
            values = jnp.concatenate([load_own(head, 1), load_more(head, 1)], axis=0)
            sums = jnp.dot(
                weights[head - start],
                jnp.concatenate([values, ones], axis=1),
                preferred_element_type=jnp.float32,
            )
            outs.append(sums[:, :HEAD] / sums[:, HEAD:])
            out_ref[:, head * HEAD : (head + 1) * HEAD] = outs[-1].astype(jnp.bfloat16)
        for pair in range(group // 2):
            at = (start // 2 + pair) * HEAD
            other = jnp.where(odd_core, outs[2 * pair], outs[2 * pair + 1])
            other_ref[:, at : at + HEAD] = other.astype(jnp.bfloat16)


def inner_kernel(clip_ref, rows_ref, out_ref, other_ref):
    ctx = lax.axis_index("ctx")
    allowed = clip_ref[0, 2 * ctx] == clip_ref[0, 2 * ctx + 1]

    def loader(block):
        def get(head, which):
            first = (head * 3 + 1 + which) * HEAD
            return rows_ref[block, :, first : first + HEAD]

        return get

    attend(
        out_ref.shape[1] // HEAD,
        lambda head: loader(0)(head, -1),
        loader(0),
        loader(1),
        allowed,
        out_ref,
        other_ref,
    )


def edge_kernel(first_head, clip_ref, rows_ref, halo_ref, out_ref, other_ref):
    ctx = lax.axis_index("ctx")
    edge_clip = clip_ref[0, 1 + ctx]
    crosses = edge_clip == clip_ref[0, 2 - ctx]
    allowed = jnp.logical_or(crosses, edge_clip == clip_ref[0, 3 * ctx])

    def load_own(head, which):
        first = ((first_head + head) * 3 + 1 + which) * HEAD
        return rows_ref[1, :, first : first + HEAD]

    def load_more(head, which):
        first = ((first_head + head) * 3 + 1 + which) * HEAD
        at = (2 * head + which) * HEAD
        return jnp.where(crosses, halo_ref[:, at : at + HEAD], rows_ref[0, :, first : first + HEAD])

    attend(
        out_ref.shape[1] // HEAD,
        lambda head: load_own(head, -1),
        load_own,
        load_more,
        allowed,
        out_ref,
        other_ref,
    )


def ring_order(lines):
    return list(range(0, lines, 2)) + list(range(1, lines, 2))[::-1]


def arrange_kernel(origins, parts, *refs):
    (inner_ref, *edge_refs), rest = refs[: 1 + parts], refs[1 + parts :]
    (their_inner_ref, *their_edge_refs), (out_ref, edge_rows, their_edge_rows) = rest[:-3], rest[-3:]
    for refs, held in ((edge_refs, edge_rows), (their_edge_refs, their_edge_rows)):
        first = 0
        for ref in refs:
            held[:, first : first + ref.shape[1]] = ref[...]
            first += ref.shape[1]
    index = lax.axis_index("dp")
    core, side, line = lax.rem(index, 2), lax.rem(index // 2, 2), index // 4
    places = ring_order(lax.axis_size("dp") // 4)
    block = inner_ref.shape[0]
    depth = out_ref.shape[1] // len(origins)
    for number, (steps, other_side) in enumerate(origins):
        from_line = line
        for at, place in enumerate(places):
            from_line = jnp.where(line == place, places[at - steps], from_line)
        pair = from_line * 2 + (1 - side if other_side else side)
        at = slice(number * depth, (number + 1) * depth)
        here = pl.ds(pl.multiple_of((pair * 2 + core) * depth, depth), depth)
        there = pl.ds(pl.multiple_of(pair * depth, depth), depth)
        out_ref[:block, at] = inner_ref[:, here]
        out_ref[block : 2 * block, at] = edge_rows[:, here]
        out_ref[2 * block : 3 * block, at] = their_inner_ref[:, there]
        out_ref[3 * block :, at] = their_edge_rows[:, there]


def project_kernel(first, features_ref, *rest):
    shard_refs, (own_total_ref, their_total_ref) = rest[:-2], rest[-2:]
    rows = own_total_ref.shape[0]
    tile = 2 * HEAD
    for at in range(0, own_total_ref.shape[1], tile):
        here = slice(at, at + tile)
        columns = slice(first + at, first + at + tile)
        weight = jnp.concatenate([ref[:, columns] for ref in shard_refs], axis=0)
        total = jnp.dot(features_ref[...], weight, preferred_element_type=jnp.float32)
        own_total_ref[:, here] = total[:rows]
        their_total_ref[:, here] = total[rows:].astype(jnp.bfloat16)


def finish_kernel(*refs):
    totals, out_ref, held, sems = refs[:-3], refs[-3], refs[-2], refs[-1]
    half = len(totals) // 2
    block = out_ref.shape[0] // 2
    ctx = lax.axis_index("ctx")
    copies = []
    for which, place in ((0, ctx), (1, 1 - ctx)):
        rows = slice(which * block, (which + 1) * block)
        first = 0
        for total_ref, more_ref in zip(totals[:half], totals[half:], strict=True):
            columns = slice(first, first + total_ref.shape[1])
            held[rows, columns] = (total_ref[rows] + more_ref[rows]).astype(jnp.bfloat16)
            first += total_ref.shape[1]
        target = out_ref.at[pl.ds(pl.multiple_of(place * block, block), block)]
        copies.append(pltpu.make_async_copy(held.at[rows], target, sems.at[which]))
        copies[-1].start()
    for copy in copies:
        copy.wait()


SMEM = functools.partial(pl.BlockSpec, memory_space=pltpu.SMEM)
VMEM = functools.partial(pl.BlockSpec, memory_space=pltpu.VMEM)
HBM = functools.partial(pl.BlockSpec, memory_space=pltpu.HBM)


def after(value, *others):
    return lax.optimization_barrier((value, *others))[0]


def body_edge(projections, block_source, clip_ids, out_weight):
    local_rows, row_width = projections.shape
    block_rows = local_rows // 2
    heads = row_width // (3 * HEAD)
    features = heads * HEAD
    depth, width = out_weight.shape
    count = lax.axis_size("dp")
    bf16 = jnp.bfloat16

    def call(kernel, name, shape, in_specs, dtypes=None, scratch=(), out_spec=VMEM()):
        many = isinstance(shape, list)
        shapes = shape if many else [shape]
        dtypes = dtypes or [bf16] * len(shapes)
        shapes = [jax.ShapeDtypeStruct(*one) for one in zip(shapes, dtypes, strict=True)]
        return pl.pallas_call(
            kernel,
            out_shape=shapes if many else shapes[0],
            in_specs=in_specs,
            out_specs=[out_spec] * len(shapes) if many else out_spec,
            scratch_shapes=scratch,
            cost_estimate=pl.CostEstimate(flops=0, bytes_accessed=0, transcendentals=0),
            compiler_params=pltpu.CompilerParams(vmem_limit_bytes=8 * MIB),
            name=name,
        )

    def around(value, step):
        places = ring_order(count // 4)
        moves = [(here, places[(at + step) % len(places)]) for at, here in enumerate(places)]
        return lax.ppermute(
            value, "dp", [(4 * here + rest, 4 * there + rest) for here, there in moves for rest in range(4)]
        )

    def to_side(value):
        return partner(value, "dp", 1)

    def to_core(value):
        return partner(value, "dp", 0)

    own = pltpu.with_memory_space_constraint(
        projections.reshape(2, block_rows, row_width), pltpu.HBM
    )
    shards = {(0, False): [out_weight]}
    from_partner = pltpu.with_memory_space_constraint(to_core(own), pltpu.VMEM)
    ahead = around(out_weight, 1)
    across = to_side(out_weight)
    staged = call(
        stage_kernel,
        "stage",
        own.shape,
        [SMEM(), HBM()],
        scratch=[pltpu.SemaphoreType.DMA],
    )(block_source, own)
    part_heads = [heads * 8 // 16, heads * 8 // 16]
    rows, *packed = call(
        pack_kernel,
        "pack",
        [(2, block_rows, row_width)] + [(block_rows, 2 * HEAD * some) for some in part_heads],
        [SMEM(), VMEM(), VMEM()],
        scratch=[pltpu.SemaphoreType.DMA((2,))],
    )(block_source, staged, from_partner)
    halos = [lax.ppermute(part, "ctx", [(0, 1), (1, 0)]) for part in packed]

    def edge_rows(part, *before):
        some = part_heads[part]
        return call(
            functools.partial(edge_kernel, sum(part_heads[:part])),
            "edge_rows",
            [(block_rows, some * HEAD), (block_rows, some // 2 * HEAD)],
            [SMEM(), VMEM(), VMEM()],
        )(after(clip_ids, *before), rows, halos[part])

    back = around(after(out_weight, staged), -1)
    ahead = after(ahead, *packed)
    shards[1, False], shards[0, True] = [ahead], [across]
    across = to_side(after(ahead, across))
    second = around(ahead, 1)
    inner, inner_other = call(
        inner_kernel,
        "inner_rows",
        [(block_rows, features), (block_rows, features // 2)],
        [SMEM(), VMEM()],
    )(after(clip_ids, ahead), rows)
    theirs = [to_core(inner_other)]

    back = after(back, inner)
    shards[3, False], shards[3, True] = [back], [to_side(back)]
    shards[1, True] = [across]
    edges, edge_others = zip(*[edge_rows(part) for part in range(len(part_heads))], strict=True)
    second = after(second, *theirs, edges[0])
    shards[2, False] = [second]
    cut = depth // 8 * 5
    shards[2, True] = [around(after(across, edges[0])[:cut], 1), to_side(second[cut:])]
    theirs += [to_core(part) for part in edge_others]

    origins = list(shards)
    arranged = call(
        functools.partial(arrange_kernel, origins, len(edges)),
        "arrange",
        (2 * local_rows, len(origins) * depth),
        [VMEM()] * (1 + len(edges) + len(theirs)),
        scratch=[
            pltpu.VMEM((block_rows, features), bf16),
            pltpu.VMEM((block_rows, features // 2), bf16),
        ],
    )(inner, *edges, *theirs)
    pieces = [piece for shard in shards.values() for piece in shard]
    totals, mores = [], []
    first = 0
    for columns in (width // 3 * 2, width // 3):
        total, their_total = call(
            functools.partial(project_kernel, first),
            "project",
            [(local_rows, columns)] * 2,
            [VMEM()] * (1 + len(pieces)),
            dtypes=[jnp.float32, bf16],
        )(arranged, *pieces)
        totals.append(total)
        mores.append(to_core(their_total))
        first += columns
    return call(
        finish_kernel,
        "finish",
        (local_rows, width),
        [VMEM()] * 4,
        scratch=[pltpu.VMEM((local_rows, width), bf16), pltpu.SemaphoreType.DMA((2,))],
        out_spec=HBM(),
    )(*totals, *mores)


def body(projections, block_source, clip_ids, out_weight):
    heads = projections.shape[1] // (3 * HEAD)
    two_and_two = lax.axis_size("ctx") == 2 and block_source.shape[2] == 2
    whole_tiles = out_weight.shape[0] % HEAD == 0 and heads % 16 == 0
    if two_and_two and whole_tiles and lax.axis_size("dp") == 16:
        return body_edge(projections, block_source, clip_ids, out_weight)
    return body_general(projections, block_source, clip_ids, out_weight)


def solution(mesh):
    return jax.shard_map(
        body,
        mesh=mesh,
        in_specs=(P(("dp", "ctx"), None), P("dp", "ctx", None), P("dp", None), P("dp", None)),
        out_specs=P(("dp", "ctx"), None),
        check_vma=False,
    )
```

```python
import functools
import math

import jax
import jax.numpy as jnp
from jax import lax
from jax.experimental import pallas as pl
from jax.experimental.pallas import tpu as pltpu
from jax.sharding import PartitionSpec as P

HEAD = 128


big_negative = -1e30
MIB = 1 << 20


def partner(value, axis, bit):
    mask = 2**bit
    pairs = [(source, source ^ mask) for source in range(lax.axis_size(axis))]
    return lax.ppermute(value, axis, pairs)


def soft_weights(scores, allowed):
    masked = jnp.where(allowed, scores, big_negative)
    row_max = jnp.max(masked, axis=-1, keepdims=True)
    exponent = jnp.exp(masked - row_max)
    return (exponent / jnp.sum(exponent, axis=-1, keepdims=True)).astype(jnp.bfloat16)


def attend_dense(queries, key_rows, value_rows, token_clip, scaling):
    token_count, head_count, head_size = queries.shape
    step_size = min(token_count, 512)
    step_count = token_count // step_size
    query_steps = queries.reshape(step_count, step_size, head_count, head_size)
    clip_steps = token_clip.reshape(step_count, step_size)

    def one_step(arguments):
        query_block, clip_block = arguments
        scores = (
            jnp.einsum("qhe,khe->hqk", query_block, key_rows, preferred_element_type=jnp.float32)
            * scaling
        )
        allowed = (clip_block[:, None] == token_clip[None, :])[None]
        weights = soft_weights(scores, allowed)
        return jnp.einsum(
            "hqk,khe->qhe", weights, value_rows, preferred_element_type=jnp.float32
        ).astype(jnp.bfloat16)

    outputs = lax.map(one_step, (query_steps, clip_steps))
    return outputs.reshape(token_count, head_count, head_size)


def body_general(projections, block_source, clip_ids, out_weight):
    ctx_count = lax.axis_size("ctx")
    local_rows, row_width = projections.shape
    local_blocks = block_source.shape[2]
    block_rows = local_rows // local_blocks
    own_blocks = projections.reshape(local_blocks, block_rows, row_width)
    partner_blocks = partner(own_blocks, "dp", 0)
    source_ids = block_source.reshape(local_blocks)
    from_partner = source_ids // (local_blocks * ctx_count) != lax.axis_index("dp")
    chosen_slot = source_ids % local_blocks + local_blocks * from_partner.astype(jnp.int32)
    candidates = jnp.concatenate([own_blocks, partner_blocks], axis=0)
    packed = jnp.take(candidates, chosen_slot, axis=0)
    local_heads = row_width // (3 * HEAD) // ctx_count
    grouped = packed.reshape(local_rows, ctx_count, local_heads, 3 * HEAD)
    block_clip = clip_ids.reshape(-1)
    token_clip = jnp.repeat(block_clip, block_rows)
    scaling = 1.0 / math.sqrt(HEAD)
    regrouped = lax.all_to_all(grouped, "ctx", split_axis=1, concat_axis=0, tiled=True)
    token_count = regrouped.shape[0]
    item_count = regrouped.shape[2]
    features = regrouped.reshape(token_count, item_count, 3 * HEAD)
    queries = features[:, :, :HEAD]
    key_rows = features[:, :, HEAD : 2 * HEAD]
    value_rows = features[:, :, 2 * HEAD :]
    attended = attend_dense(queries, key_rows, value_rows, token_clip, scaling)
    merged = attended.reshape(local_rows * ctx_count, local_heads * HEAD)
    attention_rows = lax.all_to_all(merged, "ctx", split_axis=0, concat_axis=1, tiled=True)
    result = jnp.dot(
        attention_rows,
        lax.all_gather(out_weight, "dp", axis=0, tiled=True),
        preferred_element_type=jnp.float32,
    )
    return result.astype(jnp.bfloat16)


def stage_kernel(source_ref, own_ref, out_ref, sem):
    copy = pltpu.make_async_copy(own_ref, out_ref, sem)
    copy.start()
    copy.wait()


def pack_kernel(source_ref, own_ref, partner_ref, rows_ref, *rest):
    halo_refs, sems = rest[:-1], rest[-1]
    ctx, dp = lax.axis_index("ctx"), lax.axis_index("dp")
    slots = own_ref.shape[0]
    for which, block in ((1, 1 - ctx), (0, ctx)):
        source = source_ref[0, 0, block]
        slot = lax.rem(source, slots)
        away = source // (2 * slots) != dp

        @pl.when(jnp.logical_not(away))
        def _():
            pltpu.make_async_copy(own_ref.at[slot], rows_ref.at[which], sems.at[which]).start()

        @pl.when(away)
        def _():
            pltpu.make_async_copy(partner_ref.at[slot], rows_ref.at[which], sems.at[which]).start()

    pltpu.make_async_copy(own_ref.at[0], rows_ref.at[1], sems.at[1]).wait()
    first = HEAD
    for halo_ref in halo_refs:
        for at in range(0, halo_ref.shape[1], 2 * HEAD):
            halo_ref[:, at : at + 2 * HEAD] = rows_ref[1, :, first : first + 2 * HEAD]
            first += 3 * HEAD
    pltpu.make_async_copy(own_ref.at[0], rows_ref.at[0], sems.at[0]).wait()


def attend(heads, load_queries, load_own, load_more, allowed, out_ref, other_ref):
    scaling = math.log2(math.e) / math.sqrt(HEAD)
    contract_last = (((1,), (1,)), ((), ()))
    ones = jnp.ones((2 * out_ref.shape[0], HEAD), jnp.bfloat16)
    odd_core = lax.rem(lax.axis_index("dp"), 2) == 1
    for start in range(0, heads, 4):
        group = min(4, heads - start)
        scores = []
        for head in range(start, start + group):
            queries = load_queries(head)
            pair = []
            for loader in (load_own, load_more):
                pair.append(
                    lax.dot_general(
                        queries, loader(head, 0), contract_last, preferred_element_type=jnp.float32
                    )
                    * scaling
                )
            scores.append(pair)
        weights = []
        for own, more in scores:
            more = jnp.where(allowed, more, big_negative)
            row_max = jnp.max(jnp.maximum(own, more), axis=-1, keepdims=True)
            weights.append(
                jnp.concatenate(
                    [
                        jnp.exp2(own - row_max).astype(jnp.bfloat16),
                        jnp.exp2(more - row_max).astype(jnp.bfloat16),
                    ],
                    axis=1,
                )
            )
        outs = []
        for head in range(start, start + group):
            values = jnp.concatenate([load_own(head, 1), load_more(head, 1)], axis=0)
            sums = jnp.dot(
                weights[head - start],
                jnp.concatenate([values, ones], axis=1),
                preferred_element_type=jnp.float32,
            )
            outs.append(sums[:, :HEAD] / sums[:, HEAD:])
            out_ref[:, head * HEAD : (head + 1) * HEAD] = outs[-1].astype(jnp.bfloat16)
        for pair in range(group // 2):
            at = (start // 2 + pair) * HEAD
            other = jnp.where(odd_core, outs[2 * pair], outs[2 * pair + 1])
            other_ref[:, at : at + HEAD] = other.astype(jnp.bfloat16)


def inner_kernel(clip_ref, rows_ref, out_ref, other_ref):
    ctx = lax.axis_index("ctx")
    allowed = clip_ref[0, 2 * ctx] == clip_ref[0, 2 * ctx + 1]

    def loader(block):
        def get(head, which):
            first = (head * 3 + 1 + which) * HEAD
            return rows_ref[block, :, first : first + HEAD]

        return get

    attend(
        out_ref.shape[1] // HEAD,
        lambda head: loader(0)(head, -1),
        loader(0),
        loader(1),
        allowed,
        out_ref,
        other_ref,
    )


def edge_kernel(first_head, clip_ref, rows_ref, halo_ref, out_ref, other_ref):
    ctx = lax.axis_index("ctx")
    edge_clip = clip_ref[0, 1 + ctx]
    crosses = edge_clip == clip_ref[0, 2 - ctx]
    allowed = jnp.logical_or(crosses, edge_clip == clip_ref[0, 3 * ctx])

    def load_own(head, which):
        first = ((first_head + head) * 3 + 1 + which) * HEAD
        return rows_ref[1, :, first : first + HEAD]

    def load_more(head, which):
        first = ((first_head + head) * 3 + 1 + which) * HEAD
        at = (2 * head + which) * HEAD
        return jnp.where(crosses, halo_ref[:, at : at + HEAD], rows_ref[0, :, first : first + HEAD])

    attend(
        out_ref.shape[1] // HEAD,
        lambda head: load_own(head, -1),
        load_own,
        load_more,
        allowed,
        out_ref,
        other_ref,
    )


def ring_order(lines):
    return list(range(0, lines, 2)) + list(range(1, lines, 2))[::-1]


def shard_places(origins, depth):
    index = lax.axis_index("dp")
    core, side, line = lax.rem(index, 2), lax.rem(index // 2, 2), index // 4
    places = ring_order(lax.axis_size("dp") // 4)
    found = []
    for steps, other_side in origins:
        from_line = line
        for at, place in enumerate(places):
            from_line = jnp.where(line == place, places[at - steps], from_line)
        pair = from_line * 2 + (1 - side if other_side else side)
        here = pl.ds(pl.multiple_of((pair * 2 + core) * depth, depth), depth)
        there = pl.ds(pl.multiple_of(pair * depth, depth), depth)
        found.append((here, there))
    return found


def inner_project_kernel(origins, early, inner_ref, their_ref, *rest):
    shard_refs, (total_ref, left_ref, features) = rest[:-3], rest[-3:]
    block = inner_ref.shape[0]
    depth = left_ref.shape[1] // (len(origins) - early)
    for number, (here, there) in enumerate(shard_places(origins, depth)):
        ref, at = (features, number) if number < early else (left_ref, number - early)
        ref[:block, at * depth : (at + 1) * depth] = inner_ref[:, here]
        ref[block:, at * depth : (at + 1) * depth] = their_ref[:, there]
    tile = 2 * HEAD
    for first in range(0, total_ref.shape[1], tile):
        columns = slice(first, first + tile)
        weight = jnp.concatenate([ref[:, columns] for ref in shard_refs], axis=0)
        total_ref[:, columns] = jnp.dot(
            features[...], weight, preferred_element_type=jnp.float32
        )


def arrange_kernel(origins, parts, *refs):
    edge_refs, their_refs = refs[:parts], refs[parts : 2 * parts]
    out_ref, edge_rows, their_rows = refs[2 * parts :]
    for refs, held in ((edge_refs, edge_rows), (their_refs, their_rows)):
        first = 0
        for ref in refs:
            held[:, first : first + ref.shape[1]] = ref[...]
            first += ref.shape[1]
    block = edge_rows.shape[0]
    depth = out_ref.shape[1] // len(origins)
    for number, (here, there) in enumerate(shard_places(origins, depth)):
        at = slice(number * depth, (number + 1) * depth)
        out_ref[:block, at] = edge_rows[:, here]
        out_ref[block:, at] = their_rows[:, there]


def project_kernel(first, edge_ref, left_ref, inner_total_ref, *rest):
    shard_refs, (own_total_ref, their_total_ref) = rest[:-2], rest[-2:]
    block = own_total_ref.shape[0] // 2
    left = left_ref.shape[1]
    tile = 2 * HEAD
    for at in range(0, own_total_ref.shape[1], tile):
        here = slice(at, at + tile)
        columns = slice(first + at, first + at + tile)
        weight = jnp.concatenate([ref[:, columns] for ref in shard_refs], axis=0)
        edge = jnp.dot(edge_ref[...], weight, preferred_element_type=jnp.float32)
        inner = inner_total_ref[:, columns] + jnp.dot(
            left_ref[...], weight[-left:], preferred_element_type=jnp.float32
        )
        own_total_ref[:block, here] = inner[:block]
        own_total_ref[block:, here] = edge[:block]
        their_total_ref[:block, here] = inner[block:].astype(jnp.bfloat16)
        their_total_ref[block:, here] = edge[block:].astype(jnp.bfloat16)


def finish_kernel(first, total_ref, more_ref, *rest):
    out_ref, held, sems = rest[-3:]
    block = out_ref.shape[0] // 2
    ctx = lax.axis_index("ctx")
    columns = pl.ds(first, total_ref.shape[1])
    copies = []
    for which, place in ((0, ctx), (1, 1 - ctx)):
        rows = slice(which * block, (which + 1) * block)
        held[rows] = (total_ref[rows] + more_ref[rows]).astype(jnp.bfloat16)
        target = out_ref.at[pl.ds(pl.multiple_of(place * block, block), block), columns]
        copies.append(pltpu.make_async_copy(held.at[rows], target, sems.at[which]))
        copies[-1].start()
    for copy in copies:
        copy.wait()


SMEM = functools.partial(pl.BlockSpec, memory_space=pltpu.SMEM)
VMEM = functools.partial(pl.BlockSpec, memory_space=pltpu.VMEM)
HBM = functools.partial(pl.BlockSpec, memory_space=pltpu.HBM)


def after(value, *others):
    return lax.optimization_barrier((value, *others))[0]


def body_edge(projections, block_source, clip_ids, out_weight):
    local_rows, row_width = projections.shape
    block_rows = local_rows // 2
    heads = row_width // (3 * HEAD)
    features = heads * HEAD
    depth, width = out_weight.shape
    count = lax.axis_size("dp")
    bf16 = jnp.bfloat16

    def call(kernel, name, shape, in_specs, dtypes=None, scratch=(), out_spec=VMEM(), aliases={}):
        many = isinstance(shape, list)
        shapes = shape if many else [shape]
        dtypes = dtypes or [bf16] * len(shapes)
        shapes = [jax.ShapeDtypeStruct(*one) for one in zip(shapes, dtypes, strict=True)]
        return pl.pallas_call(
            kernel,
            out_shape=shapes if many else shapes[0],
            in_specs=in_specs,
            out_specs=[out_spec] * len(shapes) if many else out_spec,
            scratch_shapes=scratch,
            input_output_aliases=aliases,
            cost_estimate=pl.CostEstimate(flops=0, bytes_accessed=0, transcendentals=0),
            compiler_params=pltpu.CompilerParams(vmem_limit_bytes=8 * MIB),
            name=name,
        )

    def around(value, step):
        places = ring_order(count // 4)
        moves = [(here, places[(at + step) % len(places)]) for at, here in enumerate(places)]
        return lax.ppermute(
            value, "dp", [(4 * here + rest, 4 * there + rest) for here, there in moves for rest in range(4)]
        )

    def to_side(value):
        return partner(value, "dp", 1)

    def to_core(value):
        return partner(value, "dp", 0)

    own = pltpu.with_memory_space_constraint(
        projections.reshape(2, block_rows, row_width), pltpu.HBM
    )
    shards = {(0, False): [out_weight]}
    from_partner = pltpu.with_memory_space_constraint(to_core(own), pltpu.VMEM)
    ahead = around(out_weight, 1)
    across = to_side(out_weight)
    staged = call(
        stage_kernel,
        "stage",
        own.shape,
        [SMEM(), HBM()],
        scratch=[pltpu.SemaphoreType.DMA],
    )(block_source, own)
    part_heads = [heads * 8 // 16, heads * 8 // 16]
    rows, *packed = call(
        pack_kernel,
        "pack",
        [(2, block_rows, row_width)] + [(block_rows, 2 * HEAD * some) for some in part_heads],
        [SMEM(), VMEM(), VMEM()],
        scratch=[pltpu.SemaphoreType.DMA((2,))],
    )(block_source, staged, from_partner)
    halos = [lax.ppermute(part, "ctx", [(0, 1), (1, 0)]) for part in packed]

    def edge_rows(part, *before):
        some = part_heads[part]
        return call(
            functools.partial(edge_kernel, sum(part_heads[:part])),
            "edge_rows",
            [(block_rows, some * HEAD), (block_rows, some // 2 * HEAD)],
            [SMEM(), VMEM(), VMEM()],
        )(after(clip_ids, *before), rows, halos[part])

    back = around(after(out_weight, staged), -1)
    ahead = after(ahead, *packed)
    shards[1, False], shards[0, True] = [ahead], [across]
    across = to_side(after(ahead, across))
    second = around(ahead, 1)
    inner, inner_other = call(
        inner_kernel,
        "inner_rows",
        [(block_rows, features), (block_rows, features // 2)],
        [SMEM(), VMEM()],
    )(after(clip_ids, ahead), rows)
    theirs = [to_core(inner_other)]

    back = after(back, inner)
    shards[3, False] = [back]
    back_across = to_side(back)
    shards[1, True] = [across]
    early = list(shards)
    origins = [*early, (2, False), (3, True), (2, True)]
    inner_total, inner_left = call(
        functools.partial(inner_project_kernel, origins, len(early)),
        "inner_project",
        [(local_rows, width), (local_rows, (len(origins) - len(early)) * depth)],
        [VMEM()] * (2 + len(early)),
        dtypes=[jnp.float32, bf16],
        scratch=[pltpu.VMEM((local_rows, len(early) * depth), bf16)],
    )(inner, *theirs, *[shards[origin][0] for origin in early])
    edges, edge_others = zip(*[edge_rows(part) for part in range(len(part_heads))], strict=True)
    second = after(second, inner_total, edges[0])
    cut = depth // 8 * 5
    shards[2, False] = [second]
    shards[3, True] = [back_across]
    shards[2, True] = [around(after(across, edges[0])[:cut], 1), to_side(second[cut:])]
    theirs = [to_core(part) for part in edge_others]

    arranged = call(
        functools.partial(arrange_kernel, origins, len(edges)),
        "arrange",
        (local_rows, len(origins) * depth),
        [VMEM()] * (len(edges) + len(theirs)),
        scratch=[
            pltpu.VMEM((block_rows, features), bf16),
            pltpu.VMEM((block_rows, features // 2), bf16),
        ],
    )(*edges, *theirs)
    pieces = [piece for origin in origins for piece in shards[origin]]
    sums = []
    first = 0
    for columns in (width // 3 * 2, width // 3):
        total, their_total = call(
            functools.partial(project_kernel, first),
            "project",
            [(local_rows, columns)] * 2,
            [VMEM()] * (3 + len(pieces)),
            dtypes=[jnp.float32, bf16],
        )(arranged, inner_left, inner_total, *pieces)
        sums.append((first, total, to_core(their_total)))
        first += columns
    out = []
    for first, total, more in sums:
        out = [
            call(
                functools.partial(finish_kernel, first),
                "finish",
                (local_rows, width),
                [VMEM()] * 2 + [HBM()] * len(out),
                scratch=[pltpu.VMEM(total.shape, bf16), pltpu.SemaphoreType.DMA((2,))],
                out_spec=HBM(),
                aliases={2: 0} if out else {},
            )(total, more, *out)
        ]
    return out[0]


def body(projections, block_source, clip_ids, out_weight):
    heads = projections.shape[1] // (3 * HEAD)
    two_and_two = lax.axis_size("ctx") == 2 and block_source.shape[2] == 2
    whole_tiles = out_weight.shape[0] % HEAD == 0 and heads % 16 == 0
    if two_and_two and whole_tiles and lax.axis_size("dp") == 16:
        return body_edge(projections, block_source, clip_ids, out_weight)
    return body_general(projections, block_source, clip_ids, out_weight)


def solution(mesh):
    return jax.shard_map(
        body,
        mesh=mesh,
        in_specs=(P(("dp", "ctx"), None), P("dp", "ctx", None), P("dp", None), P("dp", None)),
        out_specs=P(("dp", "ctx"), None),
        check_vma=False,
    )
```

```python
import functools
import math

import jax
import jax.numpy as jnp
from jax import lax
from jax.experimental import pallas as pl
from jax.experimental.pallas import tpu as pltpu
from jax.sharding import PartitionSpec as P

HEAD = 128


big_negative = -1e30
MIB = 1 << 20


def partner(value, axis, bit):
    mask = 2**bit
    pairs = [(source, source ^ mask) for source in range(lax.axis_size(axis))]
    return lax.ppermute(value, axis, pairs)


def soft_weights(scores, allowed):
    masked = jnp.where(allowed, scores, big_negative)
    row_max = jnp.max(masked, axis=-1, keepdims=True)
    exponent = jnp.exp(masked - row_max)
    return (exponent / jnp.sum(exponent, axis=-1, keepdims=True)).astype(jnp.bfloat16)


def attend_dense(queries, key_rows, value_rows, token_clip, scaling):
    token_count, head_count, head_size = queries.shape
    step_size = min(token_count, 512)
    step_count = token_count // step_size
    query_steps = queries.reshape(step_count, step_size, head_count, head_size)
    clip_steps = token_clip.reshape(step_count, step_size)

    def one_step(arguments):
        query_block, clip_block = arguments
        scores = (
            jnp.einsum("qhe,khe->hqk", query_block, key_rows, preferred_element_type=jnp.float32)
            * scaling
        )
        allowed = (clip_block[:, None] == token_clip[None, :])[None]
        weights = soft_weights(scores, allowed)
        return jnp.einsum(
            "hqk,khe->qhe", weights, value_rows, preferred_element_type=jnp.float32
        ).astype(jnp.bfloat16)

    outputs = lax.map(one_step, (query_steps, clip_steps))
    return outputs.reshape(token_count, head_count, head_size)


def body_general(projections, block_source, clip_ids, out_weight):
    ctx_count = lax.axis_size("ctx")
    local_rows, row_width = projections.shape
    local_blocks = block_source.shape[2]
    block_rows = local_rows // local_blocks
    own_blocks = projections.reshape(local_blocks, block_rows, row_width)
    partner_blocks = partner(own_blocks, "dp", 0)
    source_ids = block_source.reshape(local_blocks)
    from_partner = source_ids // (local_blocks * ctx_count) != lax.axis_index("dp")
    chosen_slot = source_ids % local_blocks + local_blocks * from_partner.astype(jnp.int32)
    candidates = jnp.concatenate([own_blocks, partner_blocks], axis=0)
    packed = jnp.take(candidates, chosen_slot, axis=0)
    local_heads = row_width // (3 * HEAD) // ctx_count
    grouped = packed.reshape(local_rows, ctx_count, local_heads, 3 * HEAD)
    block_clip = clip_ids.reshape(-1)
    token_clip = jnp.repeat(block_clip, block_rows)
    scaling = 1.0 / math.sqrt(HEAD)
    regrouped = lax.all_to_all(grouped, "ctx", split_axis=1, concat_axis=0, tiled=True)
    token_count = regrouped.shape[0]
    item_count = regrouped.shape[2]
    features = regrouped.reshape(token_count, item_count, 3 * HEAD)
    queries = features[:, :, :HEAD]
    key_rows = features[:, :, HEAD : 2 * HEAD]
    value_rows = features[:, :, 2 * HEAD :]
    attended = attend_dense(queries, key_rows, value_rows, token_clip, scaling)
    merged = attended.reshape(local_rows * ctx_count, local_heads * HEAD)
    attention_rows = lax.all_to_all(merged, "ctx", split_axis=0, concat_axis=1, tiled=True)
    result = jnp.dot(
        attention_rows,
        lax.all_gather(out_weight, "dp", axis=0, tiled=True),
        preferred_element_type=jnp.float32,
    )
    return result.astype(jnp.bfloat16)


def stage_kernel(source_ref, own_ref, out_ref, sem):
    copy = pltpu.make_async_copy(own_ref, out_ref, sem)
    copy.start()
    copy.wait()


def pack_kernel(source_ref, own_ref, partner_ref, rows_ref, *rest):
    halo_refs, sems = rest[:-1], rest[-1]
    ctx, dp = lax.axis_index("ctx"), lax.axis_index("dp")
    slots = own_ref.shape[0]
    for which, block in ((1, 1 - ctx), (0, ctx)):
        source = source_ref[0, 0, block]
        slot = lax.rem(source, slots)
        away = source // (2 * slots) != dp

        @pl.when(jnp.logical_not(away))
        def _():
            pltpu.make_async_copy(own_ref.at[slot], rows_ref.at[which], sems.at[which]).start()

        @pl.when(away)
        def _():
            pltpu.make_async_copy(partner_ref.at[slot], rows_ref.at[which], sems.at[which]).start()

    pltpu.make_async_copy(own_ref.at[0], rows_ref.at[1], sems.at[1]).wait()
    first = HEAD
    for halo_ref in halo_refs:
        for at in range(0, halo_ref.shape[1], 2 * HEAD):
            halo_ref[:, at : at + 2 * HEAD] = rows_ref[1, :, first : first + 2 * HEAD]
            first += 3 * HEAD
    pltpu.make_async_copy(own_ref.at[0], rows_ref.at[0], sems.at[0]).wait()


def attend(heads, load_queries, load_own, load_more, allowed, out_ref, other_ref):
    scaling = math.log2(math.e) / math.sqrt(HEAD)
    contract_last = (((1,), (1,)), ((), ()))
    ones = jnp.ones((2 * out_ref.shape[0], HEAD), jnp.bfloat16)
    odd_core = lax.rem(lax.axis_index("dp"), 2) == 1
    for start in range(0, heads, 4):
        group = min(4, heads - start)
        scores = []
        for head in range(start, start + group):
            queries = load_queries(head)
            pair = []
            for loader in (load_own, load_more):
                pair.append(
                    lax.dot_general(
                        queries, loader(head, 0), contract_last, preferred_element_type=jnp.float32
                    )
                    * scaling
                )
            scores.append(pair)
        weights = []
        for own, more in scores:
            more = jnp.where(allowed, more, big_negative)
            row_max = jnp.max(jnp.maximum(own, more), axis=-1, keepdims=True)
            weights.append(
                jnp.concatenate(
                    [
                        jnp.exp2(own - row_max).astype(jnp.bfloat16),
                        jnp.exp2(more - row_max).astype(jnp.bfloat16),
                    ],
                    axis=1,
                )
            )
        outs = []
        for head in range(start, start + group):
            values = jnp.concatenate([load_own(head, 1), load_more(head, 1)], axis=0)
            sums = jnp.dot(
                weights[head - start],
                jnp.concatenate([values, ones], axis=1),
                preferred_element_type=jnp.float32,
            )
            outs.append(sums[:, :HEAD] / sums[:, HEAD:])
            out_ref[:, head * HEAD : (head + 1) * HEAD] = outs[-1].astype(jnp.bfloat16)
        for pair in range(group // 2):
            at = (start // 2 + pair) * HEAD
            other = jnp.where(odd_core, outs[2 * pair], outs[2 * pair + 1])
            other_ref[:, at : at + HEAD] = other.astype(jnp.bfloat16)


def inner_kernel(clip_ref, rows_ref, out_ref, other_ref):
    ctx = lax.axis_index("ctx")
    allowed = clip_ref[0, 2 * ctx] == clip_ref[0, 2 * ctx + 1]

    def loader(block):
        def get(head, which):
            first = (head * 3 + 1 + which) * HEAD
            return rows_ref[block, :, first : first + HEAD]

        return get

    attend(
        out_ref.shape[1] // HEAD,
        lambda head: loader(0)(head, -1),
        loader(0),
        loader(1),
        allowed,
        out_ref,
        other_ref,
    )


def edge_kernel(first_head, clip_ref, rows_ref, halo_ref, out_ref, other_ref):
    ctx = lax.axis_index("ctx")
    edge_clip = clip_ref[0, 1 + ctx]
    crosses = edge_clip == clip_ref[0, 2 - ctx]
    allowed = jnp.logical_or(crosses, edge_clip == clip_ref[0, 3 * ctx])

    def load_own(head, which):
        first = ((first_head + head) * 3 + 1 + which) * HEAD
        return rows_ref[1, :, first : first + HEAD]

    def load_more(head, which):
        first = ((first_head + head) * 3 + 1 + which) * HEAD
        at = (2 * head + which) * HEAD
        return jnp.where(crosses, halo_ref[:, at : at + HEAD], rows_ref[0, :, first : first + HEAD])

    attend(
        out_ref.shape[1] // HEAD,
        lambda head: load_own(head, -1),
        load_own,
        load_more,
        allowed,
        out_ref,
        other_ref,
    )


def ring_order(lines):
    return list(range(0, lines, 2)) + list(range(1, lines, 2))[::-1]


def shard_places(origins, depth):
    index = lax.axis_index("dp")
    core, side, line = lax.rem(index, 2), lax.rem(index // 2, 2), index // 4
    places = ring_order(lax.axis_size("dp") // 4)
    found = []
    for steps, other_side in origins:
        from_line = line
        for at, place in enumerate(places):
            from_line = jnp.where(line == place, places[at - steps], from_line)
        pair = from_line * 2 + (1 - side if other_side else side)
        here = pl.ds(pl.multiple_of((pair * 2 + core) * depth, depth), depth)
        there = pl.ds(pl.multiple_of(pair * depth, depth), depth)
        found.append((here, there))
    return found


def inner_project_kernel(origins, early, inner_ref, their_ref, *rest):
    shard_refs, (total_ref, left_ref, features) = rest[:-3], rest[-3:]
    block = inner_ref.shape[0]
    depth = left_ref.shape[1] // (len(origins) - early)
    for number, (here, there) in enumerate(shard_places(origins, depth)):
        ref, at = (features, number) if number < early else (left_ref, number - early)
        ref[:block, at * depth : (at + 1) * depth] = inner_ref[:, here]
        ref[block:, at * depth : (at + 1) * depth] = their_ref[:, there]
    tile = 2 * HEAD
    for first in range(0, total_ref.shape[1], tile):
        columns = slice(first, first + tile)
        weight = jnp.concatenate([ref[:, columns] for ref in shard_refs], axis=0)
        total_ref[:, columns] = jnp.dot(
            features[...], weight, preferred_element_type=jnp.float32
        )


def arrange_kernel(origins, parts, *refs):
    edge_refs, their_refs = refs[:parts], refs[parts : 2 * parts]
    out_ref, edge_rows, their_rows = refs[2 * parts :]
    for refs, held in ((edge_refs, edge_rows), (their_refs, their_rows)):
        first = 0
        for ref in refs:
            held[:, first : first + ref.shape[1]] = ref[...]
            first += ref.shape[1]
    block = edge_rows.shape[0]
    depth = out_ref.shape[1] // len(origins)
    for number, (here, there) in enumerate(shard_places(origins, depth)):
        at = slice(number * depth, (number + 1) * depth)
        out_ref[:block, at] = edge_rows[:, here]
        out_ref[block:, at] = their_rows[:, there]


def edge_project_kernel(edge_ref, left_ref, inner_total_ref, *rest):
    shard_refs, total_ref = rest[:-1], rest[-1]
    rows = edge_ref.shape[0]
    depths = sum(ref.shape[0] for ref in shard_refs)
    depth = edge_ref.shape[1] - depths
    left = left_ref.shape[1] - depth
    tile = 2 * HEAD
    for first in range(0, total_ref.shape[1], tile):
        columns = slice(first, first + tile)
        weight = jnp.concatenate([ref[:, columns] for ref in shard_refs], axis=0)
        total_ref[:rows, columns] = inner_total_ref[:, columns] + jnp.dot(
            left_ref[:, :left], weight[-left:], preferred_element_type=jnp.float32
        )
        total_ref[rows:, columns] = jnp.dot(
            edge_ref[:, :depths], weight, preferred_element_type=jnp.float32
        )


def last_project_kernel(first, edge_ref, left_ref, total_ref, *rest):
    shard_refs, (own_total_ref, their_total_ref) = rest[:-2], rest[-2:]
    block = own_total_ref.shape[0] // 2
    depth = sum(ref.shape[0] for ref in shard_refs)
    features = jnp.concatenate([left_ref[:, -depth:], edge_ref[:, -depth:]], axis=0)
    tile = 2 * HEAD
    for at in range(0, own_total_ref.shape[1], tile):
        here = slice(at, at + tile)
        columns = slice(first + at, first + at + tile)
        weight = jnp.concatenate([ref[:, columns] for ref in shard_refs], axis=0)
        total = total_ref[:, columns] + jnp.dot(
            features, weight, preferred_element_type=jnp.float32
        )
        own_total_ref[:block, here] = total[:block]
        own_total_ref[block:, here] = total[2 * block : 3 * block]
        their_total_ref[:block, here] = total[block : 2 * block].astype(jnp.bfloat16)
        their_total_ref[block:, here] = total[3 * block :].astype(jnp.bfloat16)


def add_kernel(total_ref, more_ref, out_ref):
    out_ref[...] = (total_ref[...] + more_ref[...]).astype(jnp.bfloat16)


def finish_kernel(total_ref, more_ref, ready_ref, out_ref, held, sems):
    block = out_ref.shape[0] // 2
    ctx = lax.axis_index("ctx")
    ready = ready_ref.shape[1]
    blocks = [(slice(0, block), ctx), (slice(block, 2 * block), 1 - ctx)]

    def copy(source_ref, which, first, sem):
        rows, place = blocks[which]
        there = pl.ds(pl.multiple_of(place * block, block), block)
        columns = pl.ds(first, source_ref.shape[1])
        return pltpu.make_async_copy(source_ref.at[rows], out_ref.at[there, columns], sem)

    copies = [copy(ready_ref, which, 0, sems.at[which]) for which in range(2)]
    for one in copies:
        one.start()
    for which, (rows, _) in enumerate(blocks):
        held[rows] = (total_ref[rows] + more_ref[rows]).astype(jnp.bfloat16)
        copies.append(copy(held, which, ready, sems.at[2 + which]))
        copies[-1].start()
    for one in copies:
        one.wait()


SMEM = functools.partial(pl.BlockSpec, memory_space=pltpu.SMEM)
VMEM = functools.partial(pl.BlockSpec, memory_space=pltpu.VMEM)
HBM = functools.partial(pl.BlockSpec, memory_space=pltpu.HBM)


def after(value, *others):
    return lax.optimization_barrier((value, *others))[0]


def body_edge(projections, block_source, clip_ids, out_weight):
    local_rows, row_width = projections.shape
    block_rows = local_rows // 2
    heads = row_width // (3 * HEAD)
    features = heads * HEAD
    depth, width = out_weight.shape
    count = lax.axis_size("dp")
    bf16 = jnp.bfloat16

    def call(kernel, name, shape, in_specs, dtypes=None, scratch=(), out_spec=VMEM()):
        many = isinstance(shape, list)
        shapes = shape if many else [shape]
        dtypes = dtypes or [bf16] * len(shapes)
        shapes = [jax.ShapeDtypeStruct(*one) for one in zip(shapes, dtypes, strict=True)]
        return pl.pallas_call(
            kernel,
            out_shape=shapes if many else shapes[0],
            in_specs=in_specs,
            out_specs=[out_spec] * len(shapes) if many else out_spec,
            scratch_shapes=scratch,
            cost_estimate=pl.CostEstimate(flops=0, bytes_accessed=0, transcendentals=0),
            compiler_params=pltpu.CompilerParams(vmem_limit_bytes=8 * MIB),
            name=name,
        )

    def around(value, step):
        places = ring_order(count // 4)
        moves = [(here, places[(at + step) % len(places)]) for at, here in enumerate(places)]
        return lax.ppermute(
            value, "dp", [(4 * here + rest, 4 * there + rest) for here, there in moves for rest in range(4)]
        )

    def to_side(value):
        return partner(value, "dp", 1)

    def to_core(value):
        return partner(value, "dp", 0)

    own = pltpu.with_memory_space_constraint(
        projections.reshape(2, block_rows, row_width), pltpu.HBM
    )
    shards = {(0, False): [out_weight]}
    from_partner = pltpu.with_memory_space_constraint(to_core(own), pltpu.VMEM)
    ahead = around(out_weight, 1)
    across = to_side(out_weight)
    staged = call(
        stage_kernel,
        "stage",
        own.shape,
        [SMEM(), HBM()],
        scratch=[pltpu.SemaphoreType.DMA],
    )(block_source, own)
    part_heads = [heads * 8 // 16, heads * 8 // 16]
    rows, *packed = call(
        pack_kernel,
        "pack",
        [(2, block_rows, row_width)] + [(block_rows, 2 * HEAD * some) for some in part_heads],
        [SMEM(), VMEM(), VMEM()],
        scratch=[pltpu.SemaphoreType.DMA((2,))],
    )(block_source, staged, from_partner)
    halos = [lax.ppermute(part, "ctx", [(0, 1), (1, 0)]) for part in packed]

    def edge_rows(part, *before):
        some = part_heads[part]
        return call(
            functools.partial(edge_kernel, sum(part_heads[:part])),
            "edge_rows",
            [(block_rows, some * HEAD), (block_rows, some // 2 * HEAD)],
            [SMEM(), VMEM(), VMEM()],
        )(after(clip_ids, *before), rows, halos[part])

    back = around(after(out_weight, staged), -1)
    ahead = after(ahead, *packed)
    shards[1, False], shards[0, True] = [ahead], [across]
    across = to_side(after(ahead, across))
    second = around(ahead, 1)
    inner, inner_other = call(
        inner_kernel,
        "inner_rows",
        [(block_rows, features), (block_rows, features // 2)],
        [SMEM(), VMEM()],
    )(after(clip_ids, ahead), rows)
    theirs = [to_core(inner_other)]

    back = after(back, inner)
    shards[3, False] = [back]
    back_across = to_side(back)
    shards[1, True] = [across]
    early = list(shards)
    origins = [*early, (2, False), (3, True), (2, True)]
    inner_total, inner_left = call(
        functools.partial(inner_project_kernel, origins, len(early)),
        "inner_project",
        [(local_rows, width), (local_rows, (len(origins) - len(early)) * depth)],
        [VMEM()] * (2 + len(early)),
        dtypes=[jnp.float32, bf16],
        scratch=[pltpu.VMEM((local_rows, len(early) * depth), bf16)],
    )(inner, *theirs, *[shards[origin][0] for origin in early])
    edges, edge_others = zip(*[edge_rows(part) for part in range(len(part_heads))], strict=True)
    second = after(second, inner_total, edges[0])
    cut = depth // 8 * 5
    shards[2, False] = [second]
    shards[3, True] = [back_across]
    shards[2, True] = [around(after(across, edges[0])[:cut], 1), to_side(second[cut:])]
    theirs = [to_core(part) for part in edge_others]

    arranged = call(
        functools.partial(arrange_kernel, origins, len(edges)),
        "arrange",
        (local_rows, len(origins) * depth),
        [VMEM()] * (len(edges) + len(theirs)),
        scratch=[
            pltpu.VMEM((block_rows, features), bf16),
            pltpu.VMEM((block_rows, features // 2), bf16),
        ],
    )(*edges, *theirs)
    pieces = [piece for origin in origins[:-1] for piece in shards[origin]]
    total = call(
        edge_project_kernel,
        "edge_project",
        (2 * local_rows, width),
        [VMEM()] * (3 + len(pieces)),
        dtypes=[jnp.float32],
    )(arranged, inner_left, inner_total, *pieces)
    sums = []
    first = 0
    for columns in (width // 3 * 2, width // 3):
        own_total, their_total = call(
            functools.partial(last_project_kernel, first),
            "last_project",
            [(local_rows, columns)] * 2,
            [VMEM()] * (3 + len(shards[origins[-1]])),
            dtypes=[jnp.float32, bf16],
        )(arranged, inner_left, total, *shards[origins[-1]])
        sums.append((own_total, to_core(their_total)))
        first += columns
    ready = call(add_kernel, "add", sums[0][0].shape, [VMEM()] * 2)(*sums[0])
    return call(
        finish_kernel,
        "finish",
        (local_rows, width),
        [VMEM()] * 3,
        scratch=[pltpu.VMEM(sums[1][0].shape, bf16), pltpu.SemaphoreType.DMA((4,))],
        out_spec=HBM(),
    )(*sums[1], ready)


def body(projections, block_source, clip_ids, out_weight):
    heads = projections.shape[1] // (3 * HEAD)
    two_and_two = lax.axis_size("ctx") == 2 and block_source.shape[2] == 2
    whole_tiles = out_weight.shape[0] % HEAD == 0 and heads % 16 == 0
    if two_and_two and whole_tiles and lax.axis_size("dp") == 16:
        return body_edge(projections, block_source, clip_ids, out_weight)
    return body_general(projections, block_source, clip_ids, out_weight)


def solution(mesh):
    return jax.shard_map(
        body,
        mesh=mesh,
        in_specs=(P(("dp", "ctx"), None), P("dp", "ctx", None), P("dp", None), P("dp", None)),
        out_specs=P(("dp", "ctx"), None),
        check_vma=False,
    )
```

```python
import functools
import math

import jax
import jax.numpy as jnp
from jax import lax
from jax.experimental import pallas as pl
from jax.experimental.pallas import tpu as pltpu
from jax.sharding import PartitionSpec as P

HEAD = 128


big_negative = -1e30
MIB = 1 << 20


def partner(value, axis, bit):
    mask = 2**bit
    pairs = [(source, source ^ mask) for source in range(lax.axis_size(axis))]
    return lax.ppermute(value, axis, pairs)


def soft_weights(scores, allowed):
    masked = jnp.where(allowed, scores, big_negative)
    row_max = jnp.max(masked, axis=-1, keepdims=True)
    exponent = jnp.exp(masked - row_max)
    return (exponent / jnp.sum(exponent, axis=-1, keepdims=True)).astype(jnp.bfloat16)


def attend_dense(queries, key_rows, value_rows, token_clip, scaling):
    token_count, head_count, head_size = queries.shape
    step_size = min(token_count, 512)
    step_count = token_count // step_size
    query_steps = queries.reshape(step_count, step_size, head_count, head_size)
    clip_steps = token_clip.reshape(step_count, step_size)

    def one_step(arguments):
        query_block, clip_block = arguments
        scores = (
            jnp.einsum("qhe,khe->hqk", query_block, key_rows, preferred_element_type=jnp.float32)
            * scaling
        )
        allowed = (clip_block[:, None] == token_clip[None, :])[None]
        weights = soft_weights(scores, allowed)
        return jnp.einsum(
            "hqk,khe->qhe", weights, value_rows, preferred_element_type=jnp.float32
        ).astype(jnp.bfloat16)

    outputs = lax.map(one_step, (query_steps, clip_steps))
    return outputs.reshape(token_count, head_count, head_size)


def body_general(projections, block_source, clip_ids, out_weight):
    ctx_count = lax.axis_size("ctx")
    local_rows, row_width = projections.shape
    local_blocks = block_source.shape[2]
    block_rows = local_rows // local_blocks
    own_blocks = projections.reshape(local_blocks, block_rows, row_width)
    partner_blocks = partner(own_blocks, "dp", 0)
    source_ids = block_source.reshape(local_blocks)
    from_partner = source_ids // (local_blocks * ctx_count) != lax.axis_index("dp")
    chosen_slot = source_ids % local_blocks + local_blocks * from_partner.astype(jnp.int32)
    candidates = jnp.concatenate([own_blocks, partner_blocks], axis=0)
    packed = jnp.take(candidates, chosen_slot, axis=0)
    local_heads = row_width // (3 * HEAD) // ctx_count
    grouped = packed.reshape(local_rows, ctx_count, local_heads, 3 * HEAD)
    block_clip = clip_ids.reshape(-1)
    token_clip = jnp.repeat(block_clip, block_rows)
    scaling = 1.0 / math.sqrt(HEAD)
    regrouped = lax.all_to_all(grouped, "ctx", split_axis=1, concat_axis=0, tiled=True)
    token_count = regrouped.shape[0]
    item_count = regrouped.shape[2]
    features = regrouped.reshape(token_count, item_count, 3 * HEAD)
    queries = features[:, :, :HEAD]
    key_rows = features[:, :, HEAD : 2 * HEAD]
    value_rows = features[:, :, 2 * HEAD :]
    attended = attend_dense(queries, key_rows, value_rows, token_clip, scaling)
    merged = attended.reshape(local_rows * ctx_count, local_heads * HEAD)
    attention_rows = lax.all_to_all(merged, "ctx", split_axis=0, concat_axis=1, tiled=True)
    result = jnp.dot(
        attention_rows,
        lax.all_gather(out_weight, "dp", axis=0, tiled=True),
        preferred_element_type=jnp.float32,
    )
    return result.astype(jnp.bfloat16)


def stage_kernel(source_ref, own_ref, out_ref, sem):
    copy = pltpu.make_async_copy(own_ref, out_ref, sem)
    copy.start()
    copy.wait()


def place(source_ref, own_ref, block):
    slots = own_ref.shape[0]
    source = source_ref[0, 0, block]
    return source // (2 * slots) != lax.axis_index("dp"), lax.rem(source, slots)


def pack_first_kernel(source_ref, own_ref, partner_ref, halo_ref):
    away, slot = place(source_ref, own_ref, 1 - lax.axis_index("ctx"))
    for head in range(halo_ref.shape[1] // (2 * HEAD)):
        columns = slice(head * 3 * HEAD + HEAD, (head + 1) * 3 * HEAD)
        halo_ref[:, head * 2 * HEAD : (head + 1) * 2 * HEAD] = jnp.where(
            away, partner_ref[slot, :, columns], own_ref[slot, :, columns]
        )


def pack_kernel(source_ref, own_ref, partner_ref, rows_ref, halo_ref, sems):
    ctx = lax.axis_index("ctx")
    for which, block in ((1, 1 - ctx), (0, ctx)):
        away, slot = place(source_ref, own_ref, block)

        @pl.when(jnp.logical_not(away))
        def _():
            pltpu.make_async_copy(own_ref.at[slot], rows_ref.at[which], sems.at[which]).start()

        @pl.when(away)
        def _():
            pltpu.make_async_copy(partner_ref.at[slot], rows_ref.at[which], sems.at[which]).start()

    pltpu.make_async_copy(own_ref.at[0], rows_ref.at[1], sems.at[1]).wait()
    heads = halo_ref.shape[1] // (2 * HEAD)
    skipped = rows_ref.shape[2] // (3 * HEAD) - heads
    for head in range(heads):
        first = (skipped + head) * 3 * HEAD + HEAD
        halo_ref[:, head * 2 * HEAD : (head + 1) * 2 * HEAD] = rows_ref[
            1, :, first : first + 2 * HEAD
        ]
    pltpu.make_async_copy(own_ref.at[0], rows_ref.at[0], sems.at[0]).wait()


def attend(heads, load_queries, load_own, load_more, allowed, out_ref, other_ref):
    scaling = math.log2(math.e) / math.sqrt(HEAD)
    contract_last = (((1,), (1,)), ((), ()))
    ones = jnp.ones((2 * out_ref.shape[0], HEAD), jnp.bfloat16)
    odd_core = lax.rem(lax.axis_index("dp"), 2) == 1
    for start in range(0, heads, 4):
        group = min(4, heads - start)
        scores = []
        for head in range(start, start + group):
            queries = load_queries(head)
            pair = []
            for loader in (load_own, load_more):
                pair.append(
                    lax.dot_general(
                        queries, loader(head, 0), contract_last, preferred_element_type=jnp.float32
                    )
                    * scaling
                )
            scores.append(pair)
        weights = []
        for own, more in scores:
            more = jnp.where(allowed, more, big_negative)
            row_max = jnp.max(jnp.maximum(own, more), axis=-1, keepdims=True)
            weights.append(
                jnp.concatenate(
                    [
                        jnp.exp2(own - row_max).astype(jnp.bfloat16),
                        jnp.exp2(more - row_max).astype(jnp.bfloat16),
                    ],
                    axis=1,
                )
            )
        outs = []
        for head in range(start, start + group):
            values = jnp.concatenate([load_own(head, 1), load_more(head, 1)], axis=0)
            sums = jnp.dot(
                weights[head - start],
                jnp.concatenate([values, ones], axis=1),
                preferred_element_type=jnp.float32,
            )
            outs.append(sums[:, :HEAD] / sums[:, HEAD:])
            out_ref[:, head * HEAD : (head + 1) * HEAD] = outs[-1].astype(jnp.bfloat16)
        for pair in range(group // 2):
            at = (start // 2 + pair) * HEAD
            other = jnp.where(odd_core, outs[2 * pair], outs[2 * pair + 1])
            other_ref[:, at : at + HEAD] = other.astype(jnp.bfloat16)


def inner_kernel(clip_ref, rows_ref, out_ref, other_ref):
    ctx = lax.axis_index("ctx")
    allowed = clip_ref[0, 2 * ctx] == clip_ref[0, 2 * ctx + 1]

    def loader(block):
        def get(head, which):
            first = (head * 3 + 1 + which) * HEAD
            return rows_ref[block, :, first : first + HEAD]

        return get

    attend(
        out_ref.shape[1] // HEAD,
        lambda head: loader(0)(head, -1),
        loader(0),
        loader(1),
        allowed,
        out_ref,
        other_ref,
    )


def edge_kernel(first_head, clip_ref, rows_ref, halo_ref, out_ref, other_ref):
    ctx = lax.axis_index("ctx")
    edge_clip = clip_ref[0, 1 + ctx]
    crosses = edge_clip == clip_ref[0, 2 - ctx]
    allowed = jnp.logical_or(crosses, edge_clip == clip_ref[0, 3 * ctx])

    def load_own(head, which):
        first = ((first_head + head) * 3 + 1 + which) * HEAD
        return rows_ref[1, :, first : first + HEAD]

    def load_more(head, which):
        first = ((first_head + head) * 3 + 1 + which) * HEAD
        at = (2 * head + which) * HEAD
        return jnp.where(crosses, halo_ref[:, at : at + HEAD], rows_ref[0, :, first : first + HEAD])

    attend(
        out_ref.shape[1] // HEAD,
        lambda head: load_own(head, -1),
        load_own,
        load_more,
        allowed,
        out_ref,
        other_ref,
    )


def ring_order(lines):
    return list(range(0, lines, 2)) + list(range(1, lines, 2))[::-1]


def shard_places(origins, depth):
    index = lax.axis_index("dp")
    core, side, line = lax.rem(index, 2), lax.rem(index // 2, 2), index // 4
    places = ring_order(lax.axis_size("dp") // 4)
    found = []
    for steps, other_side in origins:
        from_line = line
        for at, place in enumerate(places):
            from_line = jnp.where(line == place, places[at - steps], from_line)
        pair = from_line * 2 + (1 - side if other_side else side)
        here = pl.ds(pl.multiple_of((pair * 2 + core) * depth, depth), depth)
        there = pl.ds(pl.multiple_of(pair * depth, depth), depth)
        found.append((here, there))
    return found


def inner_project_kernel(origins, early, inner_ref, their_ref, *rest):
    shard_refs, (total_ref, left_ref, features) = rest[:-3], rest[-3:]
    block = inner_ref.shape[0]
    depth = left_ref.shape[1] // (len(origins) - early)
    for number, (here, there) in enumerate(shard_places(origins, depth)):
        ref, at = (features, number) if number < early else (left_ref, number - early)
        ref[:block, at * depth : (at + 1) * depth] = inner_ref[:, here]
        ref[block:, at * depth : (at + 1) * depth] = their_ref[:, there]
    tile = 2 * HEAD
    for first in range(0, total_ref.shape[1], tile):
        columns = slice(first, first + tile)
        weight = jnp.concatenate([ref[:, columns] for ref in shard_refs], axis=0)
        total_ref[:, columns] = jnp.dot(
            features[...], weight, preferred_element_type=jnp.float32
        )


def arrange_kernel(origins, parts, *refs):
    edge_refs, their_refs = refs[:parts], refs[parts : 2 * parts]
    out_ref, edge_rows, their_rows = refs[2 * parts :]
    for refs, held in ((edge_refs, edge_rows), (their_refs, their_rows)):
        first = 0
        for ref in refs:
            held[:, first : first + ref.shape[1]] = ref[...]
            first += ref.shape[1]
    block = edge_rows.shape[0]
    depth = out_ref.shape[1] // len(origins)
    for number, (here, there) in enumerate(shard_places(origins, depth)):
        at = slice(number * depth, (number + 1) * depth)
        out_ref[:block, at] = edge_rows[:, here]
        out_ref[block:, at] = their_rows[:, there]


def edge_project_kernel(edge_ref, left_ref, inner_total_ref, *rest):
    shard_refs, total_ref = rest[:-1], rest[-1]
    rows = edge_ref.shape[0]
    depths = sum(ref.shape[0] for ref in shard_refs)
    depth = edge_ref.shape[1] - depths
    left = left_ref.shape[1] - depth
    tile = 2 * HEAD
    for first in range(0, total_ref.shape[1], tile):
        columns = slice(first, first + tile)
        weight = jnp.concatenate([ref[:, columns] for ref in shard_refs], axis=0)
        total_ref[:rows, columns] = inner_total_ref[:, columns] + jnp.dot(
            left_ref[:, :left], weight[-left:], preferred_element_type=jnp.float32
        )
        total_ref[rows:, columns] = jnp.dot(
            edge_ref[:, :depths], weight, preferred_element_type=jnp.float32
        )


def last_project_kernel(first, edge_ref, left_ref, total_ref, *rest):
    shard_refs, (own_total_ref, their_total_ref) = rest[:-2], rest[-2:]
    block = own_total_ref.shape[0] // 2
    depth = sum(ref.shape[0] for ref in shard_refs)
    features = jnp.concatenate([left_ref[:, -depth:], edge_ref[:, -depth:]], axis=0)
    tile = 2 * HEAD
    for at in range(0, own_total_ref.shape[1], tile):
        here = slice(at, at + tile)
        columns = slice(first + at, first + at + tile)
        weight = jnp.concatenate([ref[:, columns] for ref in shard_refs], axis=0)
        total = total_ref[:, columns] + jnp.dot(
            features, weight, preferred_element_type=jnp.float32
        )
        own_total_ref[:block, here] = total[:block]
        own_total_ref[block:, here] = total[2 * block : 3 * block]
        their_total_ref[:block, here] = total[block : 2 * block].astype(jnp.bfloat16)
        their_total_ref[block:, here] = total[3 * block :].astype(jnp.bfloat16)


def add_kernel(total_ref, more_ref, out_ref):
    out_ref[...] = (total_ref[...] + more_ref[...]).astype(jnp.bfloat16)


def finish_kernel(total_ref, more_ref, ready_ref, out_ref, held, sems):
    block = out_ref.shape[0] // 2
    ctx = lax.axis_index("ctx")
    ready = ready_ref.shape[1]
    blocks = [(slice(0, block), ctx), (slice(block, 2 * block), 1 - ctx)]

    def copy(source_ref, which, first, sem):
        rows, place = blocks[which]
        there = pl.ds(pl.multiple_of(place * block, block), block)
        columns = pl.ds(first, source_ref.shape[1])
        return pltpu.make_async_copy(source_ref.at[rows], out_ref.at[there, columns], sem)

    copies = [copy(ready_ref, which, 0, sems.at[which]) for which in range(2)]
    for one in copies:
        one.start()
    for which, (rows, _) in enumerate(blocks):
        held[rows] = (total_ref[rows] + more_ref[rows]).astype(jnp.bfloat16)
        copies.append(copy(held, which, ready, sems.at[2 + which]))
        copies[-1].start()
    for one in copies:
        one.wait()


SMEM = functools.partial(pl.BlockSpec, memory_space=pltpu.SMEM)
VMEM = functools.partial(pl.BlockSpec, memory_space=pltpu.VMEM)
HBM = functools.partial(pl.BlockSpec, memory_space=pltpu.HBM)


def after(value, *others):
    return lax.optimization_barrier((value, *others))[0]


def body_edge(projections, block_source, clip_ids, out_weight):
    local_rows, row_width = projections.shape
    block_rows = local_rows // 2
    heads = row_width // (3 * HEAD)
    features = heads * HEAD
    depth, width = out_weight.shape
    count = lax.axis_size("dp")
    bf16 = jnp.bfloat16

    def call(kernel, name, shape, in_specs, dtypes=None, scratch=(), out_spec=VMEM()):
        many = isinstance(shape, list)
        shapes = shape if many else [shape]
        dtypes = dtypes or [bf16] * len(shapes)
        shapes = [jax.ShapeDtypeStruct(*one) for one in zip(shapes, dtypes, strict=True)]
        return pl.pallas_call(
            kernel,
            out_shape=shapes if many else shapes[0],
            in_specs=in_specs,
            out_specs=[out_spec] * len(shapes) if many else out_spec,
            scratch_shapes=scratch,
            cost_estimate=pl.CostEstimate(flops=0, bytes_accessed=0, transcendentals=0),
            compiler_params=pltpu.CompilerParams(vmem_limit_bytes=8 * MIB),
            name=name,
        )

    def around(value, step):
        places = ring_order(count // 4)
        moves = [(here, places[(at + step) % len(places)]) for at, here in enumerate(places)]
        return lax.ppermute(
            value, "dp", [(4 * here + rest, 4 * there + rest) for here, there in moves for rest in range(4)]
        )

    def to_side(value):
        return partner(value, "dp", 1)

    def to_core(value):
        return partner(value, "dp", 0)

    own = pltpu.with_memory_space_constraint(
        projections.reshape(2, block_rows, row_width), pltpu.HBM
    )
    shards = {(0, False): [out_weight]}
    from_partner = pltpu.with_memory_space_constraint(to_core(own), pltpu.VMEM)
    ahead = around(out_weight, 1)
    across = to_side(out_weight)
    staged = call(
        stage_kernel,
        "stage",
        own.shape,
        [SMEM(), HBM()],
        scratch=[pltpu.SemaphoreType.DMA],
    )(block_source, own)
    part_heads = [heads * 8 // 16, heads * 8 // 16]
    packed_first = call(
        pack_first_kernel,
        "pack_first",
        (block_rows, 2 * HEAD * part_heads[0]),
        [SMEM(), VMEM(), VMEM()],
    )(block_source, staged, from_partner)
    rows, packed_last = call(
        pack_kernel,
        "pack",
        [(2, block_rows, row_width), (block_rows, 2 * HEAD * part_heads[1])],
        [SMEM(), VMEM(), VMEM()],
        scratch=[pltpu.SemaphoreType.DMA((2,))],
    )(block_source, staged, after(from_partner, packed_first))
    packed = [packed_first, packed_last]
    halos = [lax.ppermute(part, "ctx", [(0, 1), (1, 0)]) for part in packed]

    def edge_rows(part, *before):
        some = part_heads[part]
        return call(
            functools.partial(edge_kernel, sum(part_heads[:part])),
            "edge_rows",
            [(block_rows, some * HEAD), (block_rows, some // 2 * HEAD)],
            [SMEM(), VMEM(), VMEM()],
        )(after(clip_ids, *before), rows, halos[part])

    back = around(after(out_weight, staged), -1)
    ahead = after(ahead, *packed)
    shards[1, False], shards[0, True] = [ahead], [across]
    second = around(after(ahead, across), 1)
    across = to_side(ahead)
    inner, inner_other = call(
        inner_kernel,
        "inner_rows",
        [(block_rows, features), (block_rows, features // 2)],
        [SMEM(), VMEM()],
    )(after(clip_ids, ahead), rows)
    theirs = [to_core(inner_other)]

    back = after(back, inner)
    shards[3, False] = [back]
    back_across = to_side(back)
    shards[1, True] = [across]
    early = list(shards)
    origins = [*early, (2, False), (3, True), (2, True)]
    inner_total, inner_left = call(
        functools.partial(inner_project_kernel, origins, len(early)),
        "inner_project",
        [(local_rows, width), (local_rows, (len(origins) - len(early)) * depth)],
        [VMEM()] * (2 + len(early)),
        dtypes=[jnp.float32, bf16],
        scratch=[pltpu.VMEM((local_rows, len(early) * depth), bf16)],
    )(inner, *theirs, *[shards[origin][0] for origin in early])
    edges, edge_others = zip(*[edge_rows(part) for part in range(len(part_heads))], strict=True)
    second = after(second, inner_total, edges[0])
    cut = depth // 8 * 5
    shards[2, False] = [second]
    shards[3, True] = [back_across]
    shards[2, True] = [around(after(across, edges[0])[:cut], 1), to_side(second[cut:])]
    theirs = [to_core(part) for part in edge_others]

    arranged = call(
        functools.partial(arrange_kernel, origins, len(edges)),
        "arrange",
        (local_rows, len(origins) * depth),
        [VMEM()] * (len(edges) + len(theirs)),
        scratch=[
            pltpu.VMEM((block_rows, features), bf16),
            pltpu.VMEM((block_rows, features // 2), bf16),
        ],
    )(*edges, *theirs)
    pieces = [piece for origin in origins[:-1] for piece in shards[origin]]
    total = call(
        edge_project_kernel,
        "edge_project",
        (2 * local_rows, width),
        [VMEM()] * (3 + len(pieces)),
        dtypes=[jnp.float32],
    )(arranged, inner_left, inner_total, *pieces)
    sums = []
    first = 0
    for columns in (width // 3 * 2, width // 3):
        own_total, their_total = call(
            functools.partial(last_project_kernel, first),
            "last_project",
            [(local_rows, columns)] * 2,
            [VMEM()] * (3 + len(shards[origins[-1]])),
            dtypes=[jnp.float32, bf16],
        )(arranged, inner_left, total, *shards[origins[-1]])
        sums.append((own_total, to_core(their_total)))
        first += columns
    ready = call(add_kernel, "add", sums[0][0].shape, [VMEM()] * 2)(*sums[0])
    return call(
        finish_kernel,
        "finish",
        (local_rows, width),
        [VMEM()] * 3,
        scratch=[pltpu.VMEM(sums[1][0].shape, bf16), pltpu.SemaphoreType.DMA((4,))],
        out_spec=HBM(),
    )(*sums[1], ready)


def body(projections, block_source, clip_ids, out_weight):
    heads = projections.shape[1] // (3 * HEAD)
    two_and_two = lax.axis_size("ctx") == 2 and block_source.shape[2] == 2
    whole_tiles = out_weight.shape[0] % HEAD == 0 and heads % 16 == 0
    if two_and_two and whole_tiles and lax.axis_size("dp") == 16:
        return body_edge(projections, block_source, clip_ids, out_weight)
    return body_general(projections, block_source, clip_ids, out_weight)


def solution(mesh):
    return jax.shard_map(
        body,
        mesh=mesh,
        in_specs=(P(("dp", "ctx"), None), P("dp", "ctx", None), P("dp", None), P("dp", None)),
        out_specs=P(("dp", "ctx"), None),
        check_vma=False,
    )
```

```python
import functools
import math

import jax
import jax.numpy as jnp
from jax import lax
from jax.experimental import pallas as pl
from jax.experimental.pallas import tpu as pltpu
from jax.sharding import PartitionSpec as P

HEAD = 128


big_negative = -1e30
MIB = 1 << 20


def partner(value, axis, bit):
    mask = 2**bit
    pairs = [(source, source ^ mask) for source in range(lax.axis_size(axis))]
    return lax.ppermute(value, axis, pairs)


def soft_weights(scores, allowed):
    masked = jnp.where(allowed, scores, big_negative)
    row_max = jnp.max(masked, axis=-1, keepdims=True)
    exponent = jnp.exp(masked - row_max)
    return (exponent / jnp.sum(exponent, axis=-1, keepdims=True)).astype(jnp.bfloat16)


def attend_dense(queries, key_rows, value_rows, token_clip, scaling):
    token_count, head_count, head_size = queries.shape
    step_size = min(token_count, 512)
    step_count = token_count // step_size
    query_steps = queries.reshape(step_count, step_size, head_count, head_size)
    clip_steps = token_clip.reshape(step_count, step_size)

    def one_step(arguments):
        query_block, clip_block = arguments
        scores = (
            jnp.einsum("qhe,khe->hqk", query_block, key_rows, preferred_element_type=jnp.float32)
            * scaling
        )
        allowed = (clip_block[:, None] == token_clip[None, :])[None]
        weights = soft_weights(scores, allowed)
        return jnp.einsum(
            "hqk,khe->qhe", weights, value_rows, preferred_element_type=jnp.float32
        ).astype(jnp.bfloat16)

    outputs = lax.map(one_step, (query_steps, clip_steps))
    return outputs.reshape(token_count, head_count, head_size)


def body_general(projections, block_source, clip_ids, out_weight):
    ctx_count = lax.axis_size("ctx")
    local_rows, row_width = projections.shape
    local_blocks = block_source.shape[2]
    block_rows = local_rows // local_blocks
    own_blocks = projections.reshape(local_blocks, block_rows, row_width)
    partner_blocks = partner(own_blocks, "dp", 0)
    source_ids = block_source.reshape(local_blocks)
    from_partner = source_ids // (local_blocks * ctx_count) != lax.axis_index("dp")
    chosen_slot = source_ids % local_blocks + local_blocks * from_partner.astype(jnp.int32)
    candidates = jnp.concatenate([own_blocks, partner_blocks], axis=0)
    packed = jnp.take(candidates, chosen_slot, axis=0)
    local_heads = row_width // (3 * HEAD) // ctx_count
    grouped = packed.reshape(local_rows, ctx_count, local_heads, 3 * HEAD)
    block_clip = clip_ids.reshape(-1)
    token_clip = jnp.repeat(block_clip, block_rows)
    scaling = 1.0 / math.sqrt(HEAD)
    regrouped = lax.all_to_all(grouped, "ctx", split_axis=1, concat_axis=0, tiled=True)
    token_count = regrouped.shape[0]
    item_count = regrouped.shape[2]
    features = regrouped.reshape(token_count, item_count, 3 * HEAD)
    queries = features[:, :, :HEAD]
    key_rows = features[:, :, HEAD : 2 * HEAD]
    value_rows = features[:, :, 2 * HEAD :]
    attended = attend_dense(queries, key_rows, value_rows, token_clip, scaling)
    merged = attended.reshape(local_rows * ctx_count, local_heads * HEAD)
    attention_rows = lax.all_to_all(merged, "ctx", split_axis=0, concat_axis=1, tiled=True)
    result = jnp.dot(
        attention_rows,
        lax.all_gather(out_weight, "dp", axis=0, tiled=True),
        preferred_element_type=jnp.float32,
    )
    return result.astype(jnp.bfloat16)


def stage_kernel(source_ref, own_ref, out_ref, sem):
    copy = pltpu.make_async_copy(own_ref, out_ref, sem)
    copy.start()
    copy.wait()


def place(source_ref, own_ref, block):
    slots = own_ref.shape[0]
    source = source_ref[0, 0, block]
    return source // (2 * slots) != lax.axis_index("dp"), lax.rem(source, slots)


def pack_first_kernel(source_ref, own_ref, partner_ref, halo_ref):
    away, slot = place(source_ref, own_ref, 1 - lax.axis_index("ctx"))
    for head in range(halo_ref.shape[1] // (2 * HEAD)):
        columns = slice(head * 3 * HEAD + HEAD, (head + 1) * 3 * HEAD)
        halo_ref[:, head * 2 * HEAD : (head + 1) * 2 * HEAD] = jnp.where(
            away, partner_ref[slot, :, columns], own_ref[slot, :, columns]
        )


def pack_kernel(source_ref, own_ref, partner_ref, rows_ref, halo_ref, sems):
    ctx = lax.axis_index("ctx")
    for which, block in ((1, 1 - ctx), (0, ctx)):
        away, slot = place(source_ref, own_ref, block)

        @pl.when(jnp.logical_not(away))
        def _():
            pltpu.make_async_copy(own_ref.at[slot], rows_ref.at[which], sems.at[which]).start()

        @pl.when(away)
        def _():
            pltpu.make_async_copy(partner_ref.at[slot], rows_ref.at[which], sems.at[which]).start()

    pltpu.make_async_copy(own_ref.at[0], rows_ref.at[1], sems.at[1]).wait()
    heads = halo_ref.shape[1] // (2 * HEAD)
    skipped = rows_ref.shape[2] // (3 * HEAD) - heads
    for head in range(heads):
        first = (skipped + head) * 3 * HEAD + HEAD
        halo_ref[:, head * 2 * HEAD : (head + 1) * 2 * HEAD] = rows_ref[
            1, :, first : first + 2 * HEAD
        ]
    pltpu.make_async_copy(own_ref.at[0], rows_ref.at[0], sems.at[0]).wait()


def attend(heads, load_queries, load_own, load_more, allowed, out_ref, other_ref):
    scaling = math.log2(math.e) / math.sqrt(HEAD)
    contract_last = (((1,), (1,)), ((), ()))
    ones = jnp.ones((2 * out_ref.shape[0], HEAD), jnp.bfloat16)
    odd_core = lax.rem(lax.axis_index("dp"), 2) == 1
    for start in range(0, heads, 4):
        group = min(4, heads - start)
        scores = []
        for head in range(start, start + group):
            queries = load_queries(head)
            pair = []
            for loader in (load_own, load_more):
                pair.append(
                    lax.dot_general(
                        queries, loader(head, 0), contract_last, preferred_element_type=jnp.float32
                    )
                    * scaling
                )
            scores.append(pair)
        weights = []
        for own, more in scores:
            more = jnp.where(allowed, more, big_negative)
            row_max = jnp.max(jnp.maximum(own, more), axis=-1, keepdims=True)
            weights.append(
                jnp.concatenate(
                    [
                        jnp.exp2(own - row_max).astype(jnp.bfloat16),
                        jnp.exp2(more - row_max).astype(jnp.bfloat16),
                    ],
                    axis=1,
                )
            )
        outs = []
        for head in range(start, start + group):
            values = jnp.concatenate([load_own(head, 1), load_more(head, 1)], axis=0)
            sums = jnp.dot(
                weights[head - start],
                jnp.concatenate([values, ones], axis=1),
                preferred_element_type=jnp.float32,
            )
            outs.append(sums[:, :HEAD] / sums[:, HEAD:])
            out_ref[:, head * HEAD : (head + 1) * HEAD] = outs[-1].astype(jnp.bfloat16)
        for pair in range(group // 2):
            at = (start // 2 + pair) * HEAD
            other = jnp.where(odd_core, outs[2 * pair], outs[2 * pair + 1])
            other_ref[:, at : at + HEAD] = other.astype(jnp.bfloat16)


def inner_kernel(clip_ref, rows_ref, out_ref, other_ref):
    ctx = lax.axis_index("ctx")
    allowed = clip_ref[0, 2 * ctx] == clip_ref[0, 2 * ctx + 1]

    def loader(block):
        def get(head, which):
            first = (head * 3 + 1 + which) * HEAD
            return rows_ref[block, :, first : first + HEAD]

        return get

    attend(
        out_ref.shape[1] // HEAD,
        lambda head: loader(0)(head, -1),
        loader(0),
        loader(1),
        allowed,
        out_ref,
        other_ref,
    )


def edge_kernel(first_head, clip_ref, rows_ref, halo_ref, out_ref, other_ref):
    ctx = lax.axis_index("ctx")
    edge_clip = clip_ref[0, 1 + ctx]
    crosses = edge_clip == clip_ref[0, 2 - ctx]
    allowed = jnp.logical_or(crosses, edge_clip == clip_ref[0, 3 * ctx])

    def load_own(head, which):
        first = ((first_head + head) * 3 + 1 + which) * HEAD
        return rows_ref[1, :, first : first + HEAD]

    def load_more(head, which):
        first = ((first_head + head) * 3 + 1 + which) * HEAD
        at = (2 * head + which) * HEAD
        return jnp.where(crosses, halo_ref[:, at : at + HEAD], rows_ref[0, :, first : first + HEAD])

    attend(
        out_ref.shape[1] // HEAD,
        lambda head: load_own(head, -1),
        load_own,
        load_more,
        allowed,
        out_ref,
        other_ref,
    )


def ring_order(lines):
    return list(range(0, lines, 2)) + list(range(1, lines, 2))[::-1]


def shard_places(origins, depth):
    index = lax.axis_index("dp")
    core, side, line = lax.rem(index, 2), lax.rem(index // 2, 2), index // 4
    places = ring_order(lax.axis_size("dp") // 4)
    found = []
    for steps, other_side in origins:
        from_line = line
        for at, place in enumerate(places):
            from_line = jnp.where(line == place, places[at - steps], from_line)
        pair = from_line * 2 + (1 - side if other_side else side)
        here = pl.ds(pl.multiple_of((pair * 2 + core) * depth, depth), depth)
        there = pl.ds(pl.multiple_of(pair * depth, depth), depth)
        found.append((here, there))
    return found


def inner_project_kernel(origins, early, inner_ref, their_ref, *rest):
    shard_refs, (total_ref, left_ref, features) = rest[:-3], rest[-3:]
    block = inner_ref.shape[0]
    depth = left_ref.shape[1] // (len(origins) - early)
    for number, (here, there) in enumerate(shard_places(origins, depth)):
        ref, at = (features, number) if number < early else (left_ref, number - early)
        ref[:block, at * depth : (at + 1) * depth] = inner_ref[:, here]
        ref[block:, at * depth : (at + 1) * depth] = their_ref[:, there]
    tile = 2 * HEAD
    for first in range(0, total_ref.shape[1], tile):
        columns = slice(first, first + tile)
        weight = jnp.concatenate([ref[:, columns] for ref in shard_refs], axis=0)
        total_ref[:, columns] = jnp.dot(
            features[...], weight, preferred_element_type=jnp.float32
        )


def arrange_kernel(origins, parts, *refs):
    edge_refs, their_refs = refs[:parts], refs[parts : 2 * parts]
    out_ref, edge_rows, their_rows = refs[2 * parts :]
    for refs, held in ((edge_refs, edge_rows), (their_refs, their_rows)):
        first = 0
        for ref in refs:
            held[:, first : first + ref.shape[1]] = ref[...]
            first += ref.shape[1]
    block = edge_rows.shape[0]
    depth = out_ref.shape[1] // len(origins)
    for number, (here, there) in enumerate(shard_places(origins, depth)):
        at = slice(number * depth, (number + 1) * depth)
        out_ref[:block, at] = edge_rows[:, here]
        out_ref[block:, at] = their_rows[:, there]


def add_products_kernel(left_ref, inner_total_ref, *rest):
    shard_refs, total_ref = rest[:-1], rest[-1]
    depths = sum(ref.shape[0] for ref in shard_refs)
    tile = 2 * HEAD
    for first in range(0, total_ref.shape[1], tile):
        columns = slice(first, first + tile)
        weight = jnp.concatenate([ref[:, columns] for ref in shard_refs], axis=0)
        total_ref[:, columns] = inner_total_ref[:, columns] + jnp.dot(
            left_ref[:, :depths], weight, preferred_element_type=jnp.float32
        )


def edge_project_kernel(edge_ref, *rest):
    shard_refs, total_ref = rest[:-1], rest[-1]
    depths = sum(ref.shape[0] for ref in shard_refs)
    tile = 2 * HEAD
    for first in range(0, total_ref.shape[1], tile):
        columns = slice(first, first + tile)
        weight = jnp.concatenate([ref[:, columns] for ref in shard_refs], axis=0)
        total_ref[:, columns] = jnp.dot(
            edge_ref[:, :depths], weight, preferred_element_type=jnp.float32
        )


def last_project_kernel(first, edge_ref, left_ref, inner_total_ref, edge_total_ref, *rest):
    shard_refs, (own_total_ref, their_total_ref) = rest[:-2], rest[-2:]
    block = own_total_ref.shape[0] // 2
    depth = sum(ref.shape[0] for ref in shard_refs)
    features = jnp.concatenate([left_ref[:, -depth:], edge_ref[:, -depth:]], axis=0)
    tile = 2 * HEAD
    for at in range(0, own_total_ref.shape[1], tile):
        here = slice(at, at + tile)
        columns = slice(first + at, first + at + tile)
        weight = jnp.concatenate([ref[:, columns] for ref in shard_refs], axis=0)
        total = jnp.dot(features, weight, preferred_element_type=jnp.float32)
        inner = inner_total_ref[:, columns] + total[: 2 * block]
        edge = edge_total_ref[:, columns] + total[2 * block :]
        own_total_ref[:block, here] = inner[:block]
        own_total_ref[block:, here] = edge[:block]
        their_total_ref[:block, here] = inner[block:].astype(jnp.bfloat16)
        their_total_ref[block:, here] = edge[block:].astype(jnp.bfloat16)


def add_kernel(total_ref, more_ref, out_ref):
    out_ref[...] = (total_ref[...] + more_ref[...]).astype(jnp.bfloat16)


def finish_kernel(total_ref, more_ref, ready_ref, out_ref, held, sems):
    block = out_ref.shape[0] // 2
    ctx = lax.axis_index("ctx")
    ready = ready_ref.shape[1]
    blocks = [(slice(0, block), ctx), (slice(block, 2 * block), 1 - ctx)]

    def copy(source_ref, which, first, sem):
        rows, place = blocks[which]
        there = pl.ds(pl.multiple_of(place * block, block), block)
        columns = pl.ds(first, source_ref.shape[1])
        return pltpu.make_async_copy(source_ref.at[rows], out_ref.at[there, columns], sem)

    copies = [copy(ready_ref, which, 0, sems.at[which]) for which in range(2)]
    for one in copies:
        one.start()
    for which, (rows, _) in enumerate(blocks):
        held[rows] = (total_ref[rows] + more_ref[rows]).astype(jnp.bfloat16)
        copies.append(copy(held, which, ready, sems.at[2 + which]))
        copies[-1].start()
    for one in copies:
        one.wait()


SMEM = functools.partial(pl.BlockSpec, memory_space=pltpu.SMEM)
VMEM = functools.partial(pl.BlockSpec, memory_space=pltpu.VMEM)
HBM = functools.partial(pl.BlockSpec, memory_space=pltpu.HBM)


def after(value, *others):
    return lax.optimization_barrier((value, *others))[0]


def body_edge(projections, block_source, clip_ids, out_weight):
    local_rows, row_width = projections.shape
    block_rows = local_rows // 2
    heads = row_width // (3 * HEAD)
    features = heads * HEAD
    depth, width = out_weight.shape
    count = lax.axis_size("dp")
    bf16 = jnp.bfloat16

    def call(kernel, name, shape, in_specs, dtypes=None, scratch=(), out_spec=VMEM()):
        many = isinstance(shape, list)
        shapes = shape if many else [shape]
        dtypes = dtypes or [bf16] * len(shapes)
        shapes = [jax.ShapeDtypeStruct(*one) for one in zip(shapes, dtypes, strict=True)]
        return pl.pallas_call(
            kernel,
            out_shape=shapes if many else shapes[0],
            in_specs=in_specs,
            out_specs=[out_spec] * len(shapes) if many else out_spec,
            scratch_shapes=scratch,
            cost_estimate=pl.CostEstimate(flops=0, bytes_accessed=0, transcendentals=0),
            compiler_params=pltpu.CompilerParams(vmem_limit_bytes=8 * MIB),
            name=name,
        )

    def around(value, step):
        places = ring_order(count // 4)
        moves = [(here, places[(at + step) % len(places)]) for at, here in enumerate(places)]
        return lax.ppermute(
            value, "dp", [(4 * here + rest, 4 * there + rest) for here, there in moves for rest in range(4)]
        )

    def to_side(value):
        return partner(value, "dp", 1)

    def to_core(value):
        return partner(value, "dp", 0)

    own = pltpu.with_memory_space_constraint(
        projections.reshape(2, block_rows, row_width), pltpu.HBM
    )
    shards = {(0, False): [out_weight]}
    from_partner = pltpu.with_memory_space_constraint(to_core(own), pltpu.VMEM)
    ahead = around(out_weight, 1)
    across = to_side(out_weight)
    staged = call(
        stage_kernel,
        "stage",
        own.shape,
        [SMEM(), HBM()],
        scratch=[pltpu.SemaphoreType.DMA],
    )(block_source, own)
    part_heads = [heads * 8 // 16, heads * 8 // 16]
    packed_first = call(
        pack_first_kernel,
        "pack_first",
        (block_rows, 2 * HEAD * part_heads[0]),
        [SMEM(), VMEM(), VMEM()],
    )(block_source, staged, from_partner)
    rows, packed_last = call(
        pack_kernel,
        "pack",
        [(2, block_rows, row_width), (block_rows, 2 * HEAD * part_heads[1])],
        [SMEM(), VMEM(), VMEM()],
        scratch=[pltpu.SemaphoreType.DMA((2,))],
    )(block_source, staged, after(from_partner, packed_first))
    packed = [packed_first, packed_last]
    halos = [lax.ppermute(part, "ctx", [(0, 1), (1, 0)]) for part in packed]

    def edge_rows(part, *before):
        some = part_heads[part]
        return call(
            functools.partial(edge_kernel, sum(part_heads[:part])),
            "edge_rows",
            [(block_rows, some * HEAD), (block_rows, some // 2 * HEAD)],
            [SMEM(), VMEM(), VMEM()],
        )(after(clip_ids, *before), rows, halos[part])

    back = around(after(out_weight, staged), -1)
    ahead = after(ahead, *packed)
    shards[1, False], shards[0, True] = [ahead], [across]
    second = around(after(ahead, across), 1)
    across = to_side(ahead)
    inner, inner_other = call(
        inner_kernel,
        "inner_rows",
        [(block_rows, features), (block_rows, features // 2)],
        [SMEM(), VMEM()],
    )(after(clip_ids, ahead), rows)
    theirs = [to_core(inner_other)]

    back = after(back, inner)
    shards[3, False] = [back]
    back_across = to_side(back)
    shards[1, True] = [across]
    early = list(shards)
    origins = [*early, (2, False), (3, True), (2, True)]
    inner_total, inner_left = call(
        functools.partial(inner_project_kernel, origins, len(early)),
        "inner_project",
        [(local_rows, width), (local_rows, (len(origins) - len(early)) * depth)],
        [VMEM()] * (2 + len(early)),
        dtypes=[jnp.float32, bf16],
        scratch=[pltpu.VMEM((local_rows, len(early) * depth), bf16)],
    )(inner, *theirs, *[shards[origin][0] for origin in early])
    edges, edge_others = zip(*[edge_rows(part) for part in range(len(part_heads))], strict=True)
    second = after(second, inner_total, edges[0])
    cut = depth // 8 * 5
    shards[2, False] = [second]
    shards[3, True] = [back_across]
    shards[2, True] = [around(after(across, edges[0])[:cut], 1), to_side(second[cut:])]
    theirs = [to_core(part) for part in edge_others]

    more = [shards[origin][0] for origin in origins[len(early) : -1]]
    inner_total = call(
        add_products_kernel,
        "add_products",
        inner_total.shape,
        [VMEM()] * (2 + len(more)),
        dtypes=[jnp.float32],
    )(inner_left, inner_total, *more)
    theirs[-1] = after(theirs[-1], inner_total)
    arranged = call(
        functools.partial(arrange_kernel, origins, len(edges)),
        "arrange",
        (local_rows, len(origins) * depth),
        [VMEM()] * (len(edges) + len(theirs)),
        scratch=[
            pltpu.VMEM((block_rows, features), bf16),
            pltpu.VMEM((block_rows, features // 2), bf16),
        ],
    )(*edges, *theirs)
    pieces = [piece for origin in origins[:-1] for piece in shards[origin]]
    edge_total = call(
        edge_project_kernel,
        "edge_project",
        (local_rows, width),
        [VMEM()] * (1 + len(pieces)),
        dtypes=[jnp.float32],
    )(arranged, *pieces)
    sums = []
    first = 0
    for columns in (width // 3 * 2, width // 3):
        own_total, their_total = call(
            functools.partial(last_project_kernel, first),
            "last_project",
            [(local_rows, columns)] * 2,
            [VMEM()] * (4 + len(shards[origins[-1]])),
            dtypes=[jnp.float32, bf16],
        )(arranged, inner_left, inner_total, edge_total, *shards[origins[-1]])
        sums.append((own_total, to_core(their_total)))
        first += columns
    ready = call(add_kernel, "add", sums[0][0].shape, [VMEM()] * 2)(*sums[0])
    return call(
        finish_kernel,
        "finish",
        (local_rows, width),
        [VMEM()] * 3,
        scratch=[pltpu.VMEM(sums[1][0].shape, bf16), pltpu.SemaphoreType.DMA((4,))],
        out_spec=HBM(),
    )(*sums[1], ready)


def body(projections, block_source, clip_ids, out_weight):
    heads = projections.shape[1] // (3 * HEAD)
    two_and_two = lax.axis_size("ctx") == 2 and block_source.shape[2] == 2
    whole_tiles = out_weight.shape[0] % HEAD == 0 and heads % 16 == 0
    if two_and_two and whole_tiles and lax.axis_size("dp") == 16:
        return body_edge(projections, block_source, clip_ids, out_weight)
    return body_general(projections, block_source, clip_ids, out_weight)


def solution(mesh):
    return jax.shard_map(
        body,
        mesh=mesh,
        in_specs=(P(("dp", "ctx"), None), P("dp", "ctx", None), P("dp", None), P("dp", None)),
        out_specs=P(("dp", "ctx"), None),
        check_vma=False,
    )
```

```python
import functools
import math

import jax
import jax.numpy as jnp
from jax import lax
from jax.experimental import pallas as pl
from jax.experimental.pallas import tpu as pltpu
from jax.sharding import PartitionSpec as P

HEAD = 128


big_negative = -1e30
MIB = 1 << 20


def partner(value, axis, bit):
    mask = 2**bit
    pairs = [(source, source ^ mask) for source in range(lax.axis_size(axis))]
    return lax.ppermute(value, axis, pairs)


def soft_weights(scores, allowed):
    masked = jnp.where(allowed, scores, big_negative)
    row_max = jnp.max(masked, axis=-1, keepdims=True)
    exponent = jnp.exp(masked - row_max)
    return (exponent / jnp.sum(exponent, axis=-1, keepdims=True)).astype(jnp.bfloat16)


def attend_dense(queries, key_rows, value_rows, token_clip, scaling):
    token_count, head_count, head_size = queries.shape
    step_size = min(token_count, 512)
    step_count = token_count // step_size
    query_steps = queries.reshape(step_count, step_size, head_count, head_size)
    clip_steps = token_clip.reshape(step_count, step_size)

    def one_step(arguments):
        query_block, clip_block = arguments
        scores = (
            jnp.einsum("qhe,khe->hqk", query_block, key_rows, preferred_element_type=jnp.float32)
            * scaling
        )
        allowed = (clip_block[:, None] == token_clip[None, :])[None]
        weights = soft_weights(scores, allowed)
        return jnp.einsum(
            "hqk,khe->qhe", weights, value_rows, preferred_element_type=jnp.float32
        ).astype(jnp.bfloat16)

    outputs = lax.map(one_step, (query_steps, clip_steps))
    return outputs.reshape(token_count, head_count, head_size)


def body_general(projections, block_source, clip_ids, out_weight):
    ctx_count = lax.axis_size("ctx")
    local_rows, row_width = projections.shape
    local_blocks = block_source.shape[2]
    block_rows = local_rows // local_blocks
    own_blocks = projections.reshape(local_blocks, block_rows, row_width)
    partner_blocks = partner(own_blocks, "dp", 0)
    source_ids = block_source.reshape(local_blocks)
    from_partner = source_ids // (local_blocks * ctx_count) != lax.axis_index("dp")
    chosen_slot = source_ids % local_blocks + local_blocks * from_partner.astype(jnp.int32)
    candidates = jnp.concatenate([own_blocks, partner_blocks], axis=0)
    packed = jnp.take(candidates, chosen_slot, axis=0)
    local_heads = row_width // (3 * HEAD) // ctx_count
    grouped = packed.reshape(local_rows, ctx_count, local_heads, 3 * HEAD)
    block_clip = clip_ids.reshape(-1)
    token_clip = jnp.repeat(block_clip, block_rows)
    scaling = 1.0 / math.sqrt(HEAD)
    regrouped = lax.all_to_all(grouped, "ctx", split_axis=1, concat_axis=0, tiled=True)
    token_count = regrouped.shape[0]
    item_count = regrouped.shape[2]
    features = regrouped.reshape(token_count, item_count, 3 * HEAD)
    queries = features[:, :, :HEAD]
    key_rows = features[:, :, HEAD : 2 * HEAD]
    value_rows = features[:, :, 2 * HEAD :]
    attended = attend_dense(queries, key_rows, value_rows, token_clip, scaling)
    merged = attended.reshape(local_rows * ctx_count, local_heads * HEAD)
    attention_rows = lax.all_to_all(merged, "ctx", split_axis=0, concat_axis=1, tiled=True)
    result = jnp.dot(
        attention_rows,
        lax.all_gather(out_weight, "dp", axis=0, tiled=True),
        preferred_element_type=jnp.float32,
    )
    return result.astype(jnp.bfloat16)


def stage_kernel(source_ref, own_ref, out_ref, sems):
    parts = sems.shape[1]
    rows = own_ref.shape[1] // parts
    copies = []
    for block in range(own_ref.shape[0]):
        for part in range(parts):
            here = (block, pl.ds(part * rows, rows))
            copies.append(
                pltpu.make_async_copy(own_ref.at[here], out_ref.at[here], sems.at[block, part])
            )
    for copy in copies:
        copy.start()
    for copy in copies:
        copy.wait()


def place(source_ref, own_ref, block):
    slots = own_ref.shape[0]
    source = source_ref[0, 0, block]
    return source // (2 * slots) != lax.axis_index("dp"), lax.rem(source, slots)


def pack_first_kernel(source_ref, own_ref, partner_ref, halo_ref):
    away, slot = place(source_ref, own_ref, 1 - lax.axis_index("ctx"))
    for head in range(halo_ref.shape[1] // (2 * HEAD)):
        columns = slice(head * 3 * HEAD + HEAD, (head + 1) * 3 * HEAD)
        halo_ref[:, head * 2 * HEAD : (head + 1) * 2 * HEAD] = jnp.where(
            away, partner_ref[slot, :, columns], own_ref[slot, :, columns]
        )


def pack_kernel(source_ref, own_ref, partner_ref, rows_ref, halo_ref, sems):
    ctx = lax.axis_index("ctx")
    for which, block in ((1, 1 - ctx), (0, ctx)):
        away, slot = place(source_ref, own_ref, block)

        @pl.when(jnp.logical_not(away))
        def _():
            pltpu.make_async_copy(own_ref.at[slot], rows_ref.at[which], sems.at[which]).start()

        @pl.when(away)
        def _():
            pltpu.make_async_copy(partner_ref.at[slot], rows_ref.at[which], sems.at[which]).start()

    pltpu.make_async_copy(own_ref.at[0], rows_ref.at[1], sems.at[1]).wait()
    heads = halo_ref.shape[1] // (2 * HEAD)
    skipped = rows_ref.shape[2] // (3 * HEAD) - heads
    for head in range(heads):
        first = (skipped + head) * 3 * HEAD + HEAD
        halo_ref[:, head * 2 * HEAD : (head + 1) * 2 * HEAD] = rows_ref[
            1, :, first : first + 2 * HEAD
        ]
    pltpu.make_async_copy(own_ref.at[0], rows_ref.at[0], sems.at[0]).wait()


def attend(heads, load_queries, load_own, load_more, allowed, out_ref, other_ref):
    scaling = math.log2(math.e) / math.sqrt(HEAD)
    contract_last = (((1,), (1,)), ((), ()))
    ones = jnp.ones((2 * out_ref.shape[0], HEAD), jnp.bfloat16)
    odd_core = lax.rem(lax.axis_index("dp"), 2) == 1
    for start in range(0, heads, 4):
        group = min(4, heads - start)
        scores = []
        for head in range(start, start + group):
            queries = load_queries(head)
            pair = []
            for loader in (load_own, load_more):
                pair.append(
                    lax.dot_general(
                        queries, loader(head, 0), contract_last, preferred_element_type=jnp.float32
                    )
                    * scaling
                )
            scores.append(pair)
        weights = []
        for own, more in scores:
            more = jnp.where(allowed, more, big_negative)
            row_max = jnp.max(jnp.maximum(own, more), axis=-1, keepdims=True)
            weights.append(
                jnp.concatenate(
                    [
                        jnp.exp2(own - row_max).astype(jnp.bfloat16),
                        jnp.exp2(more - row_max).astype(jnp.bfloat16),
                    ],
                    axis=1,
                )
            )
        outs = []
        for head in range(start, start + group):
            values = jnp.concatenate([load_own(head, 1), load_more(head, 1)], axis=0)
            sums = jnp.dot(
                weights[head - start],
                jnp.concatenate([values, ones], axis=1),
                preferred_element_type=jnp.float32,
            )
            outs.append(sums[:, :HEAD] / sums[:, HEAD:])
            out_ref[:, head * HEAD : (head + 1) * HEAD] = outs[-1].astype(jnp.bfloat16)
        for pair in range(group // 2):
            at = (start // 2 + pair) * HEAD
            other = jnp.where(odd_core, outs[2 * pair], outs[2 * pair + 1])
            other_ref[:, at : at + HEAD] = other.astype(jnp.bfloat16)


def inner_kernel(clip_ref, rows_ref, out_ref, other_ref):
    ctx = lax.axis_index("ctx")
    allowed = clip_ref[0, 2 * ctx] == clip_ref[0, 2 * ctx + 1]

    def loader(block):
        def get(head, which):
            first = (head * 3 + 1 + which) * HEAD
            return rows_ref[block, :, first : first + HEAD]

        return get

    attend(
        out_ref.shape[1] // HEAD,
        lambda head: loader(0)(head, -1),
        loader(0),
        loader(1),
        allowed,
        out_ref,
        other_ref,
    )


def edge_kernel(first_head, clip_ref, rows_ref, halo_ref, out_ref, other_ref):
    ctx = lax.axis_index("ctx")
    edge_clip = clip_ref[0, 1 + ctx]
    crosses = edge_clip == clip_ref[0, 2 - ctx]
    allowed = jnp.logical_or(crosses, edge_clip == clip_ref[0, 3 * ctx])

    def load_own(head, which):
        first = ((first_head + head) * 3 + 1 + which) * HEAD
        return rows_ref[1, :, first : first + HEAD]

    def load_more(head, which):
        first = ((first_head + head) * 3 + 1 + which) * HEAD
        at = (2 * head + which) * HEAD
        return jnp.where(crosses, halo_ref[:, at : at + HEAD], rows_ref[0, :, first : first + HEAD])

    attend(
        out_ref.shape[1] // HEAD,
        lambda head: load_own(head, -1),
        load_own,
        load_more,
        allowed,
        out_ref,
        other_ref,
    )


def ring_order(lines):
    return list(range(0, lines, 2)) + list(range(1, lines, 2))[::-1]


def shard_places(origins, depth):
    index = lax.axis_index("dp")
    core, side, line = lax.rem(index, 2), lax.rem(index // 2, 2), index // 4
    places = ring_order(lax.axis_size("dp") // 4)
    found = []
    for steps, other_side in origins:
        from_line = line
        for at, place in enumerate(places):
            from_line = jnp.where(line == place, places[at - steps], from_line)
        pair = from_line * 2 + (1 - side if other_side else side)
        here = pl.ds(pl.multiple_of((pair * 2 + core) * depth, depth), depth)
        there = pl.ds(pl.multiple_of(pair * depth, depth), depth)
        found.append((here, there))
    return found


def inner_project_kernel(origins, early, inner_ref, their_ref, *rest):
    shard_refs, (total_ref, left_ref, features) = rest[:-3], rest[-3:]
    block = inner_ref.shape[0]
    depth = left_ref.shape[1] // (len(origins) - early)
    for number, (here, there) in enumerate(shard_places(origins, depth)):
        ref, at = (features, number) if number < early else (left_ref, number - early)
        ref[:block, at * depth : (at + 1) * depth] = inner_ref[:, here]
        ref[block:, at * depth : (at + 1) * depth] = their_ref[:, there]
    tile = 2 * HEAD
    for first in range(0, total_ref.shape[1], tile):
        columns = slice(first, first + tile)
        weight = jnp.concatenate([ref[:, columns] for ref in shard_refs], axis=0)
        total_ref[:, columns] = jnp.dot(
            features[...], weight, preferred_element_type=jnp.float32
        )


def add_products_kernel(left_ref, inner_total_ref, *rest):
    shard_refs, total_ref = rest[:-1], rest[-1]
    depths = sum(ref.shape[0] for ref in shard_refs)
    tile = 2 * HEAD
    for first in range(0, total_ref.shape[1], tile):
        columns = slice(first, first + tile)
        weight = jnp.concatenate([ref[:, columns] for ref in shard_refs], axis=0)
        total_ref[:, columns] = inner_total_ref[:, columns] + jnp.dot(
            left_ref[:, :depths], weight, preferred_element_type=jnp.float32
        )


def edge_project_kernel(origins, parts, *refs):
    edge_refs, their_refs, shard_refs = refs[:parts], refs[parts : 2 * parts], refs[2 * parts : -5]
    total_ref, left_ref, edge_rows, their_rows, features = refs[-5:]
    for refs, held in ((edge_refs, edge_rows), (their_refs, their_rows)):
        first = 0
        for ref in refs:
            held[:, first : first + ref.shape[1]] = ref[...]
            first += ref.shape[1]
    block, depth = left_ref.shape[0] // 2, left_ref.shape[1]
    for number, (here, there) in enumerate(shard_places(origins, depth)):
        last = number == len(origins) - 1
        ref, at = (left_ref, 0) if last else (features, number * depth)
        ref[:block, at : at + depth] = edge_rows[:, here]
        ref[block:, at : at + depth] = their_rows[:, there]
    tile = 2 * HEAD
    for first in range(0, total_ref.shape[1], tile):
        columns = slice(first, first + tile)
        weight = jnp.concatenate([ref[:, columns] for ref in shard_refs], axis=0)
        total_ref[:, columns] = jnp.dot(
            features[...], weight, preferred_element_type=jnp.float32
        )


def last_project_kernel(first, edge_ref, left_ref, inner_total_ref, edge_total_ref, *rest):
    shard_refs, (own_total_ref, their_total_ref) = rest[:-2], rest[-2:]
    block = own_total_ref.shape[0] // 2
    depth = sum(ref.shape[0] for ref in shard_refs)
    features = jnp.concatenate([left_ref[:, -depth:], edge_ref[...]], axis=0)
    tile = 2 * HEAD
    for at in range(0, own_total_ref.shape[1], tile):
        here = slice(at, at + tile)
        columns = slice(first + at, first + at + tile)
        weight = jnp.concatenate([ref[:, columns] for ref in shard_refs], axis=0)
        total = jnp.dot(features, weight, preferred_element_type=jnp.float32)
        inner = inner_total_ref[:, columns] + total[: 2 * block]
        edge = edge_total_ref[:, columns] + total[2 * block :]
        own_total_ref[:block, here] = inner[:block]
        own_total_ref[block:, here] = edge[:block]
        their_total_ref[:block, here] = inner[block:].astype(jnp.bfloat16)
        their_total_ref[block:, here] = edge[block:].astype(jnp.bfloat16)


def add_kernel(total_ref, more_ref, out_ref):
    out_ref[...] = (total_ref[...] + more_ref[...]).astype(jnp.bfloat16)


def finish_kernel(total_ref, more_ref, ready_ref, out_ref, held, sems):
    block = out_ref.shape[0] // 2
    ctx = lax.axis_index("ctx")
    ready = ready_ref.shape[1]
    blocks = [(slice(0, block), ctx), (slice(block, 2 * block), 1 - ctx)]

    def copy(source_ref, which, first, sem):
        rows, place = blocks[which]
        there = pl.ds(pl.multiple_of(place * block, block), block)
        columns = pl.ds(first, source_ref.shape[1])
        return pltpu.make_async_copy(source_ref.at[rows], out_ref.at[there, columns], sem)

    copies = [copy(ready_ref, which, 0, sems.at[which]) for which in range(2)]
    for one in copies:
        one.start()
    for which, (rows, _) in enumerate(blocks):
        held[rows] = (total_ref[rows] + more_ref[rows]).astype(jnp.bfloat16)
        copies.append(copy(held, which, ready, sems.at[2 + which]))
        copies[-1].start()
    for one in copies:
        one.wait()


SMEM = functools.partial(pl.BlockSpec, memory_space=pltpu.SMEM)
VMEM = functools.partial(pl.BlockSpec, memory_space=pltpu.VMEM)
HBM = functools.partial(pl.BlockSpec, memory_space=pltpu.HBM)


def after(value, *others):
    return lax.optimization_barrier((value, *others))[0]


def body_edge(projections, block_source, clip_ids, out_weight):
    local_rows, row_width = projections.shape
    block_rows = local_rows // 2
    heads = row_width // (3 * HEAD)
    features = heads * HEAD
    depth, width = out_weight.shape
    count = lax.axis_size("dp")
    bf16 = jnp.bfloat16

    def call(kernel, name, shape, in_specs, dtypes=None, scratch=(), out_spec=VMEM()):
        many = isinstance(shape, list)
        shapes = shape if many else [shape]
        dtypes = dtypes or [bf16] * len(shapes)
        shapes = [jax.ShapeDtypeStruct(*one) for one in zip(shapes, dtypes, strict=True)]
        return pl.pallas_call(
            kernel,
            out_shape=shapes if many else shapes[0],
            in_specs=in_specs,
            out_specs=[out_spec] * len(shapes) if many else out_spec,
            scratch_shapes=scratch,
            cost_estimate=pl.CostEstimate(flops=0, bytes_accessed=0, transcendentals=0),
            compiler_params=pltpu.CompilerParams(vmem_limit_bytes=8 * MIB),
            name=name,
        )

    def around(value, step):
        places = ring_order(count // 4)
        moves = [(here, places[(at + step) % len(places)]) for at, here in enumerate(places)]
        return lax.ppermute(
            value, "dp", [(4 * here + rest, 4 * there + rest) for here, there in moves for rest in range(4)]
        )

    def to_side(value):
        return partner(value, "dp", 1)

    def to_core(value):
        return partner(value, "dp", 0)

    own = pltpu.with_memory_space_constraint(
        projections.reshape(2, block_rows, row_width), pltpu.HBM
    )
    shards = {(0, False): [out_weight]}
    from_partner = pltpu.with_memory_space_constraint(to_core(own), pltpu.VMEM)
    ahead = around(out_weight, 1)
    across = to_side(out_weight)
    staged = call(
        stage_kernel,
        "stage",
        own.shape,
        [SMEM(), HBM()],
        scratch=[pltpu.SemaphoreType.DMA((2, 4))],
    )(block_source, own)
    part_heads = [heads * 8 // 16, heads * 8 // 16]
    packed_first = call(
        pack_first_kernel,
        "pack_first",
        (block_rows, 2 * HEAD * part_heads[0]),
        [SMEM(), VMEM(), VMEM()],
    )(block_source, staged, from_partner)
    rows, packed_last = call(
        pack_kernel,
        "pack",
        [(2, block_rows, row_width), (block_rows, 2 * HEAD * part_heads[1])],
        [SMEM(), VMEM(), VMEM()],
        scratch=[pltpu.SemaphoreType.DMA((2,))],
    )(block_source, staged, after(from_partner, packed_first))
    packed = [packed_first, packed_last]
    halos = [lax.ppermute(part, "ctx", [(0, 1), (1, 0)]) for part in packed]

    def edge_rows(part, *before):
        some = part_heads[part]
        return call(
            functools.partial(edge_kernel, sum(part_heads[:part])),
            "edge_rows",
            [(block_rows, some * HEAD), (block_rows, some // 2 * HEAD)],
            [SMEM(), VMEM(), VMEM()],
        )(after(clip_ids, *before), rows, halos[part])

    back = around(after(out_weight, staged), -1)
    ahead = after(ahead, *packed)
    shards[1, False], shards[0, True] = [ahead], [across]
    second = around(after(ahead, across), 1)
    across = to_side(ahead)
    inner, inner_other = call(
        inner_kernel,
        "inner_rows",
        [(block_rows, features), (block_rows, features // 2)],
        [SMEM(), VMEM()],
    )(after(clip_ids, ahead), rows)
    theirs = [to_core(inner_other)]

    back = after(back, inner)
    shards[3, False] = [back]
    back_across = to_side(back)
    shards[1, True] = [across]
    early = list(shards)
    origins = [*early, (2, False), (3, True), (2, True)]
    inner_total, inner_left = call(
        functools.partial(inner_project_kernel, origins, len(early)),
        "inner_project",
        [(local_rows, width), (local_rows, (len(origins) - len(early)) * depth)],
        [VMEM()] * (2 + len(early)),
        dtypes=[jnp.float32, bf16],
        scratch=[pltpu.VMEM((local_rows, len(early) * depth), bf16)],
    )(inner, *theirs, *[shards[origin][0] for origin in early])
    edges, edge_others = zip(*[edge_rows(part) for part in range(len(part_heads))], strict=True)
    second = after(second, inner_total, edges[0])
    cut = depth // 8 * 5
    shards[2, False] = [second]
    shards[3, True] = [back_across]
    shards[2, True] = [around(after(across, edges[0])[:cut], 1), to_side(second[cut:])]
    theirs = [to_core(part) for part in edge_others]

    more = [shards[origin][0] for origin in origins[len(early) : -1]]
    inner_total = call(
        add_products_kernel,
        "add_products",
        inner_total.shape,
        [VMEM()] * (2 + len(more)),
        dtypes=[jnp.float32],
    )(inner_left, inner_total, *more)
    theirs[-1] = after(theirs[-1], inner_total)
    pieces = [piece for origin in origins[:-1] for piece in shards[origin]]
    edge_total, edge_left = call(
        functools.partial(edge_project_kernel, origins, len(edges)),
        "edge_project",
        [(local_rows, width), (local_rows, depth)],
        [VMEM()] * (len(edges) + len(theirs) + len(pieces)),
        dtypes=[jnp.float32, bf16],
        scratch=[
            pltpu.VMEM((block_rows, features), bf16),
            pltpu.VMEM((block_rows, features // 2), bf16),
            pltpu.VMEM((local_rows, (len(origins) - 1) * depth), bf16),
        ],
    )(*edges, *theirs, *pieces)
    sums = []
    first = 0
    for columns in (width // 3 * 2, width // 3):
        own_total, their_total = call(
            functools.partial(last_project_kernel, first),
            "last_project",
            [(local_rows, columns)] * 2,
            [VMEM()] * (4 + len(shards[origins[-1]])),
            dtypes=[jnp.float32, bf16],
        )(edge_left, inner_left, inner_total, edge_total, *shards[origins[-1]])
        sums.append((own_total, to_core(their_total)))
        first += columns
    ready = call(add_kernel, "add", sums[0][0].shape, [VMEM()] * 2)(*sums[0])
    return call(
        finish_kernel,
        "finish",
        (local_rows, width),
        [VMEM()] * 3,
        scratch=[pltpu.VMEM(sums[1][0].shape, bf16), pltpu.SemaphoreType.DMA((4,))],
        out_spec=HBM(),
    )(*sums[1], ready)


def body(projections, block_source, clip_ids, out_weight):
    heads = projections.shape[1] // (3 * HEAD)
    two_and_two = lax.axis_size("ctx") == 2 and block_source.shape[2] == 2
    whole_tiles = out_weight.shape[0] % HEAD == 0 and heads % 16 == 0
    if two_and_two and whole_tiles and lax.axis_size("dp") == 16:
        return body_edge(projections, block_source, clip_ids, out_weight)
    return body_general(projections, block_source, clip_ids, out_weight)


def solution(mesh):
    return jax.shard_map(
        body,
        mesh=mesh,
        in_specs=(P(("dp", "ctx"), None), P("dp", "ctx", None), P("dp", None), P("dp", None)),
        out_specs=P(("dp", "ctx"), None),
        check_vma=False,
    )
```

```python
import functools
import math

import jax
import jax.numpy as jnp
from jax import lax
from jax.experimental import pallas as pl
from jax.experimental.pallas import tpu as pltpu
from jax.sharding import PartitionSpec as P

HEAD = 128


big_negative = -1e30
MIB = 1 << 20


def partner(value, axis, bit):
    mask = 2**bit
    pairs = [(source, source ^ mask) for source in range(lax.axis_size(axis))]
    return lax.ppermute(value, axis, pairs)


def soft_weights(scores, allowed):
    masked = jnp.where(allowed, scores, big_negative)
    row_max = jnp.max(masked, axis=-1, keepdims=True)
    exponent = jnp.exp(masked - row_max)
    return (exponent / jnp.sum(exponent, axis=-1, keepdims=True)).astype(jnp.bfloat16)


def attend_dense(queries, key_rows, value_rows, token_clip, scaling):
    token_count, head_count, head_size = queries.shape
    step_size = min(token_count, 512)
    step_count = token_count // step_size
    query_steps = queries.reshape(step_count, step_size, head_count, head_size)
    clip_steps = token_clip.reshape(step_count, step_size)

    def one_step(arguments):
        query_block, clip_block = arguments
        scores = (
            jnp.einsum("qhe,khe->hqk", query_block, key_rows, preferred_element_type=jnp.float32)
            * scaling
        )
        allowed = (clip_block[:, None] == token_clip[None, :])[None]
        weights = soft_weights(scores, allowed)
        return jnp.einsum(
            "hqk,khe->qhe", weights, value_rows, preferred_element_type=jnp.float32
        ).astype(jnp.bfloat16)

    outputs = lax.map(one_step, (query_steps, clip_steps))
    return outputs.reshape(token_count, head_count, head_size)


def body_general(projections, block_source, clip_ids, out_weight):
    ctx_count = lax.axis_size("ctx")
    local_rows, row_width = projections.shape
    local_blocks = block_source.shape[2]
    block_rows = local_rows // local_blocks
    own_blocks = projections.reshape(local_blocks, block_rows, row_width)
    partner_blocks = partner(own_blocks, "dp", 0)
    source_ids = block_source.reshape(local_blocks)
    from_partner = source_ids // (local_blocks * ctx_count) != lax.axis_index("dp")
    chosen_slot = source_ids % local_blocks + local_blocks * from_partner.astype(jnp.int32)
    candidates = jnp.concatenate([own_blocks, partner_blocks], axis=0)
    packed = jnp.take(candidates, chosen_slot, axis=0)
    local_heads = row_width // (3 * HEAD) // ctx_count
    grouped = packed.reshape(local_rows, ctx_count, local_heads, 3 * HEAD)
    block_clip = clip_ids.reshape(-1)
    token_clip = jnp.repeat(block_clip, block_rows)
    scaling = 1.0 / math.sqrt(HEAD)
    regrouped = lax.all_to_all(grouped, "ctx", split_axis=1, concat_axis=0, tiled=True)
    token_count = regrouped.shape[0]
    item_count = regrouped.shape[2]
    features = regrouped.reshape(token_count, item_count, 3 * HEAD)
    queries = features[:, :, :HEAD]
    key_rows = features[:, :, HEAD : 2 * HEAD]
    value_rows = features[:, :, 2 * HEAD :]
    attended = attend_dense(queries, key_rows, value_rows, token_clip, scaling)
    merged = attended.reshape(local_rows * ctx_count, local_heads * HEAD)
    attention_rows = lax.all_to_all(merged, "ctx", split_axis=0, concat_axis=1, tiled=True)
    result = jnp.dot(
        attention_rows,
        lax.all_gather(out_weight, "dp", axis=0, tiled=True),
        preferred_element_type=jnp.float32,
    )
    return result.astype(jnp.bfloat16)


def route_kernel(source_ref, out_ref):
    for slot in range(source_ref.shape[2]):
        out_ref[0, 0, slot] = source_ref[0, 0, slot]


def place(source_ref, own_ref, block):
    slots = own_ref.shape[0]
    source = source_ref[0, 0, block]
    return source // (2 * slots) != lax.axis_index("dp"), lax.rem(source, slots)


def pack_first_kernel(source_ref, own_ref, partner_ref, halo_ref, held, sem):
    away, slot = place(source_ref, own_ref, 1 - lax.axis_index("ctx"))
    heads = halo_ref.shape[1] // (2 * HEAD)

    def fill(load):
        for head in range(heads):
            columns = slice(head * 3 * HEAD + HEAD, (head + 1) * 3 * HEAD)
            halo_ref[:, head * 2 * HEAD : (head + 1) * 2 * HEAD] = load(columns)

    @pl.when(away)
    def _():
        fill(lambda columns: partner_ref[slot, :, columns])

    @pl.when(jnp.logical_not(away))
    def _():
        columns = pl.ds(0, held.shape[1])
        copy = pltpu.make_async_copy(own_ref.at[slot, :, columns], held, sem)
        copy.start()
        copy.wait()
        fill(lambda columns: held[:, columns])


def pack_kernel(source_ref, own_ref, partner_ref, rows_ref, halo_ref, sems):
    ctx = lax.axis_index("ctx")
    for which, block in ((1, 1 - ctx), (0, ctx)):
        away, slot = place(source_ref, own_ref, block)

        @pl.when(jnp.logical_not(away))
        def _():
            pltpu.make_async_copy(own_ref.at[slot], rows_ref.at[which], sems.at[which]).start()

        @pl.when(away)
        def _():
            pltpu.make_async_copy(partner_ref.at[slot], rows_ref.at[which], sems.at[which]).start()

    pltpu.make_async_copy(own_ref.at[0], rows_ref.at[1], sems.at[1]).wait()
    heads = halo_ref.shape[1] // (2 * HEAD)
    skipped = rows_ref.shape[2] // (3 * HEAD) - heads
    for head in range(heads):
        first = (skipped + head) * 3 * HEAD + HEAD
        halo_ref[:, head * 2 * HEAD : (head + 1) * 2 * HEAD] = rows_ref[
            1, :, first : first + 2 * HEAD
        ]
    pltpu.make_async_copy(own_ref.at[0], rows_ref.at[0], sems.at[0]).wait()


def attend(heads, load_queries, load_own, load_more, allowed, out_ref, other_ref):
    scaling = math.log2(math.e) / math.sqrt(HEAD)
    contract_last = (((1,), (1,)), ((), ()))
    ones = jnp.ones((2 * out_ref.shape[0], HEAD), jnp.bfloat16)
    odd_core = lax.rem(lax.axis_index("dp"), 2) == 1
    for start in range(0, heads, 4):
        group = min(4, heads - start)
        scores = []
        for head in range(start, start + group):
            queries = load_queries(head)
            pair = []
            for loader in (load_own, load_more):
                pair.append(
                    lax.dot_general(
                        queries, loader(head, 0), contract_last, preferred_element_type=jnp.float32
                    )
                    * scaling
                )
            scores.append(pair)
        weights = []
        for own, more in scores:
            more = jnp.where(allowed, more, big_negative)
            row_max = jnp.max(jnp.maximum(own, more), axis=-1, keepdims=True)
            weights.append(
                jnp.concatenate(
                    [
                        jnp.exp2(own - row_max).astype(jnp.bfloat16),
                        jnp.exp2(more - row_max).astype(jnp.bfloat16),
                    ],
                    axis=1,
                )
            )
        outs = []
        for head in range(start, start + group):
            values = jnp.concatenate([load_own(head, 1), load_more(head, 1)], axis=0)
            sums = jnp.dot(
                weights[head - start],
                jnp.concatenate([values, ones], axis=1),
                preferred_element_type=jnp.float32,
            )
            outs.append(sums[:, :HEAD] / sums[:, HEAD:])
            out_ref[:, head * HEAD : (head + 1) * HEAD] = outs[-1].astype(jnp.bfloat16)
        for pair in range(group // 2):
            at = (start // 2 + pair) * HEAD
            other = jnp.where(odd_core, outs[2 * pair], outs[2 * pair + 1])
            other_ref[:, at : at + HEAD] = other.astype(jnp.bfloat16)


def inner_kernel(clip_ref, rows_ref, out_ref, other_ref):
    ctx = lax.axis_index("ctx")
    allowed = clip_ref[0, 2 * ctx] == clip_ref[0, 2 * ctx + 1]

    def loader(block):
        def get(head, which):
            first = (head * 3 + 1 + which) * HEAD
            return rows_ref[block, :, first : first + HEAD]

        return get

    attend(
        out_ref.shape[1] // HEAD,
        lambda head: loader(0)(head, -1),
        loader(0),
        loader(1),
        allowed,
        out_ref,
        other_ref,
    )


def edge_kernel(first_head, clip_ref, rows_ref, halo_ref, out_ref, other_ref):
    ctx = lax.axis_index("ctx")
    edge_clip = clip_ref[0, 1 + ctx]
    crosses = edge_clip == clip_ref[0, 2 - ctx]
    allowed = jnp.logical_or(crosses, edge_clip == clip_ref[0, 3 * ctx])

    def load_own(head, which):
        first = ((first_head + head) * 3 + 1 + which) * HEAD
        return rows_ref[1, :, first : first + HEAD]

    def load_more(head, which):
        first = ((first_head + head) * 3 + 1 + which) * HEAD
        at = (2 * head + which) * HEAD
        return jnp.where(crosses, halo_ref[:, at : at + HEAD], rows_ref[0, :, first : first + HEAD])

    attend(
        out_ref.shape[1] // HEAD,
        lambda head: load_own(head, -1),
        load_own,
        load_more,
        allowed,
        out_ref,
        other_ref,
    )


def ring_order(lines):
    return list(range(0, lines, 2)) + list(range(1, lines, 2))[::-1]


def shard_places(origins, depth):
    index = lax.axis_index("dp")
    core, side, line = lax.rem(index, 2), lax.rem(index // 2, 2), index // 4
    places = ring_order(lax.axis_size("dp") // 4)
    found = []
    for steps, other_side in origins:
        from_line = line
        for at, place in enumerate(places):
            from_line = jnp.where(line == place, places[at - steps], from_line)
        pair = from_line * 2 + (1 - side if other_side else side)
        here = pl.ds(pl.multiple_of((pair * 2 + core) * depth, depth), depth)
        there = pl.ds(pl.multiple_of(pair * depth, depth), depth)
        found.append((here, there))
    return found


def inner_project_kernel(origins, early, inner_ref, their_ref, *rest):
    shard_refs, (total_ref, left_ref, features) = rest[:-3], rest[-3:]
    block = inner_ref.shape[0]
    depth = left_ref.shape[1] // (len(origins) - early)
    for number, (here, there) in enumerate(shard_places(origins, depth)):
        ref, at = (features, number) if number < early else (left_ref, number - early)
        ref[:block, at * depth : (at + 1) * depth] = inner_ref[:, here]
        ref[block:, at * depth : (at + 1) * depth] = their_ref[:, there]
    tile = 2 * HEAD
    for first in range(0, total_ref.shape[1], tile):
        columns = slice(first, first + tile)
        weight = jnp.concatenate([ref[:, columns] for ref in shard_refs], axis=0)
        total_ref[:, columns] = jnp.dot(
            features[...], weight, preferred_element_type=jnp.float32
        )


def add_products_kernel(left_ref, inner_total_ref, *rest):
    shard_refs, total_ref = rest[:-1], rest[-1]
    depths = sum(ref.shape[0] for ref in shard_refs)
    tile = 2 * HEAD
    for first in range(0, total_ref.shape[1], tile):
        columns = slice(first, first + tile)
        weight = jnp.concatenate([ref[:, columns] for ref in shard_refs], axis=0)
        total_ref[:, columns] = inner_total_ref[:, columns] + jnp.dot(
            left_ref[:, :depths], weight, preferred_element_type=jnp.float32
        )


def edge_project_kernel(origins, parts, *refs):
    edge_refs, their_refs, shard_refs = refs[:parts], refs[parts : 2 * parts], refs[2 * parts : -5]
    total_ref, left_ref, edge_rows, their_rows, features = refs[-5:]
    for refs, held in ((edge_refs, edge_rows), (their_refs, their_rows)):
        first = 0
        for ref in refs:
            held[:, first : first + ref.shape[1]] = ref[...]
            first += ref.shape[1]
    block, depth = left_ref.shape[0] // 2, left_ref.shape[1]
    for number, (here, there) in enumerate(shard_places(origins, depth)):
        last = number == len(origins) - 1
        ref, at = (left_ref, 0) if last else (features, number * depth)
        ref[:block, at : at + depth] = edge_rows[:, here]
        ref[block:, at : at + depth] = their_rows[:, there]
    tile = 2 * HEAD
    for first in range(0, total_ref.shape[1], tile):
        columns = slice(first, first + tile)
        weight = jnp.concatenate([ref[:, columns] for ref in shard_refs], axis=0)
        total_ref[:, columns] = jnp.dot(
            features[...], weight, preferred_element_type=jnp.float32
        )


def last_project_kernel(first, edge_ref, left_ref, inner_total_ref, edge_total_ref, *rest):
    shard_refs, (own_total_ref, their_total_ref) = rest[:-2], rest[-2:]
    block = own_total_ref.shape[0] // 2
    depth = sum(ref.shape[0] for ref in shard_refs)
    features = jnp.concatenate([left_ref[:, -depth:], edge_ref[...]], axis=0)
    tile = 2 * HEAD
    for at in range(0, own_total_ref.shape[1], tile):
        here = slice(at, at + tile)
        columns = slice(first + at, first + at + tile)
        weight = jnp.concatenate([ref[:, columns] for ref in shard_refs], axis=0)
        total = jnp.dot(features, weight, preferred_element_type=jnp.float32)
        inner = inner_total_ref[:, columns] + total[: 2 * block]
        edge = edge_total_ref[:, columns] + total[2 * block :]
        own_total_ref[:block, here] = inner[:block]
        own_total_ref[block:, here] = edge[:block]
        their_total_ref[:block, here] = inner[block:].astype(jnp.bfloat16)
        their_total_ref[block:, here] = edge[block:].astype(jnp.bfloat16)


def add_kernel(total_ref, more_ref, out_ref):
    out_ref[...] = (total_ref[...] + more_ref[...]).astype(jnp.bfloat16)


def finish_kernel(total_ref, more_ref, ready_ref, out_ref, held, sems):
    block = out_ref.shape[0] // 2
    ctx = lax.axis_index("ctx")
    ready = ready_ref.shape[1]
    blocks = [(slice(0, block), ctx), (slice(block, 2 * block), 1 - ctx)]

    def copy(source_ref, which, first, sem):
        rows, place = blocks[which]
        there = pl.ds(pl.multiple_of(place * block, block), block)
        columns = pl.ds(first, source_ref.shape[1])
        return pltpu.make_async_copy(source_ref.at[rows], out_ref.at[there, columns], sem)

    copies = [copy(ready_ref, which, 0, sems.at[which]) for which in range(2)]
    for one in copies:
        one.start()
    for which, (rows, _) in enumerate(blocks):
        held[rows] = (total_ref[rows] + more_ref[rows]).astype(jnp.bfloat16)
        copies.append(copy(held, which, ready, sems.at[2 + which]))
        copies[-1].start()
    for one in copies:
        one.wait()


SMEM = functools.partial(pl.BlockSpec, memory_space=pltpu.SMEM)
VMEM = functools.partial(pl.BlockSpec, memory_space=pltpu.VMEM)
HBM = functools.partial(pl.BlockSpec, memory_space=pltpu.HBM)


def after(value, *others):
    return lax.optimization_barrier((value, *others))[0]


def body_edge(projections, block_source, clip_ids, out_weight):
    local_rows, row_width = projections.shape
    block_rows = local_rows // 2
    heads = row_width // (3 * HEAD)
    features = heads * HEAD
    depth, width = out_weight.shape
    count = lax.axis_size("dp")
    bf16 = jnp.bfloat16

    def call(kernel, name, shape, in_specs, dtypes=None, scratch=(), out_spec=VMEM()):
        many = isinstance(shape, list)
        shapes = shape if many else [shape]
        dtypes = dtypes or [bf16] * len(shapes)
        shapes = [jax.ShapeDtypeStruct(*one) for one in zip(shapes, dtypes, strict=True)]
        return pl.pallas_call(
            kernel,
            out_shape=shapes if many else shapes[0],
            in_specs=in_specs,
            out_specs=[out_spec] * len(shapes) if many else out_spec,
            scratch_shapes=scratch,
            cost_estimate=pl.CostEstimate(flops=0, bytes_accessed=0, transcendentals=0),
            compiler_params=pltpu.CompilerParams(vmem_limit_bytes=8 * MIB),
            name=name,
        )

    def around(value, step):
        places = ring_order(count // 4)
        moves = [(here, places[(at + step) % len(places)]) for at, here in enumerate(places)]
        return lax.ppermute(
            value, "dp", [(4 * here + rest, 4 * there + rest) for here, there in moves for rest in range(4)]
        )

    def to_side(value):
        return partner(value, "dp", 1)

    def to_core(value):
        return partner(value, "dp", 0)

    own = pltpu.with_memory_space_constraint(
        projections.reshape(2, block_rows, row_width), pltpu.HBM
    )
    shards = {(0, False): [out_weight]}
    from_partner = pltpu.with_memory_space_constraint(to_core(own), pltpu.VMEM)
    ahead = around(out_weight, 1)
    across = to_side(out_weight)
    source = pl.pallas_call(
        route_kernel,
        out_shape=jax.ShapeDtypeStruct(block_source.shape, block_source.dtype),
        in_specs=[SMEM()],
        out_specs=SMEM(),
        name="route",
    )(block_source)
    part_heads = [heads * 8 // 16, heads * 8 // 16]
    packed_first = call(
        pack_first_kernel,
        "pack_first",
        (block_rows, 2 * HEAD * part_heads[0]),
        [SMEM(), HBM(), VMEM()],
        scratch=[
            pltpu.VMEM((block_rows, 3 * HEAD * part_heads[0]), bf16),
            pltpu.SemaphoreType.DMA,
        ],
    )(source, own, from_partner)
    rows, packed_last = call(
        pack_kernel,
        "pack",
        [(2, block_rows, row_width), (block_rows, 2 * HEAD * part_heads[1])],
        [SMEM(), HBM(), VMEM()],
        scratch=[pltpu.SemaphoreType.DMA((2,))],
    )(source, own, after(from_partner, packed_first))
    packed = [packed_first, packed_last]
    halos = [lax.ppermute(part, "ctx", [(0, 1), (1, 0)]) for part in packed]

    def edge_rows(part, *before):
        some = part_heads[part]
        return call(
            functools.partial(edge_kernel, sum(part_heads[:part])),
            "edge_rows",
            [(block_rows, some * HEAD), (block_rows, some // 2 * HEAD)],
            [SMEM(), VMEM(), VMEM()],
        )(after(clip_ids, *before), rows, halos[part])

    back = around(after(out_weight, packed_first), -1)
    ahead = after(ahead, *packed)
    shards[1, False], shards[0, True] = [ahead], [across]
    second = around(after(ahead, across), 1)
    across = to_side(ahead)
    inner, inner_other = call(
        inner_kernel,
        "inner_rows",
        [(block_rows, features), (block_rows, features // 2)],
        [SMEM(), VMEM()],
    )(after(clip_ids, ahead), rows)
    theirs = [to_core(inner_other)]

    back = after(back, inner)
    shards[3, False] = [back]
    back_across = to_side(back)
    shards[1, True] = [across]
    early = list(shards)
    origins = [*early, (2, False), (3, True), (2, True)]
    inner_total, inner_left = call(
        functools.partial(inner_project_kernel, origins, len(early)),
        "inner_project",
        [(local_rows, width), (local_rows, (len(origins) - len(early)) * depth)],
        [VMEM()] * (2 + len(early)),
        dtypes=[jnp.float32, bf16],
        scratch=[pltpu.VMEM((local_rows, len(early) * depth), bf16)],
    )(inner, *theirs, *[shards[origin][0] for origin in early])
    edges, edge_others = zip(*[edge_rows(part) for part in range(len(part_heads))], strict=True)
    second = after(second, inner_total, edges[0])
    cut = depth // 8 * 5
    shards[2, False] = [second]
    shards[3, True] = [back_across]
    shards[2, True] = [around(after(across, edges[0])[:cut], 1), to_side(second[cut:])]
    theirs = [to_core(part) for part in edge_others]

    more = [shards[origin][0] for origin in origins[len(early) : -1]]
    inner_total = call(
        add_products_kernel,
        "add_products",
        inner_total.shape,
        [VMEM()] * (2 + len(more)),
        dtypes=[jnp.float32],
    )(inner_left, inner_total, *more)
    theirs[-1] = after(theirs[-1], inner_total)
    pieces = [piece for origin in origins[:-1] for piece in shards[origin]]
    edge_total, edge_left = call(
        functools.partial(edge_project_kernel, origins, len(edges)),
        "edge_project",
        [(local_rows, width), (local_rows, depth)],
        [VMEM()] * (len(edges) + len(theirs) + len(pieces)),
        dtypes=[jnp.float32, bf16],
        scratch=[
            pltpu.VMEM((block_rows, features), bf16),
            pltpu.VMEM((block_rows, features // 2), bf16),
            pltpu.VMEM((local_rows, (len(origins) - 1) * depth), bf16),
        ],
    )(*edges, *theirs, *pieces)
    sums = []
    first = 0
    for columns in (width // 3 * 2, width // 3):
        own_total, their_total = call(
            functools.partial(last_project_kernel, first),
            "last_project",
            [(local_rows, columns)] * 2,
            [VMEM()] * (4 + len(shards[origins[-1]])),
            dtypes=[jnp.float32, bf16],
        )(edge_left, inner_left, inner_total, edge_total, *shards[origins[-1]])
        sums.append((own_total, to_core(their_total)))
        first += columns
    ready = call(add_kernel, "add", sums[0][0].shape, [VMEM()] * 2)(*sums[0])
    return call(
        finish_kernel,
        "finish",
        (local_rows, width),
        [VMEM()] * 3,
        scratch=[pltpu.VMEM(sums[1][0].shape, bf16), pltpu.SemaphoreType.DMA((4,))],
        out_spec=HBM(),
    )(*sums[1], ready)


def body(projections, block_source, clip_ids, out_weight):
    heads = projections.shape[1] // (3 * HEAD)
    two_and_two = lax.axis_size("ctx") == 2 and block_source.shape[2] == 2
    whole_tiles = out_weight.shape[0] % HEAD == 0 and heads % 16 == 0
    if two_and_two and whole_tiles and lax.axis_size("dp") == 16:
        return body_edge(projections, block_source, clip_ids, out_weight)
    return body_general(projections, block_source, clip_ids, out_weight)


def solution(mesh):
    return jax.shard_map(
        body,
        mesh=mesh,
        in_specs=(P(("dp", "ctx"), None), P("dp", "ctx", None), P("dp", None), P("dp", None)),
        out_specs=P(("dp", "ctx"), None),
        check_vma=False,
    )
```

```python
import functools
import math

import jax
import jax.numpy as jnp
from jax import lax
from jax.experimental import pallas as pl
from jax.experimental.pallas import tpu as pltpu
from jax.sharding import PartitionSpec as P

HEAD = 128


big_negative = -1e30
MIB = 1 << 20


def partner(value, axis, bit):
    mask = 2**bit
    pairs = [(source, source ^ mask) for source in range(lax.axis_size(axis))]
    return lax.ppermute(value, axis, pairs)


def soft_weights(scores, allowed):
    masked = jnp.where(allowed, scores, big_negative)
    row_max = jnp.max(masked, axis=-1, keepdims=True)
    exponent = jnp.exp(masked - row_max)
    return (exponent / jnp.sum(exponent, axis=-1, keepdims=True)).astype(jnp.bfloat16)


def attend_dense(queries, key_rows, value_rows, token_clip, scaling):
    token_count, head_count, head_size = queries.shape
    step_size = min(token_count, 512)
    step_count = token_count // step_size
    query_steps = queries.reshape(step_count, step_size, head_count, head_size)
    clip_steps = token_clip.reshape(step_count, step_size)

    def one_step(arguments):
        query_block, clip_block = arguments
        scores = (
            jnp.einsum("qhe,khe->hqk", query_block, key_rows, preferred_element_type=jnp.float32)
            * scaling
        )
        allowed = (clip_block[:, None] == token_clip[None, :])[None]
        weights = soft_weights(scores, allowed)
        return jnp.einsum(
            "hqk,khe->qhe", weights, value_rows, preferred_element_type=jnp.float32
        ).astype(jnp.bfloat16)

    outputs = lax.map(one_step, (query_steps, clip_steps))
    return outputs.reshape(token_count, head_count, head_size)


def body_general(projections, block_source, clip_ids, out_weight):
    ctx_count = lax.axis_size("ctx")
    local_rows, row_width = projections.shape
    local_blocks = block_source.shape[2]
    block_rows = local_rows // local_blocks
    own_blocks = projections.reshape(local_blocks, block_rows, row_width)
    partner_blocks = partner(own_blocks, "dp", 0)
    source_ids = block_source.reshape(local_blocks)
    from_partner = source_ids // (local_blocks * ctx_count) != lax.axis_index("dp")
    chosen_slot = source_ids % local_blocks + local_blocks * from_partner.astype(jnp.int32)
    candidates = jnp.concatenate([own_blocks, partner_blocks], axis=0)
    packed = jnp.take(candidates, chosen_slot, axis=0)
    local_heads = row_width // (3 * HEAD) // ctx_count
    grouped = packed.reshape(local_rows, ctx_count, local_heads, 3 * HEAD)
    block_clip = clip_ids.reshape(-1)
    token_clip = jnp.repeat(block_clip, block_rows)
    scaling = 1.0 / math.sqrt(HEAD)
    regrouped = lax.all_to_all(grouped, "ctx", split_axis=1, concat_axis=0, tiled=True)
    token_count = regrouped.shape[0]
    item_count = regrouped.shape[2]
    features = regrouped.reshape(token_count, item_count, 3 * HEAD)
    queries = features[:, :, :HEAD]
    key_rows = features[:, :, HEAD : 2 * HEAD]
    value_rows = features[:, :, 2 * HEAD :]
    attended = attend_dense(queries, key_rows, value_rows, token_clip, scaling)
    merged = attended.reshape(local_rows * ctx_count, local_heads * HEAD)
    attention_rows = lax.all_to_all(merged, "ctx", split_axis=0, concat_axis=1, tiled=True)
    result = jnp.dot(
        attention_rows,
        lax.all_gather(out_weight, "dp", axis=0, tiled=True),
        preferred_element_type=jnp.float32,
    )
    return result.astype(jnp.bfloat16)


EDGE_AWAY, EDGE_SLOT, INNER_AWAY, INNER_SLOT, INNER_JOINS, EDGE_JOINS, CROSSES = range(7)


def stage_kernel(source_ref, clip_ref, own_ref, out_ref, facts_ref, sems):
    parts = sems.shape[1]
    slots = own_ref.shape[0]
    rows = own_ref.shape[1] // parts
    copies = []
    for block in range(slots):
        for part in range(parts):
            here = (block, pl.ds(part * rows, rows))
            copies.append(
                pltpu.make_async_copy(own_ref.at[here], out_ref.at[here], sems.at[block, part])
            )
    for copy in copies:
        copy.start()
    ctx, dp = lax.axis_index("ctx"), lax.axis_index("dp")
    facts = {}
    for block, away, at in ((1 - ctx, EDGE_AWAY, EDGE_SLOT), (ctx, INNER_AWAY, INNER_SLOT)):
        source = source_ref[0, 0, block]
        facts[away] = (source // (2 * slots) != dp).astype(jnp.int32)
        facts[at] = lax.rem(source, slots)
    edge_clip = clip_ref[0, 1 + ctx]
    crosses = edge_clip == clip_ref[0, 2 - ctx]
    facts[CROSSES] = crosses.astype(jnp.int32)
    facts[EDGE_JOINS] = jnp.logical_or(crosses, edge_clip == clip_ref[0, 3 * ctx]).astype(jnp.int32)
    facts[INNER_JOINS] = (clip_ref[0, 2 * ctx] == clip_ref[0, 2 * ctx + 1]).astype(jnp.int32)
    for which, fact in facts.items():
        facts_ref[which] = jnp.full(facts_ref.shape[1:], fact, jnp.int32)
    for copy in copies:
        copy.wait()


def fact(facts_ref, which):
    return jnp.max(facts_ref[which])


def pack_first_kernel(facts_ref, own_ref, partner_ref, halo_ref):
    away, slot = fact(facts_ref, EDGE_AWAY) > 0, fact(facts_ref, EDGE_SLOT)

    def fill(ref):
        for head in range(halo_ref.shape[1] // (2 * HEAD)):
            columns = slice(head * 3 * HEAD + HEAD, (head + 1) * 3 * HEAD)
            halo_ref[:, head * 2 * HEAD : (head + 1) * 2 * HEAD] = ref[slot, :, columns]

    @pl.when(away)
    def _():
        fill(partner_ref)

    @pl.when(jnp.logical_not(away))
    def _():
        fill(own_ref)


def pack_kernel(facts_ref, own_ref, partner_ref, rows_ref, halo_ref, sems):
    for which, away, at in ((1, EDGE_AWAY, EDGE_SLOT), (0, INNER_AWAY, INNER_SLOT)):
        away, slot = fact(facts_ref, away) > 0, fact(facts_ref, at)

        @pl.when(jnp.logical_not(away))
        def _():
            pltpu.make_async_copy(own_ref.at[slot], rows_ref.at[which], sems.at[which]).start()

        @pl.when(away)
        def _():
            pltpu.make_async_copy(partner_ref.at[slot], rows_ref.at[which], sems.at[which]).start()

    pltpu.make_async_copy(own_ref.at[0], rows_ref.at[1], sems.at[1]).wait()
    heads = halo_ref.shape[1] // (2 * HEAD)
    skipped = rows_ref.shape[2] // (3 * HEAD) - heads
    for head in range(heads):
        first = (skipped + head) * 3 * HEAD + HEAD
        halo_ref[:, head * 2 * HEAD : (head + 1) * 2 * HEAD] = rows_ref[
            1, :, first : first + 2 * HEAD
        ]
    pltpu.make_async_copy(own_ref.at[0], rows_ref.at[0], sems.at[0]).wait()


def attend(heads, load_queries, load_own, load_more, allowed, out_ref, other_ref):
    scaling = math.log2(math.e) / math.sqrt(HEAD)
    contract_last = (((1,), (1,)), ((), ()))
    ones = jnp.ones((2 * out_ref.shape[0], HEAD), jnp.bfloat16)
    odd_core = lax.rem(lax.axis_index("dp"), 2) == 1
    for start in range(0, heads, 4):
        group = min(4, heads - start)
        scores = []
        for head in range(start, start + group):
            queries = load_queries(head)
            pair = []
            for loader in (load_own, load_more):
                pair.append(
                    lax.dot_general(
                        queries, loader(head, 0), contract_last, preferred_element_type=jnp.float32
                    )
                    * scaling
                )
            scores.append(pair)
        weights = []
        for own, more in scores:
            more = jnp.where(allowed, more, big_negative)
            row_max = jnp.max(jnp.maximum(own, more), axis=-1, keepdims=True)
            weights.append(
                jnp.concatenate(
                    [
                        jnp.exp2(own - row_max).astype(jnp.bfloat16),
                        jnp.exp2(more - row_max).astype(jnp.bfloat16),
                    ],
                    axis=1,
                )
            )
        outs = []
        for head in range(start, start + group):
            values = jnp.concatenate([load_own(head, 1), load_more(head, 1)], axis=0)
            sums = jnp.dot(
                weights[head - start],
                jnp.concatenate([values, ones], axis=1),
                preferred_element_type=jnp.float32,
            )
            outs.append(sums[:, :HEAD] / sums[:, HEAD:])
            out_ref[:, head * HEAD : (head + 1) * HEAD] = outs[-1].astype(jnp.bfloat16)
        for pair in range(group // 2):
            at = (start // 2 + pair) * HEAD
            other = jnp.where(odd_core, outs[2 * pair], outs[2 * pair + 1])
            other_ref[:, at : at + HEAD] = other.astype(jnp.bfloat16)


def inner_kernel(facts_ref, rows_ref, out_ref, other_ref):
    allowed = fact(facts_ref, INNER_JOINS) > 0

    def loader(block):
        def get(head, which):
            first = (head * 3 + 1 + which) * HEAD
            return rows_ref[block, :, first : first + HEAD]

        return get

    attend(
        out_ref.shape[1] // HEAD,
        lambda head: loader(0)(head, -1),
        loader(0),
        loader(1),
        allowed,
        out_ref,
        other_ref,
    )


def edge_kernel(first_head, facts_ref, rows_ref, halo_ref, out_ref, other_ref):
    crosses, allowed = fact(facts_ref, CROSSES) > 0, fact(facts_ref, EDGE_JOINS) > 0

    def load_own(head, which):
        first = ((first_head + head) * 3 + 1 + which) * HEAD
        return rows_ref[1, :, first : first + HEAD]

    def load_more(head, which):
        first = ((first_head + head) * 3 + 1 + which) * HEAD
        at = (2 * head + which) * HEAD
        return jnp.where(crosses, halo_ref[:, at : at + HEAD], rows_ref[0, :, first : first + HEAD])

    attend(
        out_ref.shape[1] // HEAD,
        lambda head: load_own(head, -1),
        load_own,
        load_more,
        allowed,
        out_ref,
        other_ref,
    )


def ring_order(lines):
    return list(range(0, lines, 2)) + list(range(1, lines, 2))[::-1]


def shard_places(origins, depth):
    index = lax.axis_index("dp")
    core, side, line = lax.rem(index, 2), lax.rem(index // 2, 2), index // 4
    places = ring_order(lax.axis_size("dp") // 4)
    found = []
    for steps, other_side in origins:
        from_line = line
        for at, place in enumerate(places):
            from_line = jnp.where(line == place, places[at - steps], from_line)
        pair = from_line * 2 + (1 - side if other_side else side)
        here = pl.ds(pl.multiple_of((pair * 2 + core) * depth, depth), depth)
        there = pl.ds(pl.multiple_of(pair * depth, depth), depth)
        found.append((here, there))
    return found


def inner_project_kernel(origins, early, inner_ref, their_ref, *rest):
    shard_refs, (total_ref, left_ref, features) = rest[:-3], rest[-3:]
    block = inner_ref.shape[0]
    depth = left_ref.shape[1] // (len(origins) - early)
    for number, (here, there) in enumerate(shard_places(origins, depth)):
        ref, at = (features, number) if number < early else (left_ref, number - early)
        ref[:block, at * depth : (at + 1) * depth] = inner_ref[:, here]
        ref[block:, at * depth : (at + 1) * depth] = their_ref[:, there]
    tile = 2 * HEAD
    for first in range(0, total_ref.shape[1], tile):
        columns = slice(first, first + tile)
        weight = jnp.concatenate([ref[:, columns] for ref in shard_refs], axis=0)
        total_ref[:, columns] = jnp.dot(
            features[...], weight, preferred_element_type=jnp.float32
        )


def add_products_kernel(left_ref, inner_total_ref, *rest):
    shard_refs, total_ref = rest[:-1], rest[-1]
    depths = sum(ref.shape[0] for ref in shard_refs)
    tile = 2 * HEAD
    for first in range(0, total_ref.shape[1], tile):
        columns = slice(first, first + tile)
        weight = jnp.concatenate([ref[:, columns] for ref in shard_refs], axis=0)
        total_ref[:, columns] = inner_total_ref[:, columns] + jnp.dot(
            left_ref[:, :depths], weight, preferred_element_type=jnp.float32
        )


def edge_project_kernel(origins, parts, *refs):
    edge_refs, their_refs, shard_refs = refs[:parts], refs[parts : 2 * parts], refs[2 * parts : -5]
    total_ref, left_ref, edge_rows, their_rows, features = refs[-5:]
    for refs, held in ((edge_refs, edge_rows), (their_refs, their_rows)):
        first = 0
        for ref in refs:
            held[:, first : first + ref.shape[1]] = ref[...]
            first += ref.shape[1]
    block, depth = left_ref.shape[0] // 2, left_ref.shape[1]
    for number, (here, there) in enumerate(shard_places(origins, depth)):
        last = number == len(origins) - 1
        ref, at = (left_ref, 0) if last else (features, number * depth)
        ref[:block, at : at + depth] = edge_rows[:, here]
        ref[block:, at : at + depth] = their_rows[:, there]
    tile = 2 * HEAD
    for first in range(0, total_ref.shape[1], tile):
        columns = slice(first, first + tile)
        weight = jnp.concatenate([ref[:, columns] for ref in shard_refs], axis=0)
        total_ref[:, columns] = jnp.dot(
            features[...], weight, preferred_element_type=jnp.float32
        )


def last_project_kernel(first, edge_ref, left_ref, inner_total_ref, edge_total_ref, *rest):
    shard_refs, (own_total_ref, their_total_ref) = rest[:-2], rest[-2:]
    block = own_total_ref.shape[0] // 2
    depth = sum(ref.shape[0] for ref in shard_refs)
    features = jnp.concatenate([left_ref[:, -depth:], edge_ref[...]], axis=0)
    tile = 2 * HEAD
    for at in range(0, own_total_ref.shape[1], tile):
        here = slice(at, at + tile)
        columns = slice(first + at, first + at + tile)
        weight = jnp.concatenate([ref[:, columns] for ref in shard_refs], axis=0)
        total = jnp.dot(features, weight, preferred_element_type=jnp.float32)
        inner = inner_total_ref[:, columns] + total[: 2 * block]
        edge = edge_total_ref[:, columns] + total[2 * block :]
        own_total_ref[:block, here] = inner[:block]
        own_total_ref[block:, here] = edge[:block]
        their_total_ref[:block, here] = inner[block:].astype(jnp.bfloat16)
        their_total_ref[block:, here] = edge[block:].astype(jnp.bfloat16)


def add_kernel(total_ref, more_ref, out_ref):
    out_ref[...] = (total_ref[...] + more_ref[...]).astype(jnp.bfloat16)


def finish_kernel(total_ref, more_ref, ready_ref, out_ref, held, sems):
    block = out_ref.shape[0] // 2
    ctx = lax.axis_index("ctx")
    ready = ready_ref.shape[1]
    blocks = [(slice(0, block), ctx), (slice(block, 2 * block), 1 - ctx)]

    def copy(source_ref, which, first, sem):
        rows, place = blocks[which]
        there = pl.ds(pl.multiple_of(place * block, block), block)
        columns = pl.ds(first, source_ref.shape[1])
        return pltpu.make_async_copy(source_ref.at[rows], out_ref.at[there, columns], sem)

    copies = [copy(ready_ref, which, 0, sems.at[which]) for which in range(2)]
    for one in copies:
        one.start()
    for which, (rows, _) in enumerate(blocks):
        held[rows] = (total_ref[rows] + more_ref[rows]).astype(jnp.bfloat16)
        copies.append(copy(held, which, ready, sems.at[2 + which]))
        copies[-1].start()
    for one in copies:
        one.wait()


SMEM = functools.partial(pl.BlockSpec, memory_space=pltpu.SMEM)
VMEM = functools.partial(pl.BlockSpec, memory_space=pltpu.VMEM)
HBM = functools.partial(pl.BlockSpec, memory_space=pltpu.HBM)


def after(value, *others):
    return lax.optimization_barrier((value, *others))[0]


def body_edge(projections, block_source, clip_ids, out_weight):
    local_rows, row_width = projections.shape
    block_rows = local_rows // 2
    heads = row_width // (3 * HEAD)
    features = heads * HEAD
    depth, width = out_weight.shape
    count = lax.axis_size("dp")
    bf16 = jnp.bfloat16

    def call(kernel, name, shape, in_specs, dtypes=None, scratch=(), out_spec=VMEM()):
        many = isinstance(shape, list)
        shapes = shape if many else [shape]
        dtypes = dtypes or [bf16] * len(shapes)
        shapes = [jax.ShapeDtypeStruct(*one) for one in zip(shapes, dtypes, strict=True)]
        return pl.pallas_call(
            kernel,
            out_shape=shapes if many else shapes[0],
            in_specs=in_specs,
            out_specs=[out_spec] * len(shapes) if many else out_spec,
            scratch_shapes=scratch,
            cost_estimate=pl.CostEstimate(flops=0, bytes_accessed=0, transcendentals=0),
            compiler_params=pltpu.CompilerParams(vmem_limit_bytes=8 * MIB),
            name=name,
        )

    def around(value, step):
        places = ring_order(count // 4)
        moves = [(here, places[(at + step) % len(places)]) for at, here in enumerate(places)]
        return lax.ppermute(
            value, "dp", [(4 * here + rest, 4 * there + rest) for here, there in moves for rest in range(4)]
        )

    def to_side(value):
        return partner(value, "dp", 1)

    def to_core(value):
        return partner(value, "dp", 0)

    own = pltpu.with_memory_space_constraint(
        projections.reshape(2, block_rows, row_width), pltpu.HBM
    )
    shards = {(0, False): [out_weight]}
    from_partner = pltpu.with_memory_space_constraint(to_core(own), pltpu.VMEM)
    ahead = around(out_weight, 1)
    across = to_side(out_weight)
    staged, facts = call(
        stage_kernel,
        "stage",
        [own.shape, (7, 8, 128)],
        [SMEM(), SMEM(), HBM()],
        dtypes=[bf16, jnp.int32],
        scratch=[pltpu.SemaphoreType.DMA((2, 4))],
    )(block_source, clip_ids, own)
    part_heads = [heads * 8 // 16, heads * 8 // 16]
    packed_first = call(
        pack_first_kernel,
        "pack_first",
        (block_rows, 2 * HEAD * part_heads[0]),
        [VMEM()] * 3,
    )(facts, staged, from_partner)
    rows, packed_last = call(
        pack_kernel,
        "pack",
        [(2, block_rows, row_width), (block_rows, 2 * HEAD * part_heads[1])],
        [VMEM()] * 3,
        scratch=[pltpu.SemaphoreType.DMA((2,))],
    )(facts, staged, after(from_partner, packed_first))
    packed = [packed_first, packed_last]
    halos = [lax.ppermute(part, "ctx", [(0, 1), (1, 0)]) for part in packed]

    def edge_rows(part, *before):
        some = part_heads[part]
        return call(
            functools.partial(edge_kernel, sum(part_heads[:part])),
            "edge_rows",
            [(block_rows, some * HEAD), (block_rows, some // 2 * HEAD)],
            [VMEM()] * 3,
        )(after(facts, *before), rows, halos[part])

    back = around(after(out_weight, staged), -1)
    ahead = after(ahead, *packed)
    shards[1, False], shards[0, True] = [ahead], [across]
    second = around(after(ahead, across), 1)
    across = to_side(ahead)
    inner, inner_other = call(
        inner_kernel,
        "inner_rows",
        [(block_rows, features), (block_rows, features // 2)],
        [VMEM()] * 2,
    )(after(facts, ahead), rows)
    theirs = [to_core(inner_other)]

    back = after(back, inner)
    shards[3, False] = [back]
    back_across = to_side(back)
    shards[1, True] = [across]
    early = list(shards)
    origins = [*early, (2, False), (3, True), (2, True)]
    inner_total, inner_left = call(
        functools.partial(inner_project_kernel, origins, len(early)),
        "inner_project",
        [(local_rows, width), (local_rows, (len(origins) - len(early)) * depth)],
        [VMEM()] * (2 + len(early)),
        dtypes=[jnp.float32, bf16],
        scratch=[pltpu.VMEM((local_rows, len(early) * depth), bf16)],
    )(inner, *theirs, *[shards[origin][0] for origin in early])
    edges, edge_others = zip(*[edge_rows(part) for part in range(len(part_heads))], strict=True)
    second = after(second, inner_total, edges[0])
    cut = depth // 8 * 5
    shards[2, False] = [second]
    shards[3, True] = [back_across]
    shards[2, True] = [around(after(across, edges[0])[:cut], 1), to_side(second[cut:])]
    theirs = [to_core(part) for part in edge_others]

    more = [shards[origin][0] for origin in origins[len(early) : -1]]
    inner_total = call(
        add_products_kernel,
        "add_products",
        inner_total.shape,
        [VMEM()] * (2 + len(more)),
        dtypes=[jnp.float32],
    )(inner_left, inner_total, *more)
    theirs[-1] = after(theirs[-1], inner_total)
    pieces = [piece for origin in origins[:-1] for piece in shards[origin]]
    edge_total, edge_left = call(
        functools.partial(edge_project_kernel, origins, len(edges)),
        "edge_project",
        [(local_rows, width), (local_rows, depth)],
        [VMEM()] * (len(edges) + len(theirs) + len(pieces)),
        dtypes=[jnp.float32, bf16],
        scratch=[
            pltpu.VMEM((block_rows, features), bf16),
            pltpu.VMEM((block_rows, features // 2), bf16),
            pltpu.VMEM((local_rows, (len(origins) - 1) * depth), bf16),
        ],
    )(*edges, *theirs, *pieces)
    sums = []
    first = 0
    for columns in (width // 3 * 2, width // 3):
        own_total, their_total = call(
            functools.partial(last_project_kernel, first),
            "last_project",
            [(local_rows, columns)] * 2,
            [VMEM()] * (4 + len(shards[origins[-1]])),
            dtypes=[jnp.float32, bf16],
        )(edge_left, inner_left, inner_total, edge_total, *shards[origins[-1]])
        sums.append((own_total, to_core(their_total)))
        first += columns
    ready = call(add_kernel, "add", sums[0][0].shape, [VMEM()] * 2)(*sums[0])
    return call(
        finish_kernel,
        "finish",
        (local_rows, width),
        [VMEM()] * 3,
        scratch=[pltpu.VMEM(sums[1][0].shape, bf16), pltpu.SemaphoreType.DMA((4,))],
        out_spec=HBM(),
    )(*sums[1], ready)


def body(projections, block_source, clip_ids, out_weight):
    heads = projections.shape[1] // (3 * HEAD)
    two_and_two = lax.axis_size("ctx") == 2 and block_source.shape[2] == 2
    whole_tiles = out_weight.shape[0] % HEAD == 0 and heads % 16 == 0
    if two_and_two and whole_tiles and lax.axis_size("dp") == 16:
        return body_edge(projections, block_source, clip_ids, out_weight)
    return body_general(projections, block_source, clip_ids, out_weight)


def solution(mesh):
    return jax.shard_map(
        body,
        mesh=mesh,
        in_specs=(P(("dp", "ctx"), None), P("dp", "ctx", None), P("dp", None), P("dp", None)),
        out_specs=P(("dp", "ctx"), None),
        check_vma=False,
    )
```

```python
import functools
import math

import jax
import jax.numpy as jnp
from jax import lax
from jax.experimental import pallas as pl
from jax.experimental.pallas import tpu as pltpu
from jax.sharding import PartitionSpec as P

HEAD = 128


big_negative = -1e30
MIB = 1 << 20


def partner(value, axis, bit):
    mask = 2**bit
    pairs = [(source, source ^ mask) for source in range(lax.axis_size(axis))]
    return lax.ppermute(value, axis, pairs)


def soft_weights(scores, allowed):
    masked = jnp.where(allowed, scores, big_negative)
    row_max = jnp.max(masked, axis=-1, keepdims=True)
    exponent = jnp.exp(masked - row_max)
    return (exponent / jnp.sum(exponent, axis=-1, keepdims=True)).astype(jnp.bfloat16)


def attend_dense(queries, key_rows, value_rows, token_clip, scaling):
    token_count, head_count, head_size = queries.shape
    step_size = min(token_count, 512)
    step_count = token_count // step_size
    query_steps = queries.reshape(step_count, step_size, head_count, head_size)
    clip_steps = token_clip.reshape(step_count, step_size)

    def one_step(arguments):
        query_block, clip_block = arguments
        scores = (
            jnp.einsum("qhe,khe->hqk", query_block, key_rows, preferred_element_type=jnp.float32)
            * scaling
        )
        allowed = (clip_block[:, None] == token_clip[None, :])[None]
        weights = soft_weights(scores, allowed)
        return jnp.einsum(
            "hqk,khe->qhe", weights, value_rows, preferred_element_type=jnp.float32
        ).astype(jnp.bfloat16)

    outputs = lax.map(one_step, (query_steps, clip_steps))
    return outputs.reshape(token_count, head_count, head_size)


def body_general(projections, block_source, clip_ids, out_weight):
    ctx_count = lax.axis_size("ctx")
    local_rows, row_width = projections.shape
    local_blocks = block_source.shape[2]
    block_rows = local_rows // local_blocks
    own_blocks = projections.reshape(local_blocks, block_rows, row_width)
    partner_blocks = partner(own_blocks, "dp", 0)
    source_ids = block_source.reshape(local_blocks)
    from_partner = source_ids // (local_blocks * ctx_count) != lax.axis_index("dp")
    chosen_slot = source_ids % local_blocks + local_blocks * from_partner.astype(jnp.int32)
    candidates = jnp.concatenate([own_blocks, partner_blocks], axis=0)
    packed = jnp.take(candidates, chosen_slot, axis=0)
    local_heads = row_width // (3 * HEAD) // ctx_count
    grouped = packed.reshape(local_rows, ctx_count, local_heads, 3 * HEAD)
    block_clip = clip_ids.reshape(-1)
    token_clip = jnp.repeat(block_clip, block_rows)
    scaling = 1.0 / math.sqrt(HEAD)
    regrouped = lax.all_to_all(grouped, "ctx", split_axis=1, concat_axis=0, tiled=True)
    token_count = regrouped.shape[0]
    item_count = regrouped.shape[2]
    features = regrouped.reshape(token_count, item_count, 3 * HEAD)
    queries = features[:, :, :HEAD]
    key_rows = features[:, :, HEAD : 2 * HEAD]
    value_rows = features[:, :, 2 * HEAD :]
    attended = attend_dense(queries, key_rows, value_rows, token_clip, scaling)
    merged = attended.reshape(local_rows * ctx_count, local_heads * HEAD)
    attention_rows = lax.all_to_all(merged, "ctx", split_axis=0, concat_axis=1, tiled=True)
    result = jnp.dot(
        attention_rows,
        lax.all_gather(out_weight, "dp", axis=0, tiled=True),
        preferred_element_type=jnp.float32,
    )
    return result.astype(jnp.bfloat16)


EDGE_AWAY, EDGE_SLOT, INNER_AWAY, INNER_SLOT, INNER_JOINS, EDGE_JOINS, CROSSES = range(7)


def stage_kernel(sources, clips, own_ref, out_ref, facts_ref, source_ref, clip_ref, few_sems, sems):
    parts = sems.shape[1]
    slots = own_ref.shape[0]
    rows = own_ref.shape[1] // parts
    copies = []
    for block in range(slots):
        for part in range(parts):
            here = (block, pl.ds(part * rows, rows))
            copies.append(
                pltpu.make_async_copy(own_ref.at[here], out_ref.at[here], sems.at[block, part])
            )
    few = [
        pltpu.make_async_copy(sources, source_ref, few_sems.at[0]),
        pltpu.make_async_copy(clips, clip_ref, few_sems.at[1]),
    ]
    for copy in few + copies:
        copy.start()
    for copy in few:
        copy.wait()
    ctx, dp = lax.axis_index("ctx"), lax.axis_index("dp")
    facts = {}
    for block, away, at in ((1 - ctx, EDGE_AWAY, EDGE_SLOT), (ctx, INNER_AWAY, INNER_SLOT)):
        source = source_ref[0, 0, block]
        facts[away] = (source // (2 * slots) != dp).astype(jnp.int32)
        facts[at] = lax.rem(source, slots)
    edge_clip = clip_ref[0, 1 + ctx]
    crosses = edge_clip == clip_ref[0, 2 - ctx]
    facts[CROSSES] = crosses.astype(jnp.int32)
    facts[EDGE_JOINS] = jnp.logical_or(crosses, edge_clip == clip_ref[0, 3 * ctx]).astype(jnp.int32)
    facts[INNER_JOINS] = (clip_ref[0, 2 * ctx] == clip_ref[0, 2 * ctx + 1]).astype(jnp.int32)
    for which, fact in facts.items():
        facts_ref[which] = jnp.full(facts_ref.shape[1:], fact, jnp.int32)
    for copy in copies:
        copy.wait()


def fact(facts_ref, which):
    return jnp.max(facts_ref[which])


def pack_first_kernel(facts_ref, own_ref, partner_ref, halo_ref):
    away, slot = fact(facts_ref, EDGE_AWAY) > 0, fact(facts_ref, EDGE_SLOT)

    def fill(ref):
        for head in range(halo_ref.shape[1] // (2 * HEAD)):
            columns = slice(head * 3 * HEAD + HEAD, (head + 1) * 3 * HEAD)
            halo_ref[:, head * 2 * HEAD : (head + 1) * 2 * HEAD] = ref[slot, :, columns]

    @pl.when(away)
    def _():
        fill(partner_ref)

    @pl.when(jnp.logical_not(away))
    def _():
        fill(own_ref)


def pack_kernel(facts_ref, own_ref, partner_ref, rows_ref, halo_ref, sems):
    for which, away, at in ((1, EDGE_AWAY, EDGE_SLOT), (0, INNER_AWAY, INNER_SLOT)):
        away, slot = fact(facts_ref, away) > 0, fact(facts_ref, at)

        @pl.when(jnp.logical_not(away))
        def _():
            pltpu.make_async_copy(own_ref.at[slot], rows_ref.at[which], sems.at[which]).start()

        @pl.when(away)
        def _():
            pltpu.make_async_copy(partner_ref.at[slot], rows_ref.at[which], sems.at[which]).start()

    pltpu.make_async_copy(own_ref.at[0], rows_ref.at[1], sems.at[1]).wait()
    heads = halo_ref.shape[1] // (2 * HEAD)
    skipped = rows_ref.shape[2] // (3 * HEAD) - heads
    for head in range(heads):
        first = (skipped + head) * 3 * HEAD + HEAD
        halo_ref[:, head * 2 * HEAD : (head + 1) * 2 * HEAD] = rows_ref[
            1, :, first : first + 2 * HEAD
        ]
    pltpu.make_async_copy(own_ref.at[0], rows_ref.at[0], sems.at[0]).wait()


def attend(heads, load_queries, load_own, load_more, allowed, out_ref, other_ref):
    scaling = math.log2(math.e) / math.sqrt(HEAD)
    contract_last = (((1,), (1,)), ((), ()))
    ones = jnp.ones((2 * out_ref.shape[0], HEAD), jnp.bfloat16)
    odd_core = lax.rem(lax.axis_index("dp"), 2) == 1
    for start in range(0, heads, 4):
        group = min(4, heads - start)
        scores = []
        for head in range(start, start + group):
            queries = load_queries(head)
            pair = []
            for loader in (load_own, load_more):
                pair.append(
                    lax.dot_general(
                        queries, loader(head, 0), contract_last, preferred_element_type=jnp.float32
                    )
                    * scaling
                )
            scores.append(pair)
        weights = []
        for own, more in scores:
            more = jnp.where(allowed, more, big_negative)
            row_max = jnp.max(jnp.maximum(own, more), axis=-1, keepdims=True)
            weights.append(
                jnp.concatenate(
                    [
                        jnp.exp2(own - row_max).astype(jnp.bfloat16),
                        jnp.exp2(more - row_max).astype(jnp.bfloat16),
                    ],
                    axis=1,
                )
            )
        outs = []
        for head in range(start, start + group):
            values = jnp.concatenate([load_own(head, 1), load_more(head, 1)], axis=0)
            sums = jnp.dot(
                weights[head - start],
                jnp.concatenate([values, ones], axis=1),
                preferred_element_type=jnp.float32,
            )
            outs.append(sums[:, :HEAD] / sums[:, HEAD:])
            out_ref[:, head * HEAD : (head + 1) * HEAD] = outs[-1].astype(jnp.bfloat16)
        for pair in range(group // 2):
            at = (start // 2 + pair) * HEAD
            other = jnp.where(odd_core, outs[2 * pair], outs[2 * pair + 1])
            other_ref[:, at : at + HEAD] = other.astype(jnp.bfloat16)


def inner_kernel(facts_ref, rows_ref, out_ref, other_ref):
    allowed = fact(facts_ref, INNER_JOINS) > 0

    def loader(block):
        def get(head, which):
            first = (head * 3 + 1 + which) * HEAD
            return rows_ref[block, :, first : first + HEAD]

        return get

    attend(
        out_ref.shape[1] // HEAD,
        lambda head: loader(0)(head, -1),
        loader(0),
        loader(1),
        allowed,
        out_ref,
        other_ref,
    )


def edge_kernel(first_head, facts_ref, rows_ref, halo_ref, out_ref, other_ref):
    crosses, allowed = fact(facts_ref, CROSSES) > 0, fact(facts_ref, EDGE_JOINS) > 0

    def load_own(head, which):
        first = ((first_head + head) * 3 + 1 + which) * HEAD
        return rows_ref[1, :, first : first + HEAD]

    def load_more(head, which):
        first = ((first_head + head) * 3 + 1 + which) * HEAD
        at = (2 * head + which) * HEAD
        return jnp.where(crosses, halo_ref[:, at : at + HEAD], rows_ref[0, :, first : first + HEAD])

    attend(
        out_ref.shape[1] // HEAD,
        lambda head: load_own(head, -1),
        load_own,
        load_more,
        allowed,
        out_ref,
        other_ref,
    )


def ring_order(lines):
    return list(range(0, lines, 2)) + list(range(1, lines, 2))[::-1]


def shard_places(origins, depth):
    index = lax.axis_index("dp")
    core, side, line = lax.rem(index, 2), lax.rem(index // 2, 2), index // 4
    places = ring_order(lax.axis_size("dp") // 4)
    found = []
    for steps, other_side in origins:
        from_line = line
        for at, place in enumerate(places):
            from_line = jnp.where(line == place, places[at - steps], from_line)
        pair = from_line * 2 + (1 - side if other_side else side)
        here = pl.ds(pl.multiple_of((pair * 2 + core) * depth, depth), depth)
        there = pl.ds(pl.multiple_of(pair * depth, depth), depth)
        found.append((here, there))
    return found


def inner_project_kernel(origins, early, inner_ref, their_ref, *rest):
    shard_refs, (total_ref, left_ref, features) = rest[:-3], rest[-3:]
    block = inner_ref.shape[0]
    depth = left_ref.shape[1] // (len(origins) - early)
    for number, (here, there) in enumerate(shard_places(origins, depth)):
        ref, at = (features, number) if number < early else (left_ref, number - early)
        ref[:block, at * depth : (at + 1) * depth] = inner_ref[:, here]
        ref[block:, at * depth : (at + 1) * depth] = their_ref[:, there]
    tile = 2 * HEAD
    for first in range(0, total_ref.shape[1], tile):
        columns = slice(first, first + tile)
        weight = jnp.concatenate([ref[:, columns] for ref in shard_refs], axis=0)
        total_ref[:, columns] = jnp.dot(
            features[...], weight, preferred_element_type=jnp.float32
        )


def add_products_kernel(left_ref, inner_total_ref, *rest):
    shard_refs, total_ref = rest[:-1], rest[-1]
    depths = sum(ref.shape[0] for ref in shard_refs)
    tile = 2 * HEAD
    for first in range(0, total_ref.shape[1], tile):
        columns = slice(first, first + tile)
        weight = jnp.concatenate([ref[:, columns] for ref in shard_refs], axis=0)
        total_ref[:, columns] = inner_total_ref[:, columns] + jnp.dot(
            left_ref[:, :depths], weight, preferred_element_type=jnp.float32
        )


def edge_project_kernel(origins, parts, *refs):
    edge_refs, their_refs, shard_refs = refs[:parts], refs[parts : 2 * parts], refs[2 * parts : -5]
    total_ref, left_ref, edge_rows, their_rows, features = refs[-5:]
    for refs, held in ((edge_refs, edge_rows), (their_refs, their_rows)):
        first = 0
        for ref in refs:
            held[:, first : first + ref.shape[1]] = ref[...]
            first += ref.shape[1]
    block, depth = left_ref.shape[0] // 2, left_ref.shape[1]
    for number, (here, there) in enumerate(shard_places(origins, depth)):
        last = number == len(origins) - 1
        ref, at = (left_ref, 0) if last else (features, number * depth)
        ref[:block, at : at + depth] = edge_rows[:, here]
        ref[block:, at : at + depth] = their_rows[:, there]
    tile = 2 * HEAD
    for first in range(0, total_ref.shape[1], tile):
        columns = slice(first, first + tile)
        weight = jnp.concatenate([ref[:, columns] for ref in shard_refs], axis=0)
        total_ref[:, columns] = jnp.dot(
            features[...], weight, preferred_element_type=jnp.float32
        )


def last_project_kernel(first, edge_ref, left_ref, inner_total_ref, edge_total_ref, *rest):
    shard_refs, (own_total_ref, their_total_ref) = rest[:-2], rest[-2:]
    block = own_total_ref.shape[0] // 2
    depth = sum(ref.shape[0] for ref in shard_refs)
    features = jnp.concatenate([left_ref[:, -depth:], edge_ref[...]], axis=0)
    tile = 2 * HEAD
    for at in range(0, own_total_ref.shape[1], tile):
        here = slice(at, at + tile)
        columns = slice(first + at, first + at + tile)
        weight = jnp.concatenate([ref[:, columns] for ref in shard_refs], axis=0)
        total = jnp.dot(features, weight, preferred_element_type=jnp.float32)
        inner = inner_total_ref[:, columns] + total[: 2 * block]
        edge = edge_total_ref[:, columns] + total[2 * block :]
        own_total_ref[:block, here] = inner[:block]
        own_total_ref[block:, here] = edge[:block]
        their_total_ref[:block, here] = inner[block:].astype(jnp.bfloat16)
        their_total_ref[block:, here] = edge[block:].astype(jnp.bfloat16)


def add_kernel(total_ref, more_ref, out_ref):
    out_ref[...] = (total_ref[...] + more_ref[...]).astype(jnp.bfloat16)


def finish_kernel(total_ref, more_ref, ready_ref, out_ref, held, sems):
    block = out_ref.shape[0] // 2
    ctx = lax.axis_index("ctx")
    ready = ready_ref.shape[1]
    blocks = [(slice(0, block), ctx), (slice(block, 2 * block), 1 - ctx)]

    def copy(source_ref, which, first, sem):
        rows, place = blocks[which]
        there = pl.ds(pl.multiple_of(place * block, block), block)
        columns = pl.ds(first, source_ref.shape[1])
        return pltpu.make_async_copy(source_ref.at[rows], out_ref.at[there, columns], sem)

    copies = [copy(ready_ref, which, 0, sems.at[which]) for which in range(2)]
    for one in copies:
        one.start()
    for which, (rows, _) in enumerate(blocks):
        held[rows] = (total_ref[rows] + more_ref[rows]).astype(jnp.bfloat16)
        copies.append(copy(held, which, ready, sems.at[2 + which]))
        copies[-1].start()
    for one in copies:
        one.wait()


SMEM = functools.partial(pl.BlockSpec, memory_space=pltpu.SMEM)
VMEM = functools.partial(pl.BlockSpec, memory_space=pltpu.VMEM)
HBM = functools.partial(pl.BlockSpec, memory_space=pltpu.HBM)


def after(value, *others):
    return lax.optimization_barrier((value, *others))[0]


def body_edge(projections, block_source, clip_ids, out_weight):
    local_rows, row_width = projections.shape
    block_rows = local_rows // 2
    heads = row_width // (3 * HEAD)
    features = heads * HEAD
    depth, width = out_weight.shape
    count = lax.axis_size("dp")
    bf16 = jnp.bfloat16

    def call(kernel, name, shape, in_specs, dtypes=None, scratch=(), out_spec=VMEM()):
        many = isinstance(shape, list)
        shapes = shape if many else [shape]
        dtypes = dtypes or [bf16] * len(shapes)
        shapes = [jax.ShapeDtypeStruct(*one) for one in zip(shapes, dtypes, strict=True)]
        return pl.pallas_call(
            kernel,
            out_shape=shapes if many else shapes[0],
            in_specs=in_specs,
            out_specs=[out_spec] * len(shapes) if many else out_spec,
            scratch_shapes=scratch,
            cost_estimate=pl.CostEstimate(flops=0, bytes_accessed=0, transcendentals=0),
            compiler_params=pltpu.CompilerParams(vmem_limit_bytes=8 * MIB),
            name=name,
        )

    def around(value, step):
        places = ring_order(count // 4)
        moves = [(here, places[(at + step) % len(places)]) for at, here in enumerate(places)]
        return lax.ppermute(
            value, "dp", [(4 * here + rest, 4 * there + rest) for here, there in moves for rest in range(4)]
        )

    def to_side(value):
        return partner(value, "dp", 1)

    def to_core(value):
        return partner(value, "dp", 0)

    def in_hbm(value):
        return pltpu.with_memory_space_constraint(value, pltpu.HBM)

    own = in_hbm(projections.reshape(2, block_rows, row_width))
    shards = {(0, False): [out_weight]}
    from_partner = pltpu.with_memory_space_constraint(to_core(own), pltpu.VMEM)
    ahead = around(out_weight, 1)
    across = to_side(out_weight)
    staged, facts = call(
        stage_kernel,
        "stage",
        [own.shape, (7, 8, 128)],
        [HBM()] * 3,
        dtypes=[bf16, jnp.int32],
        scratch=[
            pltpu.SMEM(block_source.shape, jnp.int32),
            pltpu.SMEM(clip_ids.shape, jnp.int32),
            pltpu.SemaphoreType.DMA((2,)),
            pltpu.SemaphoreType.DMA((2, 4)),
        ],
    )(in_hbm(block_source), in_hbm(clip_ids), own)
    part_heads = [heads * 8 // 16, heads * 8 // 16]
    packed_first = call(
        pack_first_kernel,
        "pack_first",
        (block_rows, 2 * HEAD * part_heads[0]),
        [VMEM()] * 3,
    )(facts, staged, from_partner)
    rows, packed_last = call(
        pack_kernel,
        "pack",
        [(2, block_rows, row_width), (block_rows, 2 * HEAD * part_heads[1])],
        [VMEM()] * 3,
        scratch=[pltpu.SemaphoreType.DMA((2,))],
    )(facts, staged, after(from_partner, packed_first))
    packed = [packed_first, packed_last]
    halos = [lax.ppermute(part, "ctx", [(0, 1), (1, 0)]) for part in packed]

    def edge_rows(part, *before):
        some = part_heads[part]
        return call(
            functools.partial(edge_kernel, sum(part_heads[:part])),
            "edge_rows",
            [(block_rows, some * HEAD), (block_rows, some // 2 * HEAD)],
            [VMEM()] * 3,
        )(after(facts, *before), rows, halos[part])

    back = around(after(out_weight, staged), -1)
    ahead = after(ahead, *packed)
    shards[1, False], shards[0, True] = [ahead], [across]
    second = around(after(ahead, across), 1)
    across = to_side(ahead)
    inner, inner_other = call(
        inner_kernel,
        "inner_rows",
        [(block_rows, features), (block_rows, features // 2)],
        [VMEM()] * 2,
    )(after(facts, ahead), rows)
    theirs = [to_core(inner_other)]

    back = after(back, inner)
    shards[3, False] = [back]
    back_across = to_side(back)
    shards[1, True] = [across]
    early = list(shards)
    origins = [*early, (2, False), (3, True), (2, True)]
    inner_total, inner_left = call(
        functools.partial(inner_project_kernel, origins, len(early)),
        "inner_project",
        [(local_rows, width), (local_rows, (len(origins) - len(early)) * depth)],
        [VMEM()] * (2 + len(early)),
        dtypes=[jnp.float32, bf16],
        scratch=[pltpu.VMEM((local_rows, len(early) * depth), bf16)],
    )(inner, *theirs, *[shards[origin][0] for origin in early])
    edges, edge_others = zip(*[edge_rows(part) for part in range(len(part_heads))], strict=True)
    second = after(second, inner_total, edges[0])
    cut = depth // 8 * 5
    shards[2, False] = [second]
    shards[3, True] = [back_across]
    shards[2, True] = [around(after(across, edges[0])[:cut], 1), to_side(second[cut:])]
    theirs = [to_core(part) for part in edge_others]

    more = [shards[origin][0] for origin in origins[len(early) : -1]]
    inner_total = call(
        add_products_kernel,
        "add_products",
        inner_total.shape,
        [VMEM()] * (2 + len(more)),
        dtypes=[jnp.float32],
    )(inner_left, inner_total, *more)
    theirs[-1] = after(theirs[-1], inner_total)
    pieces = [piece for origin in origins[:-1] for piece in shards[origin]]
    edge_total, edge_left = call(
        functools.partial(edge_project_kernel, origins, len(edges)),
        "edge_project",
        [(local_rows, width), (local_rows, depth)],
        [VMEM()] * (len(edges) + len(theirs) + len(pieces)),
        dtypes=[jnp.float32, bf16],
        scratch=[
            pltpu.VMEM((block_rows, features), bf16),
            pltpu.VMEM((block_rows, features // 2), bf16),
            pltpu.VMEM((local_rows, (len(origins) - 1) * depth), bf16),
        ],
    )(*edges, *theirs, *pieces)
    sums = []
    first = 0
    for columns in (width // 3 * 2, width // 3):
        own_total, their_total = call(
            functools.partial(last_project_kernel, first),
            "last_project",
            [(local_rows, columns)] * 2,
            [VMEM()] * (4 + len(shards[origins[-1]])),
            dtypes=[jnp.float32, bf16],
        )(edge_left, inner_left, inner_total, edge_total, *shards[origins[-1]])
        sums.append((own_total, to_core(their_total)))
        first += columns
    ready = call(add_kernel, "add", sums[0][0].shape, [VMEM()] * 2)(*sums[0])
    return call(
        finish_kernel,
        "finish",
        (local_rows, width),
        [VMEM()] * 3,
        scratch=[pltpu.VMEM(sums[1][0].shape, bf16), pltpu.SemaphoreType.DMA((4,))],
        out_spec=HBM(),
    )(*sums[1], ready)


def body(projections, block_source, clip_ids, out_weight):
    heads = projections.shape[1] // (3 * HEAD)
    two_and_two = lax.axis_size("ctx") == 2 and block_source.shape[2] == 2
    whole_tiles = out_weight.shape[0] % HEAD == 0 and heads % 16 == 0
    if two_and_two and whole_tiles and lax.axis_size("dp") == 16:
        return body_edge(projections, block_source, clip_ids, out_weight)
    return body_general(projections, block_source, clip_ids, out_weight)


def solution(mesh):
    return jax.shard_map(
        body,
        mesh=mesh,
        in_specs=(P(("dp", "ctx"), None), P("dp", "ctx", None), P("dp", None), P("dp", None)),
        out_specs=P(("dp", "ctx"), None),
        check_vma=False,
    )
```

```python
import functools
import math

import jax
import jax.numpy as jnp
from jax import lax
from jax.experimental import pallas as pl
from jax.experimental.pallas import tpu as pltpu
from jax.sharding import PartitionSpec as P

HEAD = 128


big_negative = -1e30
MIB = 1 << 20


def partner(value, axis, bit):
    mask = 2**bit
    pairs = [(source, source ^ mask) for source in range(lax.axis_size(axis))]
    return lax.ppermute(value, axis, pairs)


def soft_weights(scores, allowed):
    masked = jnp.where(allowed, scores, big_negative)
    row_max = jnp.max(masked, axis=-1, keepdims=True)
    exponent = jnp.exp(masked - row_max)
    return (exponent / jnp.sum(exponent, axis=-1, keepdims=True)).astype(jnp.bfloat16)


def attend_dense(queries, key_rows, value_rows, token_clip, scaling):
    token_count, head_count, head_size = queries.shape
    step_size = min(token_count, 512)
    step_count = token_count // step_size
    query_steps = queries.reshape(step_count, step_size, head_count, head_size)
    clip_steps = token_clip.reshape(step_count, step_size)

    def one_step(arguments):
        query_block, clip_block = arguments
        scores = (
            jnp.einsum("qhe,khe->hqk", query_block, key_rows, preferred_element_type=jnp.float32)
            * scaling
        )
        allowed = (clip_block[:, None] == token_clip[None, :])[None]
        weights = soft_weights(scores, allowed)
        return jnp.einsum(
            "hqk,khe->qhe", weights, value_rows, preferred_element_type=jnp.float32
        ).astype(jnp.bfloat16)

    outputs = lax.map(one_step, (query_steps, clip_steps))
    return outputs.reshape(token_count, head_count, head_size)


def body_general(projections, block_source, clip_ids, out_weight):
    ctx_count = lax.axis_size("ctx")
    local_rows, row_width = projections.shape
    local_blocks = block_source.shape[2]
    block_rows = local_rows // local_blocks
    own_blocks = projections.reshape(local_blocks, block_rows, row_width)
    partner_blocks = partner(own_blocks, "dp", 0)
    source_ids = block_source.reshape(local_blocks)
    from_partner = source_ids // (local_blocks * ctx_count) != lax.axis_index("dp")
    chosen_slot = source_ids % local_blocks + local_blocks * from_partner.astype(jnp.int32)
    candidates = jnp.concatenate([own_blocks, partner_blocks], axis=0)
    packed = jnp.take(candidates, chosen_slot, axis=0)
    local_heads = row_width // (3 * HEAD) // ctx_count
    grouped = packed.reshape(local_rows, ctx_count, local_heads, 3 * HEAD)
    block_clip = clip_ids.reshape(-1)
    token_clip = jnp.repeat(block_clip, block_rows)
    scaling = 1.0 / math.sqrt(HEAD)
    regrouped = lax.all_to_all(grouped, "ctx", split_axis=1, concat_axis=0, tiled=True)
    token_count = regrouped.shape[0]
    item_count = regrouped.shape[2]
    features = regrouped.reshape(token_count, item_count, 3 * HEAD)
    queries = features[:, :, :HEAD]
    key_rows = features[:, :, HEAD : 2 * HEAD]
    value_rows = features[:, :, 2 * HEAD :]
    attended = attend_dense(queries, key_rows, value_rows, token_clip, scaling)
    merged = attended.reshape(local_rows * ctx_count, local_heads * HEAD)
    attention_rows = lax.all_to_all(merged, "ctx", split_axis=0, concat_axis=1, tiled=True)
    result = jnp.dot(
        attention_rows,
        lax.all_gather(out_weight, "dp", axis=0, tiled=True),
        preferred_element_type=jnp.float32,
    )
    return result.astype(jnp.bfloat16)


EDGE_AWAY, EDGE_SLOT, INNER_AWAY, INNER_SLOT, INNER_JOINS, EDGE_JOINS, CROSSES = range(7)


def stage_kernel(sources, clips, own_ref, out_ref, facts_ref, source_ref, clip_ref, few_sems, sems):
    parts = sems.shape[1]
    slots = own_ref.shape[0]
    rows = own_ref.shape[1] // parts
    copies = []
    for block in range(slots):
        for part in range(parts):
            here = (block, pl.ds(part * rows, rows))
            copies.append(
                pltpu.make_async_copy(own_ref.at[here], out_ref.at[here], sems.at[block, part])
            )
    few = [
        pltpu.make_async_copy(sources, source_ref, few_sems.at[0]),
        pltpu.make_async_copy(clips, clip_ref, few_sems.at[1]),
    ]
    for copy in few + copies:
        copy.start()
    for copy in few:
        copy.wait()
    ctx, dp = lax.axis_index("ctx"), lax.axis_index("dp")
    facts = {}
    for block, away, at in ((1 - ctx, EDGE_AWAY, EDGE_SLOT), (ctx, INNER_AWAY, INNER_SLOT)):
        source = source_ref[0, 0, block]
        facts[away] = (source // (2 * slots) != dp).astype(jnp.int32)
        facts[at] = lax.rem(source, slots)
    edge_clip = clip_ref[0, 1 + ctx]
    crosses = edge_clip == clip_ref[0, 2 - ctx]
    facts[CROSSES] = crosses.astype(jnp.int32)
    facts[EDGE_JOINS] = jnp.logical_or(crosses, edge_clip == clip_ref[0, 3 * ctx]).astype(jnp.int32)
    facts[INNER_JOINS] = (clip_ref[0, 2 * ctx] == clip_ref[0, 2 * ctx + 1]).astype(jnp.int32)
    for which, fact in facts.items():
        facts_ref[which] = jnp.full(facts_ref.shape[1:], fact, jnp.int32)
    for copy in copies:
        copy.wait()


def fact(facts_ref, which):
    return jnp.max(facts_ref[which])


def pack_first_kernel(facts_ref, own_ref, partner_ref, halo_ref):
    away, slot = fact(facts_ref, EDGE_AWAY) > 0, fact(facts_ref, EDGE_SLOT)

    def fill(ref):
        for head in range(halo_ref.shape[1] // (2 * HEAD)):
            columns = slice(head * 3 * HEAD + HEAD, (head + 1) * 3 * HEAD)
            halo_ref[:, head * 2 * HEAD : (head + 1) * 2 * HEAD] = ref[slot, :, columns]

    @pl.when(away)
    def _():
        fill(partner_ref)

    @pl.when(jnp.logical_not(away))
    def _():
        fill(own_ref)


def pack_kernel(facts_ref, own_ref, partner_ref, rows_ref, halo_ref, sems):
    for which, away, at in ((1, EDGE_AWAY, EDGE_SLOT), (0, INNER_AWAY, INNER_SLOT)):
        away, slot = fact(facts_ref, away) > 0, fact(facts_ref, at)

        @pl.when(jnp.logical_not(away))
        def _():
            pltpu.make_async_copy(own_ref.at[slot], rows_ref.at[which], sems.at[which]).start()

        @pl.when(away)
        def _():
            pltpu.make_async_copy(partner_ref.at[slot], rows_ref.at[which], sems.at[which]).start()

    pltpu.make_async_copy(own_ref.at[0], rows_ref.at[1], sems.at[1]).wait()
    heads = halo_ref.shape[1] // (2 * HEAD)
    skipped = rows_ref.shape[2] // (3 * HEAD) - heads
    for head in range(heads):
        first = (skipped + head) * 3 * HEAD + HEAD
        halo_ref[:, head * 2 * HEAD : (head + 1) * 2 * HEAD] = rows_ref[
            1, :, first : first + 2 * HEAD
        ]
    pltpu.make_async_copy(own_ref.at[0], rows_ref.at[0], sems.at[0]).wait()


def attend(heads, load_queries, load_own, load_more, allowed, out_ref, other_ref):
    scaling = math.log2(math.e) / math.sqrt(HEAD)
    contract_last = (((1,), (1,)), ((), ()))
    ones = jnp.ones((2 * out_ref.shape[0], HEAD), jnp.bfloat16)
    odd_core = lax.rem(lax.axis_index("dp"), 2) == 1
    for start in range(0, heads, 4):
        group = min(4, heads - start)
        scores = []
        for head in range(start, start + group):
            queries = load_queries(head)
            pair = []
            for loader in (load_own, load_more):
                pair.append(
                    lax.dot_general(
                        queries, loader(head, 0), contract_last, preferred_element_type=jnp.float32
                    )
                    * scaling
                )
            scores.append(pair)
        weights = []
        for own, more in scores:
            more = jnp.where(allowed, more, big_negative)
            row_max = jnp.max(jnp.maximum(own, more), axis=-1, keepdims=True)
            weights.append(
                jnp.concatenate(
                    [
                        jnp.exp2(own - row_max).astype(jnp.bfloat16),
                        jnp.exp2(more - row_max).astype(jnp.bfloat16),
                    ],
                    axis=1,
                )
            )
        outs = []
        for head in range(start, start + group):
            values = jnp.concatenate([load_own(head, 1), load_more(head, 1)], axis=0)
            sums = jnp.dot(
                weights[head - start],
                jnp.concatenate([values, ones], axis=1),
                preferred_element_type=jnp.float32,
            )
            outs.append(sums[:, :HEAD] / sums[:, HEAD:])
            out_ref[:, head * HEAD : (head + 1) * HEAD] = outs[-1].astype(jnp.bfloat16)
        for pair in range(group // 2):
            at = (start // 2 + pair) * HEAD
            other = jnp.where(odd_core, outs[2 * pair], outs[2 * pair + 1])
            other_ref[:, at : at + HEAD] = other.astype(jnp.bfloat16)


def inner_kernel(facts_ref, rows_ref, out_ref, other_ref):
    allowed = fact(facts_ref, INNER_JOINS) > 0

    def loader(block):
        def get(head, which):
            first = (head * 3 + 1 + which) * HEAD
            return rows_ref[block, :, first : first + HEAD]

        return get

    attend(
        out_ref.shape[1] // HEAD,
        lambda head: loader(0)(head, -1),
        loader(0),
        loader(1),
        allowed,
        out_ref,
        other_ref,
    )


def edge_kernel(first_head, facts_ref, rows_ref, halo_ref, out_ref, other_ref):
    crosses, allowed = fact(facts_ref, CROSSES) > 0, fact(facts_ref, EDGE_JOINS) > 0

    def load_own(head, which):
        first = ((first_head + head) * 3 + 1 + which) * HEAD
        return rows_ref[1, :, first : first + HEAD]

    def load_more(head, which):
        first = ((first_head + head) * 3 + 1 + which) * HEAD
        at = (2 * head + which) * HEAD
        return jnp.where(crosses, halo_ref[:, at : at + HEAD], rows_ref[0, :, first : first + HEAD])

    attend(
        out_ref.shape[1] // HEAD,
        lambda head: load_own(head, -1),
        load_own,
        load_more,
        allowed,
        out_ref,
        other_ref,
    )


def ring_order(lines):
    return list(range(0, lines, 2)) + list(range(1, lines, 2))[::-1]


def shard_places(origins, depth):
    index = lax.axis_index("dp")
    core, side, line = lax.rem(index, 2), lax.rem(index // 2, 2), index // 4
    places = ring_order(lax.axis_size("dp") // 4)
    found = []
    for steps, other_side in origins:
        from_line = line
        for at, place in enumerate(places):
            from_line = jnp.where(line == place, places[at - steps], from_line)
        pair = from_line * 2 + (1 - side if other_side else side)
        columns = [pair * 2 + core, pair * 2 + 1 - core, pair]
        found.append([pl.ds(pl.multiple_of(column * depth, depth), depth) for column in columns])
    return found


def inner_project_kernel(origins, early, inner_ref, their_ref, *rest):
    shard_refs, (total_ref, left_ref, features) = rest[:-3], rest[-3:]
    block = inner_ref.shape[0]
    depth = left_ref.shape[1] // (len(origins) - early)
    for number, (here, _, there) in enumerate(shard_places(origins, depth)):
        ref, at = (features, number) if number < early else (left_ref, number - early)
        ref[:block, at * depth : (at + 1) * depth] = inner_ref[:, here]
        ref[block:, at * depth : (at + 1) * depth] = their_ref[:, there]
    tile = 2 * HEAD
    for first in range(0, total_ref.shape[1], tile):
        columns = slice(first, first + tile)
        weight = jnp.concatenate([ref[:, columns] for ref in shard_refs], axis=0)
        total_ref[:, columns] = jnp.dot(
            features[...], weight, preferred_element_type=jnp.float32
        )


def add_products_kernel(left_ref, inner_total_ref, *rest):
    shard_refs, total_ref = rest[:-1], rest[-1]
    tile = 2 * HEAD
    for first in range(0, total_ref.shape[1], tile):
        columns = slice(first, first + tile)
        weight = jnp.concatenate([ref[:, columns] for ref in shard_refs], axis=0)
        total_ref[:, columns] = inner_total_ref[:, columns] + jnp.dot(
            left_ref[...], weight, preferred_element_type=jnp.float32
        )


def arrange_kernel(origins, parts, inner_ref, *refs):
    edge_refs, their_refs = refs[:parts], refs[parts : 2 * parts]
    out_ref, last_ref, edge_rows, their_rows = refs[2 * parts :]
    for some_refs, held in ((edge_refs, edge_rows), (their_refs, their_rows)):
        first = 0
        for ref in some_refs:
            held[:, first : first + ref.shape[1]] = ref[...]
            first += ref.shape[1]
    block, depth = last_ref.shape[0] // 2, last_ref.shape[1] // 2
    places = shard_places(origins, depth)
    for number, (here, _, there) in enumerate(places[:-1]):
        at = slice(number * depth, (number + 1) * depth)
        out_ref[:block, at] = edge_rows[:, here]
        out_ref[block:, at] = their_rows[:, there]
    for number, here in enumerate(places[-1][:2]):
        at = slice(number * depth, (number + 1) * depth)
        last_ref[:block, at] = inner_ref[:, here]
        last_ref[block:, at] = edge_rows[:, here]


def project_kernel(first, edge_ref, inner_total_ref, *rest):
    shard_refs, (own_total_ref, their_total_ref) = rest[:-2], rest[-2:]
    block = own_total_ref.shape[0] // 2
    tile = 2 * HEAD
    for at in range(0, own_total_ref.shape[1], tile):
        here = slice(at, at + tile)
        columns = slice(first + at, first + at + tile)
        weight = jnp.concatenate([ref[:, columns] for ref in shard_refs], axis=0)
        edge = jnp.dot(edge_ref[...], weight, preferred_element_type=jnp.float32)
        own_total_ref[:block, here] = inner_total_ref[:block, columns]
        own_total_ref[block:, here] = edge[:block]
        their_total_ref[:block, here] = inner_total_ref[block:, columns].astype(jnp.bfloat16)
        their_total_ref[block:, here] = edge[block:].astype(jnp.bfloat16)


def last_project_kernel(features_ref, *rest):
    shard_refs, total_refs, out_ref = rest[:4], rest[4:-1], rest[-1]
    first = 0
    for total_ref in total_refs:
        columns = slice(first, first + total_ref.shape[1])
        weight = jnp.concatenate([ref[:, columns] for ref in shard_refs], axis=0)
        out_ref[:, columns] = total_ref[...] + jnp.dot(
            features_ref[...], weight, preferred_element_type=jnp.float32
        )
        first += total_ref.shape[1]


def finish_kernel(total_ref, *rest):
    more_refs, (out_ref, held, sems) = rest[:-3], rest[-3:]
    block = out_ref.shape[0] // 2
    ctx = lax.axis_index("ctx")
    copies = []
    for which, place in ((0, ctx), (1, 1 - ctx)):
        rows = slice(which * block, (which + 1) * block)
        first = 0
        for more_ref in more_refs:
            columns = slice(first, first + more_ref.shape[1])
            held[rows, columns] = (total_ref[rows, columns] + more_ref[rows]).astype(jnp.bfloat16)
            first += more_ref.shape[1]
        target = out_ref.at[pl.ds(pl.multiple_of(place * block, block), block)]
        copies.append(pltpu.make_async_copy(held.at[rows], target, sems.at[which]))
        copies[-1].start()
    for copy in copies:
        copy.wait()


SMEM = functools.partial(pl.BlockSpec, memory_space=pltpu.SMEM)
VMEM = functools.partial(pl.BlockSpec, memory_space=pltpu.VMEM)
HBM = functools.partial(pl.BlockSpec, memory_space=pltpu.HBM)


def after(value, *others):
    return lax.optimization_barrier((value, *others))[0]


def body_edge(projections, block_source, clip_ids, out_weight):
    local_rows, row_width = projections.shape
    block_rows = local_rows // 2
    heads = row_width // (3 * HEAD)
    features = heads * HEAD
    depth, width = out_weight.shape
    count = lax.axis_size("dp")
    bf16 = jnp.bfloat16

    def call(kernel, name, shape, in_specs, dtypes=None, scratch=(), out_spec=VMEM()):
        many = isinstance(shape, list)
        shapes = shape if many else [shape]
        dtypes = dtypes or [bf16] * len(shapes)
        shapes = [jax.ShapeDtypeStruct(*one) for one in zip(shapes, dtypes, strict=True)]
        return pl.pallas_call(
            kernel,
            out_shape=shapes if many else shapes[0],
            in_specs=in_specs,
            out_specs=[out_spec] * len(shapes) if many else out_spec,
            scratch_shapes=scratch,
            cost_estimate=pl.CostEstimate(flops=0, bytes_accessed=0, transcendentals=0),
            compiler_params=pltpu.CompilerParams(vmem_limit_bytes=8 * MIB),
            name=name,
        )

    def around(value, step):
        places = ring_order(count // 4)
        moves = [(here, places[(at + step) % len(places)]) for at, here in enumerate(places)]
        return lax.ppermute(
            value, "dp", [(4 * here + rest, 4 * there + rest) for here, there in moves for rest in range(4)]
        )

    def to_side(value):
        return partner(value, "dp", 1)

    def to_core(value):
        return partner(value, "dp", 0)

    def in_hbm(value):
        return pltpu.with_memory_space_constraint(value, pltpu.HBM)

    own = in_hbm(projections.reshape(2, block_rows, row_width))
    shards = {(0, False): [out_weight]}
    from_partner = pltpu.with_memory_space_constraint(to_core(own), pltpu.VMEM)
    ahead = around(out_weight, 1)
    across = to_side(out_weight)
    staged, facts = call(
        stage_kernel,
        "stage",
        [own.shape, (7, 8, 128)],
        [HBM()] * 3,
        dtypes=[bf16, jnp.int32],
        scratch=[
            pltpu.SMEM(block_source.shape, jnp.int32),
            pltpu.SMEM(clip_ids.shape, jnp.int32),
            pltpu.SemaphoreType.DMA((2,)),
            pltpu.SemaphoreType.DMA((2, 4)),
        ],
    )(in_hbm(block_source), in_hbm(clip_ids), own)
    part_heads = [heads * 8 // 16, heads * 8 // 16]
    packed_first = call(
        pack_first_kernel,
        "pack_first",
        (block_rows, 2 * HEAD * part_heads[0]),
        [VMEM()] * 3,
    )(facts, staged, from_partner)
    rows, packed_last = call(
        pack_kernel,
        "pack",
        [(2, block_rows, row_width), (block_rows, 2 * HEAD * part_heads[1])],
        [VMEM()] * 3,
        scratch=[pltpu.SemaphoreType.DMA((2,))],
    )(facts, staged, after(from_partner, packed_first))
    packed = [packed_first, packed_last]
    halos = [lax.ppermute(part, "ctx", [(0, 1), (1, 0)]) for part in packed]

    def edge_rows(part, *before):
        some = part_heads[part]
        return call(
            functools.partial(edge_kernel, sum(part_heads[:part])),
            "edge_rows",
            [(block_rows, some * HEAD), (block_rows, some // 2 * HEAD)],
            [VMEM()] * 3,
        )(after(facts, *before), rows, halos[part])

    back = around(after(out_weight, staged), -1)
    ahead = after(ahead, *packed)
    shards[1, False], shards[0, True] = [ahead], [across]
    second = around(after(ahead, across), 1)
    across = to_side(ahead)
    inner, inner_other = call(
        inner_kernel,
        "inner_rows",
        [(block_rows, features), (block_rows, features // 2)],
        [VMEM()] * 2,
    )(after(facts, ahead), rows)
    theirs = [to_core(inner_other)]

    back = after(back, inner)
    shards[3, False] = [back]
    back_across = to_side(back)
    shards[1, True] = [across]
    early = list(shards)
    origins = [*early, (2, False), (3, True), (2, True)]
    inner_total, inner_left = call(
        functools.partial(inner_project_kernel, origins[:-1], len(early)),
        "inner_project",
        [(local_rows, width), (local_rows, (len(origins) - 1 - len(early)) * depth)],
        [VMEM()] * (2 + len(early)),
        dtypes=[jnp.float32, bf16],
        scratch=[pltpu.VMEM((local_rows, len(early) * depth), bf16)],
    )(inner, *theirs, *[shards[origin][0] for origin in early])
    edges, edge_others = zip(*[edge_rows(part) for part in range(len(part_heads))], strict=True)
    second = after(second, inner_total, edges[0])
    cut = depth // 8 * 5
    shards[2, False] = [second]
    shards[3, True] = [back_across]
    shards[2, True] = [around(after(across, edges[0])[:cut], 1), to_side(second[cut:])]
    theirs = [to_core(part) for part in edge_others]

    more = [shards[origin][0] for origin in origins[len(early) : -1]]
    inner_total = call(
        add_products_kernel,
        "add_products",
        inner_total.shape,
        [VMEM()] * (2 + len(more)),
        dtypes=[jnp.float32],
    )(inner_left, inner_total, *more)
    theirs[-1] = after(theirs[-1], inner_total)
    arranged, last_features = call(
        functools.partial(arrange_kernel, origins, len(edges)),
        "arrange",
        [(local_rows, (len(origins) - 1) * depth), (local_rows, 2 * depth)],
        [VMEM()] * (1 + len(edges) + len(theirs)),
        scratch=[
            pltpu.VMEM((block_rows, features), bf16),
            pltpu.VMEM((block_rows, features // 2), bf16),
        ],
    )(inner, *edges, *theirs)
    last = shards[origins[-1]]
    last_swapped = [to_core(piece) for piece in last]
    pieces = [piece for origin in origins[:-1] for piece in shards[origin]]
    own_totals, mores = [], []
    parts = 3
    for part in range(parts):
        columns = width // parts
        own_total, their_total = call(
            functools.partial(project_kernel, part * columns),
            "project",
            [(local_rows, columns)] * 2,
            [VMEM()] * (2 + len(pieces)),
            dtypes=[jnp.float32, bf16],
        )(arranged, inner_total, *pieces)
        own_totals.append(own_total)
        if part == parts - 1:
            their_total = after(their_total, *last)
        mores.append(to_core(their_total))
    total = call(
        last_project_kernel,
        "last_project",
        (local_rows, width),
        [VMEM()] * (1 + 2 * len(last) + parts),
        dtypes=[jnp.float32],
    )(last_features, *last, *last_swapped, *own_totals)
    return call(
        finish_kernel,
        "finish",
        (local_rows, width),
        [VMEM()] * (1 + parts),
        scratch=[pltpu.VMEM((local_rows, width), bf16), pltpu.SemaphoreType.DMA((2,))],
        out_spec=HBM(),
    )(total, *mores)


def body(projections, block_source, clip_ids, out_weight):
    heads = projections.shape[1] // (3 * HEAD)
    two_and_two = lax.axis_size("ctx") == 2 and block_source.shape[2] == 2
    whole_tiles = out_weight.shape[0] % HEAD == 0 and heads % 16 == 0
    if two_and_two and whole_tiles and lax.axis_size("dp") == 16:
        return body_edge(projections, block_source, clip_ids, out_weight)
    return body_general(projections, block_source, clip_ids, out_weight)


def solution(mesh):
    return jax.shard_map(
        body,
        mesh=mesh,
        in_specs=(P(("dp", "ctx"), None), P("dp", "ctx", None), P("dp", None), P("dp", None)),
        out_specs=P(("dp", "ctx"), None),
        check_vma=False,
    )
```

```python
import functools
import math

import jax
import jax.numpy as jnp
from jax import lax
from jax.experimental import pallas as pl
from jax.experimental.pallas import tpu as pltpu
from jax.sharding import PartitionSpec as P

HEAD = 128


big_negative = -1e30
MIB = 1 << 20


def partner(value, axis, bit):
    mask = 2**bit
    pairs = [(source, source ^ mask) for source in range(lax.axis_size(axis))]
    return lax.ppermute(value, axis, pairs)


def soft_weights(scores, allowed):
    masked = jnp.where(allowed, scores, big_negative)
    row_max = jnp.max(masked, axis=-1, keepdims=True)
    exponent = jnp.exp(masked - row_max)
    return (exponent / jnp.sum(exponent, axis=-1, keepdims=True)).astype(jnp.bfloat16)


def attend_dense(queries, key_rows, value_rows, token_clip, scaling):
    token_count, head_count, head_size = queries.shape
    step_size = min(token_count, 512)
    step_count = token_count // step_size
    query_steps = queries.reshape(step_count, step_size, head_count, head_size)
    clip_steps = token_clip.reshape(step_count, step_size)

    def one_step(arguments):
        query_block, clip_block = arguments
        scores = (
            jnp.einsum("qhe,khe->hqk", query_block, key_rows, preferred_element_type=jnp.float32)
            * scaling
        )
        allowed = (clip_block[:, None] == token_clip[None, :])[None]
        weights = soft_weights(scores, allowed)
        return jnp.einsum(
            "hqk,khe->qhe", weights, value_rows, preferred_element_type=jnp.float32
        ).astype(jnp.bfloat16)

    outputs = lax.map(one_step, (query_steps, clip_steps))
    return outputs.reshape(token_count, head_count, head_size)


def body_general(projections, block_source, clip_ids, out_weight):
    ctx_count = lax.axis_size("ctx")
    local_rows, row_width = projections.shape
    local_blocks = block_source.shape[2]
    block_rows = local_rows // local_blocks
    own_blocks = projections.reshape(local_blocks, block_rows, row_width)
    partner_blocks = partner(own_blocks, "dp", 0)
    source_ids = block_source.reshape(local_blocks)
    from_partner = source_ids // (local_blocks * ctx_count) != lax.axis_index("dp")
    chosen_slot = source_ids % local_blocks + local_blocks * from_partner.astype(jnp.int32)
    candidates = jnp.concatenate([own_blocks, partner_blocks], axis=0)
    packed = jnp.take(candidates, chosen_slot, axis=0)
    local_heads = row_width // (3 * HEAD) // ctx_count
    grouped = packed.reshape(local_rows, ctx_count, local_heads, 3 * HEAD)
    block_clip = clip_ids.reshape(-1)
    token_clip = jnp.repeat(block_clip, block_rows)
    scaling = 1.0 / math.sqrt(HEAD)
    regrouped = lax.all_to_all(grouped, "ctx", split_axis=1, concat_axis=0, tiled=True)
    token_count = regrouped.shape[0]
    item_count = regrouped.shape[2]
    features = regrouped.reshape(token_count, item_count, 3 * HEAD)
    queries = features[:, :, :HEAD]
    key_rows = features[:, :, HEAD : 2 * HEAD]
    value_rows = features[:, :, 2 * HEAD :]
    attended = attend_dense(queries, key_rows, value_rows, token_clip, scaling)
    merged = attended.reshape(local_rows * ctx_count, local_heads * HEAD)
    attention_rows = lax.all_to_all(merged, "ctx", split_axis=0, concat_axis=1, tiled=True)
    result = jnp.dot(
        attention_rows,
        lax.all_gather(out_weight, "dp", axis=0, tiled=True),
        preferred_element_type=jnp.float32,
    )
    return result.astype(jnp.bfloat16)


EDGE_AWAY, EDGE_SLOT, INNER_AWAY, INNER_SLOT, INNER_JOINS, EDGE_JOINS, CROSSES = range(7)


def stage_kernel(sources, clips, own_ref, out_ref, facts_ref, source_ref, clip_ref, few_sems, sems):
    parts = sems.shape[1]
    slots = own_ref.shape[0]
    rows = own_ref.shape[1] // parts
    copies = []
    for block in range(slots):
        for part in range(parts):
            here = (block, pl.ds(part * rows, rows))
            copies.append(
                pltpu.make_async_copy(own_ref.at[here], out_ref.at[here], sems.at[block, part])
            )
    few = [
        pltpu.make_async_copy(sources, source_ref, few_sems.at[0]),
        pltpu.make_async_copy(clips, clip_ref, few_sems.at[1]),
    ]
    for copy in few + copies:
        copy.start()
    for copy in few:
        copy.wait()
    ctx, dp = lax.axis_index("ctx"), lax.axis_index("dp")
    facts = {}
    for block, away, at in ((1 - ctx, EDGE_AWAY, EDGE_SLOT), (ctx, INNER_AWAY, INNER_SLOT)):
        source = source_ref[0, 0, block]
        facts[away] = (source // (2 * slots) != dp).astype(jnp.int32)
        facts[at] = lax.rem(source, slots)
    edge_clip = clip_ref[0, 1 + ctx]
    crosses = edge_clip == clip_ref[0, 2 - ctx]
    facts[CROSSES] = crosses.astype(jnp.int32)
    facts[EDGE_JOINS] = jnp.logical_or(crosses, edge_clip == clip_ref[0, 3 * ctx]).astype(jnp.int32)
    facts[INNER_JOINS] = (clip_ref[0, 2 * ctx] == clip_ref[0, 2 * ctx + 1]).astype(jnp.int32)
    for which, fact in facts.items():
        facts_ref[which] = jnp.full(facts_ref.shape[1:], fact, jnp.int32)
    for copy in copies:
        copy.wait()


def fact(facts_ref, which):
    return jnp.max(facts_ref[which])


def pack_first_kernel(facts_ref, own_ref, partner_ref, halo_ref):
    away, slot = fact(facts_ref, EDGE_AWAY) > 0, fact(facts_ref, EDGE_SLOT)

    def fill(ref):
        for head in range(halo_ref.shape[1] // (2 * HEAD)):
            columns = slice(head * 3 * HEAD + HEAD, (head + 1) * 3 * HEAD)
            halo_ref[:, head * 2 * HEAD : (head + 1) * 2 * HEAD] = ref[slot, :, columns]

    @pl.when(away)
    def _():
        fill(partner_ref)

    @pl.when(jnp.logical_not(away))
    def _():
        fill(own_ref)


def pack_kernel(facts_ref, own_ref, partner_ref, rows_ref, halo_ref, sems):
    for which, away, at in ((1, EDGE_AWAY, EDGE_SLOT), (0, INNER_AWAY, INNER_SLOT)):
        away, slot = fact(facts_ref, away) > 0, fact(facts_ref, at)

        @pl.when(jnp.logical_not(away))
        def _():
            pltpu.make_async_copy(own_ref.at[slot], rows_ref.at[which], sems.at[which]).start()

        @pl.when(away)
        def _():
            pltpu.make_async_copy(partner_ref.at[slot], rows_ref.at[which], sems.at[which]).start()

    pltpu.make_async_copy(own_ref.at[0], rows_ref.at[1], sems.at[1]).wait()
    heads = halo_ref.shape[1] // (2 * HEAD)
    skipped = rows_ref.shape[2] // (3 * HEAD) - heads
    for head in range(heads):
        first = (skipped + head) * 3 * HEAD + HEAD
        halo_ref[:, head * 2 * HEAD : (head + 1) * 2 * HEAD] = rows_ref[
            1, :, first : first + 2 * HEAD
        ]
    pltpu.make_async_copy(own_ref.at[0], rows_ref.at[0], sems.at[0]).wait()


def attend(heads, load_queries, load_own, load_more, allowed, out_ref, other_ref):
    scaling = math.log2(math.e) / math.sqrt(HEAD)
    contract_last = (((1,), (1,)), ((), ()))
    ones = jnp.ones((2 * out_ref.shape[0], HEAD), jnp.bfloat16)
    odd_core = lax.rem(lax.axis_index("dp"), 2) == 1
    for start in range(0, heads, 4):
        group = min(4, heads - start)
        scores = []
        for head in range(start, start + group):
            queries = load_queries(head)
            pair = []
            for loader in (load_own, load_more):
                pair.append(
                    lax.dot_general(
                        queries, loader(head, 0), contract_last, preferred_element_type=jnp.float32
                    )
                    * scaling
                )
            scores.append(pair)
        weights = []
        for own, more in scores:
            more = jnp.where(allowed, more, big_negative)
            row_max = jnp.max(jnp.maximum(own, more), axis=-1, keepdims=True)
            weights.append(
                jnp.concatenate(
                    [
                        jnp.exp2(own - row_max).astype(jnp.bfloat16),
                        jnp.exp2(more - row_max).astype(jnp.bfloat16),
                    ],
                    axis=1,
                )
            )
        outs = []
        for head in range(start, start + group):
            values = jnp.concatenate([load_own(head, 1), load_more(head, 1)], axis=0)
            sums = jnp.dot(
                weights[head - start],
                jnp.concatenate([values, ones], axis=1),
                preferred_element_type=jnp.float32,
            )
            outs.append(sums[:, :HEAD] / sums[:, HEAD:])
            out_ref[:, head * HEAD : (head + 1) * HEAD] = outs[-1].astype(jnp.bfloat16)
        for pair in range(group // 2):
            at = (start // 2 + pair) * HEAD
            other = jnp.where(odd_core, outs[2 * pair], outs[2 * pair + 1])
            other_ref[:, at : at + HEAD] = other.astype(jnp.bfloat16)


def inner_kernel(facts_ref, rows_ref, out_ref, other_ref):
    allowed = fact(facts_ref, INNER_JOINS) > 0

    def loader(block):
        def get(head, which):
            first = (head * 3 + 1 + which) * HEAD
            return rows_ref[block, :, first : first + HEAD]

        return get

    attend(
        out_ref.shape[1] // HEAD,
        lambda head: loader(0)(head, -1),
        loader(0),
        loader(1),
        allowed,
        out_ref,
        other_ref,
    )


def edge_kernel(first_head, facts_ref, rows_ref, halo_ref, out_ref, other_ref):
    crosses, allowed = fact(facts_ref, CROSSES) > 0, fact(facts_ref, EDGE_JOINS) > 0

    def load_own(head, which):
        first = ((first_head + head) * 3 + 1 + which) * HEAD
        return rows_ref[1, :, first : first + HEAD]

    def load_more(head, which):
        first = ((first_head + head) * 3 + 1 + which) * HEAD
        at = (2 * head + which) * HEAD
        return jnp.where(crosses, halo_ref[:, at : at + HEAD], rows_ref[0, :, first : first + HEAD])

    attend(
        out_ref.shape[1] // HEAD,
        lambda head: load_own(head, -1),
        load_own,
        load_more,
        allowed,
        out_ref,
        other_ref,
    )


def ring_order(lines):
    return list(range(0, lines, 2)) + list(range(1, lines, 2))[::-1]


def shard_places(origins, depth):
    index = lax.axis_index("dp")
    core, side, line = lax.rem(index, 2), lax.rem(index // 2, 2), index // 4
    places = ring_order(lax.axis_size("dp") // 4)
    found = []
    for steps, other_side in origins:
        from_line = line
        for at, place in enumerate(places):
            from_line = jnp.where(line == place, places[at - steps], from_line)
        pair = from_line * 2 + (1 - side if other_side else side)
        columns = [pair * 2 + core, pair * 2 + 1 - core, pair]
        found.append([pl.ds(pl.multiple_of(column * depth, depth), depth) for column in columns])
    return found


def inner_project_kernel(origins, early, inner_ref, their_ref, *rest):
    shard_refs, (total_ref, left_ref, features) = rest[:-3], rest[-3:]
    block = inner_ref.shape[0]
    depth = left_ref.shape[1] // (len(origins) - early)
    for number, (here, _, there) in enumerate(shard_places(origins, depth)):
        ref, at = (features, number) if number < early else (left_ref, number - early)
        ref[:block, at * depth : (at + 1) * depth] = inner_ref[:, here]
        ref[block:, at * depth : (at + 1) * depth] = their_ref[:, there]
    tile = 2 * HEAD
    for first in range(0, total_ref.shape[1], tile):
        columns = slice(first, first + tile)
        weight = jnp.concatenate([ref[:, columns] for ref in shard_refs], axis=0)
        total_ref[:, columns] = jnp.dot(
            features[...], weight, preferred_element_type=jnp.float32
        )


def add_products_kernel(left_ref, inner_total_ref, *rest):
    shard_refs, total_ref = rest[:-1], rest[-1]
    tile = 2 * HEAD
    for first in range(0, total_ref.shape[1], tile):
        columns = slice(first, first + tile)
        weight = jnp.concatenate([ref[:, columns] for ref in shard_refs], axis=0)
        total_ref[:, columns] = inner_total_ref[:, columns] + jnp.dot(
            left_ref[...], weight, preferred_element_type=jnp.float32
        )


def arrange_kernel(origins, parts, inner_ref, *refs):
    edge_refs, their_refs = refs[:parts], refs[parts : 2 * parts]
    out_ref, last_ref, edge_rows, their_rows = refs[2 * parts :]
    for some_refs, held in ((edge_refs, edge_rows), (their_refs, their_rows)):
        first = 0
        for ref in some_refs:
            held[:, first : first + ref.shape[1]] = ref[...]
            first += ref.shape[1]
    block, depth = last_ref.shape[0] // 2, last_ref.shape[1] // 2
    places = shard_places(origins, depth)
    for number, (here, _, there) in enumerate(places[:-1]):
        at = slice(number * depth, (number + 1) * depth)
        out_ref[:block, at] = edge_rows[:, here]
        out_ref[block:, at] = their_rows[:, there]
    for number, here in enumerate(places[-1][:2]):
        at = slice(number * depth, (number + 1) * depth)
        last_ref[:block, at] = inner_ref[:, here]
        last_ref[block:, at] = edge_rows[:, here]


def project_kernel(first, edge_ref, inner_total_ref, *rest):
    shard_refs, (own_total_ref, their_total_ref) = rest[:-2], rest[-2:]
    block = own_total_ref.shape[0] // 2
    tile = 2 * HEAD
    for at in range(0, own_total_ref.shape[1], tile):
        here = slice(at, at + tile)
        columns = slice(first + at, first + at + tile)
        weight = jnp.concatenate([ref[:, columns] for ref in shard_refs], axis=0)
        edge = jnp.dot(edge_ref[...], weight, preferred_element_type=jnp.float32)
        own_total_ref[:block, here] = inner_total_ref[:block, columns]
        own_total_ref[block:, here] = edge[:block]
        their_total_ref[:block, here] = inner_total_ref[block:, columns].astype(jnp.bfloat16)
        their_total_ref[block:, here] = edge[block:].astype(jnp.bfloat16)


def finish_kernel(parts, features_ref, *rest):
    operands, (out_ref, held, sems) = rest[:-3], rest[-3:]
    shard_refs, sum_refs = operands[: -2 * parts], operands[-2 * parts :]
    total_refs, more_refs = sum_refs[:parts], sum_refs[parts:]
    block = out_ref.shape[0] // 2
    ctx = lax.axis_index("ctx")
    copies = []
    for which, place in ((0, ctx), (1, 1 - ctx)):
        rows = slice(which * block, (which + 1) * block)
        first = 0
        for total_ref, more_ref in zip(total_refs, more_refs, strict=True):
            columns = slice(first, first + total_ref.shape[1])
            weight = jnp.concatenate([ref[:, columns] for ref in shard_refs], axis=0)
            total = jnp.dot(features_ref[rows], weight, preferred_element_type=jnp.float32)
            total = total + (total_ref[rows] + more_ref[rows])
            held[rows, columns] = total.astype(jnp.bfloat16)
            first += total_ref.shape[1]
        target = out_ref.at[pl.ds(pl.multiple_of(place * block, block), block)]
        copies.append(pltpu.make_async_copy(held.at[rows], target, sems.at[which]))
        copies[-1].start()
    for copy in copies:
        copy.wait()


SMEM = functools.partial(pl.BlockSpec, memory_space=pltpu.SMEM)
VMEM = functools.partial(pl.BlockSpec, memory_space=pltpu.VMEM)
HBM = functools.partial(pl.BlockSpec, memory_space=pltpu.HBM)


def after(value, *others):
    return lax.optimization_barrier((value, *others))[0]


def body_edge(projections, block_source, clip_ids, out_weight):
    local_rows, row_width = projections.shape
    block_rows = local_rows // 2
    heads = row_width // (3 * HEAD)
    features = heads * HEAD
    depth, width = out_weight.shape
    count = lax.axis_size("dp")
    bf16 = jnp.bfloat16

    def call(kernel, name, shape, in_specs, dtypes=None, scratch=(), out_spec=VMEM()):
        many = isinstance(shape, list)
        shapes = shape if many else [shape]
        dtypes = dtypes or [bf16] * len(shapes)
        shapes = [jax.ShapeDtypeStruct(*one) for one in zip(shapes, dtypes, strict=True)]
        return pl.pallas_call(
            kernel,
            out_shape=shapes if many else shapes[0],
            in_specs=in_specs,
            out_specs=[out_spec] * len(shapes) if many else out_spec,
            scratch_shapes=scratch,
            cost_estimate=pl.CostEstimate(flops=0, bytes_accessed=0, transcendentals=0),
            compiler_params=pltpu.CompilerParams(vmem_limit_bytes=8 * MIB),
            name=name,
        )

    def around(value, step):
        places = ring_order(count // 4)
        moves = [(here, places[(at + step) % len(places)]) for at, here in enumerate(places)]
        return lax.ppermute(
            value, "dp", [(4 * here + rest, 4 * there + rest) for here, there in moves for rest in range(4)]
        )

    def to_side(value):
        return partner(value, "dp", 1)

    def to_core(value):
        return partner(value, "dp", 0)

    def in_hbm(value):
        return pltpu.with_memory_space_constraint(value, pltpu.HBM)

    own = in_hbm(projections.reshape(2, block_rows, row_width))
    shards = {(0, False): [out_weight]}
    from_partner = pltpu.with_memory_space_constraint(to_core(own), pltpu.VMEM)
    ahead = around(out_weight, 1)
    across = to_side(out_weight)
    staged, facts = call(
        stage_kernel,
        "stage",
        [own.shape, (7, 8, 128)],
        [HBM()] * 3,
        dtypes=[bf16, jnp.int32],
        scratch=[
            pltpu.SMEM(block_source.shape, jnp.int32),
            pltpu.SMEM(clip_ids.shape, jnp.int32),
            pltpu.SemaphoreType.DMA((2,)),
            pltpu.SemaphoreType.DMA((2, 4)),
        ],
    )(in_hbm(block_source), in_hbm(clip_ids), own)
    part_heads = [heads * 8 // 16, heads * 8 // 16]
    packed_first = call(
        pack_first_kernel,
        "pack_first",
        (block_rows, 2 * HEAD * part_heads[0]),
        [VMEM()] * 3,
    )(facts, staged, from_partner)
    rows, packed_last = call(
        pack_kernel,
        "pack",
        [(2, block_rows, row_width), (block_rows, 2 * HEAD * part_heads[1])],
        [VMEM()] * 3,
        scratch=[pltpu.SemaphoreType.DMA((2,))],
    )(facts, staged, after(from_partner, packed_first))
    packed = [packed_first, packed_last]
    halos = [lax.ppermute(part, "ctx", [(0, 1), (1, 0)]) for part in packed]

    def edge_rows(part, *before):
        some = part_heads[part]
        return call(
            functools.partial(edge_kernel, sum(part_heads[:part])),
            "edge_rows",
            [(block_rows, some * HEAD), (block_rows, some // 2 * HEAD)],
            [VMEM()] * 3,
        )(after(facts, *before), rows, halos[part])

    back = around(after(out_weight, staged), -1)
    ahead = after(ahead, *packed)
    shards[1, False], shards[0, True] = [ahead], [across]
    second = around(after(ahead, across), 1)
    across = to_side(ahead)
    inner, inner_other = call(
        inner_kernel,
        "inner_rows",
        [(block_rows, features), (block_rows, features // 2)],
        [VMEM()] * 2,
    )(after(facts, ahead), rows)
    theirs = [to_core(inner_other)]

    back = after(back, inner)
    shards[3, False] = [back]
    back_across = to_side(back)
    shards[1, True] = [across]
    early = list(shards)
    origins = [*early, (2, False), (3, True), (2, True)]
    inner_total, inner_left = call(
        functools.partial(inner_project_kernel, origins[:-1], len(early)),
        "inner_project",
        [(local_rows, width), (local_rows, (len(origins) - 1 - len(early)) * depth)],
        [VMEM()] * (2 + len(early)),
        dtypes=[jnp.float32, bf16],
        scratch=[pltpu.VMEM((local_rows, len(early) * depth), bf16)],
    )(inner, *theirs, *[shards[origin][0] for origin in early])
    edges, edge_others = zip(*[edge_rows(part) for part in range(len(part_heads))], strict=True)
    second = after(second, inner_total, edges[0])
    cut = depth // 8 * 5
    shards[2, False] = [second]
    shards[3, True] = [back_across]
    shards[2, True] = [around(after(across, edges[0])[:cut], 1), to_side(second[cut:])]
    theirs = [to_core(part) for part in edge_others]

    more = [shards[origin][0] for origin in origins[len(early) : -1]]
    inner_total = call(
        add_products_kernel,
        "add_products",
        inner_total.shape,
        [VMEM()] * (2 + len(more)),
        dtypes=[jnp.float32],
    )(inner_left, inner_total, *more)
    theirs[-1] = after(theirs[-1], inner_total)
    arranged, last_features = call(
        functools.partial(arrange_kernel, origins, len(edges)),
        "arrange",
        [(local_rows, (len(origins) - 1) * depth), (local_rows, 2 * depth)],
        [VMEM()] * (1 + len(edges) + len(theirs)),
        scratch=[
            pltpu.VMEM((block_rows, features), bf16),
            pltpu.VMEM((block_rows, features // 2), bf16),
        ],
    )(inner, *edges, *theirs)
    last = shards[origins[-1]]
    last_swapped = [to_core(piece) for piece in last]
    pieces = [piece for origin in origins[:-1] for piece in shards[origin]]
    own_totals, mores = [], []
    parts = 3
    for part in range(parts):
        columns = width // parts
        own_total, their_total = call(
            functools.partial(project_kernel, part * columns),
            "project",
            [(local_rows, columns)] * 2,
            [VMEM()] * (2 + len(pieces)),
            dtypes=[jnp.float32, bf16],
        )(arranged, inner_total, *pieces)
        own_totals.append(own_total)
        if part == parts - 1:
            their_total = after(their_total, *last)
        mores.append(to_core(their_total))
    return call(
        functools.partial(finish_kernel, parts),
        "finish",
        (local_rows, width),
        [VMEM()] * (1 + 2 * len(last) + 2 * parts),
        scratch=[pltpu.VMEM((local_rows, width), bf16), pltpu.SemaphoreType.DMA((2,))],
        out_spec=HBM(),
    )(last_features, *last, *last_swapped, *own_totals, *mores)


def body(projections, block_source, clip_ids, out_weight):
    heads = projections.shape[1] // (3 * HEAD)
    two_and_two = lax.axis_size("ctx") == 2 and block_source.shape[2] == 2
    whole_tiles = out_weight.shape[0] % HEAD == 0 and heads % 16 == 0
    if two_and_two and whole_tiles and lax.axis_size("dp") == 16:
        return body_edge(projections, block_source, clip_ids, out_weight)
    return body_general(projections, block_source, clip_ids, out_weight)


def solution(mesh):
    return jax.shard_map(
        body,
        mesh=mesh,
        in_specs=(P(("dp", "ctx"), None), P("dp", "ctx", None), P("dp", None), P("dp", None)),
        out_specs=P(("dp", "ctx"), None),
        check_vma=False,
    )
```

```python
import functools
import math

import jax
import jax.numpy as jnp
from jax import lax
from jax.experimental import pallas as pl
from jax.experimental.pallas import tpu as pltpu
from jax.sharding import PartitionSpec as P

HEAD = 128


big_negative = -1e30
MIB = 1 << 20


def partner(value, axis, bit):
    mask = 2**bit
    pairs = [(source, source ^ mask) for source in range(lax.axis_size(axis))]
    return lax.ppermute(value, axis, pairs)


def soft_weights(scores, allowed):
    masked = jnp.where(allowed, scores, big_negative)
    row_max = jnp.max(masked, axis=-1, keepdims=True)
    exponent = jnp.exp(masked - row_max)
    return (exponent / jnp.sum(exponent, axis=-1, keepdims=True)).astype(jnp.bfloat16)


def attend_dense(queries, key_rows, value_rows, token_clip, scaling):
    token_count, head_count, head_size = queries.shape
    step_size = min(token_count, 512)
    step_count = token_count // step_size
    query_steps = queries.reshape(step_count, step_size, head_count, head_size)
    clip_steps = token_clip.reshape(step_count, step_size)

    def one_step(arguments):
        query_block, clip_block = arguments
        scores = (
            jnp.einsum("qhe,khe->hqk", query_block, key_rows, preferred_element_type=jnp.float32)
            * scaling
        )
        allowed = (clip_block[:, None] == token_clip[None, :])[None]
        weights = soft_weights(scores, allowed)
        return jnp.einsum(
            "hqk,khe->qhe", weights, value_rows, preferred_element_type=jnp.float32
        ).astype(jnp.bfloat16)

    outputs = lax.map(one_step, (query_steps, clip_steps))
    return outputs.reshape(token_count, head_count, head_size)


def body_general(projections, block_source, clip_ids, out_weight):
    ctx_count = lax.axis_size("ctx")
    local_rows, row_width = projections.shape
    local_blocks = block_source.shape[2]
    block_rows = local_rows // local_blocks
    own_blocks = projections.reshape(local_blocks, block_rows, row_width)
    partner_blocks = partner(own_blocks, "dp", 0)
    source_ids = block_source.reshape(local_blocks)
    from_partner = source_ids // (local_blocks * ctx_count) != lax.axis_index("dp")
    chosen_slot = source_ids % local_blocks + local_blocks * from_partner.astype(jnp.int32)
    candidates = jnp.concatenate([own_blocks, partner_blocks], axis=0)
    packed = jnp.take(candidates, chosen_slot, axis=0)
    local_heads = row_width // (3 * HEAD) // ctx_count
    grouped = packed.reshape(local_rows, ctx_count, local_heads, 3 * HEAD)
    block_clip = clip_ids.reshape(-1)
    token_clip = jnp.repeat(block_clip, block_rows)
    scaling = 1.0 / math.sqrt(HEAD)
    regrouped = lax.all_to_all(grouped, "ctx", split_axis=1, concat_axis=0, tiled=True)
    token_count = regrouped.shape[0]
    item_count = regrouped.shape[2]
    features = regrouped.reshape(token_count, item_count, 3 * HEAD)
    queries = features[:, :, :HEAD]
    key_rows = features[:, :, HEAD : 2 * HEAD]
    value_rows = features[:, :, 2 * HEAD :]
    attended = attend_dense(queries, key_rows, value_rows, token_clip, scaling)
    merged = attended.reshape(local_rows * ctx_count, local_heads * HEAD)
    attention_rows = lax.all_to_all(merged, "ctx", split_axis=0, concat_axis=1, tiled=True)
    result = jnp.dot(
        attention_rows,
        lax.all_gather(out_weight, "dp", axis=0, tiled=True),
        preferred_element_type=jnp.float32,
    )
    return result.astype(jnp.bfloat16)


EDGE_AWAY, EDGE_SLOT, INNER_AWAY, INNER_SLOT, INNER_JOINS, EDGE_JOINS, CROSSES = range(7)


def stage_kernel(sources, clips, own_ref, out_ref, facts_ref, source_ref, clip_ref, few_sems, sems):
    parts = sems.shape[1]
    slots = own_ref.shape[0]
    rows = own_ref.shape[1] // parts
    copies = []
    for block in range(slots):
        for part in range(parts):
            here = (block, pl.ds(part * rows, rows))
            copies.append(
                pltpu.make_async_copy(own_ref.at[here], out_ref.at[here], sems.at[block, part])
            )
    few = [
        pltpu.make_async_copy(sources, source_ref, few_sems.at[0]),
        pltpu.make_async_copy(clips, clip_ref, few_sems.at[1]),
    ]
    for copy in few + copies:
        copy.start()
    for copy in few:
        copy.wait()
    ctx, dp = lax.axis_index("ctx"), lax.axis_index("dp")
    facts = {}
    for block, away, at in ((1 - ctx, EDGE_AWAY, EDGE_SLOT), (ctx, INNER_AWAY, INNER_SLOT)):
        source = source_ref[0, 0, block]
        facts[away] = (source // (2 * slots) != dp).astype(jnp.int32)
        facts[at] = lax.rem(source, slots)
    edge_clip = clip_ref[0, 1 + ctx]
    crosses = edge_clip == clip_ref[0, 2 - ctx]
    facts[CROSSES] = crosses.astype(jnp.int32)
    facts[EDGE_JOINS] = jnp.logical_or(crosses, edge_clip == clip_ref[0, 3 * ctx]).astype(jnp.int32)
    facts[INNER_JOINS] = (clip_ref[0, 2 * ctx] == clip_ref[0, 2 * ctx + 1]).astype(jnp.int32)
    for which, fact in facts.items():
        facts_ref[which] = jnp.full(facts_ref.shape[1:], fact, jnp.int32)
    for copy in copies:
        copy.wait()


def fact(facts_ref, which):
    return jnp.max(facts_ref[which])


def pack_first_kernel(facts_ref, own_ref, partner_ref, halo_ref):
    away, slot = fact(facts_ref, EDGE_AWAY) > 0, fact(facts_ref, EDGE_SLOT)

    def fill(ref):
        for head in range(halo_ref.shape[1] // (2 * HEAD)):
            columns = slice(head * 3 * HEAD + HEAD, (head + 1) * 3 * HEAD)
            halo_ref[:, head * 2 * HEAD : (head + 1) * 2 * HEAD] = ref[slot, :, columns]

    @pl.when(away)
    def _():
        fill(partner_ref)

    @pl.when(jnp.logical_not(away))
    def _():
        fill(own_ref)


def pack_kernel(facts_ref, own_ref, partner_ref, rows_ref, halo_ref, sems):
    for which, away, at in ((1, EDGE_AWAY, EDGE_SLOT), (0, INNER_AWAY, INNER_SLOT)):
        away, slot = fact(facts_ref, away) > 0, fact(facts_ref, at)

        @pl.when(jnp.logical_not(away))
        def _():
            pltpu.make_async_copy(own_ref.at[slot], rows_ref.at[which], sems.at[which]).start()

        @pl.when(away)
        def _():
            pltpu.make_async_copy(partner_ref.at[slot], rows_ref.at[which], sems.at[which]).start()

    pltpu.make_async_copy(own_ref.at[0], rows_ref.at[1], sems.at[1]).wait()
    heads = halo_ref.shape[1] // (2 * HEAD)
    skipped = rows_ref.shape[2] // (3 * HEAD) - heads
    for head in range(heads):
        first = (skipped + head) * 3 * HEAD + HEAD
        halo_ref[:, head * 2 * HEAD : (head + 1) * 2 * HEAD] = rows_ref[
            1, :, first : first + 2 * HEAD
        ]
    pltpu.make_async_copy(own_ref.at[0], rows_ref.at[0], sems.at[0]).wait()


def attend(heads, load_queries, load_own, load_more, allowed, out_ref, other_ref):
    scaling = math.log2(math.e) / math.sqrt(HEAD)
    contract_last = (((1,), (1,)), ((), ()))
    ones = jnp.ones((2 * out_ref.shape[0], HEAD), jnp.bfloat16)
    odd_core = lax.rem(lax.axis_index("dp"), 2) == 1
    for start in range(0, heads, 4):
        group = min(4, heads - start)
        scores = []
        for head in range(start, start + group):
            queries = load_queries(head)
            pair = []
            for loader in (load_own, load_more):
                pair.append(
                    lax.dot_general(
                        queries, loader(head, 0), contract_last, preferred_element_type=jnp.float32
                    )
                    * scaling
                )
            scores.append(pair)
        weights = []
        for own, more in scores:
            more = jnp.where(allowed, more, big_negative)
            row_max = jnp.max(jnp.maximum(own, more), axis=-1, keepdims=True)
            weights.append(
                jnp.concatenate(
                    [
                        jnp.exp2(own - row_max).astype(jnp.bfloat16),
                        jnp.exp2(more - row_max).astype(jnp.bfloat16),
                    ],
                    axis=1,
                )
            )
        outs = []
        for head in range(start, start + group):
            values = jnp.concatenate([load_own(head, 1), load_more(head, 1)], axis=0)
            sums = jnp.dot(
                weights[head - start],
                jnp.concatenate([values, ones], axis=1),
                preferred_element_type=jnp.float32,
            )
            outs.append(sums[:, :HEAD] / sums[:, HEAD:])
            out_ref[:, head * HEAD : (head + 1) * HEAD] = outs[-1].astype(jnp.bfloat16)
        for pair in range(group // 2):
            at = (start // 2 + pair) * HEAD
            other = jnp.where(odd_core, outs[2 * pair], outs[2 * pair + 1])
            other_ref[:, at : at + HEAD] = other.astype(jnp.bfloat16)


def inner_kernel(facts_ref, rows_ref, out_ref, other_ref):
    allowed = fact(facts_ref, INNER_JOINS) > 0

    def loader(block):
        def get(head, which):
            first = (head * 3 + 1 + which) * HEAD
            return rows_ref[block, :, first : first + HEAD]

        return get

    attend(
        out_ref.shape[1] // HEAD,
        lambda head: loader(0)(head, -1),
        loader(0),
        loader(1),
        allowed,
        out_ref,
        other_ref,
    )


def edge_kernel(first_head, facts_ref, rows_ref, halo_ref, out_ref, other_ref):
    crosses, allowed = fact(facts_ref, CROSSES) > 0, fact(facts_ref, EDGE_JOINS) > 0

    def load_own(head, which):
        first = ((first_head + head) * 3 + 1 + which) * HEAD
        return rows_ref[1, :, first : first + HEAD]

    def load_more(head, which):
        first = ((first_head + head) * 3 + 1 + which) * HEAD
        at = (2 * head + which) * HEAD
        return jnp.where(crosses, halo_ref[:, at : at + HEAD], rows_ref[0, :, first : first + HEAD])

    attend(
        out_ref.shape[1] // HEAD,
        lambda head: load_own(head, -1),
        load_own,
        load_more,
        allowed,
        out_ref,
        other_ref,
    )


def ring_order(lines):
    return list(range(0, lines, 2)) + list(range(1, lines, 2))[::-1]


def shard_places(origins, depth):
    index = lax.axis_index("dp")
    core, side, line = lax.rem(index, 2), lax.rem(index // 2, 2), index // 4
    places = ring_order(lax.axis_size("dp") // 4)
    found = []
    for steps, other_side in origins:
        from_line = line
        for at, place in enumerate(places):
            from_line = jnp.where(line == place, places[at - steps], from_line)
        pair = from_line * 2 + (1 - side if other_side else side)
        columns = [pair * 2 + core, pair * 2 + 1 - core, pair]
        found.append([pl.ds(pl.multiple_of(column * depth, depth), depth) for column in columns])
    return found


def inner_project_kernel(origins, early, inner_ref, their_ref, *rest):
    shard_refs, (total_ref, left_ref, features) = rest[:-3], rest[-3:]
    block = inner_ref.shape[0]
    depth = left_ref.shape[1] // (len(origins) - early)
    for number, (here, _, there) in enumerate(shard_places(origins, depth)):
        ref, at = (features, number) if number < early else (left_ref, number - early)
        ref[:block, at * depth : (at + 1) * depth] = inner_ref[:, here]
        ref[block:, at * depth : (at + 1) * depth] = their_ref[:, there]
    tile = 2 * HEAD
    for first in range(0, total_ref.shape[1], tile):
        columns = slice(first, first + tile)
        weight = jnp.concatenate([ref[:, columns] for ref in shard_refs], axis=0)
        total_ref[:, columns] = jnp.dot(
            features[...], weight, preferred_element_type=jnp.float32
        )


def add_products_kernel(left_ref, inner_total_ref, *rest):
    shard_refs, total_ref = rest[:-1], rest[-1]
    tile = 2 * HEAD
    for first in range(0, total_ref.shape[1], tile):
        columns = slice(first, first + tile)
        weight = jnp.concatenate([ref[:, columns] for ref in shard_refs], axis=0)
        total_ref[:, columns] = inner_total_ref[:, columns] + jnp.dot(
            left_ref[...], weight, preferred_element_type=jnp.float32
        )


def arrange_kernel(origins, parts, inner_ref, *refs):
    edge_refs, their_refs = refs[:parts], refs[parts : 2 * parts]
    out_ref, last_ref, edge_rows, their_rows = refs[2 * parts :]
    for some_refs, held in ((edge_refs, edge_rows), (their_refs, their_rows)):
        first = 0
        for ref in some_refs:
            held[:, first : first + ref.shape[1]] = ref[...]
            first += ref.shape[1]
    block, depth = last_ref.shape[0] // 2, last_ref.shape[1] // 2
    places = shard_places(origins, depth)
    for number, (here, _, there) in enumerate(places[:-1]):
        at = slice(number * depth, (number + 1) * depth)
        out_ref[:block, at] = edge_rows[:, here]
        out_ref[block:, at] = their_rows[:, there]
    for number, here in enumerate(places[-1][:2]):
        at = slice(number * depth, (number + 1) * depth)
        last_ref[:block, at] = inner_ref[:, here]
        last_ref[block:, at] = edge_rows[:, here]


def project_kernel(first, edge_ref, inner_total_ref, *rest):
    shard_refs, (own_total_ref, their_total_ref) = rest[:-2], rest[-2:]
    block = own_total_ref.shape[0] // 2
    tile = 2 * HEAD
    for at in range(0, own_total_ref.shape[1], tile):
        here = slice(at, at + tile)
        columns = slice(first + at, first + at + tile)
        weight = jnp.concatenate([ref[:, columns] for ref in shard_refs], axis=0)
        edge = jnp.dot(edge_ref[...], weight, preferred_element_type=jnp.float32)
        own_total_ref[:block, here] = inner_total_ref[:block, columns]
        own_total_ref[block:, here] = edge[:block]
        their_total_ref[:block, here] = inner_total_ref[block:, columns].astype(jnp.bfloat16)
        their_total_ref[block:, here] = edge[block:].astype(jnp.bfloat16)


def gather_sums_kernel(parts, features_ref, *rest):
    operands, out_ref = rest[:-1], rest[-1]
    shard_refs, sum_refs = operands[: -2 * parts + 1], operands[-2 * parts + 1 :]
    depth = sum(ref.shape[0] for ref in shard_refs)
    first = 0
    for part in range(parts):
        total_ref = sum_refs[part]
        columns = slice(first, first + total_ref.shape[1])
        weight = jnp.concatenate([ref[:, columns] for ref in shard_refs], axis=0)
        total = total_ref[...] + jnp.dot(
            features_ref[:, :depth], weight, preferred_element_type=jnp.float32
        )
        out_ref[:, columns] = total if part == parts - 1 else total + sum_refs[parts + part][...]
        first += total_ref.shape[1]


def finish_kernel(features_ref, total_ref, more_ref, *rest):
    shard_refs, (out_ref, held, sems) = rest[:-3], rest[-3:]
    depth = sum(ref.shape[0] for ref in shard_refs)
    width, late = out_ref.shape[1], more_ref.shape[1]
    block = out_ref.shape[0] // 2
    pieces = sems.shape[1]
    some = block // pieces
    ctx = lax.axis_index("ctx")
    copies = []
    for which, place in ((0, ctx), (1, 1 - ctx)):
        for piece in range(pieces):
            rows = slice(which * block + piece * some, which * block + (piece + 1) * some)
            for first in range(0, width, late):
                columns = slice(first, first + late)
                weight = jnp.concatenate([ref[:, columns] for ref in shard_refs], axis=0)
                total = total_ref[rows, columns] + jnp.dot(
                    features_ref[rows, depth:], weight, preferred_element_type=jnp.float32
                )
                if first + late == width:
                    total = total + more_ref[rows]
                held[rows, columns] = total.astype(jnp.bfloat16)
            there = pl.ds(pl.multiple_of(place * block + piece * some, some), some)
            copies.append(
                pltpu.make_async_copy(held.at[rows], out_ref.at[there], sems.at[which, piece])
            )
            copies[-1].start()
    for copy in copies:
        copy.wait()


SMEM = functools.partial(pl.BlockSpec, memory_space=pltpu.SMEM)
VMEM = functools.partial(pl.BlockSpec, memory_space=pltpu.VMEM)
HBM = functools.partial(pl.BlockSpec, memory_space=pltpu.HBM)


def after(value, *others):
    return lax.optimization_barrier((value, *others))[0]


def body_edge(projections, block_source, clip_ids, out_weight):
    local_rows, row_width = projections.shape
    block_rows = local_rows // 2
    heads = row_width // (3 * HEAD)
    features = heads * HEAD
    depth, width = out_weight.shape
    count = lax.axis_size("dp")
    bf16 = jnp.bfloat16

    def call(kernel, name, shape, in_specs, dtypes=None, scratch=(), out_spec=VMEM()):
        many = isinstance(shape, list)
        shapes = shape if many else [shape]
        dtypes = dtypes or [bf16] * len(shapes)
        shapes = [jax.ShapeDtypeStruct(*one) for one in zip(shapes, dtypes, strict=True)]
        return pl.pallas_call(
            kernel,
            out_shape=shapes if many else shapes[0],
            in_specs=in_specs,
            out_specs=[out_spec] * len(shapes) if many else out_spec,
            scratch_shapes=scratch,
            cost_estimate=pl.CostEstimate(flops=0, bytes_accessed=0, transcendentals=0),
            compiler_params=pltpu.CompilerParams(vmem_limit_bytes=8 * MIB),
            name=name,
        )

    def around(value, step):
        places = ring_order(count // 4)
        moves = [(here, places[(at + step) % len(places)]) for at, here in enumerate(places)]
        return lax.ppermute(
            value, "dp", [(4 * here + rest, 4 * there + rest) for here, there in moves for rest in range(4)]
        )

    def to_side(value):
        return partner(value, "dp", 1)

    def to_core(value):
        return partner(value, "dp", 0)

    def in_hbm(value):
        return pltpu.with_memory_space_constraint(value, pltpu.HBM)

    own = in_hbm(projections.reshape(2, block_rows, row_width))
    shards = {(0, False): [out_weight]}
    from_partner = pltpu.with_memory_space_constraint(to_core(own), pltpu.VMEM)
    ahead = around(out_weight, 1)
    across = to_side(out_weight)
    staged, facts = call(
        stage_kernel,
        "stage",
        [own.shape, (7, 8, 128)],
        [HBM()] * 3,
        dtypes=[bf16, jnp.int32],
        scratch=[
            pltpu.SMEM(block_source.shape, jnp.int32),
            pltpu.SMEM(clip_ids.shape, jnp.int32),
            pltpu.SemaphoreType.DMA((2,)),
            pltpu.SemaphoreType.DMA((2, 4)),
        ],
    )(in_hbm(block_source), in_hbm(clip_ids), own)
    part_heads = [heads * 8 // 16, heads * 8 // 16]
    packed_first = call(
        pack_first_kernel,
        "pack_first",
        (block_rows, 2 * HEAD * part_heads[0]),
        [VMEM()] * 3,
    )(facts, staged, from_partner)
    rows, packed_last = call(
        pack_kernel,
        "pack",
        [(2, block_rows, row_width), (block_rows, 2 * HEAD * part_heads[1])],
        [VMEM()] * 3,
        scratch=[pltpu.SemaphoreType.DMA((2,))],
    )(facts, staged, after(from_partner, packed_first))
    packed = [packed_first, packed_last]
    halos = [lax.ppermute(part, "ctx", [(0, 1), (1, 0)]) for part in packed]

    def edge_rows(part, *before):
        some = part_heads[part]
        return call(
            functools.partial(edge_kernel, sum(part_heads[:part])),
            "edge_rows",
            [(block_rows, some * HEAD), (block_rows, some // 2 * HEAD)],
            [VMEM()] * 3,
        )(after(facts, *before), rows, halos[part])

    back = around(after(out_weight, staged), -1)
    ahead = after(ahead, *packed)
    shards[1, False], shards[0, True] = [ahead], [across]
    second = around(after(ahead, across), 1)
    across = to_side(ahead)
    inner, inner_other = call(
        inner_kernel,
        "inner_rows",
        [(block_rows, features), (block_rows, features // 2)],
        [VMEM()] * 2,
    )(after(facts, ahead), rows)
    theirs = [to_core(inner_other)]

    back = after(back, inner)
    shards[3, False] = [back]
    back_across = to_side(back)
    shards[1, True] = [across]
    early = list(shards)
    origins = [*early, (2, False), (3, True), (2, True)]
    inner_total, inner_left = call(
        functools.partial(inner_project_kernel, origins[:-1], len(early)),
        "inner_project",
        [(local_rows, width), (local_rows, (len(origins) - 1 - len(early)) * depth)],
        [VMEM()] * (2 + len(early)),
        dtypes=[jnp.float32, bf16],
        scratch=[pltpu.VMEM((local_rows, len(early) * depth), bf16)],
    )(inner, *theirs, *[shards[origin][0] for origin in early])
    edges, edge_others = zip(*[edge_rows(part) for part in range(len(part_heads))], strict=True)
    second = after(second, inner_total, edges[0])
    cut = depth // 8 * 5
    shards[2, False] = [second]
    shards[3, True] = [back_across]
    shards[2, True] = [around(after(across, edges[0])[:cut], 1), to_side(second[cut:])]
    theirs = [to_core(part) for part in edge_others]

    more = [shards[origin][0] for origin in origins[len(early) : -1]]
    inner_total = call(
        add_products_kernel,
        "add_products",
        inner_total.shape,
        [VMEM()] * (2 + len(more)),
        dtypes=[jnp.float32],
    )(inner_left, inner_total, *more)
    theirs[-1] = after(theirs[-1], inner_total)
    arranged, last_features = call(
        functools.partial(arrange_kernel, origins, len(edges)),
        "arrange",
        [(local_rows, (len(origins) - 1) * depth), (local_rows, 2 * depth)],
        [VMEM()] * (1 + len(edges) + len(theirs)),
        scratch=[
            pltpu.VMEM((block_rows, features), bf16),
            pltpu.VMEM((block_rows, features // 2), bf16),
        ],
    )(inner, *edges, *theirs)
    last = shards[origins[-1]]
    last_swapped = [to_core(piece) for piece in last]
    pieces = [piece for origin in origins[:-1] for piece in shards[origin]]
    own_totals, mores = [], []
    parts = 3
    for part in range(parts):
        columns = width // parts
        own_total, their_total = call(
            functools.partial(project_kernel, part * columns),
            "project",
            [(local_rows, columns)] * 2,
            [VMEM()] * (2 + len(pieces)),
            dtypes=[jnp.float32, bf16],
        )(arranged, inner_total, *pieces)
        own_totals.append(own_total)
        if part == parts - 1:
            their_total = after(their_total, *last)
        mores.append(to_core(their_total))
    total = call(
        functools.partial(gather_sums_kernel, parts),
        "gather_sums",
        (local_rows, width),
        [VMEM()] * (len(last) + 2 * parts),
        dtypes=[jnp.float32],
    )(last_features, *last, *own_totals, *mores[:-1])
    return call(
        finish_kernel,
        "finish",
        (local_rows, width),
        [VMEM()] * (3 + len(last)),
        scratch=[pltpu.VMEM((local_rows, width), bf16), pltpu.SemaphoreType.DMA((2, 2))],
        out_spec=HBM(),
    )(last_features, total, mores[-1], *last_swapped)


def body(projections, block_source, clip_ids, out_weight):
    heads = projections.shape[1] // (3 * HEAD)
    two_and_two = lax.axis_size("ctx") == 2 and block_source.shape[2] == 2
    whole_tiles = out_weight.shape[0] % HEAD == 0 and heads % 16 == 0
    if two_and_two and whole_tiles and lax.axis_size("dp") == 16:
        return body_edge(projections, block_source, clip_ids, out_weight)
    return body_general(projections, block_source, clip_ids, out_weight)


def solution(mesh):
    return jax.shard_map(
        body,
        mesh=mesh,
        in_specs=(P(("dp", "ctx"), None), P("dp", "ctx", None), P("dp", None), P("dp", None)),
        out_specs=P(("dp", "ctx"), None),
        check_vma=False,
    )
```

```python
import functools
import math

import jax
import jax.numpy as jnp
from jax import lax
from jax.experimental import pallas as pl
from jax.experimental.pallas import tpu as pltpu
from jax.sharding import PartitionSpec as P

HEAD = 128


big_negative = -1e30
MIB = 1 << 20


def partner(value, axis, bit):
    mask = 2**bit
    pairs = [(source, source ^ mask) for source in range(lax.axis_size(axis))]
    return lax.ppermute(value, axis, pairs)


def soft_weights(scores, allowed):
    masked = jnp.where(allowed, scores, big_negative)
    row_max = jnp.max(masked, axis=-1, keepdims=True)
    exponent = jnp.exp(masked - row_max)
    return (exponent / jnp.sum(exponent, axis=-1, keepdims=True)).astype(jnp.bfloat16)


def attend_dense(queries, key_rows, value_rows, token_clip, scaling):
    token_count, head_count, head_size = queries.shape
    step_size = min(token_count, 512)
    step_count = token_count // step_size
    query_steps = queries.reshape(step_count, step_size, head_count, head_size)
    clip_steps = token_clip.reshape(step_count, step_size)

    def one_step(arguments):
        query_block, clip_block = arguments
        scores = (
            jnp.einsum("qhe,khe->hqk", query_block, key_rows, preferred_element_type=jnp.float32)
            * scaling
        )
        allowed = (clip_block[:, None] == token_clip[None, :])[None]
        weights = soft_weights(scores, allowed)
        return jnp.einsum(
            "hqk,khe->qhe", weights, value_rows, preferred_element_type=jnp.float32
        ).astype(jnp.bfloat16)

    outputs = lax.map(one_step, (query_steps, clip_steps))
    return outputs.reshape(token_count, head_count, head_size)


def body_general(projections, block_source, clip_ids, out_weight):
    ctx_count = lax.axis_size("ctx")
    local_rows, row_width = projections.shape
    local_blocks = block_source.shape[2]
    block_rows = local_rows // local_blocks
    own_blocks = projections.reshape(local_blocks, block_rows, row_width)
    partner_blocks = partner(own_blocks, "dp", 0)
    source_ids = block_source.reshape(local_blocks)
    from_partner = source_ids // (local_blocks * ctx_count) != lax.axis_index("dp")
    chosen_slot = source_ids % local_blocks + local_blocks * from_partner.astype(jnp.int32)
    candidates = jnp.concatenate([own_blocks, partner_blocks], axis=0)
    packed = jnp.take(candidates, chosen_slot, axis=0)
    local_heads = row_width // (3 * HEAD) // ctx_count
    grouped = packed.reshape(local_rows, ctx_count, local_heads, 3 * HEAD)
    block_clip = clip_ids.reshape(-1)
    token_clip = jnp.repeat(block_clip, block_rows)
    scaling = 1.0 / math.sqrt(HEAD)
    regrouped = lax.all_to_all(grouped, "ctx", split_axis=1, concat_axis=0, tiled=True)
    token_count = regrouped.shape[0]
    item_count = regrouped.shape[2]
    features = regrouped.reshape(token_count, item_count, 3 * HEAD)
    queries = features[:, :, :HEAD]
    key_rows = features[:, :, HEAD : 2 * HEAD]
    value_rows = features[:, :, 2 * HEAD :]
    attended = attend_dense(queries, key_rows, value_rows, token_clip, scaling)
    merged = attended.reshape(local_rows * ctx_count, local_heads * HEAD)
    attention_rows = lax.all_to_all(merged, "ctx", split_axis=0, concat_axis=1, tiled=True)
    result = jnp.dot(
        attention_rows,
        lax.all_gather(out_weight, "dp", axis=0, tiled=True),
        preferred_element_type=jnp.float32,
    )
    return result.astype(jnp.bfloat16)


EDGE_AWAY, EDGE_SLOT, INNER_AWAY, INNER_SLOT, INNER_JOINS, EDGE_JOINS, CROSSES = range(7)


def stage_kernel(sources, clips, own_ref, out_ref, facts_ref, source_ref, clip_ref, few_sems, sems):
    parts = sems.shape[1]
    slots = own_ref.shape[0]
    rows = own_ref.shape[1] // parts
    copies = []
    for block in range(slots):
        for part in range(parts):
            here = (block, pl.ds(part * rows, rows))
            copies.append(
                pltpu.make_async_copy(own_ref.at[here], out_ref.at[here], sems.at[block, part])
            )
    few = [
        pltpu.make_async_copy(sources, source_ref, few_sems.at[0]),
        pltpu.make_async_copy(clips, clip_ref, few_sems.at[1]),
    ]
    for copy in few + copies:
        copy.start()
    for copy in few:
        copy.wait()
    ctx, dp = lax.axis_index("ctx"), lax.axis_index("dp")
    facts = {}
    for block, away, at in ((1 - ctx, EDGE_AWAY, EDGE_SLOT), (ctx, INNER_AWAY, INNER_SLOT)):
        source = source_ref[0, 0, block]
        facts[away] = (source // (2 * slots) != dp).astype(jnp.int32)
        facts[at] = lax.rem(source, slots)
    edge_clip = clip_ref[0, 1 + ctx]
    crosses = edge_clip == clip_ref[0, 2 - ctx]
    facts[CROSSES] = crosses.astype(jnp.int32)
    facts[EDGE_JOINS] = jnp.logical_or(crosses, edge_clip == clip_ref[0, 3 * ctx]).astype(jnp.int32)
    facts[INNER_JOINS] = (clip_ref[0, 2 * ctx] == clip_ref[0, 2 * ctx + 1]).astype(jnp.int32)
    for which, fact in facts.items():
        facts_ref[which] = jnp.full(facts_ref.shape[1:], fact, jnp.int32)
    for copy in copies:
        copy.wait()


def fact(facts_ref, which):
    return jnp.max(facts_ref[which])


def pack_first_kernel(facts_ref, own_ref, partner_ref, halo_ref):
    away, slot = fact(facts_ref, EDGE_AWAY) > 0, fact(facts_ref, EDGE_SLOT)

    def fill(ref):
        for head in range(halo_ref.shape[1] // (2 * HEAD)):
            columns = slice(head * 3 * HEAD + HEAD, (head + 1) * 3 * HEAD)
            halo_ref[:, head * 2 * HEAD : (head + 1) * 2 * HEAD] = ref[slot, :, columns]

    @pl.when(away)
    def _():
        fill(partner_ref)

    @pl.when(jnp.logical_not(away))
    def _():
        fill(own_ref)


def pack_kernel(facts_ref, own_ref, partner_ref, rows_ref, halo_ref, sems):
    for which, away, at in ((1, EDGE_AWAY, EDGE_SLOT), (0, INNER_AWAY, INNER_SLOT)):
        away, slot = fact(facts_ref, away) > 0, fact(facts_ref, at)

        @pl.when(jnp.logical_not(away))
        def _():
            pltpu.make_async_copy(own_ref.at[slot], rows_ref.at[which], sems.at[which]).start()

        @pl.when(away)
        def _():
            pltpu.make_async_copy(partner_ref.at[slot], rows_ref.at[which], sems.at[which]).start()

    pltpu.make_async_copy(own_ref.at[0], rows_ref.at[1], sems.at[1]).wait()
    heads = halo_ref.shape[1] // (2 * HEAD)
    skipped = rows_ref.shape[2] // (3 * HEAD) - heads
    for head in range(heads):
        first = (skipped + head) * 3 * HEAD + HEAD
        halo_ref[:, head * 2 * HEAD : (head + 1) * 2 * HEAD] = rows_ref[
            1, :, first : first + 2 * HEAD
        ]
    pltpu.make_async_copy(own_ref.at[0], rows_ref.at[0], sems.at[0]).wait()


def attend(heads, load_queries, load_own, load_more, allowed, out_ref, other_ref):
    scaling = math.log2(math.e) / math.sqrt(HEAD)
    contract_last = (((1,), (1,)), ((), ()))
    ones = jnp.ones((2 * out_ref.shape[0], HEAD), jnp.bfloat16)
    odd_core = lax.rem(lax.axis_index("dp"), 2) == 1
    for start in range(0, heads, 4):
        group = min(4, heads - start)
        scores = []
        for head in range(start, start + group):
            queries = load_queries(head)
            pair = []
            for loader in (load_own, load_more):
                pair.append(
                    lax.dot_general(
                        queries, loader(head, 0), contract_last, preferred_element_type=jnp.float32
                    )
                    * scaling
                )
            scores.append(pair)
        weights = []
        for own, more in scores:
            more = jnp.where(allowed, more, big_negative)
            row_max = jnp.max(jnp.maximum(own, more), axis=-1, keepdims=True)
            weights.append(
                jnp.concatenate(
                    [
                        jnp.exp2(own - row_max).astype(jnp.bfloat16),
                        jnp.exp2(more - row_max).astype(jnp.bfloat16),
                    ],
                    axis=1,
                )
            )
        outs = []
        for head in range(start, start + group):
            values = jnp.concatenate([load_own(head, 1), load_more(head, 1)], axis=0)
            sums = jnp.dot(
                weights[head - start],
                jnp.concatenate([values, ones], axis=1),
                preferred_element_type=jnp.float32,
            )
            outs.append(sums[:, :HEAD] / sums[:, HEAD:])
            out_ref[:, head * HEAD : (head + 1) * HEAD] = outs[-1].astype(jnp.bfloat16)
        for pair in range(group // 2):
            at = (start // 2 + pair) * HEAD
            other = jnp.where(odd_core, outs[2 * pair], outs[2 * pair + 1])
            other_ref[:, at : at + HEAD] = other.astype(jnp.bfloat16)


def inner_kernel(facts_ref, rows_ref, out_ref, other_ref):
    allowed = fact(facts_ref, INNER_JOINS) > 0

    def loader(block):
        def get(head, which):
            first = (head * 3 + 1 + which) * HEAD
            return rows_ref[block, :, first : first + HEAD]

        return get

    attend(
        out_ref.shape[1] // HEAD,
        lambda head: loader(0)(head, -1),
        loader(0),
        loader(1),
        allowed,
        out_ref,
        other_ref,
    )


def edge_kernel(first_head, facts_ref, rows_ref, halo_ref, out_ref, other_ref):
    crosses, allowed = fact(facts_ref, CROSSES) > 0, fact(facts_ref, EDGE_JOINS) > 0

    def load_own(head, which):
        first = ((first_head + head) * 3 + 1 + which) * HEAD
        return rows_ref[1, :, first : first + HEAD]

    def load_more(head, which):
        first = ((first_head + head) * 3 + 1 + which) * HEAD
        at = (2 * head + which) * HEAD
        return jnp.where(crosses, halo_ref[:, at : at + HEAD], rows_ref[0, :, first : first + HEAD])

    attend(
        out_ref.shape[1] // HEAD,
        lambda head: load_own(head, -1),
        load_own,
        load_more,
        allowed,
        out_ref,
        other_ref,
    )


def ring_order(lines):
    return list(range(1, lines, 2)) + list(range(0, lines, 2))[::-1]


def shard_places(origins, depth):
    index = lax.axis_index("dp")
    core, side, line = lax.rem(index, 2), lax.rem(index // 2, 2), index // 4
    places = ring_order(lax.axis_size("dp") // 4)
    found = []
    for steps, other_side in origins:
        from_line = line
        for at, place in enumerate(places):
            from_line = jnp.where(line == place, places[at - steps], from_line)
        pair = from_line * 2 + (1 - side if other_side else side)
        columns = [pair * 2 + core, pair * 2 + 1 - core, pair]
        found.append([pl.ds(pl.multiple_of(column * depth, depth), depth) for column in columns])
    return found


def inner_project_kernel(origins, early, inner_ref, their_ref, *rest):
    shard_refs, (total_ref, left_ref, features) = rest[:-3], rest[-3:]
    block = inner_ref.shape[0]
    depth = left_ref.shape[1] // (len(origins) - early)
    for number, (here, _, there) in enumerate(shard_places(origins, depth)):
        ref, at = (features, number) if number < early else (left_ref, number - early)
        ref[:block, at * depth : (at + 1) * depth] = inner_ref[:, here]
        ref[block:, at * depth : (at + 1) * depth] = their_ref[:, there]
    tile = 2 * HEAD
    for first in range(0, total_ref.shape[1], tile):
        columns = slice(first, first + tile)
        weight = jnp.concatenate([ref[:, columns] for ref in shard_refs], axis=0)
        total_ref[:, columns] = jnp.dot(
            features[...], weight, preferred_element_type=jnp.float32
        )


def add_products_kernel(left_ref, inner_total_ref, *rest):
    shard_refs, total_ref = rest[:-1], rest[-1]
    tile = 2 * HEAD
    for first in range(0, total_ref.shape[1], tile):
        columns = slice(first, first + tile)
        weight = jnp.concatenate([ref[:, columns] for ref in shard_refs], axis=0)
        total_ref[:, columns] = inner_total_ref[:, columns] + jnp.dot(
            left_ref[...], weight, preferred_element_type=jnp.float32
        )


def arrange_kernel(origins, parts, inner_ref, *refs):
    edge_refs, their_refs = refs[:parts], refs[parts : 2 * parts]
    out_ref, last_ref, edge_rows, their_rows = refs[2 * parts :]
    for some_refs, held in ((edge_refs, edge_rows), (their_refs, their_rows)):
        first = 0
        for ref in some_refs:
            held[:, first : first + ref.shape[1]] = ref[...]
            first += ref.shape[1]
    block, depth = last_ref.shape[0] // 2, last_ref.shape[1] // 2
    places = shard_places(origins, depth)
    for number, (here, _, there) in enumerate(places[:-1]):
        at = slice(number * depth, (number + 1) * depth)
        out_ref[:block, at] = edge_rows[:, here]
        out_ref[block:, at] = their_rows[:, there]
    for number, here in enumerate(places[-1][:2]):
        at = slice(number * depth, (number + 1) * depth)
        last_ref[:block, at] = inner_ref[:, here]
        last_ref[block:, at] = edge_rows[:, here]


def project_kernel(first, edge_ref, inner_total_ref, *rest):
    shard_refs, (own_total_ref, their_total_ref) = rest[:-2], rest[-2:]
    block = own_total_ref.shape[0] // 2
    tile = 2 * HEAD
    for at in range(0, own_total_ref.shape[1], tile):
        here = slice(at, at + tile)
        columns = slice(first + at, first + at + tile)
        weight = jnp.concatenate([ref[:, columns] for ref in shard_refs], axis=0)
        edge = jnp.dot(edge_ref[...], weight, preferred_element_type=jnp.float32)
        own_total_ref[:block, here] = inner_total_ref[:block, columns]
        own_total_ref[block:, here] = edge[:block]
        their_total_ref[:block, here] = inner_total_ref[block:, columns].astype(jnp.bfloat16)
        their_total_ref[block:, here] = edge[block:].astype(jnp.bfloat16)


def gather_sums_kernel(parts, features_ref, *rest):
    operands, out_ref = rest[:-1], rest[-1]
    shard_refs, sum_refs = operands[: -2 * parts + 1], operands[-2 * parts + 1 :]
    depth = sum(ref.shape[0] for ref in shard_refs)
    first = 0
    for part in range(parts):
        total_ref = sum_refs[part]
        columns = slice(first, first + total_ref.shape[1])
        weight = jnp.concatenate([ref[:, columns] for ref in shard_refs], axis=0)
        total = total_ref[...] + jnp.dot(
            features_ref[:, :depth], weight, preferred_element_type=jnp.float32
        )
        out_ref[:, columns] = total if part == parts - 1 else total + sum_refs[parts + part][...]
        first += total_ref.shape[1]


def finish_kernel(features_ref, total_ref, more_ref, *rest):
    shard_refs, (out_ref, held, sems) = rest[:-3], rest[-3:]
    depth = sum(ref.shape[0] for ref in shard_refs)
    width, late = out_ref.shape[1], more_ref.shape[1]
    block = out_ref.shape[0] // 2
    pieces = sems.shape[1]
    some = block // pieces
    ctx = lax.axis_index("ctx")
    copies = []
    for which, place in ((0, ctx), (1, 1 - ctx)):
        for piece in range(pieces):
            rows = slice(which * block + piece * some, which * block + (piece + 1) * some)
            for first in range(0, width, late):
                columns = slice(first, first + late)
                weight = jnp.concatenate([ref[:, columns] for ref in shard_refs], axis=0)
                total = total_ref[rows, columns] + jnp.dot(
                    features_ref[rows, depth:], weight, preferred_element_type=jnp.float32
                )
                if first + late == width:
                    total = total + more_ref[rows]
                held[rows, columns] = total.astype(jnp.bfloat16)
            there = pl.ds(pl.multiple_of(place * block + piece * some, some), some)
            copies.append(
                pltpu.make_async_copy(held.at[rows], out_ref.at[there], sems.at[which, piece])
            )
            copies[-1].start()
    for copy in copies:
        copy.wait()


SMEM = functools.partial(pl.BlockSpec, memory_space=pltpu.SMEM)
VMEM = functools.partial(pl.BlockSpec, memory_space=pltpu.VMEM)
HBM = functools.partial(pl.BlockSpec, memory_space=pltpu.HBM)


def after(value, *others):
    return lax.optimization_barrier((value, *others))[0]


def body_edge(projections, block_source, clip_ids, out_weight):
    local_rows, row_width = projections.shape
    block_rows = local_rows // 2
    heads = row_width // (3 * HEAD)
    features = heads * HEAD
    depth, width = out_weight.shape
    count = lax.axis_size("dp")
    bf16 = jnp.bfloat16

    def call(kernel, name, shape, in_specs, dtypes=None, scratch=(), out_spec=VMEM()):
        many = isinstance(shape, list)
        shapes = shape if many else [shape]
        dtypes = dtypes or [bf16] * len(shapes)
        shapes = [jax.ShapeDtypeStruct(*one) for one in zip(shapes, dtypes, strict=True)]
        return pl.pallas_call(
            kernel,
            out_shape=shapes if many else shapes[0],
            in_specs=in_specs,
            out_specs=[out_spec] * len(shapes) if many else out_spec,
            scratch_shapes=scratch,
            cost_estimate=pl.CostEstimate(flops=0, bytes_accessed=0, transcendentals=0),
            compiler_params=pltpu.CompilerParams(vmem_limit_bytes=8 * MIB),
            name=name,
        )

    def around(value, step):
        places = ring_order(count // 4)
        moves = [(here, places[(at + step) % len(places)]) for at, here in enumerate(places)]
        return lax.ppermute(
            value, "dp", [(4 * here + rest, 4 * there + rest) for here, there in moves for rest in range(4)]
        )

    def to_side(value):
        return partner(value, "dp", 1)

    def to_core(value):
        return partner(value, "dp", 0)

    def in_hbm(value):
        return pltpu.with_memory_space_constraint(value, pltpu.HBM)

    own = in_hbm(projections.reshape(2, block_rows, row_width))
    shards = {(0, False): [out_weight]}
    from_partner = pltpu.with_memory_space_constraint(to_core(own), pltpu.VMEM)
    ahead = around(out_weight, 1)
    across = to_side(out_weight)
    staged, facts = call(
        stage_kernel,
        "stage",
        [own.shape, (7, 8, 128)],
        [HBM()] * 3,
        dtypes=[bf16, jnp.int32],
        scratch=[
            pltpu.SMEM(block_source.shape, jnp.int32),
            pltpu.SMEM(clip_ids.shape, jnp.int32),
            pltpu.SemaphoreType.DMA((2,)),
            pltpu.SemaphoreType.DMA((2, 4)),
        ],
    )(in_hbm(block_source), in_hbm(clip_ids), own)
    part_heads = [heads * 8 // 16, heads * 8 // 16]
    packed_first = call(
        pack_first_kernel,
        "pack_first",
        (block_rows, 2 * HEAD * part_heads[0]),
        [VMEM()] * 3,
    )(facts, staged, from_partner)
    rows, packed_last = call(
        pack_kernel,
        "pack",
        [(2, block_rows, row_width), (block_rows, 2 * HEAD * part_heads[1])],
        [VMEM()] * 3,
        scratch=[pltpu.SemaphoreType.DMA((2,))],
    )(facts, staged, after(from_partner, packed_first))
    packed = [packed_first, packed_last]
    halos = [lax.ppermute(part, "ctx", [(0, 1), (1, 0)]) for part in packed]

    def edge_rows(part, *before):
        some = part_heads[part]
        return call(
            functools.partial(edge_kernel, sum(part_heads[:part])),
            "edge_rows",
            [(block_rows, some * HEAD), (block_rows, some // 2 * HEAD)],
            [VMEM()] * 3,
        )(after(facts, *before), rows, halos[part])

    back = around(after(out_weight, staged), -1)
    ahead = after(ahead, *packed)
    shards[1, False], shards[0, True] = [ahead], [across]
    second = around(after(ahead, across), 1)
    across = to_side(ahead)
    inner, inner_other = call(
        inner_kernel,
        "inner_rows",
        [(block_rows, features), (block_rows, features // 2)],
        [VMEM()] * 2,
    )(after(facts, ahead), rows)
    theirs = [to_core(inner_other)]

    back = after(back, inner)
    shards[3, False] = [back]
    back_across = to_side(back)
    shards[1, True] = [across]
    early = list(shards)
    origins = [*early, (2, False), (3, True), (2, True)]
    inner_total, inner_left = call(
        functools.partial(inner_project_kernel, origins[:-1], len(early)),
        "inner_project",
        [(local_rows, width), (local_rows, (len(origins) - 1 - len(early)) * depth)],
        [VMEM()] * (2 + len(early)),
        dtypes=[jnp.float32, bf16],
        scratch=[pltpu.VMEM((local_rows, len(early) * depth), bf16)],
    )(inner, *theirs, *[shards[origin][0] for origin in early])
    edges, edge_others = zip(*[edge_rows(part) for part in range(len(part_heads))], strict=True)
    second = after(second, inner_total, edges[0])
    cut = depth // 8 * 5
    shards[2, False] = [second]
    shards[3, True] = [back_across]
    shards[2, True] = [around(after(across, edges[0])[:cut], 1), to_side(second[cut:])]
    theirs = [to_core(part) for part in edge_others]

    more = [shards[origin][0] for origin in origins[len(early) : -1]]
    inner_total = call(
        add_products_kernel,
        "add_products",
        inner_total.shape,
        [VMEM()] * (2 + len(more)),
        dtypes=[jnp.float32],
    )(inner_left, inner_total, *more)
    theirs[-1] = after(theirs[-1], inner_total)
    arranged, last_features = call(
        functools.partial(arrange_kernel, origins, len(edges)),
        "arrange",
        [(local_rows, (len(origins) - 1) * depth), (local_rows, 2 * depth)],
        [VMEM()] * (1 + len(edges) + len(theirs)),
        scratch=[
            pltpu.VMEM((block_rows, features), bf16),
            pltpu.VMEM((block_rows, features // 2), bf16),
        ],
    )(inner, *edges, *theirs)
    last = shards[origins[-1]]
    last_swapped = [to_core(piece) for piece in last]
    pieces = [piece for origin in origins[:-1] for piece in shards[origin]]
    own_totals, mores = [], []
    parts = 3
    for part in range(parts):
        columns = width // parts
        own_total, their_total = call(
            functools.partial(project_kernel, part * columns),
            "project",
            [(local_rows, columns)] * 2,
            [VMEM()] * (2 + len(pieces)),
            dtypes=[jnp.float32, bf16],
        )(arranged, inner_total, *pieces)
        own_totals.append(own_total)
        if part == parts - 1:
            their_total = after(their_total, *last)
        mores.append(to_core(their_total))
    total = call(
        functools.partial(gather_sums_kernel, parts),
        "gather_sums",
        (local_rows, width),
        [VMEM()] * (len(last) + 2 * parts),
        dtypes=[jnp.float32],
    )(last_features, *last, *own_totals, *mores[:-1])
    return call(
        finish_kernel,
        "finish",
        (local_rows, width),
        [VMEM()] * (3 + len(last)),
        scratch=[pltpu.VMEM((local_rows, width), bf16), pltpu.SemaphoreType.DMA((2, 2))],
        out_spec=HBM(),
    )(last_features, total, mores[-1], *last_swapped)


def body(projections, block_source, clip_ids, out_weight):
    heads = projections.shape[1] // (3 * HEAD)
    two_and_two = lax.axis_size("ctx") == 2 and block_source.shape[2] == 2
    whole_tiles = out_weight.shape[0] % HEAD == 0 and heads % 16 == 0
    if two_and_two and whole_tiles and lax.axis_size("dp") == 16:
        return body_edge(projections, block_source, clip_ids, out_weight)
    return body_general(projections, block_source, clip_ids, out_weight)


def solution(mesh):
    return jax.shard_map(
        body,
        mesh=mesh,
        in_specs=(P(("dp", "ctx"), None), P("dp", "ctx", None), P("dp", None), P("dp", None)),
        out_specs=P(("dp", "ctx"), None),
        check_vma=False,
    )
```

```python
import functools
import math

import jax
import jax.numpy as jnp
from jax import lax
from jax.experimental import pallas as pl
from jax.experimental.pallas import tpu as pltpu
from jax.sharding import PartitionSpec as P

HEAD = 128


big_negative = -1e30
MIB = 1 << 20


def partner(value, axis, bit):
    mask = 2**bit
    pairs = [(source, source ^ mask) for source in range(lax.axis_size(axis))]
    return lax.ppermute(value, axis, pairs)


def soft_weights(scores, allowed):
    masked = jnp.where(allowed, scores, big_negative)
    row_max = jnp.max(masked, axis=-1, keepdims=True)
    exponent = jnp.exp(masked - row_max)
    return (exponent / jnp.sum(exponent, axis=-1, keepdims=True)).astype(jnp.bfloat16)


def attend_dense(queries, key_rows, value_rows, token_clip, scaling):
    token_count, head_count, head_size = queries.shape
    step_size = min(token_count, 512)
    step_count = token_count // step_size
    query_steps = queries.reshape(step_count, step_size, head_count, head_size)
    clip_steps = token_clip.reshape(step_count, step_size)

    def one_step(arguments):
        query_block, clip_block = arguments
        scores = (
            jnp.einsum("qhe,khe->hqk", query_block, key_rows, preferred_element_type=jnp.float32)
            * scaling
        )
        allowed = (clip_block[:, None] == token_clip[None, :])[None]
        weights = soft_weights(scores, allowed)
        return jnp.einsum(
            "hqk,khe->qhe", weights, value_rows, preferred_element_type=jnp.float32
        ).astype(jnp.bfloat16)

    outputs = lax.map(one_step, (query_steps, clip_steps))
    return outputs.reshape(token_count, head_count, head_size)


def body_general(projections, block_source, clip_ids, out_weight):
    ctx_count = lax.axis_size("ctx")
    local_rows, row_width = projections.shape
    local_blocks = block_source.shape[2]
    block_rows = local_rows // local_blocks
    own_blocks = projections.reshape(local_blocks, block_rows, row_width)
    partner_blocks = partner(own_blocks, "dp", 0)
    source_ids = block_source.reshape(local_blocks)
    from_partner = source_ids // (local_blocks * ctx_count) != lax.axis_index("dp")
    chosen_slot = source_ids % local_blocks + local_blocks * from_partner.astype(jnp.int32)
    candidates = jnp.concatenate([own_blocks, partner_blocks], axis=0)
    packed = jnp.take(candidates, chosen_slot, axis=0)
    local_heads = row_width // (3 * HEAD) // ctx_count
    grouped = packed.reshape(local_rows, ctx_count, local_heads, 3 * HEAD)
    block_clip = clip_ids.reshape(-1)
    token_clip = jnp.repeat(block_clip, block_rows)
    scaling = 1.0 / math.sqrt(HEAD)
    regrouped = lax.all_to_all(grouped, "ctx", split_axis=1, concat_axis=0, tiled=True)
    token_count = regrouped.shape[0]
    item_count = regrouped.shape[2]
    features = regrouped.reshape(token_count, item_count, 3 * HEAD)
    queries = features[:, :, :HEAD]
    key_rows = features[:, :, HEAD : 2 * HEAD]
    value_rows = features[:, :, 2 * HEAD :]
    attended = attend_dense(queries, key_rows, value_rows, token_clip, scaling)
    merged = attended.reshape(local_rows * ctx_count, local_heads * HEAD)
    attention_rows = lax.all_to_all(merged, "ctx", split_axis=0, concat_axis=1, tiled=True)
    result = jnp.dot(
        attention_rows,
        lax.all_gather(out_weight, "dp", axis=0, tiled=True),
        preferred_element_type=jnp.float32,
    )
    return result.astype(jnp.bfloat16)


EDGE_AWAY, EDGE_SLOT, INNER_AWAY, INNER_SLOT, INNER_JOINS, EDGE_JOINS, CROSSES = range(7)


def stage_kernel(sources, clips, own_ref, out_ref, facts_ref, source_ref, clip_ref, few_sems, sems):
    parts = sems.shape[1]
    slots = own_ref.shape[0]
    rows = own_ref.shape[1] // parts
    few = [
        pltpu.make_async_copy(sources, source_ref, few_sems.at[0]),
        pltpu.make_async_copy(clips, clip_ref, few_sems.at[1]),
    ]
    for copy in few:
        copy.start()
    for copy in few:
        copy.wait()
    ctx, dp = lax.axis_index("ctx"), lax.axis_index("dp")
    facts = {}
    for block, away, at in ((1 - ctx, EDGE_AWAY, EDGE_SLOT), (ctx, INNER_AWAY, INNER_SLOT)):
        source = source_ref[0, 0, block]
        facts[away] = (source // (2 * slots) != dp).astype(jnp.int32)
        facts[at] = lax.rem(source, slots)

    def copies(slot):
        found = []
        for part in range(parts):
            here = (slot, pl.ds(part * rows, rows))
            found.append(
                pltpu.make_async_copy(own_ref.at[here], out_ref.at[here], sems.at[slot, part])
            )
        return found

    def used(slot):
        edge = jnp.logical_and(facts[EDGE_AWAY] == 0, facts[EDGE_SLOT] == slot)
        inner = jnp.logical_and(facts[INNER_AWAY] == 0, facts[INNER_SLOT] == slot)
        return jnp.logical_or(edge, inner)

    for slot in range(slots):

        @pl.when(used(slot))
        def _():
            for copy in copies(slot):
                copy.start()

    edge_clip = clip_ref[0, 1 + ctx]
    crosses = edge_clip == clip_ref[0, 2 - ctx]
    facts[CROSSES] = crosses.astype(jnp.int32)
    facts[EDGE_JOINS] = jnp.logical_or(crosses, edge_clip == clip_ref[0, 3 * ctx]).astype(jnp.int32)
    facts[INNER_JOINS] = (clip_ref[0, 2 * ctx] == clip_ref[0, 2 * ctx + 1]).astype(jnp.int32)
    for which, fact in facts.items():
        facts_ref[which] = jnp.full(facts_ref.shape[1:], fact, jnp.int32)
    for slot in range(slots):

        @pl.when(used(slot))
        def _():
            for copy in copies(slot):
                copy.wait()


def fact(facts_ref, which):
    return jnp.max(facts_ref[which])


def pack_first_kernel(facts_ref, own_ref, partner_ref, halo_ref):
    away, slot = fact(facts_ref, EDGE_AWAY) > 0, fact(facts_ref, EDGE_SLOT)

    def fill(ref):
        for head in range(halo_ref.shape[1] // (2 * HEAD)):
            columns = slice(head * 3 * HEAD + HEAD, (head + 1) * 3 * HEAD)
            halo_ref[:, head * 2 * HEAD : (head + 1) * 2 * HEAD] = ref[slot, :, columns]

    @pl.when(away)
    def _():
        fill(partner_ref)

    @pl.when(jnp.logical_not(away))
    def _():
        fill(own_ref)


def pack_kernel(facts_ref, own_ref, partner_ref, rows_ref, halo_ref, sems):
    for which, away, at in ((1, EDGE_AWAY, EDGE_SLOT), (0, INNER_AWAY, INNER_SLOT)):
        away, slot = fact(facts_ref, away) > 0, fact(facts_ref, at)

        @pl.when(jnp.logical_not(away))
        def _():
            pltpu.make_async_copy(own_ref.at[slot], rows_ref.at[which], sems.at[which]).start()

        @pl.when(away)
        def _():
            pltpu.make_async_copy(partner_ref.at[slot], rows_ref.at[which], sems.at[which]).start()

    pltpu.make_async_copy(own_ref.at[0], rows_ref.at[1], sems.at[1]).wait()
    heads = halo_ref.shape[1] // (2 * HEAD)
    skipped = rows_ref.shape[2] // (3 * HEAD) - heads
    for head in range(heads):
        first = (skipped + head) * 3 * HEAD + HEAD
        halo_ref[:, head * 2 * HEAD : (head + 1) * 2 * HEAD] = rows_ref[
            1, :, first : first + 2 * HEAD
        ]
    pltpu.make_async_copy(own_ref.at[0], rows_ref.at[0], sems.at[0]).wait()


def attend(heads, load_queries, load_own, load_more, allowed, out_ref, other_ref):
    scaling = math.log2(math.e) / math.sqrt(HEAD)
    contract_last = (((1,), (1,)), ((), ()))
    ones = jnp.ones((2 * out_ref.shape[0], HEAD), jnp.bfloat16)
    odd_core = lax.rem(lax.axis_index("dp"), 2) == 1
    for start in range(0, heads, 4):
        group = min(4, heads - start)
        scores = []
        for head in range(start, start + group):
            queries = load_queries(head)
            pair = []
            for loader in (load_own, load_more):
                pair.append(
                    lax.dot_general(
                        queries, loader(head, 0), contract_last, preferred_element_type=jnp.float32
                    )
                    * scaling
                )
            scores.append(pair)
        weights = []
        for own, more in scores:
            more = jnp.where(allowed, more, big_negative)
            row_max = jnp.max(jnp.maximum(own, more), axis=-1, keepdims=True)
            weights.append(
                jnp.concatenate(
                    [
                        jnp.exp2(own - row_max).astype(jnp.bfloat16),
                        jnp.exp2(more - row_max).astype(jnp.bfloat16),
                    ],
                    axis=1,
                )
            )
        outs = []
        for head in range(start, start + group):
            values = jnp.concatenate([load_own(head, 1), load_more(head, 1)], axis=0)
            sums = jnp.dot(
                weights[head - start],
                jnp.concatenate([values, ones], axis=1),
                preferred_element_type=jnp.float32,
            )
            outs.append(sums[:, :HEAD] / sums[:, HEAD:])
            out_ref[:, head * HEAD : (head + 1) * HEAD] = outs[-1].astype(jnp.bfloat16)
        for pair in range(group // 2):
            at = (start // 2 + pair) * HEAD
            other = jnp.where(odd_core, outs[2 * pair], outs[2 * pair + 1])
            other_ref[:, at : at + HEAD] = other.astype(jnp.bfloat16)


def inner_kernel(facts_ref, rows_ref, out_ref, other_ref):
    allowed = fact(facts_ref, INNER_JOINS) > 0

    def loader(block):
        def get(head, which):
            first = (head * 3 + 1 + which) * HEAD
            return rows_ref[block, :, first : first + HEAD]

        return get

    attend(
        out_ref.shape[1] // HEAD,
        lambda head: loader(0)(head, -1),
        loader(0),
        loader(1),
        allowed,
        out_ref,
        other_ref,
    )


def edge_kernel(first_head, facts_ref, rows_ref, halo_ref, out_ref, other_ref):
    crosses, allowed = fact(facts_ref, CROSSES) > 0, fact(facts_ref, EDGE_JOINS) > 0

    def load_own(head, which):
        first = ((first_head + head) * 3 + 1 + which) * HEAD
        return rows_ref[1, :, first : first + HEAD]

    def load_more(head, which):
        first = ((first_head + head) * 3 + 1 + which) * HEAD
        at = (2 * head + which) * HEAD
        return jnp.where(crosses, halo_ref[:, at : at + HEAD], rows_ref[0, :, first : first + HEAD])

    attend(
        out_ref.shape[1] // HEAD,
        lambda head: load_own(head, -1),
        load_own,
        load_more,
        allowed,
        out_ref,
        other_ref,
    )


def ring_order(lines):
    return list(range(0, lines, 2)) + list(range(1, lines, 2))[::-1]


def shard_places(origins, depth):
    index = lax.axis_index("dp")
    core, side, line = lax.rem(index, 2), lax.rem(index // 2, 2), index // 4
    places = ring_order(lax.axis_size("dp") // 4)
    found = []
    for steps, other_side in origins:
        from_line = line
        for at, place in enumerate(places):
            from_line = jnp.where(line == place, places[at - steps], from_line)
        pair = from_line * 2 + (1 - side if other_side else side)
        columns = [pair * 2 + core, pair * 2 + 1 - core, pair]
        found.append([pl.ds(pl.multiple_of(column * depth, depth), depth) for column in columns])
    return found


def inner_project_kernel(origins, early, inner_ref, their_ref, *rest):
    shard_refs, (total_ref, left_ref, features) = rest[:-3], rest[-3:]
    block = inner_ref.shape[0]
    depth = left_ref.shape[1] // (len(origins) - early)
    for number, (here, _, there) in enumerate(shard_places(origins, depth)):
        ref, at = (features, number) if number < early else (left_ref, number - early)
        ref[:block, at * depth : (at + 1) * depth] = inner_ref[:, here]
        ref[block:, at * depth : (at + 1) * depth] = their_ref[:, there]
    tile = 2 * HEAD
    for first in range(0, total_ref.shape[1], tile):
        columns = slice(first, first + tile)
        weight = jnp.concatenate([ref[:, columns] for ref in shard_refs], axis=0)
        total_ref[:, columns] = jnp.dot(
            features[...], weight, preferred_element_type=jnp.float32
        )


def add_products_kernel(left_ref, inner_total_ref, *rest):
    shard_refs, total_ref = rest[:-1], rest[-1]
    tile = 2 * HEAD
    for first in range(0, total_ref.shape[1], tile):
        columns = slice(first, first + tile)
        weight = jnp.concatenate([ref[:, columns] for ref in shard_refs], axis=0)
        total_ref[:, columns] = inner_total_ref[:, columns] + jnp.dot(
            left_ref[...], weight, preferred_element_type=jnp.float32
        )


def arrange_kernel(origins, parts, inner_ref, *refs):
    edge_refs, their_refs = refs[:parts], refs[parts : 2 * parts]
    out_ref, last_ref, edge_rows, their_rows = refs[2 * parts :]
    for some_refs, held in ((edge_refs, edge_rows), (their_refs, their_rows)):
        first = 0
        for ref in some_refs:
            held[:, first : first + ref.shape[1]] = ref[...]
            first += ref.shape[1]
    block, depth = last_ref.shape[0] // 2, last_ref.shape[1] // 2
    places = shard_places(origins, depth)
    for number, (here, _, there) in enumerate(places[:-1]):
        at = slice(number * depth, (number + 1) * depth)
        out_ref[:block, at] = edge_rows[:, here]
        out_ref[block:, at] = their_rows[:, there]
    for number, here in enumerate(places[-1][:2]):
        at = slice(number * depth, (number + 1) * depth)
        last_ref[:block, at] = inner_ref[:, here]
        last_ref[block:, at] = edge_rows[:, here]


def project_kernel(first, edge_ref, inner_total_ref, *rest):
    shard_refs, (own_total_ref, their_total_ref) = rest[:-2], rest[-2:]
    block = own_total_ref.shape[0] // 2
    tile = 2 * HEAD
    for at in range(0, own_total_ref.shape[1], tile):
        here = slice(at, at + tile)
        columns = slice(first + at, first + at + tile)
        weight = jnp.concatenate([ref[:, columns] for ref in shard_refs], axis=0)
        edge = jnp.dot(edge_ref[...], weight, preferred_element_type=jnp.float32)
        own_total_ref[:block, here] = inner_total_ref[:block, columns]
        own_total_ref[block:, here] = edge[:block]
        their_total_ref[:block, here] = inner_total_ref[block:, columns].astype(jnp.bfloat16)
        their_total_ref[block:, here] = edge[block:].astype(jnp.bfloat16)


def gather_sums_kernel(parts, features_ref, *rest):
    operands, out_ref = rest[:-1], rest[-1]
    shard_refs, sum_refs = operands[: -2 * parts + 1], operands[-2 * parts + 1 :]
    depth = sum(ref.shape[0] for ref in shard_refs)
    first = 0
    for part in range(parts):
        total_ref = sum_refs[part]
        columns = slice(first, first + total_ref.shape[1])
        weight = jnp.concatenate([ref[:, columns] for ref in shard_refs], axis=0)
        total = total_ref[...] + jnp.dot(
            features_ref[:, :depth], weight, preferred_element_type=jnp.float32
        )
        out_ref[:, columns] = total if part == parts - 1 else total + sum_refs[parts + part][...]
        first += total_ref.shape[1]


def finish_kernel(features_ref, total_ref, more_ref, *rest):
    shard_refs, (out_ref, held, sems) = rest[:-3], rest[-3:]
    depth = sum(ref.shape[0] for ref in shard_refs)
    width, late = out_ref.shape[1], more_ref.shape[1]
    block = out_ref.shape[0] // 2
    pieces = sems.shape[1]
    some = block // pieces
    ctx = lax.axis_index("ctx")
    copies = []
    for which, place in ((0, ctx), (1, 1 - ctx)):
        for piece in range(pieces):
            rows = slice(which * block + piece * some, which * block + (piece + 1) * some)
            for first in range(0, width, late):
                columns = slice(first, first + late)
                weight = jnp.concatenate([ref[:, columns] for ref in shard_refs], axis=0)
                total = total_ref[rows, columns] + jnp.dot(
                    features_ref[rows, depth:], weight, preferred_element_type=jnp.float32
                )
                if first + late == width:
                    total = total + more_ref[rows]
                held[rows, columns] = total.astype(jnp.bfloat16)
            there = pl.ds(pl.multiple_of(place * block + piece * some, some), some)
            copies.append(
                pltpu.make_async_copy(held.at[rows], out_ref.at[there], sems.at[which, piece])
            )
            copies[-1].start()
    for copy in copies:
        copy.wait()


SMEM = functools.partial(pl.BlockSpec, memory_space=pltpu.SMEM)
VMEM = functools.partial(pl.BlockSpec, memory_space=pltpu.VMEM)
HBM = functools.partial(pl.BlockSpec, memory_space=pltpu.HBM)


def after(value, *others):
    return lax.optimization_barrier((value, *others))[0]


def body_edge(projections, block_source, clip_ids, out_weight):
    local_rows, row_width = projections.shape
    block_rows = local_rows // 2
    heads = row_width // (3 * HEAD)
    features = heads * HEAD
    depth, width = out_weight.shape
    count = lax.axis_size("dp")
    bf16 = jnp.bfloat16

    def call(kernel, name, shape, in_specs, dtypes=None, scratch=(), out_spec=VMEM()):
        many = isinstance(shape, list)
        shapes = shape if many else [shape]
        dtypes = dtypes or [bf16] * len(shapes)
        shapes = [jax.ShapeDtypeStruct(*one) for one in zip(shapes, dtypes, strict=True)]
        return pl.pallas_call(
            kernel,
            out_shape=shapes if many else shapes[0],
            in_specs=in_specs,
            out_specs=[out_spec] * len(shapes) if many else out_spec,
            scratch_shapes=scratch,
            cost_estimate=pl.CostEstimate(flops=0, bytes_accessed=0, transcendentals=0),
            compiler_params=pltpu.CompilerParams(vmem_limit_bytes=8 * MIB),
            name=name,
        )

    def around(value, step):
        places = ring_order(count // 4)
        moves = [(here, places[(at + step) % len(places)]) for at, here in enumerate(places)]
        return lax.ppermute(
            value, "dp", [(4 * here + rest, 4 * there + rest) for here, there in moves for rest in range(4)]
        )

    def to_side(value):
        return partner(value, "dp", 1)

    def to_core(value):
        return partner(value, "dp", 0)

    def in_hbm(value):
        return pltpu.with_memory_space_constraint(value, pltpu.HBM)

    own = in_hbm(projections.reshape(2, block_rows, row_width))
    shards = {(0, False): [out_weight]}
    from_partner = pltpu.with_memory_space_constraint(to_core(own), pltpu.VMEM)
    ahead = around(out_weight, 1)
    across = to_side(out_weight)
    staged, facts = call(
        stage_kernel,
        "stage",
        [own.shape, (7, 8, 128)],
        [HBM()] * 3,
        dtypes=[bf16, jnp.int32],
        scratch=[
            pltpu.SMEM(block_source.shape, jnp.int32),
            pltpu.SMEM(clip_ids.shape, jnp.int32),
            pltpu.SemaphoreType.DMA((2,)),
            pltpu.SemaphoreType.DMA((2, 4)),
        ],
    )(in_hbm(block_source), in_hbm(clip_ids), own)
    part_heads = [heads * 8 // 16, heads * 8 // 16]
    packed_first = call(
        pack_first_kernel,
        "pack_first",
        (block_rows, 2 * HEAD * part_heads[0]),
        [VMEM()] * 3,
    )(facts, staged, from_partner)
    rows, packed_last = call(
        pack_kernel,
        "pack",
        [(2, block_rows, row_width), (block_rows, 2 * HEAD * part_heads[1])],
        [VMEM()] * 3,
        scratch=[pltpu.SemaphoreType.DMA((2,))],
    )(facts, staged, after(from_partner, packed_first))
    packed = [packed_first, packed_last]
    halos = [lax.ppermute(part, "ctx", [(0, 1), (1, 0)]) for part in packed]

    def edge_rows(part, *before):
        some = part_heads[part]
        return call(
            functools.partial(edge_kernel, sum(part_heads[:part])),
            "edge_rows",
            [(block_rows, some * HEAD), (block_rows, some // 2 * HEAD)],
            [VMEM()] * 3,
        )(after(facts, *before), rows, halos[part])

    back = around(after(out_weight, staged), -1)
    ahead = after(ahead, *packed)
    shards[1, False], shards[0, True] = [ahead], [across]
    second = around(after(ahead, across), 1)
    across = to_side(ahead)
    inner, inner_other = call(
        inner_kernel,
        "inner_rows",
        [(block_rows, features), (block_rows, features // 2)],
        [VMEM()] * 2,
    )(after(facts, ahead), rows)
    theirs = [to_core(inner_other)]

    back = after(back, inner)
    shards[3, False] = [back]
    back_across = to_side(back)
    shards[1, True] = [across]
    early = list(shards)
    origins = [*early, (2, False), (3, True), (2, True)]
    inner_total, inner_left = call(
        functools.partial(inner_project_kernel, origins[:-1], len(early)),
        "inner_project",
        [(local_rows, width), (local_rows, (len(origins) - 1 - len(early)) * depth)],
        [VMEM()] * (2 + len(early)),
        dtypes=[jnp.float32, bf16],
        scratch=[pltpu.VMEM((local_rows, len(early) * depth), bf16)],
    )(inner, *theirs, *[shards[origin][0] for origin in early])
    edges, edge_others = zip(*[edge_rows(part) for part in range(len(part_heads))], strict=True)
    second = after(second, inner_total, edges[0])
    cut = depth // 8 * 5
    shards[2, False] = [second]
    shards[3, True] = [back_across]
    shards[2, True] = [around(after(across, edges[0])[:cut], 1), to_side(second[cut:])]
    theirs = [to_core(part) for part in edge_others]

    more = [shards[origin][0] for origin in origins[len(early) : -1]]
    inner_total = call(
        add_products_kernel,
        "add_products",
        inner_total.shape,
        [VMEM()] * (2 + len(more)),
        dtypes=[jnp.float32],
    )(inner_left, inner_total, *more)
    theirs[-1] = after(theirs[-1], inner_total)
    arranged, last_features = call(
        functools.partial(arrange_kernel, origins, len(edges)),
        "arrange",
        [(local_rows, (len(origins) - 1) * depth), (local_rows, 2 * depth)],
        [VMEM()] * (1 + len(edges) + len(theirs)),
        scratch=[
            pltpu.VMEM((block_rows, features), bf16),
            pltpu.VMEM((block_rows, features // 2), bf16),
        ],
    )(inner, *edges, *theirs)
    last = shards[origins[-1]]
    last_swapped = [to_core(piece) for piece in last]
    pieces = [piece for origin in origins[:-1] for piece in shards[origin]]
    own_totals, mores = [], []
    parts = 3
    for part in range(parts):
        columns = width // parts
        own_total, their_total = call(
            functools.partial(project_kernel, part * columns),
            "project",
            [(local_rows, columns)] * 2,
            [VMEM()] * (2 + len(pieces)),
            dtypes=[jnp.float32, bf16],
        )(arranged, inner_total, *pieces)
        own_totals.append(own_total)
        if part == parts - 1:
            their_total = after(their_total, *last)
        mores.append(to_core(their_total))
    total = call(
        functools.partial(gather_sums_kernel, parts),
        "gather_sums",
        (local_rows, width),
        [VMEM()] * (len(last) + 2 * parts),
        dtypes=[jnp.float32],
    )(last_features, *last, *own_totals, *mores[:-1])
    return call(
        finish_kernel,
        "finish",
        (local_rows, width),
        [VMEM()] * (3 + len(last)),
        scratch=[pltpu.VMEM((local_rows, width), bf16), pltpu.SemaphoreType.DMA((2, 2))],
        out_spec=HBM(),
    )(last_features, total, mores[-1], *last_swapped)


def body(projections, block_source, clip_ids, out_weight):
    heads = projections.shape[1] // (3 * HEAD)
    two_and_two = lax.axis_size("ctx") == 2 and block_source.shape[2] == 2
    whole_tiles = out_weight.shape[0] % HEAD == 0 and heads % 16 == 0
    if two_and_two and whole_tiles and lax.axis_size("dp") == 16:
        return body_edge(projections, block_source, clip_ids, out_weight)
    return body_general(projections, block_source, clip_ids, out_weight)


def solution(mesh):
    return jax.shard_map(
        body,
        mesh=mesh,
        in_specs=(P(("dp", "ctx"), None), P("dp", "ctx", None), P("dp", None), P("dp", None)),
        out_specs=P(("dp", "ctx"), None),
        check_vma=False,
    )
```

```python
import functools
import math

import jax
import jax.numpy as jnp
from jax import lax
from jax.experimental import pallas as pl
from jax.experimental.pallas import tpu as pltpu
from jax.sharding import PartitionSpec as P

HEAD = 128


big_negative = -1e30
MIB = 1 << 20


def partner(value, axis, bit):
    mask = 2**bit
    pairs = [(source, source ^ mask) for source in range(lax.axis_size(axis))]
    return lax.ppermute(value, axis, pairs)


def soft_weights(scores, allowed):
    masked = jnp.where(allowed, scores, big_negative)
    row_max = jnp.max(masked, axis=-1, keepdims=True)
    exponent = jnp.exp(masked - row_max)
    return (exponent / jnp.sum(exponent, axis=-1, keepdims=True)).astype(jnp.bfloat16)


def attend_dense(queries, key_rows, value_rows, token_clip, scaling):
    token_count, head_count, head_size = queries.shape
    step_size = min(token_count, 512)
    step_count = token_count // step_size
    query_steps = queries.reshape(step_count, step_size, head_count, head_size)
    clip_steps = token_clip.reshape(step_count, step_size)

    def one_step(arguments):
        query_block, clip_block = arguments
        scores = (
            jnp.einsum("qhe,khe->hqk", query_block, key_rows, preferred_element_type=jnp.float32)
            * scaling
        )
        allowed = (clip_block[:, None] == token_clip[None, :])[None]
        weights = soft_weights(scores, allowed)
        return jnp.einsum(
            "hqk,khe->qhe", weights, value_rows, preferred_element_type=jnp.float32
        ).astype(jnp.bfloat16)

    outputs = lax.map(one_step, (query_steps, clip_steps))
    return outputs.reshape(token_count, head_count, head_size)


def body_general(projections, block_source, clip_ids, out_weight):
    ctx_count = lax.axis_size("ctx")
    local_rows, row_width = projections.shape
    local_blocks = block_source.shape[2]
    block_rows = local_rows // local_blocks
    own_blocks = projections.reshape(local_blocks, block_rows, row_width)
    partner_blocks = partner(own_blocks, "dp", 0)
    source_ids = block_source.reshape(local_blocks)
    from_partner = source_ids // (local_blocks * ctx_count) != lax.axis_index("dp")
    chosen_slot = source_ids % local_blocks + local_blocks * from_partner.astype(jnp.int32)
    candidates = jnp.concatenate([own_blocks, partner_blocks], axis=0)
    packed = jnp.take(candidates, chosen_slot, axis=0)
    local_heads = row_width // (3 * HEAD) // ctx_count
    grouped = packed.reshape(local_rows, ctx_count, local_heads, 3 * HEAD)
    block_clip = clip_ids.reshape(-1)
    token_clip = jnp.repeat(block_clip, block_rows)
    scaling = 1.0 / math.sqrt(HEAD)
    regrouped = lax.all_to_all(grouped, "ctx", split_axis=1, concat_axis=0, tiled=True)
    token_count = regrouped.shape[0]
    item_count = regrouped.shape[2]
    features = regrouped.reshape(token_count, item_count, 3 * HEAD)
    queries = features[:, :, :HEAD]
    key_rows = features[:, :, HEAD : 2 * HEAD]
    value_rows = features[:, :, 2 * HEAD :]
    attended = attend_dense(queries, key_rows, value_rows, token_clip, scaling)
    merged = attended.reshape(local_rows * ctx_count, local_heads * HEAD)
    attention_rows = lax.all_to_all(merged, "ctx", split_axis=0, concat_axis=1, tiled=True)
    result = jnp.dot(
        attention_rows,
        lax.all_gather(out_weight, "dp", axis=0, tiled=True),
        preferred_element_type=jnp.float32,
    )
    return result.astype(jnp.bfloat16)


EDGE_AWAY, EDGE_SLOT, INNER_AWAY, INNER_SLOT, INNER_JOINS, EDGE_JOINS, CROSSES = range(7)


def stage_kernel(sources, clips, own_ref, out_ref, facts_ref, source_ref, clip_ref, few_sems, sems):
    parts = sems.shape[1]
    slots = own_ref.shape[0]
    rows = own_ref.shape[1] // parts
    few = [
        pltpu.make_async_copy(sources, source_ref, few_sems.at[0]),
        pltpu.make_async_copy(clips, clip_ref, few_sems.at[1]),
    ]
    for copy in few:
        copy.start()
    for copy in few:
        copy.wait()
    ctx, dp = lax.axis_index("ctx"), lax.axis_index("dp")
    facts = {}
    for block, away, at in ((1 - ctx, EDGE_AWAY, EDGE_SLOT), (ctx, INNER_AWAY, INNER_SLOT)):
        source = source_ref[0, 0, block]
        facts[away] = (source // (2 * slots) != dp).astype(jnp.int32)
        facts[at] = lax.rem(source, slots)

    def copies(slot):
        found = []
        for part in range(parts):
            here = (slot, pl.ds(part * rows, rows))
            found.append(
                pltpu.make_async_copy(own_ref.at[here], out_ref.at[here], sems.at[slot, part])
            )
        return found

    def used(slot):
        edge = jnp.logical_and(facts[EDGE_AWAY] == 0, facts[EDGE_SLOT] == slot)
        inner = jnp.logical_and(facts[INNER_AWAY] == 0, facts[INNER_SLOT] == slot)
        return jnp.logical_or(edge, inner)

    for slot in range(slots):

        @pl.when(used(slot))
        def _():
            for copy in copies(slot):
                copy.start()

    edge_clip = clip_ref[0, 1 + ctx]
    crosses = edge_clip == clip_ref[0, 2 - ctx]
    facts[CROSSES] = crosses.astype(jnp.int32)
    facts[EDGE_JOINS] = jnp.logical_or(crosses, edge_clip == clip_ref[0, 3 * ctx]).astype(jnp.int32)
    facts[INNER_JOINS] = (clip_ref[0, 2 * ctx] == clip_ref[0, 2 * ctx + 1]).astype(jnp.int32)
    for which, fact in facts.items():
        facts_ref[which] = jnp.full(facts_ref.shape[1:], fact, jnp.int32)
    for slot in range(slots):

        @pl.when(used(slot))
        def _():
            for copy in copies(slot):
                copy.wait()


def fact(facts_ref, which):
    return jnp.max(facts_ref[which])


def pack_first_kernel(facts_ref, own_ref, partner_ref, halo_ref):
    away, slot = fact(facts_ref, EDGE_AWAY) > 0, fact(facts_ref, EDGE_SLOT)

    def fill(ref):
        for head in range(halo_ref.shape[1] // (2 * HEAD)):
            columns = slice(head * 3 * HEAD + HEAD, (head + 1) * 3 * HEAD)
            halo_ref[:, head * 2 * HEAD : (head + 1) * 2 * HEAD] = ref[slot, :, columns]

    @pl.when(away)
    def _():
        fill(partner_ref)

    @pl.when(jnp.logical_not(away))
    def _():
        fill(own_ref)


def pack_kernel(facts_ref, own_ref, partner_ref, rows_ref, halo_ref, sems):
    for which, away, at in ((1, EDGE_AWAY, EDGE_SLOT), (0, INNER_AWAY, INNER_SLOT)):
        away, slot = fact(facts_ref, away) > 0, fact(facts_ref, at)

        @pl.when(jnp.logical_not(away))
        def _():
            pltpu.make_async_copy(own_ref.at[slot], rows_ref.at[which], sems.at[which]).start()

        @pl.when(away)
        def _():
            pltpu.make_async_copy(partner_ref.at[slot], rows_ref.at[which], sems.at[which]).start()

    pltpu.make_async_copy(own_ref.at[0], rows_ref.at[1], sems.at[1]).wait()
    heads = halo_ref.shape[1] // (2 * HEAD)
    skipped = rows_ref.shape[2] // (3 * HEAD) - heads
    for head in range(heads):
        first = (skipped + head) * 3 * HEAD + HEAD
        halo_ref[:, head * 2 * HEAD : (head + 1) * 2 * HEAD] = rows_ref[
            1, :, first : first + 2 * HEAD
        ]
    pltpu.make_async_copy(own_ref.at[0], rows_ref.at[0], sems.at[0]).wait()


def attend(heads, load_queries, load_own, load_more, allowed, out_ref, other_ref):
    scaling = math.log2(math.e) / math.sqrt(HEAD)
    contract_last = (((1,), (1,)), ((), ()))
    ones = jnp.ones((2 * out_ref.shape[0], HEAD), jnp.bfloat16)
    odd_core = lax.rem(lax.axis_index("dp"), 2) == 1
    for start in range(0, heads, 8):
        group = min(8, heads - start)
        scores = []
        for head in range(start, start + group):
            queries = load_queries(head)
            pair = []
            for loader in (load_own, load_more):
                pair.append(
                    lax.dot_general(
                        queries, loader(head, 0), contract_last, preferred_element_type=jnp.float32
                    )
                    * scaling
                )
            scores.append(pair)
        weights = []
        for own, more in scores:
            more = jnp.where(allowed, more, big_negative)
            row_max = jnp.max(jnp.maximum(own, more), axis=-1, keepdims=True)
            weights.append(
                jnp.concatenate(
                    [
                        jnp.exp2(own - row_max).astype(jnp.bfloat16),
                        jnp.exp2(more - row_max).astype(jnp.bfloat16),
                    ],
                    axis=1,
                )
            )
        outs = []
        for head in range(start, start + group):
            values = jnp.concatenate([load_own(head, 1), load_more(head, 1)], axis=0)
            sums = jnp.dot(
                weights[head - start],
                jnp.concatenate([values, ones], axis=1),
                preferred_element_type=jnp.float32,
            )
            outs.append(sums[:, :HEAD] / sums[:, HEAD:])
            out_ref[:, head * HEAD : (head + 1) * HEAD] = outs[-1].astype(jnp.bfloat16)
        for pair in range(group // 2):
            at = (start // 2 + pair) * HEAD
            other = jnp.where(odd_core, outs[2 * pair], outs[2 * pair + 1])
            other_ref[:, at : at + HEAD] = other.astype(jnp.bfloat16)


def inner_kernel(facts_ref, rows_ref, out_ref, other_ref):
    allowed = fact(facts_ref, INNER_JOINS) > 0

    def loader(block):
        def get(head, which):
            first = (head * 3 + 1 + which) * HEAD
            return rows_ref[block, :, first : first + HEAD]

        return get

    attend(
        out_ref.shape[1] // HEAD,
        lambda head: loader(0)(head, -1),
        loader(0),
        loader(1),
        allowed,
        out_ref,
        other_ref,
    )


def edge_kernel(first_head, facts_ref, rows_ref, halo_ref, out_ref, other_ref):
    crosses, allowed = fact(facts_ref, CROSSES) > 0, fact(facts_ref, EDGE_JOINS) > 0

    def load_own(head, which):
        first = ((first_head + head) * 3 + 1 + which) * HEAD
        return rows_ref[1, :, first : first + HEAD]

    def load_more(head, which):
        first = ((first_head + head) * 3 + 1 + which) * HEAD
        at = (2 * head + which) * HEAD
        return jnp.where(crosses, halo_ref[:, at : at + HEAD], rows_ref[0, :, first : first + HEAD])

    attend(
        out_ref.shape[1] // HEAD,
        lambda head: load_own(head, -1),
        load_own,
        load_more,
        allowed,
        out_ref,
        other_ref,
    )


def ring_order(lines):
    return list(range(0, lines, 2)) + list(range(1, lines, 2))[::-1]


def shard_places(origins, depth):
    index = lax.axis_index("dp")
    core, side, line = lax.rem(index, 2), lax.rem(index // 2, 2), index // 4
    places = ring_order(lax.axis_size("dp") // 4)
    found = []
    for steps, other_side in origins:
        from_line = line
        for at, place in enumerate(places):
            from_line = jnp.where(line == place, places[at - steps], from_line)
        pair = from_line * 2 + (1 - side if other_side else side)
        columns = [pair * 2 + core, pair * 2 + 1 - core, pair]
        found.append([pl.ds(pl.multiple_of(column * depth, depth), depth) for column in columns])
    return found


def inner_project_kernel(origins, early, inner_ref, their_ref, *rest):
    shard_refs, (total_ref, left_ref, features) = rest[:-3], rest[-3:]
    block = inner_ref.shape[0]
    depth = left_ref.shape[1] // (len(origins) - early)
    for number, (here, _, there) in enumerate(shard_places(origins, depth)):
        ref, at = (features, number) if number < early else (left_ref, number - early)
        ref[:block, at * depth : (at + 1) * depth] = inner_ref[:, here]
        ref[block:, at * depth : (at + 1) * depth] = their_ref[:, there]
    tile = 2 * HEAD
    for first in range(0, total_ref.shape[1], tile):
        columns = slice(first, first + tile)
        weight = jnp.concatenate([ref[:, columns] for ref in shard_refs], axis=0)
        total_ref[:, columns] = jnp.dot(
            features[...], weight, preferred_element_type=jnp.float32
        )


def add_products_kernel(left_ref, inner_total_ref, *rest):
    shard_refs, total_ref = rest[:-1], rest[-1]
    tile = 2 * HEAD
    for first in range(0, total_ref.shape[1], tile):
        columns = slice(first, first + tile)
        weight = jnp.concatenate([ref[:, columns] for ref in shard_refs], axis=0)
        total_ref[:, columns] = inner_total_ref[:, columns] + jnp.dot(
            left_ref[...], weight, preferred_element_type=jnp.float32
        )


def arrange_kernel(origins, parts, inner_ref, *refs):
    edge_refs, their_refs = refs[:parts], refs[parts : 2 * parts]
    out_ref, last_ref, edge_rows, their_rows = refs[2 * parts :]
    for some_refs, held in ((edge_refs, edge_rows), (their_refs, their_rows)):
        first = 0
        for ref in some_refs:
            held[:, first : first + ref.shape[1]] = ref[...]
            first += ref.shape[1]
    block, depth = last_ref.shape[0] // 2, last_ref.shape[1] // 2
    places = shard_places(origins, depth)
    for number, (here, _, there) in enumerate(places[:-1]):
        at = slice(number * depth, (number + 1) * depth)
        out_ref[:block, at] = edge_rows[:, here]
        out_ref[block:, at] = their_rows[:, there]
    for number, here in enumerate(places[-1][:2]):
        at = slice(number * depth, (number + 1) * depth)
        last_ref[:block, at] = inner_ref[:, here]
        last_ref[block:, at] = edge_rows[:, here]


def project_kernel(first, edge_ref, inner_total_ref, *rest):
    shard_refs, (own_total_ref, their_total_ref) = rest[:-2], rest[-2:]
    block = own_total_ref.shape[0] // 2
    tile = 2 * HEAD
    for at in range(0, own_total_ref.shape[1], tile):
        here = slice(at, at + tile)
        columns = slice(first + at, first + at + tile)
        weight = jnp.concatenate([ref[:, columns] for ref in shard_refs], axis=0)
        edge = jnp.dot(edge_ref[...], weight, preferred_element_type=jnp.float32)
        own_total_ref[:block, here] = inner_total_ref[:block, columns]
        own_total_ref[block:, here] = edge[:block]
        their_total_ref[:block, here] = inner_total_ref[block:, columns].astype(jnp.bfloat16)
        their_total_ref[block:, here] = edge[block:].astype(jnp.bfloat16)


def gather_sums_kernel(parts, features_ref, *rest):
    operands, out_ref = rest[:-1], rest[-1]
    shard_refs, sum_refs = operands[: -2 * parts + 1], operands[-2 * parts + 1 :]
    depth = sum(ref.shape[0] for ref in shard_refs)
    first = 0
    for part in range(parts):
        total_ref = sum_refs[part]
        columns = slice(first, first + total_ref.shape[1])
        weight = jnp.concatenate([ref[:, columns] for ref in shard_refs], axis=0)
        total = total_ref[...] + jnp.dot(
            features_ref[:, :depth], weight, preferred_element_type=jnp.float32
        )
        out_ref[:, columns] = total if part == parts - 1 else total + sum_refs[parts + part][...]
        first += total_ref.shape[1]


def finish_kernel(features_ref, total_ref, more_ref, *rest):
    shard_refs, (out_ref, held, sems) = rest[:-3], rest[-3:]
    depth = sum(ref.shape[0] for ref in shard_refs)
    width, late = out_ref.shape[1], more_ref.shape[1]
    block = out_ref.shape[0] // 2
    pieces = sems.shape[1]
    some = block // pieces
    ctx = lax.axis_index("ctx")
    copies = []
    for which, place in ((0, ctx), (1, 1 - ctx)):
        for piece in range(pieces):
            rows = slice(which * block + piece * some, which * block + (piece + 1) * some)
            for first in range(0, width, late):
                columns = slice(first, first + late)
                weight = jnp.concatenate([ref[:, columns] for ref in shard_refs], axis=0)
                total = total_ref[rows, columns] + jnp.dot(
                    features_ref[rows, depth:], weight, preferred_element_type=jnp.float32
                )
                if first + late == width:
                    total = total + more_ref[rows]
                held[rows, columns] = total.astype(jnp.bfloat16)
            there = pl.ds(pl.multiple_of(place * block + piece * some, some), some)
            copies.append(
                pltpu.make_async_copy(held.at[rows], out_ref.at[there], sems.at[which, piece])
            )
            copies[-1].start()
    for copy in copies:
        copy.wait()


SMEM = functools.partial(pl.BlockSpec, memory_space=pltpu.SMEM)
VMEM = functools.partial(pl.BlockSpec, memory_space=pltpu.VMEM)
HBM = functools.partial(pl.BlockSpec, memory_space=pltpu.HBM)


def after(value, *others):
    return lax.optimization_barrier((value, *others))[0]


def body_edge(projections, block_source, clip_ids, out_weight):
    local_rows, row_width = projections.shape
    block_rows = local_rows // 2
    heads = row_width // (3 * HEAD)
    features = heads * HEAD
    depth, width = out_weight.shape
    count = lax.axis_size("dp")
    bf16 = jnp.bfloat16

    def call(kernel, name, shape, in_specs, dtypes=None, scratch=(), out_spec=VMEM()):
        many = isinstance(shape, list)
        shapes = shape if many else [shape]
        dtypes = dtypes or [bf16] * len(shapes)
        shapes = [jax.ShapeDtypeStruct(*one) for one in zip(shapes, dtypes, strict=True)]
        return pl.pallas_call(
            kernel,
            out_shape=shapes if many else shapes[0],
            in_specs=in_specs,
            out_specs=[out_spec] * len(shapes) if many else out_spec,
            scratch_shapes=scratch,
            cost_estimate=pl.CostEstimate(flops=0, bytes_accessed=0, transcendentals=0),
            compiler_params=pltpu.CompilerParams(vmem_limit_bytes=8 * MIB),
            name=name,
        )

    def around(value, step):
        places = ring_order(count // 4)
        moves = [(here, places[(at + step) % len(places)]) for at, here in enumerate(places)]
        return lax.ppermute(
            value, "dp", [(4 * here + rest, 4 * there + rest) for here, there in moves for rest in range(4)]
        )

    def to_side(value):
        return partner(value, "dp", 1)

    def to_core(value):
        return partner(value, "dp", 0)

    def in_hbm(value):
        return pltpu.with_memory_space_constraint(value, pltpu.HBM)

    own = in_hbm(projections.reshape(2, block_rows, row_width))
    shards = {(0, False): [out_weight]}
    from_partner = pltpu.with_memory_space_constraint(to_core(own), pltpu.VMEM)
    ahead = around(out_weight, 1)
    across = to_side(out_weight)
    staged, facts = call(
        stage_kernel,
        "stage",
        [own.shape, (7, 8, 128)],
        [HBM()] * 3,
        dtypes=[bf16, jnp.int32],
        scratch=[
            pltpu.SMEM(block_source.shape, jnp.int32),
            pltpu.SMEM(clip_ids.shape, jnp.int32),
            pltpu.SemaphoreType.DMA((2,)),
            pltpu.SemaphoreType.DMA((2, 4)),
        ],
    )(in_hbm(block_source), in_hbm(clip_ids), own)
    part_heads = [heads * 8 // 16, heads * 8 // 16]
    packed_first = call(
        pack_first_kernel,
        "pack_first",
        (block_rows, 2 * HEAD * part_heads[0]),
        [VMEM()] * 3,
    )(facts, staged, from_partner)
    rows, packed_last = call(
        pack_kernel,
        "pack",
        [(2, block_rows, row_width), (block_rows, 2 * HEAD * part_heads[1])],
        [VMEM()] * 3,
        scratch=[pltpu.SemaphoreType.DMA((2,))],
    )(facts, staged, after(from_partner, packed_first))
    packed = [packed_first, packed_last]
    halos = [lax.ppermute(part, "ctx", [(0, 1), (1, 0)]) for part in packed]

    def edge_rows(part, *before):
        some = part_heads[part]
        return call(
            functools.partial(edge_kernel, sum(part_heads[:part])),
            "edge_rows",
            [(block_rows, some * HEAD), (block_rows, some // 2 * HEAD)],
            [VMEM()] * 3,
        )(after(facts, *before), rows, halos[part])

    back = around(after(out_weight, staged), -1)
    ahead = after(ahead, *packed)
    shards[1, False], shards[0, True] = [ahead], [across]
    second = around(after(ahead, across), 1)
    across = to_side(ahead)
    inner, inner_other = call(
        inner_kernel,
        "inner_rows",
        [(block_rows, features), (block_rows, features // 2)],
        [VMEM()] * 2,
    )(after(facts, ahead), rows)
    theirs = [to_core(inner_other)]

    back = after(back, inner)
    shards[3, False] = [back]
    back_across = to_side(back)
    shards[1, True] = [across]
    early = list(shards)
    origins = [*early, (2, False), (3, True), (2, True)]
    inner_total, inner_left = call(
        functools.partial(inner_project_kernel, origins[:-1], len(early)),
        "inner_project",
        [(local_rows, width), (local_rows, (len(origins) - 1 - len(early)) * depth)],
        [VMEM()] * (2 + len(early)),
        dtypes=[jnp.float32, bf16],
        scratch=[pltpu.VMEM((local_rows, len(early) * depth), bf16)],
    )(inner, *theirs, *[shards[origin][0] for origin in early])
    edges, edge_others = zip(*[edge_rows(part) for part in range(len(part_heads))], strict=True)
    second = after(second, inner_total, edges[0])
    cut = depth // 8 * 5
    shards[2, False] = [second]
    shards[3, True] = [back_across]
    shards[2, True] = [around(after(across, edges[0])[:cut], 1), to_side(second[cut:])]
    theirs = [to_core(part) for part in edge_others]

    more = [shards[origin][0] for origin in origins[len(early) : -1]]
    inner_total = call(
        add_products_kernel,
        "add_products",
        inner_total.shape,
        [VMEM()] * (2 + len(more)),
        dtypes=[jnp.float32],
    )(inner_left, inner_total, *more)
    theirs[-1] = after(theirs[-1], inner_total)
    arranged, last_features = call(
        functools.partial(arrange_kernel, origins, len(edges)),
        "arrange",
        [(local_rows, (len(origins) - 1) * depth), (local_rows, 2 * depth)],
        [VMEM()] * (1 + len(edges) + len(theirs)),
        scratch=[
            pltpu.VMEM((block_rows, features), bf16),
            pltpu.VMEM((block_rows, features // 2), bf16),
        ],
    )(inner, *edges, *theirs)
    last = shards[origins[-1]]
    last_swapped = [to_core(piece) for piece in last]
    pieces = [piece for origin in origins[:-1] for piece in shards[origin]]
    own_totals, mores = [], []
    parts = 3
    for part in range(parts):
        columns = width // parts
        own_total, their_total = call(
            functools.partial(project_kernel, part * columns),
            "project",
            [(local_rows, columns)] * 2,
            [VMEM()] * (2 + len(pieces)),
            dtypes=[jnp.float32, bf16],
        )(arranged, inner_total, *pieces)
        own_totals.append(own_total)
        if part == parts - 1:
            their_total = after(their_total, *last)
        mores.append(to_core(their_total))
    total = call(
        functools.partial(gather_sums_kernel, parts),
        "gather_sums",
        (local_rows, width),
        [VMEM()] * (len(last) + 2 * parts),
        dtypes=[jnp.float32],
    )(last_features, *last, *own_totals, *mores[:-1])
    return call(
        finish_kernel,
        "finish",
        (local_rows, width),
        [VMEM()] * (3 + len(last)),
        scratch=[pltpu.VMEM((local_rows, width), bf16), pltpu.SemaphoreType.DMA((2, 2))],
        out_spec=HBM(),
    )(last_features, total, mores[-1], *last_swapped)


def body(projections, block_source, clip_ids, out_weight):
    heads = projections.shape[1] // (3 * HEAD)
    two_and_two = lax.axis_size("ctx") == 2 and block_source.shape[2] == 2
    whole_tiles = out_weight.shape[0] % HEAD == 0 and heads % 16 == 0
    if two_and_two and whole_tiles and lax.axis_size("dp") == 16:
        return body_edge(projections, block_source, clip_ids, out_weight)
    return body_general(projections, block_source, clip_ids, out_weight)


def solution(mesh):
    return jax.shard_map(
        body,
        mesh=mesh,
        in_specs=(P(("dp", "ctx"), None), P("dp", "ctx", None), P("dp", None), P("dp", None)),
        out_specs=P(("dp", "ctx"), None),
        check_vma=False,
    )
```

```python
import functools
import math

import jax
import jax.numpy as jnp
from jax import lax
from jax.experimental import pallas as pl
from jax.experimental.pallas import tpu as pltpu
from jax.sharding import PartitionSpec as P

HEAD = 128


big_negative = -1e30
MIB = 1 << 20


def partner(value, axis, bit):
    mask = 2**bit
    pairs = [(source, source ^ mask) for source in range(lax.axis_size(axis))]
    return lax.ppermute(value, axis, pairs)


def soft_weights(scores, allowed):
    masked = jnp.where(allowed, scores, big_negative)
    row_max = jnp.max(masked, axis=-1, keepdims=True)
    exponent = jnp.exp(masked - row_max)
    return (exponent / jnp.sum(exponent, axis=-1, keepdims=True)).astype(jnp.bfloat16)


def attend_dense(queries, key_rows, value_rows, token_clip, scaling):
    token_count, head_count, head_size = queries.shape
    step_size = min(token_count, 512)
    step_count = token_count // step_size
    query_steps = queries.reshape(step_count, step_size, head_count, head_size)
    clip_steps = token_clip.reshape(step_count, step_size)

    def one_step(arguments):
        query_block, clip_block = arguments
        scores = (
            jnp.einsum("qhe,khe->hqk", query_block, key_rows, preferred_element_type=jnp.float32)
            * scaling
        )
        allowed = (clip_block[:, None] == token_clip[None, :])[None]
        weights = soft_weights(scores, allowed)
        return jnp.einsum(
            "hqk,khe->qhe", weights, value_rows, preferred_element_type=jnp.float32
        ).astype(jnp.bfloat16)

    outputs = lax.map(one_step, (query_steps, clip_steps))
    return outputs.reshape(token_count, head_count, head_size)


def body_general(projections, block_source, clip_ids, out_weight):
    ctx_count = lax.axis_size("ctx")
    local_rows, row_width = projections.shape
    local_blocks = block_source.shape[2]
    block_rows = local_rows // local_blocks
    own_blocks = projections.reshape(local_blocks, block_rows, row_width)
    partner_blocks = partner(own_blocks, "dp", 0)
    source_ids = block_source.reshape(local_blocks)
    from_partner = source_ids // (local_blocks * ctx_count) != lax.axis_index("dp")
    chosen_slot = source_ids % local_blocks + local_blocks * from_partner.astype(jnp.int32)
    candidates = jnp.concatenate([own_blocks, partner_blocks], axis=0)
    packed = jnp.take(candidates, chosen_slot, axis=0)
    local_heads = row_width // (3 * HEAD) // ctx_count
    grouped = packed.reshape(local_rows, ctx_count, local_heads, 3 * HEAD)
    block_clip = clip_ids.reshape(-1)
    token_clip = jnp.repeat(block_clip, block_rows)
    scaling = 1.0 / math.sqrt(HEAD)
    regrouped = lax.all_to_all(grouped, "ctx", split_axis=1, concat_axis=0, tiled=True)
    token_count = regrouped.shape[0]
    item_count = regrouped.shape[2]
    features = regrouped.reshape(token_count, item_count, 3 * HEAD)
    queries = features[:, :, :HEAD]
    key_rows = features[:, :, HEAD : 2 * HEAD]
    value_rows = features[:, :, 2 * HEAD :]
    attended = attend_dense(queries, key_rows, value_rows, token_clip, scaling)
    merged = attended.reshape(local_rows * ctx_count, local_heads * HEAD)
    attention_rows = lax.all_to_all(merged, "ctx", split_axis=0, concat_axis=1, tiled=True)
    result = jnp.dot(
        attention_rows,
        lax.all_gather(out_weight, "dp", axis=0, tiled=True),
        preferred_element_type=jnp.float32,
    )
    return result.astype(jnp.bfloat16)


EDGE_AWAY, EDGE_SLOT, INNER_AWAY, INNER_SLOT, INNER_JOINS, EDGE_JOINS, CROSSES = range(7)


def stage_kernel(sources, clips, own_ref, out_ref, facts_ref, source_ref, clip_ref, few_sems, sems):
    parts = sems.shape[1]
    slots = own_ref.shape[0]
    rows = own_ref.shape[1] // parts
    few = [
        pltpu.make_async_copy(sources, source_ref, few_sems.at[0]),
        pltpu.make_async_copy(clips, clip_ref, few_sems.at[1]),
    ]
    for copy in few:
        copy.start()
    for copy in few:
        copy.wait()
    ctx, dp = lax.axis_index("ctx"), lax.axis_index("dp")
    facts = {}
    for block, away, at in ((1 - ctx, EDGE_AWAY, EDGE_SLOT), (ctx, INNER_AWAY, INNER_SLOT)):
        source = source_ref[0, 0, block]
        facts[away] = (source // (2 * slots) != dp).astype(jnp.int32)
        facts[at] = lax.rem(source, slots)

    def copies(slot):
        found = []
        for part in range(parts):
            here = (slot, pl.ds(part * rows, rows))
            found.append(
                pltpu.make_async_copy(own_ref.at[here], out_ref.at[here], sems.at[slot, part])
            )
        return found

    def used(slot):
        edge = jnp.logical_and(facts[EDGE_AWAY] == 0, facts[EDGE_SLOT] == slot)
        inner = jnp.logical_and(facts[INNER_AWAY] == 0, facts[INNER_SLOT] == slot)
        return jnp.logical_or(edge, inner)

    for slot in range(slots):

        @pl.when(used(slot))
        def _():
            for copy in copies(slot):
                copy.start()

    edge_clip = clip_ref[0, 1 + ctx]
    crosses = edge_clip == clip_ref[0, 2 - ctx]
    facts[CROSSES] = crosses.astype(jnp.int32)
    facts[EDGE_JOINS] = jnp.logical_or(crosses, edge_clip == clip_ref[0, 3 * ctx]).astype(jnp.int32)
    facts[INNER_JOINS] = (clip_ref[0, 2 * ctx] == clip_ref[0, 2 * ctx + 1]).astype(jnp.int32)
    for which, fact in facts.items():
        facts_ref[which] = jnp.full(facts_ref.shape[1:], fact, jnp.int32)
    for slot in range(slots):

        @pl.when(used(slot))
        def _():
            for copy in copies(slot):
                copy.wait()


def fact(facts_ref, which):
    return jnp.max(facts_ref[which])


def pack_first_kernel(facts_ref, own_ref, partner_ref, halo_ref):
    away, slot = fact(facts_ref, EDGE_AWAY) > 0, fact(facts_ref, EDGE_SLOT)

    def fill(ref):
        for head in range(halo_ref.shape[1] // (2 * HEAD)):
            columns = slice(head * 3 * HEAD + HEAD, (head + 1) * 3 * HEAD)
            halo_ref[:, head * 2 * HEAD : (head + 1) * 2 * HEAD] = ref[slot, :, columns]

    @pl.when(away)
    def _():
        fill(partner_ref)

    @pl.when(jnp.logical_not(away))
    def _():
        fill(own_ref)


def pack_kernel(facts_ref, own_ref, partner_ref, rows_ref, halo_ref, sems):
    for which, away, at in ((1, EDGE_AWAY, EDGE_SLOT), (0, INNER_AWAY, INNER_SLOT)):
        away, slot = fact(facts_ref, away) > 0, fact(facts_ref, at)

        @pl.when(jnp.logical_not(away))
        def _():
            pltpu.make_async_copy(own_ref.at[slot], rows_ref.at[which], sems.at[which]).start()

        @pl.when(away)
        def _():
            pltpu.make_async_copy(partner_ref.at[slot], rows_ref.at[which], sems.at[which]).start()

    pltpu.make_async_copy(own_ref.at[0], rows_ref.at[1], sems.at[1]).wait()
    heads = halo_ref.shape[1] // (2 * HEAD)
    skipped = rows_ref.shape[2] // (3 * HEAD) - heads
    for head in range(heads):
        first = (skipped + head) * 3 * HEAD + HEAD
        halo_ref[:, head * 2 * HEAD : (head + 1) * 2 * HEAD] = rows_ref[
            1, :, first : first + 2 * HEAD
        ]
    pltpu.make_async_copy(own_ref.at[0], rows_ref.at[0], sems.at[0]).wait()


def attend(heads, load_queries, load_own, load_more, allowed, out_ref, other_ref):
    scaling = math.log2(math.e) / math.sqrt(HEAD)
    contract_last = (((1,), (1,)), ((), ()))
    ones = jnp.ones((2 * out_ref.shape[0], HEAD), jnp.bfloat16)
    odd_core = lax.rem(lax.axis_index("dp"), 2) == 1
    for start in range(0, heads, 2):
        group = min(2, heads - start)
        scores = []
        for head in range(start, start + group):
            queries = load_queries(head)
            pair = []
            for loader in (load_own, load_more):
                pair.append(
                    lax.dot_general(
                        queries, loader(head, 0), contract_last, preferred_element_type=jnp.float32
                    )
                    * scaling
                )
            scores.append(pair)
        weights = []
        for own, more in scores:
            more = jnp.where(allowed, more, big_negative)
            row_max = jnp.max(jnp.maximum(own, more), axis=-1, keepdims=True)
            weights.append(
                jnp.concatenate(
                    [
                        jnp.exp2(own - row_max).astype(jnp.bfloat16),
                        jnp.exp2(more - row_max).astype(jnp.bfloat16),
                    ],
                    axis=1,
                )
            )
        outs = []
        for head in range(start, start + group):
            values = jnp.concatenate([load_own(head, 1), load_more(head, 1)], axis=0)
            sums = jnp.dot(
                weights[head - start],
                jnp.concatenate([values, ones], axis=1),
                preferred_element_type=jnp.float32,
            )
            outs.append(sums[:, :HEAD] / sums[:, HEAD:])
            out_ref[:, head * HEAD : (head + 1) * HEAD] = outs[-1].astype(jnp.bfloat16)
        for pair in range(group // 2):
            at = (start // 2 + pair) * HEAD
            other = jnp.where(odd_core, outs[2 * pair], outs[2 * pair + 1])
            other_ref[:, at : at + HEAD] = other.astype(jnp.bfloat16)


def inner_kernel(facts_ref, rows_ref, out_ref, other_ref):
    allowed = fact(facts_ref, INNER_JOINS) > 0

    def loader(block):
        def get(head, which):
            first = (head * 3 + 1 + which) * HEAD
            return rows_ref[block, :, first : first + HEAD]

        return get

    attend(
        out_ref.shape[1] // HEAD,
        lambda head: loader(0)(head, -1),
        loader(0),
        loader(1),
        allowed,
        out_ref,
        other_ref,
    )


def edge_kernel(first_head, facts_ref, rows_ref, halo_ref, out_ref, other_ref):
    crosses, allowed = fact(facts_ref, CROSSES) > 0, fact(facts_ref, EDGE_JOINS) > 0

    def load_own(head, which):
        first = ((first_head + head) * 3 + 1 + which) * HEAD
        return rows_ref[1, :, first : first + HEAD]

    def load_more(head, which):
        first = ((first_head + head) * 3 + 1 + which) * HEAD
        at = (2 * head + which) * HEAD
        return jnp.where(crosses, halo_ref[:, at : at + HEAD], rows_ref[0, :, first : first + HEAD])

    attend(
        out_ref.shape[1] // HEAD,
        lambda head: load_own(head, -1),
        load_own,
        load_more,
        allowed,
        out_ref,
        other_ref,
    )


def ring_order(lines):
    return list(range(0, lines, 2)) + list(range(1, lines, 2))[::-1]


def shard_places(origins, depth):
    index = lax.axis_index("dp")
    core, side, line = lax.rem(index, 2), lax.rem(index // 2, 2), index // 4
    places = ring_order(lax.axis_size("dp") // 4)
    found = []
    for steps, other_side in origins:
        from_line = line
        for at, place in enumerate(places):
            from_line = jnp.where(line == place, places[at - steps], from_line)
        pair = from_line * 2 + (1 - side if other_side else side)
        columns = [pair * 2 + core, pair * 2 + 1 - core, pair]
        found.append([pl.ds(pl.multiple_of(column * depth, depth), depth) for column in columns])
    return found


def inner_project_kernel(origins, early, inner_ref, their_ref, *rest):
    shard_refs, (total_ref, left_ref, features) = rest[:-3], rest[-3:]
    block = inner_ref.shape[0]
    depth = left_ref.shape[1] // (len(origins) - early)
    for number, (here, _, there) in enumerate(shard_places(origins, depth)):
        ref, at = (features, number) if number < early else (left_ref, number - early)
        ref[:block, at * depth : (at + 1) * depth] = inner_ref[:, here]
        ref[block:, at * depth : (at + 1) * depth] = their_ref[:, there]
    tile = 2 * HEAD
    for first in range(0, total_ref.shape[1], tile):
        columns = slice(first, first + tile)
        weight = jnp.concatenate([ref[:, columns] for ref in shard_refs], axis=0)
        total_ref[:, columns] = jnp.dot(
            features[...], weight, preferred_element_type=jnp.float32
        )


def add_products_kernel(left_ref, inner_total_ref, *rest):
    shard_refs, total_ref = rest[:-1], rest[-1]
    tile = 2 * HEAD
    for first in range(0, total_ref.shape[1], tile):
        columns = slice(first, first + tile)
        weight = jnp.concatenate([ref[:, columns] for ref in shard_refs], axis=0)
        total_ref[:, columns] = inner_total_ref[:, columns] + jnp.dot(
            left_ref[...], weight, preferred_element_type=jnp.float32
        )


def arrange_kernel(origins, parts, inner_ref, *refs):
    edge_refs, their_refs = refs[:parts], refs[parts : 2 * parts]
    out_ref, last_ref, edge_rows, their_rows = refs[2 * parts :]
    for some_refs, held in ((edge_refs, edge_rows), (their_refs, their_rows)):
        first = 0
        for ref in some_refs:
            held[:, first : first + ref.shape[1]] = ref[...]
            first += ref.shape[1]
    block, depth = last_ref.shape[0] // 2, last_ref.shape[1] // 2
    places = shard_places(origins, depth)
    for number, (here, _, there) in enumerate(places[:-1]):
        at = slice(number * depth, (number + 1) * depth)
        out_ref[:block, at] = edge_rows[:, here]
        out_ref[block:, at] = their_rows[:, there]
    for number, here in enumerate(places[-1][:2]):
        at = slice(number * depth, (number + 1) * depth)
        last_ref[:block, at] = inner_ref[:, here]
        last_ref[block:, at] = edge_rows[:, here]


def project_kernel(first, edge_ref, inner_total_ref, *rest):
    shard_refs, (own_total_ref, their_total_ref) = rest[:-2], rest[-2:]
    block = own_total_ref.shape[0] // 2
    tile = 2 * HEAD
    for at in range(0, own_total_ref.shape[1], tile):
        here = slice(at, at + tile)
        columns = slice(first + at, first + at + tile)
        weight = jnp.concatenate([ref[:, columns] for ref in shard_refs], axis=0)
        edge = jnp.dot(edge_ref[...], weight, preferred_element_type=jnp.float32)
        own_total_ref[:block, here] = inner_total_ref[:block, columns]
        own_total_ref[block:, here] = edge[:block]
        their_total_ref[:block, here] = inner_total_ref[block:, columns].astype(jnp.bfloat16)
        their_total_ref[block:, here] = edge[block:].astype(jnp.bfloat16)


def gather_sums_kernel(parts, features_ref, *rest):
    operands, out_ref = rest[:-1], rest[-1]
    shard_refs, sum_refs = operands[: -2 * parts + 1], operands[-2 * parts + 1 :]
    depth = sum(ref.shape[0] for ref in shard_refs)
    first = 0
    for part in range(parts):
        total_ref = sum_refs[part]
        columns = slice(first, first + total_ref.shape[1])
        weight = jnp.concatenate([ref[:, columns] for ref in shard_refs], axis=0)
        total = total_ref[...] + jnp.dot(
            features_ref[:, :depth], weight, preferred_element_type=jnp.float32
        )
        out_ref[:, columns] = total if part == parts - 1 else total + sum_refs[parts + part][...]
        first += total_ref.shape[1]


def finish_kernel(features_ref, total_ref, more_ref, *rest):
    shard_refs, (out_ref, held, sems) = rest[:-3], rest[-3:]
    depth = sum(ref.shape[0] for ref in shard_refs)
    width, late = out_ref.shape[1], more_ref.shape[1]
    block = out_ref.shape[0] // 2
    pieces = sems.shape[1]
    some = block // pieces
    ctx = lax.axis_index("ctx")
    copies = []
    for which, place in ((0, ctx), (1, 1 - ctx)):
        for piece in range(pieces):
            rows = slice(which * block + piece * some, which * block + (piece + 1) * some)
            for first in range(0, width, late):
                columns = slice(first, first + late)
                weight = jnp.concatenate([ref[:, columns] for ref in shard_refs], axis=0)
                total = total_ref[rows, columns] + jnp.dot(
                    features_ref[rows, depth:], weight, preferred_element_type=jnp.float32
                )
                if first + late == width:
                    total = total + more_ref[rows]
                held[rows, columns] = total.astype(jnp.bfloat16)
            there = pl.ds(pl.multiple_of(place * block + piece * some, some), some)
            copies.append(
                pltpu.make_async_copy(held.at[rows], out_ref.at[there], sems.at[which, piece])
            )
            copies[-1].start()
    for copy in copies:
        copy.wait()


SMEM = functools.partial(pl.BlockSpec, memory_space=pltpu.SMEM)
VMEM = functools.partial(pl.BlockSpec, memory_space=pltpu.VMEM)
HBM = functools.partial(pl.BlockSpec, memory_space=pltpu.HBM)


def after(value, *others):
    return lax.optimization_barrier((value, *others))[0]


def body_edge(projections, block_source, clip_ids, out_weight):
    local_rows, row_width = projections.shape
    block_rows = local_rows // 2
    heads = row_width // (3 * HEAD)
    features = heads * HEAD
    depth, width = out_weight.shape
    count = lax.axis_size("dp")
    bf16 = jnp.bfloat16

    def call(kernel, name, shape, in_specs, dtypes=None, scratch=(), out_spec=VMEM()):
        many = isinstance(shape, list)
        shapes = shape if many else [shape]
        dtypes = dtypes or [bf16] * len(shapes)
        shapes = [jax.ShapeDtypeStruct(*one) for one in zip(shapes, dtypes, strict=True)]
        return pl.pallas_call(
            kernel,
            out_shape=shapes if many else shapes[0],
            in_specs=in_specs,
            out_specs=[out_spec] * len(shapes) if many else out_spec,
            scratch_shapes=scratch,
            cost_estimate=pl.CostEstimate(flops=0, bytes_accessed=0, transcendentals=0),
            compiler_params=pltpu.CompilerParams(vmem_limit_bytes=8 * MIB),
            name=name,
        )

    def around(value, step):
        places = ring_order(count // 4)
        moves = [(here, places[(at + step) % len(places)]) for at, here in enumerate(places)]
        return lax.ppermute(
            value, "dp", [(4 * here + rest, 4 * there + rest) for here, there in moves for rest in range(4)]
        )

    def to_side(value):
        return partner(value, "dp", 1)

    def to_core(value):
        return partner(value, "dp", 0)

    def in_hbm(value):
        return pltpu.with_memory_space_constraint(value, pltpu.HBM)

    own = in_hbm(projections.reshape(2, block_rows, row_width))
    shards = {(0, False): [out_weight]}
    from_partner = pltpu.with_memory_space_constraint(to_core(own), pltpu.VMEM)
    ahead = around(out_weight, 1)
    across = to_side(out_weight)
    staged, facts = call(
        stage_kernel,
        "stage",
        [own.shape, (7, 8, 128)],
        [HBM()] * 3,
        dtypes=[bf16, jnp.int32],
        scratch=[
            pltpu.SMEM(block_source.shape, jnp.int32),
            pltpu.SMEM(clip_ids.shape, jnp.int32),
            pltpu.SemaphoreType.DMA((2,)),
            pltpu.SemaphoreType.DMA((2, 4)),
        ],
    )(in_hbm(block_source), in_hbm(clip_ids), own)
    part_heads = [heads * 8 // 16, heads * 8 // 16]
    packed_first = call(
        pack_first_kernel,
        "pack_first",
        (block_rows, 2 * HEAD * part_heads[0]),
        [VMEM()] * 3,
    )(facts, staged, from_partner)
    rows, packed_last = call(
        pack_kernel,
        "pack",
        [(2, block_rows, row_width), (block_rows, 2 * HEAD * part_heads[1])],
        [VMEM()] * 3,
        scratch=[pltpu.SemaphoreType.DMA((2,))],
    )(facts, staged, after(from_partner, packed_first))
    packed = [packed_first, packed_last]
    halos = [lax.ppermute(part, "ctx", [(0, 1), (1, 0)]) for part in packed]

    def edge_rows(part, *before):
        some = part_heads[part]
        return call(
            functools.partial(edge_kernel, sum(part_heads[:part])),
            "edge_rows",
            [(block_rows, some * HEAD), (block_rows, some // 2 * HEAD)],
            [VMEM()] * 3,
        )(after(facts, *before), rows, halos[part])

    back = around(after(out_weight, staged), -1)
    ahead = after(ahead, *packed)
    shards[1, False], shards[0, True] = [ahead], [across]
    second = around(after(ahead, across), 1)
    across = to_side(ahead)
    inner, inner_other = call(
        inner_kernel,
        "inner_rows",
        [(block_rows, features), (block_rows, features // 2)],
        [VMEM()] * 2,
    )(after(facts, ahead), rows)
    theirs = [to_core(inner_other)]

    back = after(back, inner)
    shards[3, False] = [back]
    back_across = to_side(back)
    shards[1, True] = [across]
    early = list(shards)
    origins = [*early, (2, False), (3, True), (2, True)]
    inner_total, inner_left = call(
        functools.partial(inner_project_kernel, origins[:-1], len(early)),
        "inner_project",
        [(local_rows, width), (local_rows, (len(origins) - 1 - len(early)) * depth)],
        [VMEM()] * (2 + len(early)),
        dtypes=[jnp.float32, bf16],
        scratch=[pltpu.VMEM((local_rows, len(early) * depth), bf16)],
    )(inner, *theirs, *[shards[origin][0] for origin in early])
    edges, edge_others = zip(*[edge_rows(part) for part in range(len(part_heads))], strict=True)
    second = after(second, inner_total, edges[0])
    cut = depth // 8 * 5
    shards[2, False] = [second]
    shards[3, True] = [back_across]
    shards[2, True] = [around(after(across, edges[0])[:cut], 1), to_side(second[cut:])]
    theirs = [to_core(part) for part in edge_others]

    more = [shards[origin][0] for origin in origins[len(early) : -1]]
    inner_total = call(
        add_products_kernel,
        "add_products",
        inner_total.shape,
        [VMEM()] * (2 + len(more)),
        dtypes=[jnp.float32],
    )(inner_left, inner_total, *more)
    theirs[-1] = after(theirs[-1], inner_total)
    arranged, last_features = call(
        functools.partial(arrange_kernel, origins, len(edges)),
        "arrange",
        [(local_rows, (len(origins) - 1) * depth), (local_rows, 2 * depth)],
        [VMEM()] * (1 + len(edges) + len(theirs)),
        scratch=[
            pltpu.VMEM((block_rows, features), bf16),
            pltpu.VMEM((block_rows, features // 2), bf16),
        ],
    )(inner, *edges, *theirs)
    last = shards[origins[-1]]
    last_swapped = [to_core(piece) for piece in last]
    pieces = [piece for origin in origins[:-1] for piece in shards[origin]]
    own_totals, mores = [], []
    parts = 3
    for part in range(parts):
        columns = width // parts
        own_total, their_total = call(
            functools.partial(project_kernel, part * columns),
            "project",
            [(local_rows, columns)] * 2,
            [VMEM()] * (2 + len(pieces)),
            dtypes=[jnp.float32, bf16],
        )(arranged, inner_total, *pieces)
        own_totals.append(own_total)
        if part == parts - 1:
            their_total = after(their_total, *last)
        mores.append(to_core(their_total))
    total = call(
        functools.partial(gather_sums_kernel, parts),
        "gather_sums",
        (local_rows, width),
        [VMEM()] * (len(last) + 2 * parts),
        dtypes=[jnp.float32],
    )(last_features, *last, *own_totals, *mores[:-1])
    return call(
        finish_kernel,
        "finish",
        (local_rows, width),
        [VMEM()] * (3 + len(last)),
        scratch=[pltpu.VMEM((local_rows, width), bf16), pltpu.SemaphoreType.DMA((2, 2))],
        out_spec=HBM(),
    )(last_features, total, mores[-1], *last_swapped)


def body(projections, block_source, clip_ids, out_weight):
    heads = projections.shape[1] // (3 * HEAD)
    two_and_two = lax.axis_size("ctx") == 2 and block_source.shape[2] == 2
    whole_tiles = out_weight.shape[0] % HEAD == 0 and heads % 16 == 0
    if two_and_two and whole_tiles and lax.axis_size("dp") == 16:
        return body_edge(projections, block_source, clip_ids, out_weight)
    return body_general(projections, block_source, clip_ids, out_weight)


def solution(mesh):
    return jax.shard_map(
        body,
        mesh=mesh,
        in_specs=(P(("dp", "ctx"), None), P("dp", "ctx", None), P("dp", None), P("dp", None)),
        out_specs=P(("dp", "ctx"), None),
        check_vma=False,
    )
```
